32 devices in a mesh: wide: 8 (over z, x), narrow: 4 (over y, core).
Axes of the slice: x: 2, y: 2, z: 4, core: 2. Of those that a mesh axis runs over, the one named last changes fastest.
Arguments:
- tokens: bfloat16 [4, 2048, 2048], P('narrow', 'wide'), may hold values from -6 to 6
- gain_one: float32 [2048], replicated, may hold values from 0.5 to 1.5
- w_qkv: bfloat16 [2048, 6144], P(('wide', 'narrow')), may hold values from -0.125 to 0.125
- w_out: bfloat16 [2048, 2048], P(('wide', 'narrow')), may hold values from -1 to 1
- gain_two: float32 [2048], replicated, may hold values from 0.5 to 1.5
- bias_two: float32 [2048], replicated, may hold values from -2 to 2
- router: float32 [2048, 4], replicated, may hold values from -0.13258252 to 0.13258252
- w_up: bfloat16 [2048, 8192], P(('wide', 'narrow')), may hold values from -0.125 to 0.125
- w_down: bfloat16 [8192, 2048], P(('wide', 'narrow')), may hold values from -0.125 to 0.125
- doc_split: int32 [4], P('narrow'), may hold values from 1 to 2048, as said below
- head_count: int32 [4, 2], P('narrow'), may hold values from 4 to 16
- width_choice: int32 [4, 2048], P('narrow', 'wide'), may hold values from 0 to 3
- out_grad: bfloat16 [4, 2048, 2048], P('narrow', 'wide'), may hold values from -6 to 6
Outputs:
- block_out: bfloat16 [4, 2048, 2048], P('narrow', 'wide')
- input_grad: float32 [4, 2048, 2048], P('narrow', 'wide')
- qkv_grad: float32 [2048, 6144], P(('wide', 'narrow'))
- out_proj_grad: float32 [2048, 2048], P(('wide', 'narrow'))
- up_grad: float32 [2048, 8192], P(('wide', 'narrow'))
- down_grad: float32 [8192, 2048], P(('wide', 'narrow'))
- gain_one_grad: float32 [2048], replicated
- gain_two_grad: float32 [2048], replicated
- bias_two_grad: float32 [2048], replicated
- router_grad: float32 [2048, 4], replicated
- width_counts: int32 [4], replicated
The draws below stay inside these ranges and needn't reach their ends.
Inputs may be any that keep to these rules, and one draw needn't show every extreme that they name: `doc_split`: in each aligned block of 1 row one row has a value of at most 64 or of more than 1984; the other rows have values from 512 to 2048.
All inputs are finite; a program needn't handle non-finite values.
Results may differ from the reference program's by a relative error of at most 0.03.
Values may be sent and summed in bfloat16 or wider, within the bound.
A program may use at most 576 MiB of HBM per device.

```python
import jax
import jax.numpy as jnp
from jax import lax

D = 2048
HEADS = 16
HEAD_DIM = 128
FF = 8192
WIDTHS = 4
LEN = 2048
ROWS_DEV = 1
ROWS = 4


def draw_doc_split(key, part):
    split_key = jax.random.fold_in(key, 11)
    pick_key = jax.random.fold_in(key, 12)
    edge_key = jax.random.fold_in(key, 13)
    side_key = jax.random.fold_in(key, 14)
    splits = jax.random.randint(split_key, (ROWS,), LEN // 4, LEN + 1, dtype=jnp.int32)
    picked = jax.random.randint(pick_key, (ROWS // ROWS_DEV,), 0, ROWS_DEV, dtype=jnp.int32)
    marked = jnp.arange(ROWS, dtype=jnp.int32) % ROWS_DEV == jnp.repeat(picked, ROWS_DEV)
    near = jax.random.randint(edge_key, (ROWS,), 1, LEN // 32 + 1, dtype=jnp.int32)
    side = jax.random.randint(side_key, (ROWS,), 0, 2, dtype=jnp.int32)
    edge = jnp.where(side == 0, near, LEN + 1 - near)
    return jnp.where(marked, edge, splits).astype(jnp.int32)


def touch_ends(entries, stream_key, least, top_value):
    longest = entries.shape.index(max(entries.shape))
    spots = []
    for shift in (0, 1):
        where = [jax.random.randint(jax.random.fold_in(stream_key, axis), (), 0, length) for axis, length in enumerate(entries.shape)]
        where[longest] = (where[longest] + shift) % entries.shape[longest]
        spots.append(tuple(where))
    return entries.at[spots[0]].set(least).at[spots[1]].set(top_value)


def level_of(key, shape, cuts, least, largest):
    factor_of = 1.0
    for dim, parts in cuts:
        heights = jax.random.uniform(jax.random.fold_in(jax.random.fold_in(key, 6), dim), (parts,), jnp.float32, least / len(cuts), largest / len(cuts))
        factor_of = factor_of * jnp.repeat(jnp.exp(heights), shape[dim] // parts).reshape((-1,) + (1,) * (len(shape) - 1 - dim))
    return factor_of


def centred(key, shape, scale, bound, split=(), kind=jnp.bfloat16):
    factor_of = level_of(key, shape, split, -0.22, 0.18) if split else 1.0
    values = jax.random.normal(key, shape, jnp.float32) * scale * factor_of
    return jnp.minimum(jnp.maximum(values, -bound), bound).astype(kind)


def setup_inputs(seed: int = 0) -> dict:
    seeds = jax.random.split(jax.random.key(seed), 14)
    tokens = centred(seeds[0], (ROWS, LEN, D), 1.0, 6.0, ((0, 4), (1, 8)))
    gain_one = jnp.clip(1.0 + 0.1 * jax.random.normal(seeds[1], (D,), jnp.float32), 0.5, 1.5)
    w_qkv = centred(seeds[2], (D, 3 * D), D ** -0.5, 0.125, ((0, 32),))
    w_out = centred(seeds[3], (D, D), (D // 64) ** -0.5, 1.0, ((0, 32),))
    gain_two = jnp.clip(1.0 + 0.1 * jax.random.normal(seeds[4], (D,), jnp.float32), 0.5, 1.5)
    bias_two = centred(seeds[5], (D,), 0.3, 2.0, (), jnp.float32)
    router = centred(seeds[6], (D, WIDTHS), (0.75 / D ** 0.5), 0.13258252, (), jnp.float32)
    w_up = centred(seeds[7], (D, FF), D ** -0.5, 0.125, ((0, 32),))
    w_down = centred(seeds[8], (FF, D), (FF // 4) ** -0.5, 0.125, ((0, 32),))
    doc_split = draw_doc_split(jax.random.fold_in(seeds[13], 71), 0)
    head_count = touch_ends(jax.random.randint(seeds[10], (ROWS, 2), max(1, HEADS // 4), HEADS + 1), jax.random.fold_in(seeds[10], 1), max(1, HEADS // 4), HEADS).astype(jnp.int32)
    width_choice = touch_ends(jax.random.randint(seeds[11], (ROWS, LEN), 0, WIDTHS), jax.random.fold_in(seeds[11], 1), 0, WIDTHS - 1).astype(jnp.int32)
    out_grad = centred(seeds[12], (ROWS, LEN, D), 1.0, 6.0, ((0, 4), (1, 8)))
    return dict(tokens=tokens, gain_one=gain_one, w_qkv=w_qkv, w_out=w_out, gain_two=gain_two, bias_two=bias_two, router=router, w_up=w_up, w_down=w_down, doc_split=doc_split, head_count=head_count, width_choice=width_choice, out_grad=out_grad)


@jax.custom_vjp
def low(v):
    return lax.optimization_barrier(v.astype(jnp.bfloat16)).astype(jnp.float32)

@jax.custom_vjp
def low_back(v):
    return v

def low_keep(v):
    return (low(v), None)

def low_pass(kept, grad):
    return (grad,)

def back_keep(v):
    return (v, None)

def back_low(kept, grad):
    return (low(grad),)
low.defvjp(low_keep, low_pass)
low_back.defvjp(back_keep, back_low)
highest = lax.Precision.HIGHEST
norm_eps = 1e-05
rope_base = 10000.0
masked_score = -1e+30

def rotary_tables(positions, head_size):
    half_size = head_size // 2
    exponent = jnp.arange(half_size, dtype=jnp.float32) * (2.0 / head_size)
    frequency = jnp.power(rope_base, -exponent)
    angles = positions.astype(jnp.float32)[:, None] * frequency[None, :]
    return (jnp.cos(angles), jnp.sin(angles))

def rotate(values, cosine, sine):
    half_size = values.shape[-1] // 2
    cos_part = cosine[:, None, :]
    sin_part = sine[:, None, :]
    lower = values[..., :half_size]
    upper = values[..., half_size:]
    return jnp.concatenate([lower * cos_part - upper * sin_part, upper * cos_part + lower * sin_part], axis=-1)

def attend_row(packed):
    queries, keys, values, documents = packed
    length = keys.shape[0]
    block_rows = min(512, length)
    positions = jnp.arange(length, dtype=jnp.int32)
    scale = keys.shape[-1] ** (-0.5)

    def one_block(block_index):
        offset = block_index * block_rows
        query_block = lax.dynamic_slice_in_dim(queries, offset, block_rows, 0)
        query_pos = offset + jnp.arange(block_rows, dtype=jnp.int32)
        query_doc = lax.dynamic_slice_in_dim(documents, offset, block_rows, 0)
        scores = low_back(jnp.einsum('qhe,khe->hqk', query_block, keys, precision=highest) * scale)
        allowed = (positions[None, :] <= query_pos[:, None]) & (documents[None, :] == query_doc[:, None])
        scores = jnp.where(allowed[None], scores, masked_score)
        row_max = lax.optimization_barrier(jnp.max(scores, axis=-1, keepdims=True))
        weights = jnp.exp(scores - row_max)
        chance = low(weights / lax.optimization_barrier(jnp.sum(weights, axis=-1, keepdims=True)))
        return jnp.einsum('hqk,khe->qhe', chance, values, precision=highest)
    blocks = lax.map(jax.checkpoint(one_block), jnp.arange(length // block_rows, dtype=jnp.int32))
    return blocks.reshape(queries.shape)

def reference(tokens, gain_one, w_qkv, w_out, gain_two, bias_two, router, w_up, w_down, doc_split, head_count, width_choice, out_grad):
    positions = jnp.arange(LEN, dtype=jnp.int32)
    documents = (positions[None, :] >= doc_split[:, None]).astype(jnp.int32)
    head_limit = jnp.where(documents == 0, head_count[:, 0:1], head_count[:, 1:2])
    active = (jnp.arange(HEADS, dtype=jnp.int32)[None, None, :] < head_limit[:, :, None]).astype(jnp.float32)
    width_onehot = (width_choice[:, :, None] == jnp.arange(WIDTHS, dtype=jnp.int32)[None, None, :]).astype(jnp.float32)
    column_block = jnp.arange(FF, dtype=jnp.int32) // (FF // WIDTHS)
    column_mask = (column_block[None, None, :] <= width_choice[:, :, None]).astype(jnp.float32)
    cosine, sine = rotary_tables(positions, HEAD_DIM)

    def forward(inputs, gain_a, qkv_weight, out_weight, gain_b, bias_b, router_weight, up_weight, down_weight):
        inv_one = lax.rsqrt(lax.optimization_barrier(jnp.mean(inputs * inputs, axis=-1, keepdims=True)) + norm_eps)
        act_one = low(inputs * inv_one * gain_a)
        projected = low_back(jnp.einsum('rld,de->rle', act_one, qkv_weight, precision=highest))
        split_qkv = projected.reshape(ROWS, LEN, 3, HEADS, HEAD_DIM)
        queries = low(rotate(split_qkv[:, :, 0], cosine, sine))
        keys = low(rotate(split_qkv[:, :, 1], cosine, sine))
        values = low(split_qkv[:, :, 2])
        attended = lax.map(jax.checkpoint(attend_row), (queries, keys, values, documents))
        att_low = low_back(low(attended * active[..., None])).reshape(ROWS, LEN, D)
        branch = low_back(jnp.einsum('rld,de->rle', att_low, out_weight, precision=highest))
        x_one = inputs + branch
        center = x_one - lax.optimization_barrier(jnp.mean(x_one, axis=-1, keepdims=True))
        inv_two = lax.rsqrt(lax.optimization_barrier(jnp.mean(center * center, axis=-1, keepdims=True)) + norm_eps)
        ln_out = center * inv_two * gain_b + bias_b
        logits = jnp.einsum('rld,dw->rlw', ln_out, router_weight, precision=highest)
        chosen = lax.optimization_barrier(jnp.sum(jax.nn.softmax(logits, axis=-1) * width_onehot, axis=-1))
        act_two = low(ln_out)
        pre = low_back(jnp.einsum('rld,df->rlf', act_two, up_weight, precision=highest))
        hidden = low(jnp.square(jnp.maximum(pre, 0.0)) * column_mask)
        mixed = low_back(jnp.einsum('rlf,fd->rld', hidden, down_weight, precision=highest))
        return x_one + mixed * chosen[..., None]
    floats = (tokens.astype(jnp.float32), gain_one, w_qkv.astype(jnp.float32), w_out.astype(jnp.float32), gain_two, bias_two, router, w_up.astype(jnp.float32), w_down.astype(jnp.float32))
    result, pullback = jax.vjp(forward, *floats)
    grads = pullback(out_grad.astype(jnp.float32))
    counts = lax.optimization_barrier(jnp.sum((width_choice[:, :, None] == jnp.arange(WIDTHS, dtype=jnp.int32)[None, None, :]).astype(jnp.int32), axis=(0, 1)))
    return (result.astype(jnp.bfloat16), grads[0], grads[2], grads[3], grads[7], grads[8], grads[1], grads[4], grads[5], grads[6], counts)
```

```python
import functools

import jax
import jax.numpy as jnp
from jax import lax
from jax.experimental import pallas as pl
from jax.experimental.pallas import tpu as pltpu
from jax.sharding import PartitionSpec as P

HEAD_DIM = 128
WIDTHS = 4
BLOCK = 512

highest = lax.Precision.HIGHEST
norm_eps = 1e-05
rope_base = 10000.0
masked_score = -1e30
f32 = jnp.float32
bf16 = jnp.bfloat16


def dot(a, b, contract):
    return lax.dot_general(a, b, (contract, ((), ())), preferred_element_type=f32)


def turn(u, cos2, sin2):
    return u * cos2 + pltpu.roll(u, HEAD_DIM // 2, 1) * sin2


def first_key(split, row):
    return jnp.where(row >= split, split, 0)


def attend_kernel(heads, length, split_ref, limit_ref, proj_ref, cos_ref, sin_ref, qkv_ref, att_ref, low_ref, lse_ref):
    row = pl.program_id(0)
    split = split_ref[row]
    scale = HEAD_DIM ** (-0.5)
    block = min(BLOCK, length)
    blocks = length // block
    width = heads * HEAD_DIM

    def rotate_block(i, carry):
        rows = pl.ds(pl.multiple_of(i * block, block), block)
        cos2 = cos_ref[rows, :]
        sin2 = sin_ref[rows, :]
        for part in range(2 * heads):
            cols = pl.ds(part * HEAD_DIM, HEAD_DIM)
            qkv_ref[rows, cols] = turn(proj_ref[rows, cols], cos2, sin2).astype(bf16)
        cols = pl.ds(2 * width, width)
        qkv_ref[rows, cols] = proj_ref[rows, cols].astype(bf16)
        return carry

    lax.fori_loop(0, blocks, rotate_block, 0)
    for h in range(heads):
        qcol = pl.ds(h * HEAD_DIM, HEAD_DIM)
        kcol = pl.ds(width + h * HEAD_DIM, HEAD_DIM)
        vcol = pl.ds(2 * width + h * HEAD_DIM, HEAD_DIM)

        def query_block(i, carry):
            rows = pl.ds(pl.multiple_of(i * block, block), block)
            q = qkv_ref[rows, qcol]
            at = i * block + lax.broadcasted_iota(jnp.int32, (block, 1), 0)
            low = first_key(split, at)

            def key_block(j, state):
                top, total, acc = state
                keys = pl.ds(pl.multiple_of(j * block, block), block)
                s = dot(q, qkv_ref[keys, kcol], ((1,), (1,))) * scale
                kat = j * block + lax.broadcasted_iota(jnp.int32, (block, block), 1)
                ok = (kat <= at) & (kat >= low)
                s = jnp.where(ok, s, masked_score)
                new_top = jnp.maximum(top, jnp.max(s, axis=1, keepdims=True))
                p = jnp.where(ok, jnp.exp(s - new_top), 0.0)
                fade = jnp.exp(top - new_top)
                total = total * fade + jnp.sum(p, axis=1, keepdims=True)
                acc = acc * fade + dot(p.astype(bf16), qkv_ref[keys, vcol], ((1,), (0,)))
                return new_top, total, acc

            start = jnp.where(i * block >= split, split // block, 0)
            top, total, acc = lax.fori_loop(
                start,
                i + 1,
                key_block,
                (
                    jnp.full((block, 1), masked_score, f32),
                    jnp.zeros((block, 1), f32),
                    jnp.zeros((block, HEAD_DIM), f32),
                ),
            )
            att = acc / total
            limit = jnp.where(at < split, limit_ref[row, 0], limit_ref[row, 1])
            active = (limit_ref[row, 2] + h < limit).astype(f32)
            att_ref[rows, qcol] = att
            low_ref[rows, qcol] = (att * active).astype(bf16)
            lse_ref[rows, qcol] = jnp.broadcast_to(top + jnp.log(total), (block, HEAD_DIM))
            return carry

        lax.fori_loop(0, blocks, query_block, 0)


def attend(proj, split, limits, cos2, sin2, heads):
    rows, length, _ = proj.shape
    width = heads * HEAD_DIM
    smem = pl.BlockSpec(memory_space=pltpu.SMEM)
    table = pl.BlockSpec((length, HEAD_DIM), lambda r: (0, 0))

    def whole(cols):
        return pl.BlockSpec((None, length, cols), lambda r: (r, 0, 0))

    flops = rows * heads * 4 * length * length * HEAD_DIM
    return pl.pallas_call(
        functools.partial(attend_kernel, heads, length),
        grid=(rows,),
        in_specs=[smem, smem, whole(3 * width), table, table],
        out_specs=[whole(3 * width), whole(width), whole(width), whole(width)],
        out_shape=[
            jax.ShapeDtypeStruct((rows, length, 3 * width), bf16),
            jax.ShapeDtypeStruct((rows, length, width), f32),
            jax.ShapeDtypeStruct((rows, length, width), bf16),
            jax.ShapeDtypeStruct((rows, length, width), f32),
        ],
        compiler_params=pltpu.CompilerParams(vmem_limit_bytes=56 * 2**20),
        cost_estimate=pl.CostEstimate(flops=flops, bytes_accessed=2**24, transcendentals=flops // 512),
    )(split, limits, proj, cos2, sin2)


def attend_back_kernel(heads, length, split_ref, limit_ref, qkv_ref, att_ref, lse_ref, dat_ref, cos_ref, sin_ref, dproj_ref, datt_ref, delta_ref, dq_ref):
    row = pl.program_id(0)
    split = split_ref[row]
    scale = HEAD_DIM ** (-0.5)
    block = min(BLOCK, length)
    blocks = length // block
    width = heads * HEAD_DIM
    for h in range(heads):
        qcol = pl.ds(h * HEAD_DIM, HEAD_DIM)
        kcol = pl.ds(width + h * HEAD_DIM, HEAD_DIM)
        vcol = pl.ds(2 * width + h * HEAD_DIM, HEAD_DIM)

        def prepare(i, carry):
            rows = pl.ds(pl.multiple_of(i * block, block), block)
            at = i * block + lax.broadcasted_iota(jnp.int32, (block, 1), 0)
            limit = jnp.where(at < split, limit_ref[row, 0], limit_ref[row, 1])
            active = (limit_ref[row, 2] + h < limit).astype(f32)
            datt = dat_ref[rows, qcol].astype(f32) * active
            datt_ref[rows, :] = datt.astype(bf16)
            delta = jnp.sum(datt * att_ref[rows, qcol], axis=1, keepdims=True)
            delta_ref[rows, :] = jnp.broadcast_to(delta, (block, HEAD_DIM))
            dq_ref[rows, :] = jnp.zeros((block, HEAD_DIM), f32)
            return carry

        lax.fori_loop(0, blocks, prepare, 0)

        def key_block(j, carry):
            keys = pl.ds(pl.multiple_of(j * block, block), block)
            k = qkv_ref[keys, kcol]
            v = qkv_ref[keys, vcol]
            kat = j * block + lax.broadcasted_iota(jnp.int32, (block, block), 1)

            def query_block(i, state):
                dk, dv = state
                rows = pl.ds(pl.multiple_of(i * block, block), block)
                q = qkv_ref[rows, qcol]
                datt = datt_ref[rows, :]
                at = i * block + lax.broadcasted_iota(jnp.int32, (block, 1), 0)
                low = first_key(split, at)
                ok = (kat <= at) & (kat >= low)
                s = dot(q, k, ((1,), (1,))) * scale
                lse = lse_ref[rows, qcol][:, :1]
                p = jnp.where(ok, jnp.exp(s - lse), 0.0)
                dp = dot(datt, v, ((1,), (1,)))
                ds = (p * (dp - delta_ref[rows, :][:, :1])).astype(bf16)
                dv = dv + dot(p.astype(bf16), datt, ((0,), (0,)))
                dk = dk + dot(ds, q, ((0,), (0,)))
                dq_ref[rows, :] += dot(ds, k, ((1,), (0,)))
                return dk, dv

            stop = jnp.where((j + 1) * block <= split, (split - 1) // block + 1, blocks)
            zero = jnp.zeros((block, HEAD_DIM), f32)
            dk, dv = lax.fori_loop(j, stop, query_block, (zero, zero))
            dproj_ref[keys, kcol] = turn(dk * scale, cos_ref[keys, :], -sin_ref[keys, :]).astype(bf16)
            dproj_ref[keys, vcol] = dv.astype(bf16)
            return carry

        lax.fori_loop(0, blocks, key_block, 0)

        def finish(i, carry):
            rows = pl.ds(pl.multiple_of(i * block, block), block)
            dq = dq_ref[rows, :] * scale
            dproj_ref[rows, qcol] = turn(dq, cos_ref[rows, :], -sin_ref[rows, :]).astype(bf16)
            return carry

        lax.fori_loop(0, blocks, finish, 0)


def attend_back(qkv, att, lse, dat, split, limits, cos2, sin2, heads):
    rows, length, _ = qkv.shape
    width = heads * HEAD_DIM
    smem = pl.BlockSpec(memory_space=pltpu.SMEM)
    table = pl.BlockSpec((length, HEAD_DIM), lambda r: (0, 0))

    def whole(cols):
        return pl.BlockSpec((None, length, cols), lambda r: (r, 0, 0))

    flops = rows * heads * 10 * length * length * HEAD_DIM
    return pl.pallas_call(
        functools.partial(attend_back_kernel, heads, length),
        grid=(rows,),
        in_specs=[smem, smem, whole(3 * width), whole(width), whole(width), whole(width), table, table],
        out_specs=whole(3 * width),
        out_shape=jax.ShapeDtypeStruct((rows, length, 3 * width), bf16),
        scratch_shapes=[
            pltpu.VMEM((length, HEAD_DIM), bf16),
            pltpu.VMEM((length, HEAD_DIM), f32),
            pltpu.VMEM((length, HEAD_DIM), f32),
        ],
        compiler_params=pltpu.CompilerParams(vmem_limit_bytes=56 * 2**20),
        cost_estimate=pl.CostEstimate(flops=flops, bytes_accessed=2**24, transcendentals=flops // 1280),
    )(split, limits, qkv, att, lse, dat, cos2, sin2)


class Ring:
    def __init__(self, axis, size):
        self.axis = axis
        self.size = size
        self.order = list(range(0, size, 2)) + list(range(1, size, 2))[::-1]
        place = {w: p for p, w in enumerate(self.order)}
        self.right = [(w, self.order[(place[w] + 1) % size]) for w in range(size)]
        self.left = [(w, self.order[(place[w] - 1) % size]) for w in range(size)]
        self.places = [place[w] for w in range(size)]

    def at(self, shift):
        here = jnp.array(self.places, jnp.int32)[lax.axis_index(self.axis)]
        return jnp.array(self.order, jnp.int32)[(here + shift) % self.size]

    def gather(self, part):
        found = [(self.at(0), part)]
        onward, back = part, part
        half = self.size // 2
        for step in range(1, half):
            onward = lax.ppermute(onward, self.axis, self.right)
            back = lax.ppermute(back, self.axis, self.left)
            found += [(self.at(-step), onward), (self.at(step), back)]
        cut = part.shape[0] // 2
        first = lax.ppermute(onward[:cut], self.axis, self.right)
        second = lax.ppermute(back[cut:], self.axis, self.left)
        found.append((self.at(half), jnp.concatenate([first, second], axis=0)))
        return found

    def gather_rows(self, part):
        rows = part.shape[0]
        whole = jnp.zeros((self.size * rows,) + part.shape[1:], part.dtype)
        for owner, piece in self.gather(part):
            whole = lax.dynamic_update_slice_in_dim(whole, piece, owner * rows, 0)
        return whole

    def scatter(self, term):
        sums = [term(self.at(-1), 0), term(self.at(1), 1)]
        for step in range(2, self.size + 1):
            for side, perm, sign in ((0, self.right, -1), (1, self.left, 1)):
                come = lax.ppermute(sums[side].astype(bf16), self.axis, perm)
                sums[side] = come.astype(f32) + term(self.at(sign * step), side)
        return sums


def swap(array, axis, size, bits):
    return lax.ppermute(array, axis, [(i, i ^ bits) for i in range(size)])


def on_device(
    wide,
    narrow,
    tokens,
    gain_one,
    w_qkv,
    w_out,
    gain_two,
    bias_two,
    router,
    w_up,
    w_down,
    doc_split,
    head_count,
    width_choice,
    out_grad,
):
    rows, part_len, dim = tokens.shape
    length = part_len * wide
    heads = dim // HEAD_DIM
    hidden = w_up.shape[1]
    head_groups = wide if heads % wide == 0 else heads
    row_groups = wide // head_groups
    my_heads = heads // head_groups
    my_rows = rows // row_groups
    cols = my_heads * HEAD_DIM
    count = rows * part_len
    w_at = lax.axis_index("wide")
    n_at = lax.axis_index("narrow")
    head_at = w_at % head_groups
    row_at = (w_at // head_groups) * my_rows
    ring = Ring("wide", wide)
    slots = (0, 2, 1, 3)

    def pick_rows(array):
        return lax.dynamic_slice_in_dim(array, row_at, my_rows, 0) if row_groups > 1 else array

    def put_rows(array):
        if row_groups == 1:
            return array
        whole = jnp.zeros((rows,) + array.shape[1:], array.dtype)
        return lax.dynamic_update_slice_in_dim(whole, array, row_at, 0)

    def narrow_gather(part):
        other = swap(part, "narrow", narrow, 2)
        both = jnp.stack([part, other])
        return jnp.concatenate([both, swap(both, "narrow", narrow, 1)])

    def narrow_scatter(terms):
        come = swap(terms[2:].astype(bf16), "narrow", narrow, 1)
        pair = terms[:2] + come.astype(f32)
        return pair[0] + swap(pair[1].astype(bf16), "narrow", narrow, 2).astype(f32)

    def in_order(parts):
        whole = jnp.zeros(parts.shape, parts.dtype)
        for place, slot in enumerate(slots):
            whole = lax.dynamic_update_slice_in_dim(whole, parts[place : place + 1], n_at ^ slot, 0)
        return whole

    def out_of_order(whole):
        return jnp.concatenate([lax.dynamic_slice_in_dim(whole, n_at ^ slot, 1, 0) for slot in slots])

    def narrow_all_to_all(blocks):
        return lax.all_to_all(blocks, "narrow", 0, 0, tiled=True)

    exponent = jnp.arange(HEAD_DIM // 2, dtype=f32) * (2.0 / HEAD_DIM)
    angles = jnp.arange(length, dtype=f32)[:, None] * jnp.power(rope_base, -exponent)[None, :]
    cosine, sine = jnp.cos(angles), jnp.sin(angles)
    cos2 = jnp.concatenate([cosine, cosine], axis=1)
    sin2 = jnp.concatenate([-sine, sine], axis=1)
    split = pick_rows(doc_split)
    limits = jnp.concatenate(
        [pick_rows(head_count), jnp.full((my_rows, 1), head_at * my_heads, jnp.int32)], axis=1
    )

    inputs = tokens.astype(f32)
    inv_one = lax.rsqrt(jnp.mean(inputs * inputs, axis=-1, keepdims=True) + norm_eps)
    normed_one = inputs * inv_one
    act_one = (normed_one * gain_one).astype(bf16)

    shard = w_qkv.shape[0]
    blocks = w_qkv.reshape(shard, 3, head_groups, cols).transpose(2, 0, 1, 3)
    blocks = jnp.tile(blocks.reshape(head_groups, shard, 3 * cols), (row_groups, 1, 1))
    blocks = lax.all_to_all(blocks, "wide", 0, 0, tiled=True)
    my_qkv = in_order(narrow_gather(blocks)).transpose(1, 0, 2, 3).reshape(dim, 3 * cols)

    act_all = jnp.zeros((my_rows, length, dim), bf16)
    for owner, piece in ring.gather(act_one.transpose(1, 0, 2)):
        piece = pick_rows(piece.transpose(1, 0, 2))
        act_all = lax.dynamic_update_slice_in_dim(act_all, piece, owner * part_len, 1)
    act_flat = act_all.reshape(my_rows * length, dim)
    proj = dot(act_flat, my_qkv, ((1,), (0,))).reshape(my_rows, length, 3 * cols)
    qkv, att, att_part, lse = attend(proj, split, limits, cos2, sin2, my_heads)

    sends = att_part.reshape(my_rows, wide, part_len, cols).transpose(1, 0, 2, 3)
    come = lax.all_to_all(sends, "wide", 0, 0, tiled=True)
    come = come.reshape(row_groups, head_groups, my_rows, part_len, cols)
    att_low = come.transpose(0, 2, 3, 1, 4).reshape(count, dim)
    out_full = lax.all_gather(w_out, ("wide", "narrow"), axis=0, tiled=True)
    x_one = inputs.reshape(count, dim) + dot(att_low, out_full, ((1,), (0,)))

    center = x_one - jnp.mean(x_one, axis=-1, keepdims=True)
    inv_two = lax.rsqrt(jnp.mean(center * center, axis=-1, keepdims=True) + norm_eps)
    normed_two = center * inv_two
    ln_out = normed_two * gain_two + bias_two
    width_flat = width_choice.reshape(count)
    onehot = (width_flat[:, None] == jnp.arange(WIDTHS, dtype=jnp.int32)[None, :]).astype(f32)
    router_prob = jax.nn.softmax(jnp.dot(ln_out, router, precision=highest), axis=-1)
    chosen = jnp.sum(router_prob * onehot, axis=-1)
    act_two = ln_out.astype(bf16)
    grad_top = out_grad.reshape(count, dim).astype(f32)

    piece_rows = w_down.shape[0]
    up_blocks = w_up.reshape(shard, wide, narrow, piece_rows).transpose(2, 0, 1, 3)
    up_part = narrow_all_to_all(up_blocks.reshape(narrow, shard, wide * piece_rows))
    up_mine = ring.gather_rows(up_part.reshape(narrow * shard, wide * piece_rows))
    down_mine = ring.gather_rows(w_down)
    top_all = narrow_gather(out_grad.reshape(count, dim)).reshape(narrow * count, dim)
    facts = narrow_gather(jnp.stack([chosen, width_flat.astype(f32)]))
    chosen_all = facts[:, 0].reshape(narrow * count, 1)
    width_all = facts[:, 1].reshape(narrow * count, 1)
    act_many = narrow_gather(act_two).reshape(narrow * count, dim)
    units = (jnp.arange(wide, dtype=jnp.int32)[:, None] * narrow + n_at) * piece_rows
    units = (units + jnp.arange(piece_rows, dtype=jnp.int32)[None, :]).reshape(-1)
    need = (units // (hidden // WIDTHS)).astype(f32)
    mask = need[None, :] <= width_all

    pre = jnp.maximum(dot(act_many, up_mine, ((1,), (0,))), 0.0)
    pre = jnp.where(mask, pre, 0.0)
    hid = (pre * pre).astype(bf16)
    dmix = (top_all.astype(f32) * chosen_all).astype(bf16)
    mixed = dot(hid, down_mine, ((1,), (0,)))
    dhid = dot(dmix, down_mine, ((1,), (1,)))
    dpre = (dhid * 2.0 * pre).astype(bf16)
    dact = dot(dpre, up_mine, ((1,), (1,)))
    mixed = narrow_scatter(mixed.reshape(narrow, count, dim))
    grad_act_two = narrow_scatter(dact.reshape(narrow, count, dim))

    half = dim // 2

    def up_term(owner, side):
        rows_of = lax.dynamic_slice_in_dim(act_many, owner * (narrow * shard), narrow * shard, 1)
        wide_half = dpre.shape[1] // 2
        return dot(rows_of, dpre[:, side * wide_half : (side + 1) * wide_half], ((0,), (0,)))

    def down_term(owner, side):
        rows_of = lax.dynamic_slice_in_dim(hid, owner * piece_rows, piece_rows, 1)
        return dot(rows_of, dmix[:, side * half : (side + 1) * half], ((0,), (0,)))

    down_grad = jnp.concatenate(ring.scatter(down_term), axis=1)
    up_sum = jnp.concatenate(ring.scatter(up_term), axis=1).astype(bf16)
    up_sum = narrow_all_to_all(up_sum.reshape(narrow, shard, wide * piece_rows))
    up_grad = up_sum.reshape(narrow, shard, wide, piece_rows).transpose(1, 2, 0, 3)
    up_grad = up_grad.reshape(shard, hidden).astype(f32)

    block_out = (x_one + mixed * chosen[:, None]).astype(bf16)
    grad_prob = jnp.sum(grad_top * mixed, axis=-1)
    grad_logits = (grad_prob * chosen)[:, None] * (onehot - router_prob)
    grad_router = lax.dot_general(ln_out, grad_logits, (((0,), (0,)), ((), ())), precision=highest)
    grad_ln = grad_act_two + jnp.dot(grad_logits, router.T, precision=highest)
    grad_gain_two = jnp.sum(grad_ln * normed_two, axis=0)
    grad_bias_two = jnp.sum(grad_ln, axis=0)
    grad_normed = grad_ln * gain_two
    grad_x_one = grad_top + inv_two * (
        grad_normed
        - jnp.mean(grad_normed, axis=-1, keepdims=True)
        - normed_two * jnp.mean(grad_normed * normed_two, axis=-1, keepdims=True)
    )

    grad_branch = grad_x_one.astype(bf16)
    grad_att = dot(grad_branch, out_full, ((1,), (1,))).astype(bf16)
    sends = grad_att.reshape(row_groups, my_rows, part_len, head_groups, cols)
    sends = sends.transpose(0, 3, 1, 2, 4).reshape(wide, my_rows, part_len, cols)
    come = lax.all_to_all(sends, "wide", 0, 0, tiled=True)
    dat = come.transpose(1, 0, 2, 3).reshape(my_rows, length, cols)
    dproj = attend_back(qkv, att, lse, dat, split, limits, cos2, sin2, my_heads)
    grad_out = dot(att_low, grad_branch, ((0,), (0,))).astype(bf16)
    out_proj_grad = lax.psum_scatter(
        grad_out, ("wide", "narrow"), scatter_dimension=0, tiled=True
    ).astype(f32)

    def one_term(owner, side):
        rows_of = lax.dynamic_slice_in_dim(dproj, owner * part_len, part_len, 1)
        rows_of = rows_of.reshape(my_rows * part_len, 3 * cols)
        term = dot(rows_of, my_qkv[side * half : (side + 1) * half], ((1,), (1,)))
        return put_rows(term.reshape(my_rows, part_len, half)).reshape(count, half)

    grad_act_one = jnp.concatenate(ring.scatter(one_term), axis=1)

    grad_qkv = dot(act_flat, dproj.reshape(my_rows * length, 3 * cols), ((0,), (0,)))
    grad_qkv = grad_qkv.reshape(wide, narrow, shard, 3 * cols).transpose(1, 0, 2, 3)
    grad_qkv = narrow_scatter(out_of_order(grad_qkv)).astype(bf16)
    grad_qkv = lax.all_to_all(grad_qkv, "wide", 0, 0, tiled=True).astype(f32)
    grad_qkv = jnp.sum(grad_qkv.reshape(row_groups, head_groups, shard, 3, cols), axis=0)
    qkv_grad = grad_qkv.transpose(1, 2, 0, 3).reshape(shard, 3 * dim)

    normed_flat = normed_one.reshape(count, dim)
    grad_gain_one = jnp.sum(grad_act_one * normed_flat, axis=0)
    grad_scaled = grad_act_one * gain_one
    input_grad = grad_x_one + inv_one.reshape(count, 1) * (
        grad_scaled - normed_flat * jnp.mean(grad_scaled * normed_flat, axis=-1, keepdims=True)
    )
    router_grad, gain_one_grad, gain_two_grad, bias_two_grad, counts_all = lax.psum(
        (grad_router, grad_gain_one, grad_gain_two, grad_bias_two, jnp.sum(onehot, axis=0)),
        ("wide", "narrow"),
    )
    return (
        block_out.reshape(rows, part_len, dim),
        input_grad.reshape(rows, part_len, dim),
        qkv_grad,
        out_proj_grad,
        up_grad,
        down_grad,
        gain_one_grad,
        gain_two_grad,
        bias_two_grad,
        router_grad,
        counts_all.astype(jnp.int32),
    )


def solution(mesh):
    in_specs = (
        P("narrow", "wide", None),
        P(),
        P(("wide", "narrow"), None),
        P(("wide", "narrow"), None),
        P(),
        P(),
        P(),
        P(("wide", "narrow"), None),
        P(("wide", "narrow"), None),
        P("narrow"),
        P("narrow", None),
        P("narrow", "wide"),
        P("narrow", "wide", None),
    )
    out_specs = (
        P("narrow", "wide", None),
        P("narrow", "wide", None),
        P(("wide", "narrow"), None),
        P(("wide", "narrow"), None),
        P(("wide", "narrow"), None),
        P(("wide", "narrow"), None),
        P(),
        P(),
        P(),
        P(),
        P(),
    )
    step = functools.partial(on_device, mesh.shape["wide"], mesh.shape["narrow"])
    return jax.shard_map(step, mesh=mesh, in_specs=in_specs, out_specs=out_specs, check_vma=False)
```

```python
import functools

import jax
import jax.numpy as jnp
from jax import lax
from jax.experimental import pallas as pl
from jax.experimental.pallas import tpu as pltpu
from jax.sharding import PartitionSpec as P

HEAD_DIM = 128
WIDTHS = 4
BLOCK = 512

highest = lax.Precision.HIGHEST
norm_eps = 1e-05
rope_base = 10000.0
masked_score = -1e30
f32 = jnp.float32
bf16 = jnp.bfloat16


def dot(a, b, contract):
    return lax.dot_general(a, b, (contract, ((), ())), preferred_element_type=f32)


def turn(u, cos2, sin2):
    return u * cos2 + pltpu.roll(u, HEAD_DIM // 2, 1) * sin2


def first_key(split, row):
    return jnp.where(row >= split, split, 0)


def attend_kernel(heads, length, split_ref, limit_ref, proj_ref, cos_ref, sin_ref, qkv_ref, att_ref, low_ref, lse_ref):
    row = pl.program_id(0)
    split = split_ref[row]
    scale = HEAD_DIM ** (-0.5)
    block = min(BLOCK, length)
    blocks = length // block
    width = heads * HEAD_DIM

    def rotate_block(i, carry):
        rows = pl.ds(pl.multiple_of(i * block, block), block)
        cos2 = cos_ref[rows, :]
        sin2 = sin_ref[rows, :]
        for part in range(2 * heads):
            cols = pl.ds(part * HEAD_DIM, HEAD_DIM)
            qkv_ref[rows, cols] = turn(proj_ref[rows, cols], cos2, sin2).astype(bf16)
        cols = pl.ds(2 * width, width)
        qkv_ref[rows, cols] = proj_ref[rows, cols].astype(bf16)
        return carry

    lax.fori_loop(0, blocks, rotate_block, 0)
    for h in range(heads):
        qcol = pl.ds(h * HEAD_DIM, HEAD_DIM)
        kcol = pl.ds(width + h * HEAD_DIM, HEAD_DIM)
        vcol = pl.ds(2 * width + h * HEAD_DIM, HEAD_DIM)

        def query_block(i, carry):
            rows = pl.ds(pl.multiple_of(i * block, block), block)
            q = qkv_ref[rows, qcol]
            at = i * block + lax.broadcasted_iota(jnp.int32, (block, 1), 0)
            low = first_key(split, at)

            def key_block(j, state):
                top, total, acc = state
                keys = pl.ds(pl.multiple_of(j * block, block), block)
                s = dot(q, qkv_ref[keys, kcol], ((1,), (1,))) * scale
                kat = j * block + lax.broadcasted_iota(jnp.int32, (block, block), 1)
                ok = (kat <= at) & (kat >= low)
                s = jnp.where(ok, s, masked_score)
                new_top = jnp.maximum(top, jnp.max(s, axis=1, keepdims=True))
                p = jnp.where(ok, jnp.exp(s - new_top), 0.0)
                fade = jnp.exp(top - new_top)
                total = total * fade + jnp.sum(p, axis=1, keepdims=True)
                acc = acc * fade + dot(p.astype(bf16), qkv_ref[keys, vcol], ((1,), (0,)))
                return new_top, total, acc

            start = jnp.where(i * block >= split, split // block, 0)
            top, total, acc = lax.fori_loop(
                start,
                i + 1,
                key_block,
                (
                    jnp.full((block, 1), masked_score, f32),
                    jnp.zeros((block, 1), f32),
                    jnp.zeros((block, HEAD_DIM), f32),
                ),
            )
            att = acc / total
            limit = jnp.where(at < split, limit_ref[row, 0], limit_ref[row, 1])
            active = (limit_ref[row, 2] + h < limit).astype(f32)
            att_ref[rows, qcol] = att
            low_ref[rows, qcol] = (att * active).astype(bf16)
            lse_ref[rows, qcol] = jnp.broadcast_to(top + jnp.log(total), (block, HEAD_DIM))
            return carry

        lax.fori_loop(0, blocks, query_block, 0)


def attend(proj, split, limits, cos2, sin2, heads):
    rows, length, _ = proj.shape
    width = heads * HEAD_DIM
    smem = pl.BlockSpec(memory_space=pltpu.SMEM)
    table = pl.BlockSpec((length, HEAD_DIM), lambda r: (0, 0))

    def whole(cols):
        return pl.BlockSpec((None, length, cols), lambda r: (r, 0, 0))

    flops = rows * heads * 4 * length * length * HEAD_DIM
    return pl.pallas_call(
        functools.partial(attend_kernel, heads, length),
        grid=(rows,),
        in_specs=[smem, smem, whole(3 * width), table, table],
        out_specs=[whole(3 * width), whole(width), whole(width), whole(width)],
        out_shape=[
            jax.ShapeDtypeStruct((rows, length, 3 * width), bf16),
            jax.ShapeDtypeStruct((rows, length, width), f32),
            jax.ShapeDtypeStruct((rows, length, width), bf16),
            jax.ShapeDtypeStruct((rows, length, width), f32),
        ],
        compiler_params=pltpu.CompilerParams(vmem_limit_bytes=56 * 2**20),
        cost_estimate=pl.CostEstimate(flops=flops, bytes_accessed=2**24, transcendentals=flops // 512),
    )(split, limits, proj, cos2, sin2)


def attend_back_kernel(heads, length, split_ref, limit_ref, qkv_ref, att_ref, lse_ref, dat_ref, cos_ref, sin_ref, dproj_ref, datt_ref, delta_ref, dq_ref):
    row = pl.program_id(0)
    split = split_ref[row]
    scale = HEAD_DIM ** (-0.5)
    block = min(BLOCK, length)
    blocks = length // block
    width = heads * HEAD_DIM
    for h in range(heads):
        qcol = pl.ds(h * HEAD_DIM, HEAD_DIM)
        kcol = pl.ds(width + h * HEAD_DIM, HEAD_DIM)
        vcol = pl.ds(2 * width + h * HEAD_DIM, HEAD_DIM)

        def prepare(i, carry):
            rows = pl.ds(pl.multiple_of(i * block, block), block)
            at = i * block + lax.broadcasted_iota(jnp.int32, (block, 1), 0)
            limit = jnp.where(at < split, limit_ref[row, 0], limit_ref[row, 1])
            active = (limit_ref[row, 2] + h < limit).astype(f32)
            datt = dat_ref[rows, qcol].astype(f32) * active
            datt_ref[rows, :] = datt.astype(bf16)
            delta = jnp.sum(datt * att_ref[rows, qcol], axis=1, keepdims=True)
            delta_ref[rows, :] = jnp.broadcast_to(delta, (block, HEAD_DIM))
            dq_ref[rows, :] = jnp.zeros((block, HEAD_DIM), f32)
            return carry

        lax.fori_loop(0, blocks, prepare, 0)

        def key_block(j, carry):
            keys = pl.ds(pl.multiple_of(j * block, block), block)
            k = qkv_ref[keys, kcol]
            v = qkv_ref[keys, vcol]
            kat = j * block + lax.broadcasted_iota(jnp.int32, (block, block), 1)

            def query_block(i, state):
                dk, dv = state
                rows = pl.ds(pl.multiple_of(i * block, block), block)
                q = qkv_ref[rows, qcol]
                datt = datt_ref[rows, :]
                at = i * block + lax.broadcasted_iota(jnp.int32, (block, 1), 0)
                low = first_key(split, at)
                ok = (kat <= at) & (kat >= low)
                s = dot(q, k, ((1,), (1,))) * scale
                lse = lse_ref[rows, qcol][:, :1]
                p = jnp.where(ok, jnp.exp(s - lse), 0.0)
                dp = dot(datt, v, ((1,), (1,)))
                ds = (p * (dp - delta_ref[rows, :][:, :1])).astype(bf16)
                dv = dv + dot(p.astype(bf16), datt, ((0,), (0,)))
                dk = dk + dot(ds, q, ((0,), (0,)))
                dq_ref[rows, :] += dot(ds, k, ((1,), (0,)))
                return dk, dv

            stop = jnp.where((j + 1) * block <= split, (split - 1) // block + 1, blocks)
            zero = jnp.zeros((block, HEAD_DIM), f32)
            dk, dv = lax.fori_loop(j, stop, query_block, (zero, zero))
            dproj_ref[keys, kcol] = turn(dk * scale, cos_ref[keys, :], -sin_ref[keys, :]).astype(bf16)
            dproj_ref[keys, vcol] = dv.astype(bf16)
            return carry

        lax.fori_loop(0, blocks, key_block, 0)

        def finish(i, carry):
            rows = pl.ds(pl.multiple_of(i * block, block), block)
            dq = dq_ref[rows, :] * scale
            dproj_ref[rows, qcol] = turn(dq, cos_ref[rows, :], -sin_ref[rows, :]).astype(bf16)
            return carry

        lax.fori_loop(0, blocks, finish, 0)


def attend_back(qkv, att, lse, dat, split, limits, cos2, sin2, heads):
    rows, length, _ = qkv.shape
    width = heads * HEAD_DIM
    smem = pl.BlockSpec(memory_space=pltpu.SMEM)
    table = pl.BlockSpec((length, HEAD_DIM), lambda r: (0, 0))

    def whole(cols):
        return pl.BlockSpec((None, length, cols), lambda r: (r, 0, 0))

    flops = rows * heads * 10 * length * length * HEAD_DIM
    return pl.pallas_call(
        functools.partial(attend_back_kernel, heads, length),
        grid=(rows,),
        in_specs=[smem, smem, whole(3 * width), whole(width), whole(width), whole(width), table, table],
        out_specs=whole(3 * width),
        out_shape=jax.ShapeDtypeStruct((rows, length, 3 * width), bf16),
        scratch_shapes=[
            pltpu.VMEM((length, HEAD_DIM), bf16),
            pltpu.VMEM((length, HEAD_DIM), f32),
            pltpu.VMEM((length, HEAD_DIM), f32),
        ],
        compiler_params=pltpu.CompilerParams(vmem_limit_bytes=56 * 2**20),
        cost_estimate=pl.CostEstimate(flops=flops, bytes_accessed=2**24, transcendentals=flops // 1280),
    )(split, limits, qkv, att, lse, dat, cos2, sin2)


class Ring:
    def __init__(self, axis, size):
        self.axis = axis
        self.size = size
        self.order = list(range(0, size, 2)) + list(range(1, size, 2))[::-1]
        place = {w: p for p, w in enumerate(self.order)}
        self.table = [[self.order[(place[w] + k) % size] for k in range(size)] for w in range(size)]
        self.near = None
        self.right = [(w, self.order[(place[w] + 1) % size]) for w in range(size)]
        self.left = [(w, self.order[(place[w] - 1) % size]) for w in range(size)]

    def at(self, shift):
        if self.near is None:
            row = lax.dynamic_slice_in_dim(jnp.array(self.table, jnp.int32), lax.axis_index(self.axis), 1, 0)
            self.near = [row[0, k] for k in range(self.size)]
        return self.near[shift % self.size]

    def gather(self, part):
        found = [(self.at(0), part)]
        onward, back = part, part
        half = self.size // 2
        for step in range(1, half):
            onward = lax.ppermute(onward, self.axis, self.right)
            back = lax.ppermute(back, self.axis, self.left)
            found += [(self.at(-step), onward), (self.at(step), back)]
        cut = part.shape[0] // 2
        first = lax.ppermute(onward[:cut], self.axis, self.right)
        second = lax.ppermute(back[cut:], self.axis, self.left)
        found.append((self.at(half), jnp.concatenate([first, second], axis=0)))
        return found

    def gather_whole(self, part):
        whole = jnp.zeros((self.size,) + part.shape, part.dtype)
        for owner, piece in self.gather(part):
            whole = lax.dynamic_update_slice_in_dim(whole, piece[None], owner, 0)
        return whole

    def scatter(self, term):
        sums = [term(self.at(-1), 0), term(self.at(1), 1)]
        for step in range(2, self.size + 1):
            for side, perm, sign in ((0, self.right, -1), (1, self.left, 1)):
                come = lax.ppermute(sums[side].astype(bf16), self.axis, perm)
                sums[side] = come.astype(f32) + term(self.at(sign * step), side)
        return sums


def join(*arrays):
    return lax.optimization_barrier(arrays)


def after(array, *others):
    return lax.optimization_barrier((array,) + others)[0]


def place_kernel(count, targets, *refs):
    pieces, whole, held, in_sems, out_sems = refs[:-4], refs[-4], refs[-3], refs[-2], refs[-1]
    spots = [(i, k) for i in range(len(pieces)) for k in range(count)]
    loads = [
        pltpu.make_async_copy(pieces[i].at[k], held.at[at], in_sems.at[at]) for at, (i, k) in enumerate(spots)
    ]
    stores = [
        pltpu.make_async_copy(held.at[at], whole.at[targets(i, k)], out_sems.at[at])
        for at, (i, k) in enumerate(spots)
    ]
    for load in loads:
        load.start()
    for load, store in zip(loads, stores):
        load.wait()
        store.start()
    for store in stores:
        store.wait()


def place(pieces, total, targets):
    count = pieces[0].shape[0]
    anywhere = pl.BlockSpec(memory_space=pl.ANY)
    shape = (total,) + pieces[0].shape[1:]
    size = 2 * 2 * total * pieces[0][0].size
    return pl.pallas_call(
        functools.partial(place_kernel, count, targets),
        in_specs=[anywhere] * len(pieces),
        out_specs=anywhere,
        out_shape=jax.ShapeDtypeStruct(shape, pieces[0].dtype),
        scratch_shapes=[
            pltpu.VMEM((len(pieces) * count,) + pieces[0].shape[1:], pieces[0].dtype),
            pltpu.SemaphoreType.DMA((len(pieces) * count,)),
            pltpu.SemaphoreType.DMA((len(pieces) * count,)),
        ],
        compiler_params=pltpu.CompilerParams(vmem_limit_bytes=40 * 2**20),
        cost_estimate=pl.CostEstimate(flops=0, bytes_accessed=size, transcendentals=0),
    )(*pieces)


def up_sum_kernel(narrow, act_ref, dpre_ref, out_ref):
    shard = out_ref.shape[-2]
    total = dot(act_ref[...], dpre_ref[...], ((0,), (0,))).astype(bf16)
    for y in range(2):
        for core in range(2):
            at = (2 * y + core) * shard
            out_ref[core, 0, 0, y] = total[at : at + shard]


def up_sums(act, dpre, wide, narrow, shard):
    tokens, cols = dpre.shape
    upper = wide // 4
    if (narrow * shard) % 128:
        total = dot(act, dpre, ((0,), (0,))).astype(bf16)
        total = total.reshape(upper, 2, 2, 2, 2, shard, cols).transpose(4, 2, 0, 1, 3, 5, 6)
        return total.reshape(2, 2, upper, 4, shard, cols)
    return pl.pallas_call(
        functools.partial(up_sum_kernel, narrow),
        grid=(wide,),
        in_specs=[
            pl.BlockSpec((tokens, narrow * shard), lambda w: (0, w)),
            pl.BlockSpec((tokens, cols), lambda w: (0, 0)),
        ],
        out_specs=pl.BlockSpec((2, 1, 1, 2, shard, cols), lambda w: (0, w % 2, w // 4, (w // 2) % 2, 0, 0)),
        out_shape=jax.ShapeDtypeStruct((2, 2, upper, 4, shard, cols), bf16),
        compiler_params=pltpu.CompilerParams(vmem_limit_bytes=40 * 2**20),
        cost_estimate=pl.CostEstimate(
            flops=2 * tokens * cols * act.shape[1], bytes_accessed=2**24, transcendentals=0
        ),
    )(act, dpre)


MESH = pl.DeviceIdType.MESH
TILE = 512
Y, Z, CORE, X, FAR = range(5)


def each(count, body):
    def step(i, carry):
        body(i)
        return carry

    lax.fori_loop(0, count, step, 0)


def feed_kernel(
    act_ref,
    top_zero,
    top_one,
    top_two,
    top_three,
    chosen_ref,
    width_ref,
    need_ref,
    up_zero,
    up_far,
    up_next,
    up_both,
    down_zero,
    down_far,
    down_next,
    down_both,
    mixed_own,
    mixed_come,
    dact_own,
    dact_come,
    down_own,
    down_come,
    up_own,
    up_come,
    down_core,
    up_core,
    up,
    down,
    act,
    dmix,
    scale,
    hid,
    dpre,
    relu,
    mixed,
    dact,
    mixed_low,
    dact_low,
    down_near,
    up_near,
    down_held,
    up_held,
    load_sem,
    send_sem,
    recv_sem,
):
    w = lax.axis_index("wide")
    n = lax.axis_index("narrow")
    core, x, far = n % 2, w % 2, w // 4
    peers = {
        Y: {"narrow": (n + 2) % 4},
        Z: {"wide": w + 2 - 4 * ((w // 2) % 2)},
        CORE: {"narrow": n + 1 - 2 * core},
        X: {"wide": w + 1 - 2 * x},
        FAR: {"wide": (w + 4) % 8},
    }
    rows = act_ref.shape[0]
    dim = act_ref.shape[1]
    started = []

    def send(source, target, peer):
        at = len(started)
        copy = pltpu.make_async_remote_copy(
            src_ref=source,
            dst_ref=target,
            send_sem=send_sem.at[at],
            recv_sem=recv_sem.at[at],
            device_id=peers[peer],
            device_id_type=MESH,
        )
        copy.start()
        started.append(copy)
        return copy

    def load(source, target, at):
        copy = pltpu.make_async_copy(source, target, load_sem.at[at])
        copy.start()
        return copy

    def slot(k):
        return pl.ds(k * rows, rows)

    barrier = pltpu.get_barrier_semaphore()
    for peer in peers.values():
        pl.semaphore_signal(barrier, inc=1, device_id=peer, device_id_type=MESH)
    pl.semaphore_wait(barrier, len(peers))

    to_y = send(act_ref, act.at[slot(1)], Y)
    to_z = send(act_ref, act.at[slot(2)], Z)
    scale_y = send(chosen_ref, scale.at[slot(1)], Y)
    scale_z = send(chosen_ref, scale.at[slot(2)], Z)
    loads = [load(act_ref, act.at[slot(0)], 0)]
    for k, top in enumerate((top_zero, top_one, top_two, top_three)):
        loads.append(load(top, dmix.at[slot(k)], 1 + k))
    weights = []
    for k, (up_part, down_part) in enumerate(
        ((up_zero, down_zero), (up_far, down_far), (up_next, down_next), (up_both, down_both))
    ):
        its_far = far + (1 - 2 * far) * (k % 2)
        its_x = x + (1 - 2 * x) * (k // 2)
        up_slot = up.at[its_far, :, its_x, :, core]
        down_slot = down.at[core, its_x, its_far]
        weights += [send(up_part, up_slot, CORE), send(down_part, down_slot, CORE)]
        loads += [load(up_part, up_slot, 5 + 2 * k), load(down_part, down_slot, 6 + 2 * k)]
    scale[slot(0), :] = chosen_ref[...]
    for copy in loads:
        copy.wait()
    for copy in weights:
        copy.wait_recv()
    half = rows // 2
    to_y.wait_recv()
    to_z.wait_recv()
    scale_y.wait_recv()
    scale_z.wait_recv()
    both_y = send(act.at[pl.ds(2 * rows, half)], act.at[pl.ds(3 * rows, half)], Y)
    both_z = send(act.at[pl.ds(rows + half, half)], act.at[pl.ds(3 * rows + half, half)], Z)
    scale_both = send(scale.at[slot(2)], scale.at[slot(3)], Y)

    def columns(t):
        return pl.ds(pl.multiple_of(t * TILE, TILE), TILE)

    def forward(pair):
        group = pl.ds(pair * 2 * rows, 2 * rows)
        width = width_ref[group, :]

        def scaled(i):
            at = pl.ds(pl.multiple_of(pair * 2 * rows + i * 32, 32), 32)
            dmix[at, :] = (dmix[at, :].astype(f32) * scale[at, :][:, :1]).astype(bf16)

        each(2 * rows // 32, scaled)

        def first(t, carry):
            at = columns(t)
            weight = up[:, :, :, :, :, :, at].reshape(dim, TILE)
            pre = jnp.maximum(dot(act[group, :], weight, ((1,), (0,))), 0.0)
            pre = jnp.where(need_ref[:, at] <= width, pre, 0.0)
            relu[:, at] = pre.astype(bf16)
            hid[group, at] = (pre * pre).astype(bf16)
            return carry

        def second(t, carry):
            at = columns(t)
            weight = down[:, :, :, :, at].reshape(dim, TILE)
            value = dot(hid[group, :], weight, ((1,), (0,)))
            mixed[group, at] = value.astype(bf16)
            return carry

        def third(t, carry):
            at = columns(t)
            weight = down[t // 2, t % 2].reshape(TILE, dim)
            value = dot(dmix[group, :], weight, ((1,), (1,)))
            dpre[group, at] = (value * 2.0 * relu[:, at].astype(f32)).astype(bf16)
            return carry

        def fourth(t, carry):
            at = columns(t)
            weight = up[t // 2, t % 2].reshape(TILE, dim)
            value = dot(dpre[group, :], weight, ((1,), (1,)))
            dact[group, at] = value.astype(bf16)
            return carry

        lax.fori_loop(0, dim // TILE, first, 0)
        lax.fori_loop(0, dim // TILE, second, 0)
        lax.fori_loop(0, dim // TILE, third, 0)
        lax.fori_loop(0, dim // TILE, fourth, 0)

    forward(0)
    mixed_one = send(mixed.at[slot(1)], mixed_low.at[0], Y)
    both_y.wait_recv()
    both_z.wait_recv()
    scale_both.wait_recv()
    forward(1)
    mixed_three = send(mixed.at[slot(3)], mixed_low.at[1], Y)
    dact_two = send(dact.at[slot(2)], dact_low.at[0], Z)
    dact_three = send(dact.at[slot(3)], dact_low.at[1], Z)

    cut = dim // 2

    def down_terms(side):
        at = pl.ds(side * cut, cut)

        def block(k, carry):
            rows_of = hid[:, pl.ds(pl.multiple_of(k * TILE, TILE), TILE)]
            value = dot(rows_of, dmix[:, at], ((0,), (0,))).astype(bf16)
            down[k // 2, k % 2, :, :, at] = value.reshape(2, TILE // 2, cut)
            return carry

        lax.fori_loop(0, dim // TILE, block, 0)

    def up_terms(side):
        at = pl.ds(side * cut, cut)

        def block(k, carry):
            rows_of = act[:, pl.ds(pl.multiple_of(k * TILE, TILE), TILE)]
            value = dot(rows_of, dpre[:, at], ((0,), (0,))).astype(bf16)
            up[k // 2, k % 2, :, :, :, :, at] = value.reshape(2, 2, 2, TILE // 8, cut)
            return carry

        lax.fori_loop(0, dim // TILE, block, 0)

    cores = []
    for side in range(2):
        at = pl.ds(side * cut, cut)
        down_terms(side)
        cores.append(send(down.at[1 - core, :, :, :, at], down_core.at[side], CORE))
    for side in range(2):
        at = pl.ds(side * cut, cut)
        up_terms(side)
        cores.append(send(up.at[:, :, :, :, 1 - core, :, at], up_core.at[side], CORE))

    def core_sum(k):
        side = k % 2
        at = pl.ds(side * cut, cut)
        cores[k].wait_recv()
        source = (down_core if k < 2 else up_core).at[side]
        copy = load(source, down_held if k < 2 else up_held, 13 + k)
        copy.wait()
        if k < 2:

            def add_down(i):
                a, b, part = i // 16, (i // 8) % 2, pl.ds(pl.multiple_of((i % 8) * 32, 32), 32)
                here = down[core, a, b, part, at].astype(f32)
                down[core, a, b, part, at] = (here + down_held[a, b, part, :].astype(f32)).astype(bf16)

            each(32, add_down)
            return send(down.at[core, 1 - x, :, :, at], down_near.at[:, :, at], X)

        def add_up(i):
            a, b, c, d = i // 8, (i // 4) % 2, (i // 2) % 2, i % 2
            here = up[a, b, c, d, core, :, at].astype(f32)
            up[a, b, c, d, core, :, at] = (here + up_held[a, b, c, d].astype(f32)).astype(bf16)

        each(16, add_up)
        return send(up.at[:, :, 1 - x, :, core, :, at], up_near.at[:, :, :, :, at], X)

    nears = [core_sum(k) for k in range(4)]

    mixed_one.wait_recv()
    mixed_three.wait_recv()

    def add_low(total, k, low, side):
        def step(i):
            at = pl.ds(pl.multiple_of(k * rows + i * 32, 32), 32)
            come = low[side, pl.ds(pl.multiple_of(i * 32, 32), 32), :].astype(f32)
            total[at, :] = (total[at, :].astype(f32) + come).astype(bf16)

        each(rows // 32, step)

    add_low(mixed, 2, mixed_low, 1)
    mixed_last = send(mixed.at[slot(2)], mixed_come, Z)
    add_low(mixed, 0, mixed_low, 0)
    keep = [load(mixed.at[slot(0)], mixed_own, 17)]
    dact_two.wait_recv()
    dact_three.wait_recv()
    add_low(dact, 1, dact_low, 1)
    dact_last = send(dact.at[slot(1)], dact_come, Y)
    add_low(dact, 0, dact_low, 0)
    keep.append(load(dact.at[slot(0)], dact_own, 18))

    fars = []
    for k in range(4):
        at = pl.ds((k % 2) * cut, cut)
        nears[k].wait_recv()
        if k < 2:

            def add_down(i, at=at):
                b, part = i // 8, pl.ds(pl.multiple_of((i % 8) * 32, 32), 32)
                here = down[core, x, b, part, at].astype(f32)
                down[core, x, b, part, at] = (here + down_near[b, part, at].astype(f32)).astype(bf16)

            each(16, add_down)
            fars.append(send(down.at[core, x, 1 - far, :, at], down_come.at[:, at], FAR))
            keep.append(load(down.at[core, x, far, :, at], down_own.at[:, at], 19 + k))
        else:

            def add_up(i, at=at):
                a, b, d = i // 4, (i // 2) % 2, i % 2
                here = up[a, b, x, d, core, :, at].astype(f32)
                up[a, b, x, d, core, :, at] = (here + up_near[a, b, d, :, at].astype(f32)).astype(bf16)

            each(8, add_up)
            fars.append(send(up.at[1 - far, :, x, :, core, :, at], up_come.at[:, :, :, at], FAR))
            keep.append(load(up.at[far, :, x, :, core, :, at], up_own.at[:, :, :, at], 19 + k))
    for copy in keep:
        copy.wait()
    for copy in [mixed_last, dact_last] + fars:
        copy.wait_recv()
    for copy in started:
        copy.wait_send()


def feed_forward(act, tops, chosen, width_all, need, ups, downs):
    rows, dim = act.shape
    any_space = pl.BlockSpec(memory_space=pl.ANY)
    in_vmem = pl.BlockSpec(memory_space=pltpu.VMEM)
    tokens = 4 * rows
    cut = dim // 2
    shard = dim // 32

    def shape(*dims):
        return jax.ShapeDtypeStruct(dims, bf16)

    return pl.pallas_call(
        feed_kernel,
        in_specs=[any_space] * 5 + [in_vmem] * 3 + [any_space] * 8,
        out_specs=[any_space] * 10,
        out_shape=[
            shape(rows, dim),
            shape(rows, dim),
            shape(rows, dim),
            shape(rows, dim),
            shape(dim // 8, dim),
            shape(dim // 8, dim),
            shape(2, 2, shard, dim),
            shape(2, 2, shard, dim),
            shape(2, 2, 2, dim // 8, cut),
            shape(2, 2, 2, 2, 2, shard, cut),
        ],
        scratch_shapes=[
            pltpu.VMEM((2, 2, 2, 2, 2, shard, dim), bf16),
            pltpu.VMEM((2, 2, 2, dim // 8, dim), bf16),
            pltpu.VMEM((tokens, dim), bf16),
            pltpu.VMEM((tokens, dim), bf16),
            pltpu.VMEM((tokens, 128), f32),
            pltpu.VMEM((tokens, dim), bf16),
            pltpu.VMEM((tokens, dim), bf16),
            pltpu.VMEM((2 * rows, dim), bf16),
            pltpu.VMEM((tokens, dim), bf16),
            pltpu.VMEM((tokens, dim), bf16),
            pltpu.VMEM((2, rows, dim), bf16),
            pltpu.VMEM((2, rows, dim), bf16),
            pltpu.VMEM((2, dim // 8, dim), bf16),
            pltpu.VMEM((2, 2, 2, shard, dim), bf16),
            pltpu.VMEM((2, 2, dim // 8, cut), bf16),
            pltpu.VMEM((2, 2, 2, 2, shard, cut), bf16),
            pltpu.SemaphoreType.DMA((23,)),
            pltpu.SemaphoreType.DMA((36,)),
            pltpu.SemaphoreType.DMA((36,)),
        ],
        compiler_params=pltpu.CompilerParams(
            collective_id=0, has_side_effects=True, vmem_limit_bytes=62 * 2**20
        ),
        cost_estimate=pl.CostEstimate(
            flops=12 * tokens * dim * dim, bytes_accessed=2**25, transcendentals=0
        ),
    )(act, *tops, chosen, width_all, need, *ups, *downs)


def swap(array, axis, size, bits):
    return lax.ppermute(array, axis, [(i, i ^ bits) for i in range(size)])


def on_device(
    wide,
    narrow,
    tokens,
    gain_one,
    w_qkv,
    w_out,
    gain_two,
    bias_two,
    router,
    w_up,
    w_down,
    doc_split,
    head_count,
    width_choice,
    out_grad,
):
    rows, part_len, dim = tokens.shape
    length = part_len * wide
    heads = dim // HEAD_DIM
    hidden = w_up.shape[1]
    head_groups = wide if heads % wide == 0 else heads
    row_groups = wide // head_groups
    my_heads = heads // head_groups
    my_rows = rows // row_groups
    cols = my_heads * HEAD_DIM
    count = rows * part_len
    w_at = lax.axis_index("wide")
    n_at = lax.axis_index("narrow")
    head_at = w_at % head_groups
    row_at = (w_at // head_groups) * my_rows
    ring = Ring("wide", wide)

    def pick_rows(array):
        return lax.dynamic_slice_in_dim(array, row_at, my_rows, 0) if row_groups > 1 else array

    def put_rows(array):
        if row_groups == 1:
            return array
        whole = jnp.zeros((rows,) + array.shape[1:], array.dtype)
        return lax.dynamic_update_slice_in_dim(whole, array, row_at, 0)

    def narrow_gather(part):
        found = part[None]
        for bits in [2**k for k in range(narrow.bit_length() - 1)]:
            other = swap(found, "narrow", narrow, bits)
            mine = (n_at & bits) == 0
            found = jnp.concatenate([jnp.where(mine, found, other), jnp.where(mine, other, found)])
        return found

    def narrow_scatter(array):
        for bits in [2**k for k in range(narrow.bit_length() - 1)]:
            array = array.reshape((-1, 2) + array.shape[1:])
            at = (n_at // bits) & 1
            others = lax.dynamic_index_in_dim(array, 1 - at, 1, keepdims=False)
            array = lax.dynamic_index_in_dim(array, at, 1, keepdims=False)
            come = swap(others.astype(bf16), "narrow", narrow, bits)
            array = array + come.astype(f32)
        return array[0]

    shares = wide
    upper = wide // 4
    upper_bits = [2**k for k in range(2, wide.bit_length() - 1)][::-1]

    def share_of(w, n):
        return ((n & 1) * 2 + (w & 1)) * upper + (w >> 2)

    def wide_of(share, team):
        return (share % upper) * 4 + ((team >> 1) << 1) + ((share // upper) & 1)

    def narrow_of(share, team):
        return ((team & 1) << 1) + share // (2 * upper)

    def team_of(w, n):
        return ((w >> 1) & 1) * 2 + (n >> 1)

    def beside(part):
        return swap(part, "narrow", narrow, 2)

    def across(part):
        return swap(part, "wide", wide, 2)

    def team_swap(blocks):
        team = team_of(w_at, n_at)
        mine = [lax.dynamic_index_in_dim(blocks, team ^ k, 0, keepdims=False) for k in range(4)]
        both = [(i, i ^ (2 * narrow + 2)) for i in range(wide * narrow)]
        come = jnp.stack(
            [
                mine[0],
                beside(mine[1]),
                across(mine[2]),
                lax.ppermute(mine[3], ("wide", "narrow"), both),
            ]
        )
        return jnp.stack([lax.dynamic_index_in_dim(come, team ^ k, 0, keepdims=False) for k in range(4)])

    def pick(array, at):
        return lax.dynamic_index_in_dim(array, at, 0, keepdims=False)

    exponent = jnp.arange(HEAD_DIM // 2, dtype=f32) * (2.0 / HEAD_DIM)
    angles = jnp.arange(length, dtype=f32)[:, None] * jnp.power(rope_base, -exponent)[None, :]
    cosine, sine = jnp.cos(angles), jnp.sin(angles)
    cos2 = jnp.concatenate([cosine, cosine], axis=1)
    sin2 = jnp.concatenate([-sine, sine], axis=1)
    split = pick_rows(doc_split)
    limits = jnp.concatenate(
        [pick_rows(head_count), jnp.full((my_rows, 1), head_at * my_heads, jnp.int32)], axis=1
    )

    inputs = tokens.astype(f32)
    inv_one = lax.rsqrt(jnp.mean(inputs * inputs, axis=-1, keepdims=True) + norm_eps)
    normed_one = inputs * inv_one
    act_one = (normed_one * gain_one).astype(bf16)

    shard = w_qkv.shape[0]
    blocks = w_qkv.reshape(shard, 3, head_groups, cols).transpose(2, 0, 1, 3)
    blocks = jnp.tile(blocks.reshape(head_groups, shard, 3 * cols), (row_groups, 1, 1))
    blocks = lax.all_to_all(blocks, "wide", 0, 0, tiled=True)
    my_qkv = narrow_gather(blocks).transpose(1, 0, 2, 3).reshape(dim, 3 * cols)
    out_parts = narrow_gather(lax.all_gather(w_out, "wide", axis=0, tiled=False))
    out_full = out_parts.transpose(1, 0, 2, 3).reshape(dim, dim)

    piece_rows = w_down.shape[0]
    up_blocks = w_up.reshape(shard, upper, 2, 2, 2, 2, piece_rows).transpose(2, 4, 0, 5, 3, 1, 6)
    up_part = team_swap(up_blocks.reshape(4, shard, shares * piece_rows))
    top = out_grad.reshape(count, dim)
    top_beside = beside(top)
    width_flat = width_choice.reshape(count)
    width_across = across(width_flat)
    width_all = jnp.concatenate([width_flat, beside(width_flat), width_across, beside(width_across)])

    act_all = jnp.zeros((my_rows, wide, part_len, dim), bf16)
    for owner, piece in ring.gather(act_one.reshape(count, dim)):
        piece = pick_rows(piece.reshape(rows, part_len, dim))
        act_all = lax.dynamic_update_slice(act_all, piece[:, None], (0, owner, 0, 0))
    act_flat = act_all.reshape(my_rows * length, dim)
    act_flat, my_qkv, up_part, top_beside, width_all, down_part, top = join(
        act_flat, my_qkv, up_part, top_beside, width_all, w_down, top
    )

    up_found = [((0, 0), up_part)]
    down_found = [((0, 0), down_part)]

    def spread(found, bit):
        return found + [((w ^ bit, n), swap(piece, "wide", wide, bit)) for (w, n), piece in found]

    for bit in upper_bits:
        up_found = spread(up_found, bit)
    up_near = ((1, 0), swap(up_part, "wide", wide, 1))
    down_near = ((1, 0), swap(down_part, "wide", wide, 1))
    proj = dot(act_flat, my_qkv, ((1,), (0,))).reshape(my_rows, length, 3 * cols)
    qkv, att, att_part, lse = attend(proj, split, limits, cos2, sin2, my_heads)
    sends = att_part.reshape(my_rows, wide, part_len, cols).transpose(1, 0, 2, 3)
    joined = join(sends, up_near[1], down_near[1], *[piece for _, piece in up_found])
    sends = joined[0]
    up_near, down_near = (up_near[0], joined[1]), (down_near[0], joined[2])
    up_found = [(at, piece) for (at, _), piece in zip(up_found, joined[3:])]

    come = lax.all_to_all(sends, "wide", 0, 0, tiled=True)
    up_far = [((w ^ 1, n), swap(piece, "wide", wide, 1)) for (w, n), piece in up_found[1:]]
    top_across = across(top)
    joined = join(come, top_across, down_part, *[piece for _, piece in up_far])
    come, top_across, down_part = joined[:3]
    up_found = up_found + [up_near] + [(at, piece) for (at, _), piece in zip(up_far, joined[3:])]
    come = come.reshape(row_groups, head_groups, my_rows, part_len, cols)
    att_low = come.transpose(0, 2, 3, 1, 4).reshape(count, dim)

    down_found = [((0, 0), down_part)]
    for bit in upper_bits:
        down_found = spread(down_found, bit)
    down_far = [((w ^ 1, n), swap(piece, "wide", wide, 1)) for (w, n), piece in down_found[1:]]
    down_found = down_found + [down_near] + down_far
    top_both = beside(top_across)
    x_one = inputs.reshape(count, dim) + dot(att_low, out_full, ((1,), (0,)))

    center = x_one - jnp.mean(x_one, axis=-1, keepdims=True)
    inv_two = lax.rsqrt(jnp.mean(center * center, axis=-1, keepdims=True) + norm_eps)
    normed_two = center * inv_two
    ln_out = normed_two * gain_two + bias_two
    act_two = ln_out.astype(bf16)
    onehot = (width_flat[:, None] == jnp.arange(WIDTHS, dtype=jnp.int32)[None, :]).astype(f32)
    router_prob = jax.nn.softmax(jnp.dot(ln_out, router, precision=highest), axis=-1)
    chosen = jnp.sum(router_prob * onehot, axis=-1)
    grad_top = top.astype(f32)
    share = jnp.arange(shares, dtype=jnp.int32)[:, None]
    team = team_of(w_at, n_at)
    units = (wide_of(share, team) * narrow + narrow_of(share, team)) * piece_rows
    units = (units + jnp.arange(piece_rows, dtype=jnp.int32)[None, :]).reshape(1, -1)
    need = units // (hidden // WIDTHS)

    def share_core(array):
        return pick(array, n_at & 1) + swap(pick(array, 1 - (n_at & 1)), "narrow", narrow, 1)

    def share_near(array):
        return pick(array, w_at & 1) + swap(pick(array, 1 - (w_at & 1)), "wide", wide, 1)

    def share_far(array):
        for bit in upper_bits:
            array = array.reshape((2, -1) + array.shape[1:])
            at = (w_at // bit) & 1
            array = pick(array, at) + swap(pick(array, 1 - at), "wide", wide, bit)
        return array[0]

    tops = (top, top_beside, top_across, top_both)
    if wide == 8 and narrow == 4:
        mixed, mixed_come, grad_act_two, dact_come, down_grad, down_come, up_sum, up_come, _, _ = feed_forward(
            act_two,
            tops,
            jnp.broadcast_to(chosen[:, None], (count, 128)),
            width_all[:, None].astype(f32),
            need.astype(f32),
            [piece.reshape(2, 2, shard, shares * piece_rows) for _, piece in up_found],
            [piece for _, piece in down_found],
        )
        mixed = mixed.astype(f32) + mixed_come.astype(f32)
        grad_act_two = grad_act_two.astype(f32) + dact_come.astype(f32)
        down_grad = down_grad.astype(f32) + down_come.astype(f32)
        up_sum = up_sum + up_come
        up_sum = up_sum.reshape(4, shard, shares * piece_rows)
    else:
        up_found = up_found + [((w, n ^ 1), swap(piece, "narrow", narrow, 1)) for (w, n), piece in up_found]
        down_found = down_found + [((w, n ^ 1), swap(p, "narrow", narrow, 1)) for (w, n), p in down_found]

        def up_target(i, k):
            w, n = lax.axis_index("wide"), lax.axis_index("narrow")
            dw, dn = up_found[i][0]
            return ((w ^ dw) & ~2 | (k & 2)) * narrow + ((n ^ dn) & 1 | ((k & 1) * 2))

        def down_target(i, k):
            dw, dn = down_found[i][0]
            return share_of(lax.axis_index("wide") ^ dw, lax.axis_index("narrow") ^ dn)

        up_mine = place([piece for _, piece in up_found], wide * narrow, up_target)
        up_mine = up_mine.reshape(dim, shares * piece_rows)
        down_mine = place([piece[None] for _, piece in down_found], shares, down_target)
        down_mine = down_mine.reshape(shares * piece_rows, dim)

        def team_gather(part):
            far = across(part)
            return jnp.concatenate([part, beside(part), far, beside(far)])

        def team_scatter(terms):
            low = beside(jnp.stack([terms[1], terms[3]])).astype(f32)
            near, far = terms[0] + low[0], terms[2] + low[1]
            return near + across(far.astype(bf16)).astype(f32)

        act_many = team_gather(act_two)
        mask = need <= width_all[:, None]
        pre = jnp.maximum(dot(act_many, up_mine, ((1,), (0,))), 0.0)
        pre = jnp.where(mask, pre, 0.0).astype(bf16).astype(f32)
        hid = (pre * pre).astype(bf16)
        dmix = (jnp.concatenate(tops).astype(f32) * team_gather(chosen)[:, None]).astype(bf16)
        mixed = dot(hid, down_mine, ((1,), (0,))).astype(bf16)
        dhid = dot(dmix, down_mine, ((1,), (1,)))
        dpre = (dhid * 2.0 * pre).astype(bf16)
        dact = dot(dpre, up_mine, ((1,), (1,))).astype(bf16)
        mixed = team_scatter(mixed.reshape(4, count, dim))
        grad_act_two = team_scatter(dact.reshape(4, count, dim))
        down_sum = dot(hid, dmix, ((0,), (0,))).astype(bf16).reshape(2, 2, upper, piece_rows, dim)
        down_grad = share_far(share_near(share_core(down_sum))).astype(f32)
        up_sum = up_sums(act_many, dpre, wide, narrow, shard)
        up_sum = share_far(share_near(share_core(up_sum)))

    block_out = (x_one + mixed * chosen[:, None]).astype(bf16)
    grad_prob = jnp.sum(grad_top * mixed, axis=-1)
    grad_logits = (grad_prob * chosen)[:, None] * (onehot - router_prob)
    grad_router = lax.dot_general(ln_out, grad_logits, (((0,), (0,)), ((), ())), precision=highest)
    grad_ln = grad_act_two + jnp.dot(grad_logits, router.T, precision=highest)
    grad_gain_two = jnp.sum(grad_ln * normed_two, axis=0)
    grad_bias_two = jnp.sum(grad_ln, axis=0)
    grad_normed = grad_ln * gain_two
    grad_x_one = grad_top + inv_two * (
        grad_normed
        - jnp.mean(grad_normed, axis=-1, keepdims=True)
        - normed_two * jnp.mean(grad_normed * normed_two, axis=-1, keepdims=True)
    )

    grad_branch = grad_x_one.astype(bf16)
    grad_att = dot(grad_branch, out_full, ((1,), (1,))).astype(bf16)
    sends = grad_att.reshape(row_groups, my_rows, part_len, head_groups, cols)
    sends = sends.transpose(0, 3, 1, 2, 4).reshape(wide, my_rows, part_len, cols)
    come = lax.all_to_all(sends, "wide", 0, 0, tiled=True)
    dat = come.transpose(1, 0, 2, 3).reshape(my_rows, length, cols)
    dproj = attend_back(qkv, att, lse, dat, split, limits, cos2, sin2, my_heads)
    grad_out = dot(att_low, grad_branch, ((0,), (0,)))
    grad_out = grad_out.reshape(wide, narrow, shard, dim).transpose(1, 0, 2, 3)
    grad_out = narrow_scatter(grad_out).astype(bf16).reshape(wide * shard, dim)
    dproj, act_flat, grad_out = join(dproj, act_flat, grad_out)
    out_proj_grad = lax.psum_scatter(grad_out, "wide", scatter_dimension=0, tiled=True).astype(f32)
    up_sum = team_swap(up_sum)
    up_grad = up_sum.reshape(2, 2, shard, 2, 2, upper, piece_rows).transpose(2, 5, 0, 4, 1, 3, 6)
    up_grad = up_grad.reshape(shard, hidden).astype(f32)
    half = dim // 2

    def one_term(owner, side):
        rows_of = lax.dynamic_slice_in_dim(dproj, owner * part_len, part_len, 1)
        rows_of = rows_of.reshape(my_rows * part_len, 3 * cols)
        term = dot(rows_of, my_qkv[side * half : (side + 1) * half], ((1,), (1,)))
        return put_rows(term.reshape(my_rows, part_len, half)).reshape(count, half)

    grad_act_one = jnp.concatenate(ring.scatter(one_term), axis=1)

    grad_qkv = dot(act_flat, dproj.reshape(my_rows * length, 3 * cols), ((0,), (0,)))
    gain_one_part = jnp.sum(grad_qkv * my_qkv.astype(f32), axis=1) / gain_one
    grad_qkv = grad_qkv.reshape(wide, narrow, shard, 3 * cols).transpose(1, 0, 2, 3)
    grad_qkv = narrow_scatter(grad_qkv).astype(bf16)
    grad_qkv = lax.all_to_all(grad_qkv, "wide", 0, 0, tiled=True).astype(f32)
    grad_qkv = jnp.sum(grad_qkv.reshape(row_groups, head_groups, shard, 3, cols), axis=0)
    qkv_grad = grad_qkv.transpose(1, 2, 0, 3).reshape(shard, 3 * dim)

    normed_flat = normed_one.reshape(count, dim)
    grad_scaled = grad_act_one * gain_one
    input_grad = grad_x_one + inv_one.reshape(count, 1) * (
        grad_scaled - normed_flat * jnp.mean(grad_scaled * normed_flat, axis=-1, keepdims=True)
    )
    small = jnp.concatenate(
        [gain_one_part, grad_gain_two, grad_bias_two, grad_router.T.reshape(-1), jnp.sum(onehot, axis=0)]
    )
    for bits in (1, 2):
        small = small + swap(small, "narrow", narrow, bits)
    for bits in [2**k for k in range(wide.bit_length() - 1)]:
        small = small + swap(small, "wide", wide, bits)
    gain_one_grad, gain_two_grad, bias_two_grad = (small[k * dim : (k + 1) * dim] for k in range(3))
    router_grad = small[3 * dim : (3 + WIDTHS) * dim].reshape(WIDTHS, dim).T
    counts_all = small[(3 + WIDTHS) * dim :]
    return (
        block_out.reshape(rows, part_len, dim),
        input_grad.reshape(rows, part_len, dim),
        qkv_grad,
        out_proj_grad,
        up_grad,
        down_grad,
        gain_one_grad,
        gain_two_grad,
        bias_two_grad,
        router_grad,
        counts_all.astype(jnp.int32),
    )


def solution(mesh):
    in_specs = (
        P("narrow", "wide", None),
        P(),
        P(("wide", "narrow"), None),
        P(("wide", "narrow"), None),
        P(),
        P(),
        P(),
        P(("wide", "narrow"), None),
        P(("wide", "narrow"), None),
        P("narrow"),
        P("narrow", None),
        P("narrow", "wide"),
        P("narrow", "wide", None),
    )
    out_specs = (
        P("narrow", "wide", None),
        P("narrow", "wide", None),
        P(("wide", "narrow"), None),
        P(("wide", "narrow"), None),
        P(("wide", "narrow"), None),
        P(("wide", "narrow"), None),
        P(),
        P(),
        P(),
        P(),
        P(),
    )
    step = functools.partial(on_device, mesh.shape["wide"], mesh.shape["narrow"])
    return jax.shard_map(step, mesh=mesh, in_specs=in_specs, out_specs=out_specs, check_vma=False)
```

```python
import functools

import jax
import jax.numpy as jnp
from jax import lax
from jax.experimental import pallas as pl
from jax.experimental.pallas import tpu as pltpu
from jax.sharding import PartitionSpec as P

HEAD_DIM = 128
WIDTHS = 4
BLOCK = 512

highest = lax.Precision.HIGHEST
norm_eps = 1e-05
rope_base = 10000.0
masked_score = -1e30
LOG2E = 1.4426950408889634
f32 = jnp.float32
bf16 = jnp.bfloat16


def dot(a, b, contract):
    return lax.dot_general(a, b, (contract, ((), ())), preferred_element_type=f32)


def turn(u, cos2, sin2):
    return u * cos2 + pltpu.roll(u, HEAD_DIM // 2, 1) * sin2


def first_key(split, row):
    return jnp.where(row >= split, split, 0)


def attend_kernel(heads, length, split_ref, limit_ref, proj_ref, cos_ref, sin_ref, qkv_ref, att_ref, low_ref, lse_ref):
    row = pl.program_id(0)
    split = split_ref[row]
    scale = HEAD_DIM ** (-0.5) * LOG2E
    block = min(BLOCK, length)
    blocks = length // block
    width = heads * HEAD_DIM

    def rotate_block(i, carry):
        rows = pl.ds(pl.multiple_of(i * block, block), block)
        cos2 = cos_ref[rows, :]
        sin2 = sin_ref[rows, :]
        for part in range(2 * heads):
            cols = pl.ds(part * HEAD_DIM, HEAD_DIM)
            qkv_ref[rows, cols] = turn(proj_ref[rows, cols], cos2, sin2).astype(bf16)
        cols = pl.ds(2 * width, width)
        qkv_ref[rows, cols] = proj_ref[rows, cols].astype(bf16)
        return carry

    lax.fori_loop(0, blocks, rotate_block, 0)
    for h in range(heads):
        qcol = pl.ds(h * HEAD_DIM, HEAD_DIM)
        kcol = pl.ds(width + h * HEAD_DIM, HEAD_DIM)
        vcol = pl.ds(2 * width + h * HEAD_DIM, HEAD_DIM)

        def query_block(i, carry):
            rows = pl.ds(pl.multiple_of(i * block, block), block)
            q = qkv_ref[rows, qcol]
            at = i * block + lax.broadcasted_iota(jnp.int32, (block, 1), 0)
            low = first_key(split, at)

            def key_block(j, state):
                top, total, acc = state
                keys = pl.ds(pl.multiple_of(j * block, block), block)
                s = dot(q, qkv_ref[keys, kcol], ((1,), (1,))) * scale
                kat = j * block + lax.broadcasted_iota(jnp.int32, (block, block), 1)
                ok = (kat <= at) & (kat >= low)
                s = jnp.where(ok, s, masked_score)
                new_top = jnp.maximum(top, jnp.max(s, axis=1, keepdims=True))
                p = jnp.exp2(s - new_top)
                fade = jnp.exp2(top - new_top)
                total = total * fade + jnp.sum(p, axis=1, keepdims=True)
                acc = acc * fade + dot(p.astype(bf16), qkv_ref[keys, vcol], ((1,), (0,)))
                return new_top, total, acc

            start = jnp.where(i * block >= split, split // block, 0)
            top, total, acc = lax.fori_loop(
                start,
                i + 1,
                key_block,
                (
                    jnp.full((block, 1), masked_score, f32),
                    jnp.zeros((block, 1), f32),
                    jnp.zeros((block, HEAD_DIM), f32),
                ),
            )
            att = acc / total
            limit = jnp.where(at < split, limit_ref[row, 0], limit_ref[row, 1])
            active = (limit_ref[row, 2] + h < limit).astype(f32)
            att_ref[rows, qcol] = att
            low_ref[rows, qcol] = (att * active).astype(bf16)
            lse_ref[rows, qcol] = jnp.broadcast_to(top + jnp.log2(total), (block, HEAD_DIM))
            return carry

        lax.fori_loop(0, blocks, query_block, 0)


def attend(proj, split, limits, cos2, sin2, heads):
    rows, length, _ = proj.shape
    width = heads * HEAD_DIM
    smem = pl.BlockSpec(memory_space=pltpu.SMEM)
    table = pl.BlockSpec((length, HEAD_DIM), lambda r: (0, 0))

    def whole(cols):
        return pl.BlockSpec((None, length, cols), lambda r: (r, 0, 0))

    flops = rows * heads * 4 * length * length * HEAD_DIM
    return pl.pallas_call(
        functools.partial(attend_kernel, heads, length),
        grid=(rows,),
        in_specs=[smem, smem, whole(3 * width), table, table],
        out_specs=[whole(3 * width), whole(width), whole(width), whole(width)],
        out_shape=[
            jax.ShapeDtypeStruct((rows, length, 3 * width), bf16),
            jax.ShapeDtypeStruct((rows, length, width), f32),
            jax.ShapeDtypeStruct((rows, length, width), bf16),
            jax.ShapeDtypeStruct((rows, length, width), f32),
        ],
        compiler_params=pltpu.CompilerParams(vmem_limit_bytes=56 * 2**20),
        cost_estimate=pl.CostEstimate(flops=flops, bytes_accessed=2**24, transcendentals=flops // 512),
    )(split, limits, proj, cos2, sin2)


def attend_back_kernel(heads, length, split_ref, limit_ref, qkv_ref, att_ref, lse_ref, dat_ref, cos_ref, sin_ref, dproj_ref, datt_ref, delta_ref, dq_ref):
    row = pl.program_id(0)
    split = split_ref[row]
    scale = HEAD_DIM ** (-0.5)
    block = min(BLOCK, length)
    blocks = length // block
    width = heads * HEAD_DIM
    for h in range(heads):
        qcol = pl.ds(h * HEAD_DIM, HEAD_DIM)
        kcol = pl.ds(width + h * HEAD_DIM, HEAD_DIM)
        vcol = pl.ds(2 * width + h * HEAD_DIM, HEAD_DIM)

        def prepare(i, carry):
            rows = pl.ds(pl.multiple_of(i * block, block), block)
            at = i * block + lax.broadcasted_iota(jnp.int32, (block, 1), 0)
            limit = jnp.where(at < split, limit_ref[row, 0], limit_ref[row, 1])
            active = (limit_ref[row, 2] + h < limit).astype(f32)
            datt = dat_ref[rows, qcol].astype(f32) * active
            datt_ref[rows, :] = datt.astype(bf16)
            delta = jnp.sum(datt * att_ref[rows, qcol], axis=1, keepdims=True)
            delta_ref[rows, :] = jnp.broadcast_to(delta, (block, HEAD_DIM))
            dq_ref[rows, :] = jnp.zeros((block, HEAD_DIM), f32)
            return carry

        lax.fori_loop(0, blocks, prepare, 0)

        def key_block(j, carry):
            keys = pl.ds(pl.multiple_of(j * block, block), block)
            k = qkv_ref[keys, kcol]
            v = qkv_ref[keys, vcol]
            kat = j * block + lax.broadcasted_iota(jnp.int32, (block, block), 1)

            def query_block(i, state):
                dk, dv = state
                rows = pl.ds(pl.multiple_of(i * block, block), block)
                q = qkv_ref[rows, qcol]
                datt = datt_ref[rows, :]
                at = i * block + lax.broadcasted_iota(jnp.int32, (block, 1), 0)
                low = first_key(split, at)
                ok = (kat <= at) & (kat >= low)
                s = dot(q, k, ((1,), (1,))) * (scale * LOG2E)
                lse = lse_ref[rows, qcol][:, :1]
                p = jnp.exp2(jnp.where(ok, s - lse, masked_score))
                dp = dot(datt, v, ((1,), (1,)))
                ds = (p * (dp - delta_ref[rows, :][:, :1])).astype(bf16)
                dv = dv + dot(p.astype(bf16), datt, ((0,), (0,)))
                dk = dk + dot(ds, q, ((0,), (0,)))
                dq_ref[rows, :] += dot(ds, k, ((1,), (0,)))
                return dk, dv

            stop = jnp.where((j + 1) * block <= split, (split - 1) // block + 1, blocks)
            zero = jnp.zeros((block, HEAD_DIM), f32)
            dk, dv = lax.fori_loop(j, stop, query_block, (zero, zero))
            dproj_ref[keys, kcol] = turn(dk * scale, cos_ref[keys, :], -sin_ref[keys, :]).astype(bf16)
            dproj_ref[keys, vcol] = dv.astype(bf16)
            return carry

        lax.fori_loop(0, blocks, key_block, 0)

        def finish(i, carry):
            rows = pl.ds(pl.multiple_of(i * block, block), block)
            dq = dq_ref[rows, :] * scale
            dproj_ref[rows, qcol] = turn(dq, cos_ref[rows, :], -sin_ref[rows, :]).astype(bf16)
            return carry

        lax.fori_loop(0, blocks, finish, 0)


def attend_back(qkv, att, lse, dat, split, limits, cos2, sin2, heads):
    rows, length, _ = qkv.shape
    width = heads * HEAD_DIM
    smem = pl.BlockSpec(memory_space=pltpu.SMEM)
    table = pl.BlockSpec((length, HEAD_DIM), lambda r: (0, 0))

    def whole(cols):
        return pl.BlockSpec((None, length, cols), lambda r: (r, 0, 0))

    flops = rows * heads * 10 * length * length * HEAD_DIM
    return pl.pallas_call(
        functools.partial(attend_back_kernel, heads, length),
        grid=(rows,),
        in_specs=[smem, smem, whole(3 * width), whole(width), whole(width), whole(width), table, table],
        out_specs=whole(3 * width),
        out_shape=jax.ShapeDtypeStruct((rows, length, 3 * width), bf16),
        scratch_shapes=[
            pltpu.VMEM((length, HEAD_DIM), bf16),
            pltpu.VMEM((length, HEAD_DIM), f32),
            pltpu.VMEM((length, HEAD_DIM), f32),
        ],
        compiler_params=pltpu.CompilerParams(vmem_limit_bytes=56 * 2**20),
        cost_estimate=pl.CostEstimate(flops=flops, bytes_accessed=2**24, transcendentals=flops // 1280),
    )(split, limits, qkv, att, lse, dat, cos2, sin2)


class Ring:
    def __init__(self, axis, size):
        self.axis = axis
        self.size = size
        self.order = list(range(0, size, 2)) + list(range(1, size, 2))[::-1]
        place = {w: p for p, w in enumerate(self.order)}
        self.table = [[self.order[(place[w] + k) % size] for k in range(size)] for w in range(size)]
        self.near = None
        self.right = [(w, self.order[(place[w] + 1) % size]) for w in range(size)]
        self.left = [(w, self.order[(place[w] - 1) % size]) for w in range(size)]

    def at(self, shift):
        if self.near is None:
            row = lax.dynamic_slice_in_dim(jnp.array(self.table, jnp.int32), lax.axis_index(self.axis), 1, 0)
            self.near = [row[0, k] for k in range(self.size)]
        return self.near[shift % self.size]

    def gather(self, part):
        found = [(self.at(0), part)]
        onward, back = part, part
        half = self.size // 2
        for step in range(1, half):
            onward = lax.ppermute(onward, self.axis, self.right)
            back = lax.ppermute(back, self.axis, self.left)
            found += [(self.at(-step), onward), (self.at(step), back)]
        cut = part.shape[0] // 2
        first = lax.ppermute(onward[:cut], self.axis, self.right)
        second = lax.ppermute(back[cut:], self.axis, self.left)
        found.append((self.at(half), jnp.concatenate([first, second], axis=0)))
        return found

    def gather_whole(self, part):
        whole = jnp.zeros((self.size,) + part.shape, part.dtype)
        for owner, piece in self.gather(part):
            whole = lax.dynamic_update_slice_in_dim(whole, piece[None], owner, 0)
        return whole

    def scatter(self, term):
        sums = [term(self.at(-1), 0), term(self.at(1), 1)]
        for step in range(2, self.size + 1):
            for side, perm, sign in ((0, self.right, -1), (1, self.left, 1)):
                come = lax.ppermute(sums[side].astype(bf16), self.axis, perm)
                sums[side] = come.astype(f32) + term(self.at(sign * step), side)
        return sums


def join(*arrays):
    return lax.optimization_barrier(arrays)


def after(array, *others):
    return lax.optimization_barrier((array,) + others)[0]


def place_kernel(count, targets, *refs):
    pieces, whole, held, in_sems, out_sems = refs[:-4], refs[-4], refs[-3], refs[-2], refs[-1]
    spots = [(i, k) for i in range(len(pieces)) for k in range(count)]
    loads = [
        pltpu.make_async_copy(pieces[i].at[k], held.at[at], in_sems.at[at]) for at, (i, k) in enumerate(spots)
    ]
    stores = [
        pltpu.make_async_copy(held.at[at], whole.at[targets(i, k)], out_sems.at[at])
        for at, (i, k) in enumerate(spots)
    ]
    for load in loads:
        load.start()
    for load, store in zip(loads, stores):
        load.wait()
        store.start()
    for store in stores:
        store.wait()


def place(pieces, total, targets):
    count = pieces[0].shape[0]
    anywhere = pl.BlockSpec(memory_space=pl.ANY)
    shape = (total,) + pieces[0].shape[1:]
    size = 2 * 2 * total * pieces[0][0].size
    return pl.pallas_call(
        functools.partial(place_kernel, count, targets),
        in_specs=[anywhere] * len(pieces),
        out_specs=anywhere,
        out_shape=jax.ShapeDtypeStruct(shape, pieces[0].dtype),
        scratch_shapes=[
            pltpu.VMEM((len(pieces) * count,) + pieces[0].shape[1:], pieces[0].dtype),
            pltpu.SemaphoreType.DMA((len(pieces) * count,)),
            pltpu.SemaphoreType.DMA((len(pieces) * count,)),
        ],
        compiler_params=pltpu.CompilerParams(vmem_limit_bytes=40 * 2**20),
        cost_estimate=pl.CostEstimate(flops=0, bytes_accessed=size, transcendentals=0),
    )(*pieces)


def up_sum_kernel(narrow, act_ref, dpre_ref, out_ref):
    shard = out_ref.shape[-2]
    total = dot(act_ref[...], dpre_ref[...], ((0,), (0,))).astype(bf16)
    for y in range(2):
        for core in range(2):
            at = (2 * y + core) * shard
            out_ref[core, 0, 0, y] = total[at : at + shard]


def up_sums(act, dpre, wide, narrow, shard):
    tokens, cols = dpre.shape
    upper = wide // 4
    if (narrow * shard) % 128:
        total = dot(act, dpre, ((0,), (0,))).astype(bf16)
        total = total.reshape(upper, 2, 2, 2, 2, shard, cols).transpose(4, 2, 0, 1, 3, 5, 6)
        return total.reshape(2, 2, upper, 4, shard, cols)
    return pl.pallas_call(
        functools.partial(up_sum_kernel, narrow),
        grid=(wide,),
        in_specs=[
            pl.BlockSpec((tokens, narrow * shard), lambda w: (0, w)),
            pl.BlockSpec((tokens, cols), lambda w: (0, 0)),
        ],
        out_specs=pl.BlockSpec((2, 1, 1, 2, shard, cols), lambda w: (0, w % 2, w // 4, (w // 2) % 2, 0, 0)),
        out_shape=jax.ShapeDtypeStruct((2, 2, upper, 4, shard, cols), bf16),
        compiler_params=pltpu.CompilerParams(vmem_limit_bytes=40 * 2**20),
        cost_estimate=pl.CostEstimate(
            flops=2 * tokens * cols * act.shape[1], bytes_accessed=2**24, transcendentals=0
        ),
    )(act, dpre)


MESH = pl.DeviceIdType.MESH
TILE = 512
Y, Z, CORE, X, FAR = range(5)


def each(count, body):
    def step(i, carry):
        body(i)
        return carry

    lax.fori_loop(0, count, step, 0)


def feed_kernel(
    act_ref,
    top_zero,
    top_one,
    top_two,
    top_three,
    chosen_ref,
    width_ref,
    need_ref,
    up_zero,
    up_far,
    up_next,
    up_both,
    down_zero,
    down_next,
    mixed_own,
    mixed_come,
    dact_own,
    dact_come,
    down_own,
    down_come,
    up_own,
    up_come,
    down_core,
    up_core,
    up,
    down,
    act,
    dmix,
    scale,
    hid,
    dpre,
    mixed,
    dact,
    mixed_low,
    dact_low,
    down_near,
    up_near,
    held,
    down_sum,
    load_sem,
    send_sem,
    recv_sem,
):
    w = lax.axis_index("wide")
    n = lax.axis_index("narrow")
    core, x, far = n % 2, w % 2, w // 4
    peers = {
        Y: {"narrow": (n + 2) % 4},
        Z: {"wide": w + 2 - 4 * ((w // 2) % 2)},
        CORE: {"narrow": n + 1 - 2 * core},
        X: {"wide": w + 1 - 2 * x},
        FAR: {"wide": (w + 4) % 8},
    }
    rows = act_ref.shape[0]
    dim = act_ref.shape[1]
    started = []

    def send(source, target, peer):
        at = len(started)
        copy = pltpu.make_async_remote_copy(
            src_ref=source,
            dst_ref=target,
            send_sem=send_sem.at[at],
            recv_sem=recv_sem.at[at],
            device_id=peers[peer],
            device_id_type=MESH,
        )
        copy.start()
        started.append(copy)
        return copy

    def load(source, target, at):
        copy = pltpu.make_async_copy(source, target, load_sem.at[at])
        copy.start()
        return copy

    def slot(k):
        return pl.ds(k * rows, rows)

    barrier = pltpu.get_barrier_semaphore()
    for peer in peers.values():
        pl.semaphore_signal(barrier, inc=1, device_id=peer, device_id_type=MESH)
    pl.semaphore_wait(barrier, len(peers))

    to_y = send(act_ref, act.at[slot(1)], Y)
    to_z = send(act_ref, act.at[slot(2)], Z)
    scale_y = send(chosen_ref, scale.at[slot(1)], Y)
    scale_z = send(chosen_ref, scale.at[slot(2)], Z)
    loads = [load(act_ref, act.at[slot(0)], 0)]
    for k, top in enumerate((top_zero, top_one, top_two, top_three)):
        loads.append(load(top, dmix.at[slot(k)], 1 + k))
    down_to_far = send(down_zero, down.at[core, x, far], FAR)
    weights = []
    for k, up_part in enumerate((up_zero, up_far, up_next, up_both)):
        its_far = far + (1 - 2 * far) * (k % 2)
        its_x = x + (1 - 2 * x) * (k // 2)
        up_slot = up.at[its_far, :, its_x, :, core]
        weights.append(send(up_part, up_slot, CORE))
        loads.append(load(up_part, up_slot, 5 + k))
    for k, down_part in enumerate((down_zero, down_next)):
        down_slot = down.at[core, x + (1 - 2 * x) * k, far]
        weights.append(send(down_part, down_slot, CORE))
        loads.append(load(down_part, down_slot, 9 + k))
    scale[slot(0), :] = chosen_ref[...]
    for copy in loads:
        copy.wait()
    for copy in weights:
        copy.wait_recv()
    half = rows // 2
    to_y.wait_recv()
    to_z.wait_recv()
    scale_y.wait_recv()
    scale_z.wait_recv()
    both_y = send(act.at[pl.ds(2 * rows, half)], act.at[pl.ds(3 * rows, half)], Y)
    both_z = send(act.at[pl.ds(rows + half, half)], act.at[pl.ds(3 * rows + half, half)], Z)
    scale_both = send(scale.at[slot(2)], scale.at[slot(3)], Y)

    def columns(t):
        return pl.ds(pl.multiple_of(t * TILE, TILE), TILE)

    def group_of(pair):
        return pl.ds(pair * 2 * rows, 2 * rows)

    def hidden_of(pair):
        group = group_of(pair)
        width = width_ref[group, :]

        def scaled(i):
            at = pl.ds(pl.multiple_of(pair * 2 * rows + i * 32, 32), 32)
            dmix[at, :] = (dmix[at, :].astype(f32) * scale[at, :][:, :1]).astype(bf16)

        def first(t):
            at = columns(t)
            weight = up[:, :, :, :, :, :, at].reshape(dim, TILE)
            pre = jnp.maximum(dot(act[group, :], weight, ((1,), (0,))), 0.0)
            pre = jnp.where(need_ref[:, at] <= width, pre, 0.0)
            dpre[group, at] = pre.astype(bf16)
            hid[group, at] = (pre * pre).astype(bf16)

        each(2 * rows // 32, scaled)
        each(dim // TILE, first)

    def mixed_of(pair):
        group = group_of(pair)

        def second(t):
            at = columns(t)
            weight = down[:, :, :, :, at].reshape(dim, TILE)
            mixed[group, at] = dot(hid[group, :], weight, ((1,), (0,))).astype(bf16)

        each(dim // TILE, second)

    def dact_of(pair):
        group = group_of(pair)

        def third(t):
            at = columns(t)
            weight = down[t // 2, t % 2].reshape(TILE, dim)
            value = dot(dmix[group, :], weight, ((1,), (1,)))
            dpre[group, at] = (value * 2.0 * dpre[group, at].astype(f32)).astype(bf16)

        def fourth(t):
            at = columns(t)
            weight = up[t // 2, t % 2].reshape(TILE, dim)
            dact[group, at] = dot(dpre[group, :], weight, ((1,), (1,))).astype(bf16)

        each(dim // TILE, third)
        each(dim // TILE, fourth)

    cut = dim // 2

    def side_of(k):
        return pl.ds((k % 2) * cut, cut)

    def down_terms(k):
        def block(i):
            rows_of = hid[:, columns(i)]
            value = dot(rows_of, dmix[:, side_of(k)], ((0,), (0,))).astype(bf16)
            down_sum[i // 2, i % 2, :, :, :, :, side_of(k)] = value.reshape(2, 2, 2, TILE // 8, cut)

        each(dim // TILE, block)
        return send(down_sum.at[1 - core, :, :, :, :, :, side_of(k)], down_core.at[k], CORE)

    def up_terms(k):
        def block(i):
            rows_of = act[:, columns(i)]
            value = dot(rows_of, dpre[:, side_of(k)], ((0,), (0,))).astype(bf16)
            up[i // 2, i % 2, :, :, :, :, side_of(k)] = value.reshape(2, 2, 2, TILE // 8, cut)

        each(dim // TILE, block)
        return send(up.at[:, :, :, :, 1 - core, :, side_of(k)], up_core.at[k % 2], CORE)

    def core_sum(k):
        cores[k].wait_recv()
        load((down_core if k < 2 else up_core).at[k % 2], held, 13 + k).wait()

        def add(i):
            a, b, c, d = i // 8, (i // 4) % 2, (i // 2) % 2, i % 2
            come = held[a, b, c, d].astype(f32)
            if k < 2:
                here = down_sum[core, a, b, c, d, :, side_of(k)].astype(f32)
                down_sum[core, a, b, c, d, :, side_of(k)] = (here + come).astype(bf16)
            else:
                here = up[a, b, c, d, core, :, side_of(k)].astype(f32)
                up[a, b, c, d, core, :, side_of(k)] = (here + come).astype(bf16)

        each(16, add)
        if k < 2:
            source = down_sum.at[core, 1 - x, :, :, :, :, side_of(k)]
            return send(source, down_near.at[:, :, :, :, side_of(k)], X)
        source = up.at[:, :, 1 - x, :, core, :, side_of(k)]
        return send(source, up_near.at[:, :, :, :, side_of(k)], X)

    def near_sum(k):
        nears[k].wait_recv()

        def add(i):
            a, b, c = i // 4, (i // 2) % 2, i % 2
            if k < 2:
                here = down_sum[core, x, a, b, c, :, side_of(k)].astype(f32)
                come = down_near[a, b, c, :, side_of(k)].astype(f32)
                down_sum[core, x, a, b, c, :, side_of(k)] = (here + come).astype(bf16)
            else:
                here = up[a, b, x, c, core, :, side_of(k)].astype(f32)
                come = up_near[a, b, c, :, side_of(k)].astype(f32)
                up[a, b, x, c, core, :, side_of(k)] = (here + come).astype(bf16)

        each(8, add)
        if k < 2:
            fars.append(
                send(
                    down_sum.at[core, x, 1 - far, :, :, :, side_of(k)],
                    down_come.at[:, :, :, side_of(k)],
                    FAR,
                )
            )
            source = down_sum.at[core, x, far, :, :, :, side_of(k)]
            keep.append(load(source, down_own.at[:, :, :, side_of(k)], 19 + k))
        else:
            source = up.at[1 - far, :, x, :, core, :, side_of(k)]
            fars.append(send(source, up_come.at[:, :, :, side_of(k)], FAR))
            source = up.at[far, :, x, :, core, :, side_of(k)]
            keep.append(load(source, up_own.at[:, :, :, side_of(k)], 19 + k))

    def add_low(total, k, low, side):
        def step(i):
            at = pl.ds(pl.multiple_of(k * rows + i * 32, 32), 32)
            come = low[side, pl.ds(pl.multiple_of(i * 32, 32), 32), :].astype(f32)
            total[at, :] = (total[at, :].astype(f32) + come).astype(bf16)

        each(rows // 32, step)

    cores, nears, fars, keep = [], [], [], []
    hidden_of(0)
    both_y.wait_recv()
    both_z.wait_recv()
    scale_both.wait_recv()
    hidden_of(1)
    down_to_far.wait_recv()
    down_slot = down.at[core, x, 1 - far]
    down_to_x = send(down_slot, down_slot, X)
    down_to_core = send(down_slot, down_slot, CORE)
    cores.append(down_terms(0))
    cores.append(down_terms(1))
    down_to_x.wait_recv()
    down_slot = down.at[core, 1 - x, 1 - far]
    down_last = send(down_slot, down_slot, CORE)
    down_to_core.wait_recv()
    down_last.wait_recv()
    mixed_of(0)
    mixed_one = send(mixed.at[slot(1)], mixed_low.at[0], Y)
    nears.append(core_sum(0))
    mixed_of(1)
    mixed_three = send(mixed.at[slot(3)], mixed_low.at[1], Y)
    nears.append(core_sum(1))
    dact_of(1)
    dact_two = send(dact.at[slot(2)], dact_low.at[0], Z)
    dact_three = send(dact.at[slot(3)], dact_low.at[1], Z)
    dact_of(0)
    near_sum(0)
    cores.append(up_terms(2))
    cores.append(up_terms(3))
    nears.append(core_sum(2))
    nears.append(core_sum(3))

    mixed_one.wait_recv()
    mixed_three.wait_recv()
    add_low(mixed, 2, mixed_low, 1)
    mixed_last = send(mixed.at[slot(2)], mixed_come, Z)
    near_sum(1)
    add_low(mixed, 0, mixed_low, 0)
    keep.append(load(mixed.at[slot(0)], mixed_own, 17))
    dact_two.wait_recv()
    dact_three.wait_recv()
    add_low(dact, 1, dact_low, 1)
    dact_last = send(dact.at[slot(1)], dact_come, Y)
    add_low(dact, 0, dact_low, 0)
    keep.append(load(dact.at[slot(0)], dact_own, 18))
    near_sum(2)
    near_sum(3)
    for copy in keep:
        copy.wait()
    for copy in [mixed_last, dact_last] + fars:
        copy.wait_recv()
    for copy in started:
        copy.wait_send()


def feed_forward(act, tops, chosen, width_all, need, ups, downs):
    rows, dim = act.shape
    any_space = pl.BlockSpec(memory_space=pl.ANY)
    in_vmem = pl.BlockSpec(memory_space=pltpu.VMEM)
    tokens = 4 * rows
    cut = dim // 2
    shard = dim // 32

    def shape(*dims):
        return jax.ShapeDtypeStruct(dims, bf16)

    return pl.pallas_call(
        feed_kernel,
        in_specs=[any_space] * 5 + [in_vmem] * 3 + [any_space] * 6,
        out_specs=[any_space] * 10,
        out_shape=[
            shape(rows, dim),
            shape(rows, dim),
            shape(rows, dim),
            shape(rows, dim),
            shape(2, 2, shard, dim),
            shape(2, 2, shard, dim),
            shape(2, 2, shard, dim),
            shape(2, 2, shard, dim),
            shape(2, 2, 2, 2, 2, shard, cut),
            shape(2, 2, 2, 2, 2, shard, cut),
        ],
        scratch_shapes=[
            pltpu.VMEM((2, 2, 2, 2, 2, shard, dim), bf16),
            pltpu.VMEM((2, 2, 2, dim // 8, dim), bf16),
            pltpu.VMEM((tokens, dim), bf16),
            pltpu.VMEM((tokens, dim), bf16),
            pltpu.VMEM((tokens, 128), f32),
            pltpu.VMEM((tokens, dim), bf16),
            pltpu.VMEM((tokens, dim), bf16),
            pltpu.VMEM((tokens, dim), bf16),
            pltpu.VMEM((tokens, dim), bf16),
            pltpu.VMEM((2, rows, dim), bf16),
            pltpu.VMEM((2, rows, dim), bf16),
            pltpu.VMEM((2, 2, 2, shard, dim), bf16),
            pltpu.VMEM((2, 2, 2, shard, dim), bf16),
            pltpu.VMEM((2, 2, 2, 2, shard, cut), bf16),
            pltpu.VMEM((2, 2, 2, 2, 2, shard, dim), bf16),
            pltpu.SemaphoreType.DMA((23,)),
            pltpu.SemaphoreType.DMA((36,)),
            pltpu.SemaphoreType.DMA((36,)),
        ],
        compiler_params=pltpu.CompilerParams(
            collective_id=0, has_side_effects=True, vmem_limit_bytes=62 * 2**20
        ),
        cost_estimate=pl.CostEstimate(
            flops=12 * tokens * dim * dim, bytes_accessed=2**25, transcendentals=0
        ),
    )(act, *tops, chosen, width_all, need, *ups, *downs)


def ring_index(place):
    place = place % 8
    upper = place // 4
    return (1 - upper) * 2 * place + upper * (2 * (7 - place) + 1)


def first_kernel(
    split_ref,
    limit_ref,
    tokens_ref,
    gain_ref,
    cos_ref,
    sin_ref,
    qkv_part,
    out_part,
    up_blocks,
    down_part,
    top_zero,
    qkv,
    att,
    lse,
    act_out,
    weight_out,
    low_out,
    out_full,
    up_zero,
    up_far,
    up_next,
    up_both,
    down_next,
    top_one,
    top_two,
    top_three,
    act,
    weight,
    low,
    local_sem,
    send_sem,
    recv_sem,
    qkv_send_sem,
    qkv_recv_sem,
    low_send_sem,
    low_recv_sem,
):
    w = lax.axis_index("wide")
    n = lax.axis_index("narrow")
    core, y, far, z = n % 2, n // 2, w // 4, (w // 2) % 2
    odd = w % 2
    place = w // 2 + odd * (7 - 2 * (w // 2))
    rows, dim = tokens_ref.shape
    cols = weight.shape[3] // 3
    heads = cols // HEAD_DIM
    right, left = {"wide": ring_index(place + 1)}, {"wide": ring_index(place + 7)}
    to_y, to_core = {"narrow": (n + 2) % 4}, {"narrow": n + 1 - 2 * core}
    to_z, to_x = {"wide": w + 2 - 4 * z}, {"wide": w + 1 - 2 * odd}
    to_far = {"wide": (w + 4) % 8}
    to_both = {"wide": w + 2 - 4 * z, "narrow": (n + 2) % 4}
    barrier = pltpu.get_barrier_semaphore()
    peers = [{"wide": (w + k) % 8} for k in range(1, 8)] + [to_y, to_core, to_both]
    for peer in peers:
        pl.semaphore_signal(barrier, inc=1, device_id=peer, device_id_type=MESH)
    pl.semaphore_wait(barrier, len(peers))
    started, kept = [], []

    def send(source, target, peer):
        at = len(started)
        copy = pltpu.make_async_remote_copy(
            src_ref=source,
            dst_ref=target,
            send_sem=send_sem.at[at],
            recv_sem=recv_sem.at[at],
            device_id=peer,
            device_id_type=MESH,
        )
        copy.start()
        started.append(copy)
        return copy

    def keep(source, target):
        copy = pltpu.make_async_copy(source, target, local_sem.at[len(kept)])
        copy.start()
        kept.append(copy)
        return copy

    def norm(i):
        at = pl.ds(pl.multiple_of(i * 32, 32), 32)
        value = tokens_ref[at, :].astype(f32)
        inv = lax.rsqrt(jnp.mean(value * value, axis=-1, keepdims=True) + norm_eps)
        act[w, at, :] = (value * inv * gain_ref[...]).astype(bf16)

    each(rows // 32, norm)

    first, second = pl.ds(0, rows // 2), pl.ds(rows // 2, rows // 2)
    shard = out_part.shape[0]
    out_first, out_second = pl.ds(0, shard // 2), pl.ds(shard // 2, shard // 2)
    onward = send(act.at[w], act.at[w], right)
    back = send(act.at[w], act.at[w], left)
    exchanges = []
    for k in range(1, 8):
        target = (w + k) % 8
        for part in range(3):
            source = qkv_part.at[:, pl.ds(pl.multiple_of(part * dim + target * cols, cols), cols)]
            copy = pltpu.make_async_remote_copy(
                src_ref=source,
                dst_ref=weight.at[w, n, :, pl.ds(part * cols, cols)],
                send_sem=qkv_send_sem.at[k - 1, part],
                recv_sem=qkv_recv_sem.at[k - 1, part],
                device_id={"wide": target},
                device_id_type=MESH,
            )
            copy.start()
            exchanges.append(copy)
    for part in range(3):
        source = qkv_part.at[:, pl.ds(pl.multiple_of(part * dim + w * cols, cols), cols)]
        keep(source, weight.at[w, n, :, pl.ds(part * cols, cols)])
    out_onward = send(out_part, out_full.at[w, n], right)
    out_back = send(out_part, out_full.at[w, n], left)
    out_own = keep(out_part, out_full.at[w, n])
    team = z * 2 + y
    swaps = [
        send(up_blocks.at[z * 2 + 1 - y], up_zero.at[team], to_y),
        send(up_blocks.at[(1 - z) * 2 + y], up_zero.at[team], to_z),
        send(up_blocks.at[(1 - z) * 2 + 1 - y], up_zero.at[team], to_both),
    ]
    up_own = keep(up_blocks.at[team], up_zero.at[team])

    def ring_hop(step):
        nonlocal onward, back, out_onward, out_back
        behind, ahead = ring_index(place + 8 - step), ring_index(place + step)
        onward.wait_recv()
        back.wait_recv()
        if step < 3:
            onward = send(act.at[behind], act.at[behind], right)
            back = send(act.at[ahead], act.at[ahead], left)
        else:
            onward = send(act.at[behind, first], act.at[behind, first], right)
            back = send(act.at[ahead, second], act.at[ahead, second], left)
        out_onward.wait_recv()
        out_back.wait_recv()
        if step < 3:
            out_onward = send(out_full.at[behind, n], out_full.at[behind, n], right)
            out_back = send(out_full.at[ahead, n], out_full.at[ahead, n], left)
        else:
            out_onward = send(out_full.at[behind, n, out_first], out_full.at[behind, n, out_first], right)
            out_back = send(out_full.at[ahead, n, out_second], out_full.at[ahead, n, out_second], left)

    def project(owner):
        at = pl.ds(pl.multiple_of(owner * rows, rows), rows)
        for part in range(3):
            its = weight[:, :, :, pl.ds(part * cols, cols)].reshape(dim, cols)
            value = dot(act[owner], its, ((1,), (0,)))
            for h in range(heads):
                piece = value[:, h * HEAD_DIM : (h + 1) * HEAD_DIM]
                if part < 2:
                    piece = turn(piece, cos_ref[at, :], sin_ref[at, :])
                qkv[at, pl.ds(part * cols + h * HEAD_DIM, HEAD_DIM)] = piece.astype(bf16)

    def project_pair(step):
        each(2, lambda i: project(ring_index(place + 8 - step + 2 * step * i)))

    for copy in kept[:3]:
        copy.wait()
    for copy in exchanges:
        copy.wait_recv()
    weight_y = send(weight.at[:, n], weight.at[:, n], to_y)
    ring_hop(1)
    weight_y.wait_recv()
    weight_core = [
        send(weight.at[:, n], weight.at[:, n], to_core),
        send(weight.at[:, (n + 2) % 4], weight.at[:, (n + 2) % 4], to_core),
    ]
    beside = send(top_zero, top_one, to_y)
    for copy in weight_core:
        copy.wait_recv()
    each(1, lambda i: project(w + i))
    project_pair(1)
    ring_hop(2)
    project_pair(2)
    ring_hop(3)
    for copy in swaps:
        copy.wait_recv()
    up_own.wait()
    up_to_far = send(up_zero, up_far, to_far)
    up_to_x = send(up_zero, up_next, to_x)
    down_to_x = send(down_part, down_next, to_x)
    project_pair(3)
    onward.wait_recv()
    back.wait_recv()
    project(ring_index(place + 4))
    out_onward.wait_recv()
    out_back.wait_recv()
    out_own.wait()
    out_y = send(out_full.at[:, n], out_full.at[:, n], to_y)
    across = send(top_zero, top_two, to_z)
    keep(act, act_out)
    keep(weight, weight_out)

    split = split_ref[0]
    factor = HEAD_DIM ** (-0.5) * LOG2E
    block = 2 * rows
    limit_one, limit_two, head_first = limit_ref[0, 0], limit_ref[0, 1], limit_ref[0, 2]

    def low_send(target):
        return pltpu.make_async_remote_copy(
            src_ref=low.at[pl.ds(target * rows, rows)],
            dst_ref=low_out.at[:, pl.ds(pl.multiple_of(w * cols, cols), cols)],
            send_sem=low_send_sem.at[target],
            recv_sem=low_recv_sem.at[w],
            device_id={"wide": target},
            device_id_type=MESH,
        )

    def low_come(source):
        return pltpu.make_async_remote_copy(
            src_ref=low.at[pl.ds(source * rows, rows)],
            dst_ref=low_out.at[:, pl.ds(source * cols, cols)],
            send_sem=low_send_sem.at[source],
            recv_sem=low_recv_sem.at[source],
            device_id={"wide": source},
            device_id_type=MESH,
        )

    def low_keep(target):
        return pltpu.make_async_copy(
            low.at[pl.ds(target * rows, rows)],
            low_out.at[:, pl.ds(target * cols, cols)],
            low_send_sem.at[target],
        )

    for i in range(4):
        at_rows = pl.ds(i * block, block)
        at = i * block + lax.broadcasted_iota(jnp.int32, (block, 1), 0)
        lowest = jnp.where(at >= split, split, 0)

        def keys_of(j, state, diagonal):
            keys = pl.ds(pl.multiple_of(j * block, block), block)
            kat = j * block + lax.broadcasted_iota(jnp.int32, (block, block), 1)
            ok = kat >= lowest
            if diagonal:
                ok = ok & (kat <= at)
            found = []
            for h in range(heads):
                top, total, acc = state[h]
                q = qkv[at_rows, pl.ds(h * HEAD_DIM, HEAD_DIM)]
                k = qkv[keys, pl.ds(cols + h * HEAD_DIM, HEAD_DIM)]
                v = qkv[keys, pl.ds(2 * cols + h * HEAD_DIM, HEAD_DIM)]
                s = jnp.where(ok, dot(q, k, ((1,), (1,))) * factor, masked_score)
                new_top = jnp.maximum(top, jnp.max(s, axis=1, keepdims=True))
                p = jnp.exp2(s - new_top)
                fade = jnp.exp2(top - new_top)
                total = total * fade + jnp.sum(p, axis=1, keepdims=True)
                acc = acc * fade + dot(p.astype(bf16), v, ((1,), (0,)))
                found.append((new_top, total, acc))
            return tuple(found)

        start = (
            jnp.full((block, 1), masked_score, f32),
            jnp.zeros((block, 1), f32),
            jnp.zeros((block, HEAD_DIM), f32),
        )
        state = (start,) * heads
        if i:
            state = lax.fori_loop(0, i, functools.partial(keys_of, diagonal=False), state)
        state = keys_of(i, state, True)
        limit = jnp.where(at < split, limit_one, limit_two)
        for h in range(heads):
            top, total, acc = state[h]
            value = acc / total
            head = pl.ds(h * HEAD_DIM, HEAD_DIM)
            active = (head_first + h < limit).astype(f32)
            att[at_rows, head] = value
            low[at_rows, head] = (value * active).astype(bf16)
            lse[at_rows, head] = jnp.broadcast_to(top + jnp.log2(total), (block, HEAD_DIM))
        for target in (2 * i, 2 * i + 1):

            @pl.when(w != target)
            def _():
                low_send(target).start()

            @pl.when(w == target)
            def _():
                low_keep(target).start()

        if i == 2:
            out_y.wait_recv()
            out_core = [
                send(out_full.at[:, n], out_full.at[:, n], to_core),
                send(out_full.at[:, (n + 2) % 4], out_full.at[:, (n + 2) % 4], to_core),
            ]
    across.wait_recv()
    both = send(top_two, top_three, to_y)
    up_to_far.wait_recv()
    up_to_both = send(up_far, up_both, to_x)
    for copy in out_core + [beside, both, up_to_x, up_to_both, down_to_x]:
        copy.wait_recv()
    for target in range(8):

        @pl.when(w != target)
        def _():
            low_send(target).wait_send()
            low_come(target).wait_recv()

        @pl.when(w == target)
        def _():
            low_keep(target).wait()

    for copy in kept[3:]:
        if copy is not up_own and copy is not out_own:
            copy.wait()
    for copy in started + exchanges:
        copy.wait_send()


def first_sums(split, limits, tokens, gain, cos2, sin2, w_qkv, w_out, up_blocks, w_down, top):
    rows, dim = tokens.shape
    length = 8 * rows
    shard, wide_cols = w_qkv.shape
    cols = wide_cols // 24
    any_space = pl.BlockSpec(memory_space=pl.ANY)
    in_vmem = pl.BlockSpec(memory_space=pltpu.VMEM)
    smem = pl.BlockSpec(memory_space=pltpu.SMEM)
    dma = pltpu.SemaphoreType.DMA

    def shape(*dims):
        return jax.ShapeDtypeStruct(dims, bf16)

    flops = 6 * length * dim * cols + 4 * length * length * cols
    return pl.pallas_call(
        first_kernel,
        in_specs=[smem] * 2 + [in_vmem] * 4 + [any_space] * 5,
        out_specs=[in_vmem] * 3 + [any_space] * 12,
        out_shape=[
            shape(length, 3 * cols),
            jax.ShapeDtypeStruct((length, cols), f32),
            jax.ShapeDtypeStruct((length, cols), f32),
            shape(8, rows, dim),
            shape(8, 4, shard, 3 * cols),
            shape(rows, dim),
            shape(8, 4, shard, dim),
            shape(4, shard, dim),
            shape(4, shard, dim),
            shape(4, shard, dim),
            shape(4, shard, dim),
            shape(*w_down.shape),
            shape(rows, dim),
            shape(rows, dim),
            shape(rows, dim),
        ],
        scratch_shapes=[
            pltpu.VMEM((8, rows, dim), bf16),
            pltpu.VMEM((8, 4, shard, 3 * cols), bf16),
            pltpu.VMEM((length, cols), bf16),
            dma((8,)),
            dma((32,)),
            dma((32,)),
            dma((7, 3)),
            dma((7, 3)),
            dma((8,)),
            dma((8,)),
        ],
        compiler_params=pltpu.CompilerParams(
            collective_id=2, has_side_effects=True, vmem_limit_bytes=56 * 2**20
        ),
        cost_estimate=pl.CostEstimate(flops=flops, bytes_accessed=2**25, transcendentals=2**22),
    )(split, limits, tokens, gain, cos2, sin2, w_qkv, w_out, up_blocks, w_down, top)


STRIP = 128


def last_kernel(
    dproj,
    weight,
    act_ref,
    out_terms,
    small_ref,
    base_ref,
    tokens_ref,
    inv_ref,
    gain_ref,
    input_grad,
    out_grad,
    qkv_grad,
    small_out,
    act_grad,
    qkv_come,
    act,
    terms,
    core_come,
    side_come,
    act_send,
    act_recv,
    out_send,
    out_recv,
    small_sum,
    small_recv,
    load_sem,
    ring_send_sem,
    ring_recv_sem,
    send_sem,
    recv_sem,
):
    w = lax.axis_index("wide")
    n = lax.axis_index("narrow")
    core, y = n % 2, n // 2
    odd = w % 2
    place = w // 2 + odd * (7 - 2 * (w // 2))
    dim = weight.shape[0]
    half = dim // 2
    rows = act_grad.shape[0]
    shard = out_grad.shape[0]
    aims = ({"wide": ring_index(place + 1)}, {"wide": ring_index(place + 7)})
    other_core = {"narrow": n + 1 - 2 * core}
    other_y = {"narrow": (n + 2) % 4}
    others = [{"wide": (w + k) % 8} for k in range(1, 8)]
    barrier = pltpu.get_barrier_semaphore()
    for peer in others + [other_core, other_y]:
        pl.semaphore_signal(barrier, inc=1, device_id=peer, device_id_type=MESH)
    pl.semaphore_wait(barrier, len(others) + 2)
    load = pltpu.make_async_copy(act_ref, act, load_sem)
    load.start()
    started = []

    def send(source, target, peer):
        at = len(started)
        copy = pltpu.make_async_remote_copy(
            src_ref=source,
            dst_ref=target,
            send_sem=send_sem.at[at],
            recv_sem=recv_sem.at[at],
            device_id=peer,
            device_id_type=MESH,
        )
        copy.start()
        started.append(copy)
        return copy

    def hop(step, stream):
        if stream < 4:
            source, target, side = act_send.at[step, stream], act_recv.at[step, stream], stream // 2
        else:
            source, target, side = out_send.at[step, stream - 4], out_recv.at[step, stream - 4], stream - 4
        return pltpu.make_async_remote_copy(
            src_ref=source,
            dst_ref=target,
            send_sem=ring_send_sem.at[step, stream],
            recv_sem=ring_recv_sem.at[step, stream],
            device_id=aims[side],
            device_id_type=MESH,
        )

    def owner_of(step, side):
        return ring_index(place + 7 - step) if side == 0 else ring_index(place + 1 + step)

    def ring_step(step):
        for stream in range(4):
            side, strip = stream // 2, stream % 2
            owner = owner_of(step, side)
            at = pl.ds(pl.multiple_of(owner * rows + strip * STRIP, STRIP), STRIP)
            for part in range(2):
                cols = pl.ds(part * 512, 512)
                wide_cols = pl.ds(side * half + part * 512, 512)
                value = dot(dproj[at, :], weight[wide_cols, :], ((1,), (1,)))
                if step == 0:
                    act_send[0, stream, :, cols] = value.astype(bf16)
                elif step < 7:
                    act_send[step, stream, :, cols] = value.astype(bf16)
                else:
                    act_grad[pl.ds(strip * STRIP, STRIP), wide_cols] = value
            if step > 0:
                hop(step - 1, stream).wait_recv()

                def add(i):
                    part = pl.ds(pl.multiple_of(i * 32, 32), 32)
                    come = act_recv[step - 1, stream, part, :].astype(f32)
                    if step < 7:
                        act_send[step, stream, part, :] = (
                            act_send[step, stream, part, :].astype(f32) + come
                        ).astype(bf16)
                    else:
                        row = pl.ds(pl.multiple_of(strip * STRIP + i * 32, 32), 32)
                        act_grad[row, pl.ds(side * half, half)] += come

                each(STRIP // 32, add)
            if step < 7:
                hop(step, stream).start()
        for stream in (4, 5):
            side = stream - 4
            value = out_terms[owner_of(step, side), :, pl.ds(side * half, half)]
            if step > 0:
                hop(step - 1, stream).wait_recv()
                value = value.astype(f32) + out_recv[step - 1, side].astype(f32)
            if step < 7:
                out_send[step, side] = value.astype(bf16)
                hop(step, stream).start()
            else:
                out_grad[:, pl.ds(side * half, half)] = value

    ring_step(0)
    load.wait()
    small_sum[0] = small_ref[...]

    def weight_terms(k):
        at = pl.ds(pl.multiple_of(k * rows, rows), rows)
        value = dot(act[:, at], dproj[...], ((0,), (0,)))
        product = value * weight[at, :].astype(f32)
        ones = jnp.ones((8, product.shape[1]), f32)
        sums = lax.dot_general(
            ones, product, (((1,), (1,)), ((), ())), precision=highest, preferred_element_type=f32
        )
        small_sum[0, 0:1, at] = small_sum[0, 0:1, at] + sums[0:1]
        terms[k] = value.astype(bf16).reshape(2, 2, shard, value.shape[1])

    each(8, weight_terms)
    to_core = send(terms.at[:, :, 1 - core], core_come, other_core)

    small_peers = [other_core, other_y] + [{"wide": w + b - 2 * b * ((w // b) % 2)} for b in (1, 2, 4)]

    def small_step(k):
        if k:
            pending.pop().wait_recv()
            small_sum[k] = small_sum[k - 1] + small_recv[k - 1]
        if k < 5:
            pending.append(send(small_sum.at[k], small_recv.at[k], small_peers[k]))
        else:
            small_out[...] = small_sum[k]

    pending = []
    small_step(0)
    ring_step(1)
    to_core.wait_recv()

    def add_core(i):
        a, b = i // 2, i % 2
        here = terms[a, b, core].astype(f32)
        terms[a, b, core] = (here + core_come[a, b].astype(f32)).astype(bf16)

    each(16, add_core)
    to_side = send(terms.at[:, 1 - y, core], side_come, other_y)
    small_step(1)
    ring_step(2)
    small_step(2)
    ring_step(3)
    to_side.wait_recv()

    def add_side(i):
        here = terms[i, y, core].astype(f32)
        terms[i, y, core] = (here + side_come[i].astype(f32)).astype(bf16)

    each(8, add_side)
    own = pltpu.make_async_copy(terms.at[w, y, core], qkv_come.at[w], load_sem)
    own.start()
    blocks = []
    for k, peer in enumerate(others):
        target = (w + 1 + k) % 8
        blocks.append(send(terms.at[target, y, core], qkv_come.at[w], peer))
    small_step(3)
    ring_step(4)
    small_step(4)
    ring_step(5)
    small_step(5)
    ring_step(6)
    ring_step(7)

    def finish(i):
        at = pl.ds(pl.multiple_of(i * 32, 32), 32)
        inv = inv_ref[at, :]
        normed = tokens_ref[at, :].astype(f32) * inv
        scaled = act_grad[at, :] * gain_ref[...]
        mean = jnp.mean(scaled * normed, axis=-1, keepdims=True)
        input_grad[at, :] = base_ref[at, :] + inv * (scaled - normed * mean)

    each(rows // 32, finish)
    own.wait()
    for copy in blocks:
        copy.wait_recv()
    cols = weight.shape[1] // 3
    for k in range(8):
        for part in range(3):
            value = qkv_come[k, :, pl.ds(part * cols, cols)].astype(f32)
            qkv_grad[:, pl.ds(part * dim + k * cols, cols)] = value
    for copy in started:
        copy.wait_send()
    for step in range(7):
        for stream in range(6):
            hop(step, stream).wait_send()


def last_sums(dproj, weight, act, out_terms, small, base, tokens_in, inv, gain):
    tokens, cols = dproj.shape
    dim = weight.shape[0]
    rows, shard, half = tokens // 8, dim // 32, dim // 2
    any_space = pl.BlockSpec(memory_space=pl.ANY)
    in_vmem = pl.BlockSpec(memory_space=pltpu.VMEM)
    dma = pltpu.SemaphoreType.DMA
    return pl.pallas_call(
        last_kernel,
        in_specs=[in_vmem, in_vmem, any_space] + [in_vmem] * 6,
        out_specs=[in_vmem] * 4,
        out_shape=[
            jax.ShapeDtypeStruct((rows, dim), f32),
            jax.ShapeDtypeStruct((shard, dim), f32),
            jax.ShapeDtypeStruct((shard, 3 * dim), f32),
            jax.ShapeDtypeStruct((8, dim), f32),
        ],
        scratch_shapes=[
            pltpu.VMEM((rows, dim), f32),
            pltpu.VMEM((8, shard, cols), bf16),
            pltpu.VMEM((tokens, dim), bf16),
            pltpu.VMEM((8, 2, 2, shard, cols), bf16),
            pltpu.VMEM((8, 2, shard, cols), bf16),
            pltpu.VMEM((8, shard, cols), bf16),
            pltpu.VMEM((7, 4, STRIP, half), bf16),
            pltpu.VMEM((7, 4, STRIP, half), bf16),
            pltpu.VMEM((7, 2, shard, half), bf16),
            pltpu.VMEM((7, 2, shard, half), bf16),
            pltpu.VMEM((6, 8, dim), f32),
            pltpu.VMEM((5, 8, dim), f32),
            dma,
            dma((7, 6)),
            dma((7, 6)),
            dma((16,)),
            dma((16,)),
        ],
        compiler_params=pltpu.CompilerParams(
            collective_id=1, has_side_effects=True, vmem_limit_bytes=60 * 2**20
        ),
        cost_estimate=pl.CostEstimate(
            flops=4 * tokens * cols * dim, bytes_accessed=2**24, transcendentals=0
        ),
    )(dproj, weight, act, out_terms, small, base, tokens_in, inv, gain)


def swap(array, axis, size, bits):
    return lax.ppermute(array, axis, [(i, i ^ bits) for i in range(size)])


def on_device(
    wide,
    narrow,
    tokens,
    gain_one,
    w_qkv,
    w_out,
    gain_two,
    bias_two,
    router,
    w_up,
    w_down,
    doc_split,
    head_count,
    width_choice,
    out_grad,
):
    rows, part_len, dim = tokens.shape
    length = part_len * wide
    heads = dim // HEAD_DIM
    hidden = w_up.shape[1]
    head_groups = wide if heads % wide == 0 else heads
    row_groups = wide // head_groups
    my_heads = heads // head_groups
    my_rows = rows // row_groups
    cols = my_heads * HEAD_DIM
    count = rows * part_len
    w_at = lax.axis_index("wide")
    n_at = lax.axis_index("narrow")
    head_at = w_at % head_groups
    row_at = (w_at // head_groups) * my_rows
    ring = Ring("wide", wide)

    def pick_rows(array):
        return lax.dynamic_slice_in_dim(array, row_at, my_rows, 0) if row_groups > 1 else array

    def put_rows(array):
        if row_groups == 1:
            return array
        whole = jnp.zeros((rows,) + array.shape[1:], array.dtype)
        return lax.dynamic_update_slice_in_dim(whole, array, row_at, 0)

    def narrow_gather(part):
        found = part[None]
        for bits in [2**k for k in range(narrow.bit_length() - 1)]:
            other = swap(found, "narrow", narrow, bits)
            mine = (n_at & bits) == 0
            found = jnp.concatenate([jnp.where(mine, found, other), jnp.where(mine, other, found)])
        return found

    def narrow_scatter(array):
        for bits in [2**k for k in range(narrow.bit_length() - 1)]:
            array = array.reshape((wide, -1, 2) + array.shape[2:])
            at = (n_at // bits) & 1
            others = lax.dynamic_index_in_dim(array, 1 - at, 2, keepdims=False)
            array = lax.dynamic_index_in_dim(array, at, 2, keepdims=False)
            array = array + swap(others, "narrow", narrow, bits)
        return array[:, 0]

    shares = wide
    upper = wide // 4
    upper_bits = [2**k for k in range(2, wide.bit_length() - 1)][::-1]

    def share_of(w, n):
        return ((n & 1) * 2 + (w & 1)) * upper + (w >> 2)

    def wide_of(share, team):
        return (share % upper) * 4 + ((team >> 1) << 1) + ((share // upper) & 1)

    def narrow_of(share, team):
        return ((team & 1) << 1) + share // (2 * upper)

    def team_of(w, n):
        return ((w >> 1) & 1) * 2 + (n >> 1)

    def beside(part):
        return swap(part, "narrow", narrow, 2)

    def across(part):
        return swap(part, "wide", wide, 2)

    def team_swap(blocks):
        team = team_of(w_at, n_at)
        mine = [lax.dynamic_index_in_dim(blocks, team ^ k, 0, keepdims=False) for k in range(4)]
        both = [(i, i ^ (2 * narrow + 2)) for i in range(wide * narrow)]
        come = jnp.stack(
            [
                mine[0],
                beside(mine[1]),
                across(mine[2]),
                lax.ppermute(mine[3], ("wide", "narrow"), both),
            ]
        )
        return jnp.stack([lax.dynamic_index_in_dim(come, team ^ k, 0, keepdims=False) for k in range(4)])

    def pick(array, at):
        return lax.dynamic_index_in_dim(array, at, 0, keepdims=False)

    exponent = jnp.arange(HEAD_DIM // 2, dtype=f32) * (2.0 / HEAD_DIM)
    angles = jnp.arange(length, dtype=f32)[:, None] * jnp.power(rope_base, -exponent)[None, :]
    cosine, sine = jnp.cos(angles), jnp.sin(angles)
    cos2 = jnp.concatenate([cosine, cosine], axis=1)
    sin2 = jnp.concatenate([-sine, sine], axis=1)
    split = pick_rows(doc_split)
    limits = jnp.concatenate(
        [pick_rows(head_count), jnp.full((my_rows, 1), head_at * my_heads, jnp.int32)], axis=1
    )

    inputs = tokens.astype(f32)
    inv_one = lax.rsqrt(jnp.mean(inputs * inputs, axis=-1, keepdims=True) + norm_eps)
    normed_one = inputs * inv_one
    act_one = (normed_one * gain_one).astype(bf16)

    shard = w_qkv.shape[0]
    piece_rows = w_down.shape[0]
    up_blocks = w_up.reshape(shard, upper, 2, 2, 2, 2, piece_rows).transpose(2, 4, 0, 5, 3, 1, 6)
    up_blocks = up_blocks.reshape(4, shard, shares * piece_rows)
    top = out_grad.reshape(count, dim)
    width_flat = width_choice.reshape(count)
    width_across = across(width_flat)
    width_all = jnp.concatenate([width_flat, beside(width_flat), width_across, beside(width_across)])

    kernels = wide == 8 and narrow == 4 and rows == 1
    if kernels:
        qkv, att, lse, act_flat, my_qkv, att_low, out_full, *found = first_sums(
            split,
            limits,
            tokens.reshape(count, dim),
            gain_one[None],
            cos2,
            sin2,
            w_qkv,
            w_out,
            up_blocks,
            w_down,
            top,
        )
        qkv, att, lse = qkv[None], att[None], lse[None]
        act_flat = act_flat.reshape(length, dim)
        my_qkv = my_qkv.reshape(dim, 3 * cols)
        out_full = out_full.reshape(dim, dim)
        ups, downs = found[:4], [w_down, found[4]]
        tops = (top, *found[5:])
    else:
        blocks = w_qkv.reshape(shard, 3, head_groups, cols).transpose(2, 0, 1, 3)
        blocks = jnp.tile(blocks.reshape(head_groups, shard, 3 * cols), (row_groups, 1, 1))
        blocks = lax.all_to_all(blocks, "wide", 0, 0, tiled=True)
        my_qkv = narrow_gather(blocks).transpose(1, 0, 2, 3).reshape(dim, 3 * cols)
        out_parts = narrow_gather(lax.all_gather(w_out, "wide", axis=0, tiled=False))
        out_full = out_parts.transpose(1, 0, 2, 3).reshape(dim, dim)

        up_part = team_swap(up_blocks)
        top_beside = beside(top)
        act_all = jnp.zeros((my_rows, wide, part_len, dim), bf16)
        for owner, piece in ring.gather(act_one.reshape(count, dim)):
            piece = pick_rows(piece.reshape(rows, part_len, dim))
            act_all = lax.dynamic_update_slice(act_all, piece[:, None], (0, owner, 0, 0))
        act_flat = act_all.reshape(my_rows * length, dim)
        act_flat, my_qkv, up_part, top_beside, down_part, top = join(
            act_flat, my_qkv, up_part, top_beside, w_down, top
        )

        up_found = [((0, 0), up_part)]

        def spread(found, bit):
            return found + [((w ^ bit, n), swap(piece, "wide", wide, bit)) for (w, n), piece in found]

        for bit in upper_bits:
            up_found = spread(up_found, bit)
        up_near = ((1, 0), swap(up_part, "wide", wide, 1))
        down_near = ((1, 0), swap(down_part, "wide", wide, 1))
        proj = dot(act_flat, my_qkv, ((1,), (0,))).reshape(my_rows, length, 3 * cols)
        qkv, att, att_part, lse = attend(proj, split, limits, cos2, sin2, my_heads)
        sends = att_part.reshape(my_rows, wide, part_len, cols).transpose(1, 0, 2, 3)
        sends, down_part = join(sends, down_part)

        come = lax.all_to_all(sends, "wide", 0, 0, tiled=True)
        down_found = [((0, 0), down_part)]
        for bit in upper_bits:
            down_found = spread(down_found, bit)
        come, out_full = join(come, out_full)
        up_far = [((w ^ 1, n), swap(piece, "wide", wide, 1)) for (w, n), piece in up_found[1:]]
        up_found = up_found + [up_near] + up_far
        top_across = across(top)
        come = come.reshape(row_groups, head_groups, my_rows, part_len, cols)
        att_low = come.transpose(0, 2, 3, 1, 4).reshape(count, dim)

        down_far = [((w ^ 1, n), swap(piece, "wide", wide, 1)) for (w, n), piece in down_found[1:]]
        down_found = down_found + [down_near] + down_far
        top_both = beside(top_across)
        tops = (top, top_beside, top_across, top_both)
    x_one = inputs.reshape(count, dim) + dot(att_low, out_full, ((1,), (0,)))

    center = x_one - jnp.mean(x_one, axis=-1, keepdims=True)
    inv_two = lax.rsqrt(jnp.mean(center * center, axis=-1, keepdims=True) + norm_eps)
    normed_two = center * inv_two
    ln_out = normed_two * gain_two + bias_two
    act_two = ln_out.astype(bf16)
    onehot = (width_flat[:, None] == jnp.arange(WIDTHS, dtype=jnp.int32)[None, :]).astype(f32)
    router_prob = jax.nn.softmax(jnp.dot(ln_out, router, precision=highest), axis=-1)
    chosen = jnp.sum(router_prob * onehot, axis=-1)
    grad_top = top.astype(f32)
    share = jnp.arange(shares, dtype=jnp.int32)[:, None]
    team = team_of(w_at, n_at)
    units = (wide_of(share, team) * narrow + narrow_of(share, team)) * piece_rows
    units = (units + jnp.arange(piece_rows, dtype=jnp.int32)[None, :]).reshape(1, -1)
    need = units // (hidden // WIDTHS)

    def share_core(array):
        return pick(array, n_at & 1) + swap(pick(array, 1 - (n_at & 1)), "narrow", narrow, 1)

    def share_near(array):
        return pick(array, w_at & 1) + swap(pick(array, 1 - (w_at & 1)), "wide", wide, 1)

    def share_far(array):
        for bit in upper_bits:
            array = array.reshape((2, -1) + array.shape[1:])
            at = (w_at // bit) & 1
            array = pick(array, at) + swap(pick(array, 1 - at), "wide", wide, bit)
        return array[0]

    if kernels:
        mixed, mixed_come, grad_act_two, dact_come, down_grad, down_come, up_sum, up_come, _, _ = feed_forward(
            act_two,
            tops,
            jnp.broadcast_to(chosen[:, None], (count, 128)),
            width_all[:, None].astype(f32),
            need.astype(f32),
            [piece.reshape(2, 2, shard, shares * piece_rows) for piece in ups],
            downs,
        )
        mixed = mixed.astype(f32) + mixed_come.astype(f32)
        grad_act_two = grad_act_two.astype(f32) + dact_come.astype(f32)
        down_grad = (down_grad.astype(f32) + down_come.astype(f32)).reshape(piece_rows, dim)
        up_sum = up_sum + up_come
        up_sum = up_sum.reshape(4, shard, shares * piece_rows)
    else:
        up_found = up_found + [((w, n ^ 1), swap(piece, "narrow", narrow, 1)) for (w, n), piece in up_found]
        down_found = down_found + [((w, n ^ 1), swap(p, "narrow", narrow, 1)) for (w, n), p in down_found]

        def up_target(i, k):
            w, n = lax.axis_index("wide"), lax.axis_index("narrow")
            dw, dn = up_found[i][0]
            return ((w ^ dw) & ~2 | (k & 2)) * narrow + ((n ^ dn) & 1 | ((k & 1) * 2))

        def down_target(i, k):
            dw, dn = down_found[i][0]
            return share_of(lax.axis_index("wide") ^ dw, lax.axis_index("narrow") ^ dn)

        up_mine = place([piece for _, piece in up_found], wide * narrow, up_target)
        up_mine = up_mine.reshape(dim, shares * piece_rows)
        down_mine = place([piece[None] for _, piece in down_found], shares, down_target)
        down_mine = down_mine.reshape(shares * piece_rows, dim)

        def team_gather(part):
            far = across(part)
            return jnp.concatenate([part, beside(part), far, beside(far)])

        def team_scatter(terms):
            low = beside(jnp.stack([terms[1], terms[3]])).astype(f32)
            near, far = terms[0] + low[0], terms[2] + low[1]
            return near + across(far.astype(bf16)).astype(f32)

        act_many = team_gather(act_two)
        mask = need <= width_all[:, None]
        pre = jnp.maximum(dot(act_many, up_mine, ((1,), (0,))), 0.0)
        pre = jnp.where(mask, pre, 0.0).astype(bf16).astype(f32)
        hid = (pre * pre).astype(bf16)
        dmix = (jnp.concatenate(tops).astype(f32) * team_gather(chosen)[:, None]).astype(bf16)
        mixed = dot(hid, down_mine, ((1,), (0,))).astype(bf16)
        dhid = dot(dmix, down_mine, ((1,), (1,)))
        dpre = (dhid * 2.0 * pre).astype(bf16)
        dact = dot(dpre, up_mine, ((1,), (1,))).astype(bf16)
        mixed = team_scatter(mixed.reshape(4, count, dim))
        grad_act_two = team_scatter(dact.reshape(4, count, dim))
        down_sum = dot(hid, dmix, ((0,), (0,))).astype(bf16).reshape(2, 2, upper, piece_rows, dim)
        down_grad = share_far(share_near(share_core(down_sum))).astype(f32)
        up_sum = up_sums(act_many, dpre, wide, narrow, shard)
        up_sum = share_far(share_near(share_core(up_sum)))

    block_out = (x_one + mixed * chosen[:, None]).astype(bf16)
    grad_prob = jnp.sum(grad_top * mixed, axis=-1)
    grad_logits = (grad_prob * chosen)[:, None] * (onehot - router_prob)
    grad_router = lax.dot_general(ln_out, grad_logits, (((0,), (0,)), ((), ())), precision=highest)
    grad_ln = grad_act_two + jnp.dot(grad_logits, router.T, precision=highest)
    grad_gain_two = jnp.sum(grad_ln * normed_two, axis=0)
    grad_bias_two = jnp.sum(grad_ln, axis=0)
    grad_normed = grad_ln * gain_two
    grad_x_one = grad_top + inv_two * (
        grad_normed
        - jnp.mean(grad_normed, axis=-1, keepdims=True)
        - normed_two * jnp.mean(grad_normed * normed_two, axis=-1, keepdims=True)
    )

    grad_branch = grad_x_one.astype(bf16)
    grad_att = dot(grad_branch, out_full, ((1,), (1,))).astype(bf16)
    sends = grad_att.reshape(row_groups, my_rows, part_len, head_groups, cols)
    sends = sends.transpose(0, 3, 1, 2, 4).reshape(wide, my_rows, part_len, cols)
    come = lax.all_to_all(sends, "wide", 0, 0, tiled=True)
    dat = come.transpose(1, 0, 2, 3).reshape(my_rows, length, cols)
    dproj = attend_back(qkv, att, lse, dat, split, limits, cos2, sin2, my_heads)
    grad_out = dot(att_low, grad_branch, ((0,), (0,))).astype(bf16)
    grad_out = narrow_scatter(grad_out.reshape(wide, narrow, shard, dim))
    dproj, act_flat, grad_out = join(dproj, act_flat, grad_out)
    up_sum = team_swap(up_sum)
    up_grad = up_sum.reshape(2, 2, shard, 2, 2, upper, piece_rows).transpose(2, 5, 0, 4, 1, 3, 6)
    up_grad = up_grad.reshape(shard, hidden).astype(f32)
    normed_flat = normed_one.reshape(count, dim)
    counts = jnp.pad(jnp.sum(onehot, axis=0), (0, dim - WIDTHS))[None]
    small = [grad_gain_two[None], grad_bias_two[None], grad_router.T, counts]

    if kernels:
        small = jnp.concatenate([jnp.zeros((1, dim), f32)] + small)
        input_grad, out_proj_grad, qkv_grad, small = last_sums(
            dproj[0],
            my_qkv,
            act_flat,
            grad_out,
            small,
            grad_x_one,
            tokens.reshape(count, dim),
            inv_one.reshape(count, 1),
            gain_one[None],
        )
    else:
        half = dim // 2

        def one_term(owner, side):
            rows_of = lax.dynamic_slice_in_dim(dproj, owner * part_len, part_len, 1)
            rows_of = rows_of.reshape(my_rows * part_len, 3 * cols)
            term = dot(rows_of, my_qkv[side * half : (side + 1) * half], ((1,), (1,)))
            return put_rows(term.reshape(my_rows, part_len, half)).reshape(count, half)

        out_proj_grad = lax.psum_scatter(
            grad_out.reshape(wide * shard, dim), "wide", scatter_dimension=0, tiled=True
        ).astype(f32)
        grad_act_one = jnp.concatenate(ring.scatter(one_term), axis=1)
        grad_qkv = dot(act_flat, dproj.reshape(my_rows * length, 3 * cols), ((0,), (0,)))
        gain_one_part = jnp.sum(grad_qkv * my_qkv.astype(f32), axis=1)
        small = jnp.concatenate([gain_one_part[None]] + small)
        grad_qkv = narrow_scatter(grad_qkv.astype(bf16).reshape(wide, narrow, shard, 3 * cols))
        grad_qkv = lax.all_to_all(grad_qkv, "wide", 0, 0, tiled=True).astype(f32)
        for bits in (1, 2):
            small = small + swap(small, "narrow", narrow, bits)
        for bits in [2**k for k in range(wide.bit_length() - 1)]:
            small = small + swap(small, "wide", wide, bits)
        grad_qkv = jnp.sum(grad_qkv.reshape(row_groups, head_groups, shard, 3, cols), axis=0)
        qkv_grad = grad_qkv.transpose(1, 2, 0, 3).reshape(shard, 3 * dim)
        grad_scaled = grad_act_one * gain_one
        input_grad = grad_x_one + inv_one.reshape(count, 1) * (
            grad_scaled - normed_flat * jnp.mean(grad_scaled * normed_flat, axis=-1, keepdims=True)
        )
    gain_one_grad = small[0] / gain_one
    gain_two_grad, bias_two_grad = small[1], small[2]
    router_grad = small[3 : 3 + WIDTHS].T
    counts_all = small[3 + WIDTHS, :WIDTHS]
    return (
        block_out.reshape(rows, part_len, dim),
        input_grad.reshape(rows, part_len, dim),
        qkv_grad,
        out_proj_grad,
        up_grad,
        down_grad,
        gain_one_grad,
        gain_two_grad,
        bias_two_grad,
        router_grad,
        counts_all.astype(jnp.int32),
    )


def solution(mesh):
    in_specs = (
        P("narrow", "wide", None),
        P(),
        P(("wide", "narrow"), None),
        P(("wide", "narrow"), None),
        P(),
        P(),
        P(),
        P(("wide", "narrow"), None),
        P(("wide", "narrow"), None),
        P("narrow"),
        P("narrow", None),
        P("narrow", "wide"),
        P("narrow", "wide", None),
    )
    out_specs = (
        P("narrow", "wide", None),
        P("narrow", "wide", None),
        P(("wide", "narrow"), None),
        P(("wide", "narrow"), None),
        P(("wide", "narrow"), None),
        P(("wide", "narrow"), None),
        P(),
        P(),
        P(),
        P(),
        P(),
    )
    step = functools.partial(on_device, mesh.shape["wide"], mesh.shape["narrow"])
    return jax.shard_map(step, mesh=mesh, in_specs=in_specs, out_specs=out_specs, check_vma=False)
```

```python
import functools

import jax
import jax.numpy as jnp
import numpy as np
from jax import lax
from jax.experimental import pallas as pl
from jax.experimental.pallas import tpu as pltpu
from jax.sharding import PartitionSpec as P

HEAD_DIM = 128
WIDTHS = 4
BLOCK = 512

highest = lax.Precision.HIGHEST
norm_eps = 1e-05
rope_base = 10000.0
masked_score = -1e30
LOG2E = 1.4426950408889634
f32 = jnp.float32
bf16 = jnp.bfloat16


def dot(a, b, contract):
    return lax.dot_general(a, b, (contract, ((), ())), preferred_element_type=f32)


def turn(u, cos2, sin2):
    return u * cos2 + pltpu.roll(u, HEAD_DIM // 2, 1) * sin2


def first_key(split, row):
    return jnp.where(row >= split, split, 0)


def attend_kernel(heads, length, split_ref, limit_ref, proj_ref, cos_ref, sin_ref, qkv_ref, att_ref, low_ref, lse_ref):
    row = pl.program_id(0)
    split = split_ref[row]
    scale = HEAD_DIM ** (-0.5) * LOG2E
    block = min(BLOCK, length)
    blocks = length // block
    width = heads * HEAD_DIM

    def rotate_block(i, carry):
        rows = pl.ds(pl.multiple_of(i * block, block), block)
        cos2 = cos_ref[rows, :]
        sin2 = sin_ref[rows, :]
        for part in range(2 * heads):
            cols = pl.ds(part * HEAD_DIM, HEAD_DIM)
            qkv_ref[rows, cols] = turn(proj_ref[rows, cols], cos2, sin2).astype(bf16)
        cols = pl.ds(2 * width, width)
        qkv_ref[rows, cols] = proj_ref[rows, cols].astype(bf16)
        return carry

    lax.fori_loop(0, blocks, rotate_block, 0)
    for h in range(heads):
        qcol = pl.ds(h * HEAD_DIM, HEAD_DIM)
        kcol = pl.ds(width + h * HEAD_DIM, HEAD_DIM)
        vcol = pl.ds(2 * width + h * HEAD_DIM, HEAD_DIM)

        def query_block(i, carry):
            rows = pl.ds(pl.multiple_of(i * block, block), block)
            q = qkv_ref[rows, qcol]
            at = i * block + lax.broadcasted_iota(jnp.int32, (block, 1), 0)
            low = first_key(split, at)

            def key_block(j, state):
                top, total, acc = state
                keys = pl.ds(pl.multiple_of(j * block, block), block)
                s = dot(q, qkv_ref[keys, kcol], ((1,), (1,))) * scale
                kat = j * block + lax.broadcasted_iota(jnp.int32, (block, block), 1)
                ok = (kat <= at) & (kat >= low)
                s = jnp.where(ok, s, masked_score)
                new_top = jnp.maximum(top, jnp.max(s, axis=1, keepdims=True))
                p = jnp.exp2(s - new_top)
                fade = jnp.exp2(top - new_top)
                total = total * fade + jnp.sum(p, axis=1, keepdims=True)
                acc = acc * fade + dot(p.astype(bf16), qkv_ref[keys, vcol], ((1,), (0,)))
                return new_top, total, acc

            start = jnp.where(i * block >= split, split // block, 0)
            top, total, acc = lax.fori_loop(
                start,
                i + 1,
                key_block,
                (
                    jnp.full((block, 1), masked_score, f32),
                    jnp.zeros((block, 1), f32),
                    jnp.zeros((block, HEAD_DIM), f32),
                ),
            )
            att = acc / total
            limit = jnp.where(at < split, limit_ref[row, 0], limit_ref[row, 1])
            active = (limit_ref[row, 2] + h < limit).astype(f32)
            att_ref[rows, qcol] = att
            low_ref[rows, qcol] = (att * active).astype(bf16)
            lse_ref[rows, qcol] = jnp.broadcast_to(top + jnp.log2(total), (block, HEAD_DIM))
            return carry

        lax.fori_loop(0, blocks, query_block, 0)


def attend(proj, split, limits, cos2, sin2, heads):
    rows, length, _ = proj.shape
    width = heads * HEAD_DIM
    smem = pl.BlockSpec(memory_space=pltpu.SMEM)
    table = pl.BlockSpec((length, HEAD_DIM), lambda r: (0, 0))

    def whole(cols):
        return pl.BlockSpec((None, length, cols), lambda r: (r, 0, 0))

    flops = rows * heads * 4 * length * length * HEAD_DIM
    return pl.pallas_call(
        functools.partial(attend_kernel, heads, length),
        grid=(rows,),
        in_specs=[smem, smem, whole(3 * width), table, table],
        out_specs=[whole(3 * width), whole(width), whole(width), whole(width)],
        out_shape=[
            jax.ShapeDtypeStruct((rows, length, 3 * width), bf16),
            jax.ShapeDtypeStruct((rows, length, width), f32),
            jax.ShapeDtypeStruct((rows, length, width), bf16),
            jax.ShapeDtypeStruct((rows, length, width), f32),
        ],
        compiler_params=pltpu.CompilerParams(vmem_limit_bytes=56 * 2**20),
        cost_estimate=pl.CostEstimate(flops=flops, bytes_accessed=2**24, transcendentals=flops // 512),
    )(split, limits, proj, cos2, sin2)


def attend_back_kernel(heads, length, split_ref, limit_ref, qkv_ref, att_ref, lse_ref, dat_ref, cos_ref, sin_ref, dproj_ref, datt_ref, delta_ref, dq_ref):
    row = pl.program_id(0)
    split = split_ref[row]
    scale = HEAD_DIM ** (-0.5)
    block = min(BLOCK, length)
    blocks = length // block
    width = heads * HEAD_DIM
    for h in range(heads):
        qcol = pl.ds(h * HEAD_DIM, HEAD_DIM)
        kcol = pl.ds(width + h * HEAD_DIM, HEAD_DIM)
        vcol = pl.ds(2 * width + h * HEAD_DIM, HEAD_DIM)

        def prepare(i, carry):
            rows = pl.ds(pl.multiple_of(i * block, block), block)
            at = i * block + lax.broadcasted_iota(jnp.int32, (block, 1), 0)
            limit = jnp.where(at < split, limit_ref[row, 0], limit_ref[row, 1])
            active = (limit_ref[row, 2] + h < limit).astype(f32)
            datt = dat_ref[rows, qcol].astype(f32) * active
            datt_ref[rows, :] = datt.astype(bf16)
            delta = jnp.sum(datt * att_ref[rows, qcol], axis=1, keepdims=True)
            delta_ref[rows, :] = jnp.broadcast_to(delta, (block, HEAD_DIM))
            dq_ref[rows, :] = jnp.zeros((block, HEAD_DIM), f32)
            return carry

        lax.fori_loop(0, blocks, prepare, 0)

        def key_block(j, carry):
            keys = pl.ds(pl.multiple_of(j * block, block), block)
            k = qkv_ref[keys, kcol]
            v = qkv_ref[keys, vcol]
            kat = j * block + lax.broadcasted_iota(jnp.int32, (block, block), 1)

            def query_block(i, state):
                dk, dv = state
                rows = pl.ds(pl.multiple_of(i * block, block), block)
                q = qkv_ref[rows, qcol]
                datt = datt_ref[rows, :]
                at = i * block + lax.broadcasted_iota(jnp.int32, (block, 1), 0)
                low = first_key(split, at)
                ok = (kat <= at) & (kat >= low)
                s = dot(q, k, ((1,), (1,))) * (scale * LOG2E)
                lse = lse_ref[rows, qcol][:, :1]
                p = jnp.exp2(jnp.where(ok, s - lse, masked_score))
                dp = dot(datt, v, ((1,), (1,)))
                ds = (p * (dp - delta_ref[rows, :][:, :1])).astype(bf16)
                dv = dv + dot(p.astype(bf16), datt, ((0,), (0,)))
                dk = dk + dot(ds, q, ((0,), (0,)))
                dq_ref[rows, :] += dot(ds, k, ((1,), (0,)))
                return dk, dv

            stop = jnp.where((j + 1) * block <= split, (split - 1) // block + 1, blocks)
            zero = jnp.zeros((block, HEAD_DIM), f32)
            dk, dv = lax.fori_loop(j, stop, query_block, (zero, zero))
            dproj_ref[keys, kcol] = turn(dk * scale, cos_ref[keys, :], -sin_ref[keys, :]).astype(bf16)
            dproj_ref[keys, vcol] = dv.astype(bf16)
            return carry

        lax.fori_loop(0, blocks, key_block, 0)

        def finish(i, carry):
            rows = pl.ds(pl.multiple_of(i * block, block), block)
            dq = dq_ref[rows, :] * scale
            dproj_ref[rows, qcol] = turn(dq, cos_ref[rows, :], -sin_ref[rows, :]).astype(bf16)
            return carry

        lax.fori_loop(0, blocks, finish, 0)


def attend_back(qkv, att, lse, dat, split, limits, cos2, sin2, heads):
    rows, length, _ = qkv.shape
    width = heads * HEAD_DIM
    smem = pl.BlockSpec(memory_space=pltpu.SMEM)
    table = pl.BlockSpec((length, HEAD_DIM), lambda r: (0, 0))

    def whole(cols):
        return pl.BlockSpec((None, length, cols), lambda r: (r, 0, 0))

    flops = rows * heads * 10 * length * length * HEAD_DIM
    return pl.pallas_call(
        functools.partial(attend_back_kernel, heads, length),
        grid=(rows,),
        in_specs=[smem, smem, whole(3 * width), whole(width), whole(width), whole(width), table, table],
        out_specs=whole(3 * width),
        out_shape=jax.ShapeDtypeStruct((rows, length, 3 * width), bf16),
        scratch_shapes=[
            pltpu.VMEM((length, HEAD_DIM), bf16),
            pltpu.VMEM((length, HEAD_DIM), f32),
            pltpu.VMEM((length, HEAD_DIM), f32),
        ],
        compiler_params=pltpu.CompilerParams(vmem_limit_bytes=56 * 2**20),
        cost_estimate=pl.CostEstimate(flops=flops, bytes_accessed=2**24, transcendentals=flops // 1280),
    )(split, limits, qkv, att, lse, dat, cos2, sin2)


class Ring:
    def __init__(self, axis, size):
        self.axis = axis
        self.size = size
        self.order = list(range(0, size, 2)) + list(range(1, size, 2))[::-1]
        place = {w: p for p, w in enumerate(self.order)}
        self.table = [[self.order[(place[w] + k) % size] for k in range(size)] for w in range(size)]
        self.near = None
        self.right = [(w, self.order[(place[w] + 1) % size]) for w in range(size)]
        self.left = [(w, self.order[(place[w] - 1) % size]) for w in range(size)]

    def at(self, shift):
        if self.near is None:
            row = lax.dynamic_slice_in_dim(jnp.array(self.table, jnp.int32), lax.axis_index(self.axis), 1, 0)
            self.near = [row[0, k] for k in range(self.size)]
        return self.near[shift % self.size]

    def gather(self, part):
        found = [(self.at(0), part)]
        onward, back = part, part
        half = self.size // 2
        for step in range(1, half):
            onward = lax.ppermute(onward, self.axis, self.right)
            back = lax.ppermute(back, self.axis, self.left)
            found += [(self.at(-step), onward), (self.at(step), back)]
        cut = part.shape[0] // 2
        first = lax.ppermute(onward[:cut], self.axis, self.right)
        second = lax.ppermute(back[cut:], self.axis, self.left)
        found.append((self.at(half), jnp.concatenate([first, second], axis=0)))
        return found

    def gather_whole(self, part):
        whole = jnp.zeros((self.size,) + part.shape, part.dtype)
        for owner, piece in self.gather(part):
            whole = lax.dynamic_update_slice_in_dim(whole, piece[None], owner, 0)
        return whole

    def scatter(self, term):
        sums = [term(self.at(-1), 0), term(self.at(1), 1)]
        for step in range(2, self.size + 1):
            for side, perm, sign in ((0, self.right, -1), (1, self.left, 1)):
                come = lax.ppermute(sums[side].astype(bf16), self.axis, perm)
                sums[side] = come.astype(f32) + term(self.at(sign * step), side)
        return sums


def join(*arrays):
    return lax.optimization_barrier(arrays)


def after(array, *others):
    return lax.optimization_barrier((array,) + others)[0]


def place_kernel(count, targets, *refs):
    pieces, whole, held, in_sems, out_sems = refs[:-4], refs[-4], refs[-3], refs[-2], refs[-1]
    spots = [(i, k) for i in range(len(pieces)) for k in range(count)]
    loads = [
        pltpu.make_async_copy(pieces[i].at[k], held.at[at], in_sems.at[at]) for at, (i, k) in enumerate(spots)
    ]
    stores = [
        pltpu.make_async_copy(held.at[at], whole.at[targets(i, k)], out_sems.at[at])
        for at, (i, k) in enumerate(spots)
    ]
    for load in loads:
        load.start()
    for load, store in zip(loads, stores):
        load.wait()
        store.start()
    for store in stores:
        store.wait()


def place(pieces, total, targets):
    count = pieces[0].shape[0]
    anywhere = pl.BlockSpec(memory_space=pl.ANY)
    shape = (total,) + pieces[0].shape[1:]
    size = 2 * 2 * total * pieces[0][0].size
    return pl.pallas_call(
        functools.partial(place_kernel, count, targets),
        in_specs=[anywhere] * len(pieces),
        out_specs=anywhere,
        out_shape=jax.ShapeDtypeStruct(shape, pieces[0].dtype),
        scratch_shapes=[
            pltpu.VMEM((len(pieces) * count,) + pieces[0].shape[1:], pieces[0].dtype),
            pltpu.SemaphoreType.DMA((len(pieces) * count,)),
            pltpu.SemaphoreType.DMA((len(pieces) * count,)),
        ],
        compiler_params=pltpu.CompilerParams(vmem_limit_bytes=40 * 2**20),
        cost_estimate=pl.CostEstimate(flops=0, bytes_accessed=size, transcendentals=0),
    )(*pieces)


def up_sum_kernel(narrow, act_ref, dpre_ref, out_ref):
    shard = out_ref.shape[-2]
    total = dot(act_ref[...], dpre_ref[...], ((0,), (0,))).astype(bf16)
    for y in range(2):
        for core in range(2):
            at = (2 * y + core) * shard
            out_ref[core, 0, 0, y] = total[at : at + shard]


def up_sums(act, dpre, wide, narrow, shard):
    tokens, cols = dpre.shape
    upper = wide // 4
    if (narrow * shard) % 128:
        total = dot(act, dpre, ((0,), (0,))).astype(bf16)
        total = total.reshape(upper, 2, 2, 2, 2, shard, cols).transpose(4, 2, 0, 1, 3, 5, 6)
        return total.reshape(2, 2, upper, 4, shard, cols)
    return pl.pallas_call(
        functools.partial(up_sum_kernel, narrow),
        grid=(wide,),
        in_specs=[
            pl.BlockSpec((tokens, narrow * shard), lambda w: (0, w)),
            pl.BlockSpec((tokens, cols), lambda w: (0, 0)),
        ],
        out_specs=pl.BlockSpec((2, 1, 1, 2, shard, cols), lambda w: (0, w % 2, w // 4, (w // 2) % 2, 0, 0)),
        out_shape=jax.ShapeDtypeStruct((2, 2, upper, 4, shard, cols), bf16),
        compiler_params=pltpu.CompilerParams(vmem_limit_bytes=40 * 2**20),
        cost_estimate=pl.CostEstimate(
            flops=2 * tokens * cols * act.shape[1], bytes_accessed=2**24, transcendentals=0
        ),
    )(act, dpre)


MESH = pl.DeviceIdType.MESH
TILE = 512
Y, Z, CORE, X, FAR = range(5)


def each(count, body):
    def step(i, carry):
        body(i)
        return carry

    lax.fori_loop(0, count, step, 0)


def feed_kernel(
    act_many,
    top_zero,
    top_one,
    top_two,
    top_three,
    scale,
    ups,
    downs,
    down_zero,
    x_ref,
    low_ref,
    out_ref,
    coef_ref,
    router_ref,
    small,
    block_out,
    grad_x,
    branch,
    dat_out,
    out_own,
    out_come,
    out_other,
    down_own,
    down_come,
    up_own,
    up_come,
    down_core,
    up_core,
    up,
    down,
    act,
    dmix,
    hid,
    dpre,
    mixed,
    dact,
    mixed_low,
    dact_low,
    down_near,
    up_near,
    held,
    down_sum,
    mixed_come,
    dact_come,
    x_one,
    load_sem,
    send_sem,
    recv_sem,
    dat_send_sem,
    dat_recv_sem,
    out_send_sem,
    out_recv_sem,
    side_send_sem,
    side_recv_sem,
):
    w = lax.axis_index("wide")
    n = lax.axis_index("narrow")
    core, x, far = n % 2, w % 2, w // 4
    peers = {
        Y: {"narrow": (n + 2) % 4},
        Z: {"wide": w + 2 - 4 * ((w // 2) % 2)},
        CORE: {"narrow": n + 1 - 2 * core},
        X: {"wide": w + 1 - 2 * x},
        FAR: {"wide": (w + 4) % 8},
    }
    rows, dim = x_ref.shape
    started = []

    def send(source, target, peer):
        at = len(started)
        copy = pltpu.make_async_remote_copy(
            src_ref=source,
            dst_ref=target,
            send_sem=send_sem.at[at],
            recv_sem=recv_sem.at[at],
            device_id=peers[peer],
            device_id_type=MESH,
        )
        copy.start()
        started.append(copy)
        return copy

    def load(source, target, at):
        copy = pltpu.make_async_copy(source, target, load_sem.at[at])
        copy.start()
        return copy

    def slot(k):
        return pl.ds(k * rows, rows)

    barrier = pltpu.get_barrier_semaphore()
    others = [{"wide": (w + k) % 8} for k in range(1, 8)]
    for peer in others + [peers[Y], peers[CORE]]:
        pl.semaphore_signal(barrier, inc=1, device_id=peer, device_id_type=MESH)
    pl.semaphore_wait(barrier, len(others) + 2)

    loads = [load(act_many, act, 0)]
    for k, top in enumerate((top_zero, top_one, top_two, top_three)):
        loads.append(load(top, dmix.at[slot(k)], 1 + k))
    up_loads, down_loads = [], []
    for its in range(2):
        its_core = core + (1 - 2 * core) * its
        for k in range(4):
            its_far = far + (1 - 2 * far) * (k % 2)
            its_x = x + (1 - 2 * x) * (k // 2)
            source = downs.at[its, k] if its or k else down_zero
            up_loads.append(load(ups.at[its, k], up.at[its_far, :, its_x, :, its_core], 27 + 4 * its + k))
            down_loads.append(load(source, down.at[its_core, its_x, its_far], 35 + 4 * its + k))
    for copy in loads + up_loads:
        copy.wait()

    def columns(t):
        return pl.ds(pl.multiple_of(t * TILE, TILE), TILE)

    def group_of(pair):
        return pl.ds(pair * 2 * rows, 2 * rows)

    def hidden_of(pair):
        group = group_of(pair)
        width = scale[group, :][:, 1:2]

        def scaled(i):
            at = pl.ds(pl.multiple_of(pair * 2 * rows + i * 32, 32), 32)
            dmix[at, :] = (dmix[at, :].astype(f32) * scale[at, :][:, :1]).astype(bf16)

        def first(t):
            at = columns(t)
            weight = up[:, :, :, :, :, :, at].reshape(dim, TILE)
            pre = jnp.maximum(dot(act[group, :], weight, ((1,), (0,))), 0.0)
            pre = jnp.where(router_ref[6:7, at] <= width, pre, 0.0)
            dpre[group, at] = pre.astype(bf16)
            hid[group, at] = (pre * pre).astype(bf16)

        each(2 * rows // 32, scaled)
        each(dim // TILE, first)

    def mixed_of(pair):
        group = group_of(pair)

        def second(t):
            at = columns(t)
            weight = down[:, :, :, :, at].reshape(dim, TILE)
            mixed[group, at] = dot(hid[group, :], weight, ((1,), (0,))).astype(bf16)

        each(dim // TILE, second)

    def dact_of(pair):
        group = group_of(pair)

        def third(t):
            at = columns(t)
            weight = down[t // 2, t % 2].reshape(TILE, dim)
            value = dot(dmix[group, :], weight, ((1,), (1,)))
            dpre[group, at] = (value * 2.0 * dpre[group, at].astype(f32)).astype(bf16)

        def fourth(t):
            at = columns(t)
            weight = up[t // 2, t % 2].reshape(TILE, dim)
            dact[group, at] = dot(dpre[group, :], weight, ((1,), (1,))).astype(bf16)

        each(dim // TILE, third)
        each(dim // TILE, fourth)

    cut = dim // 2

    def side_of(k):
        return pl.ds((k % 2) * cut, cut)

    def down_terms(k):
        def block(i):
            rows_of = hid[:, columns(i)]
            value = dot(rows_of, dmix[:, side_of(k)], ((0,), (0,))).astype(bf16)
            down_sum[i // 2, i % 2, :, :, :, :, side_of(k)] = value.reshape(2, 2, 2, TILE // 8, cut)

        each(dim // TILE, block)
        return send(down_sum.at[1 - core, :, :, :, :, :, side_of(k)], down_core.at[k], CORE)

    def up_terms(k):
        def block(i):
            rows_of = act[:, columns(i)]
            value = dot(rows_of, dpre[:, side_of(k)], ((0,), (0,))).astype(bf16)
            up[i // 2, i % 2, :, :, :, :, side_of(k)] = value.reshape(2, 2, 2, TILE // 8, cut)

        each(dim // TILE, block)
        return send(up.at[:, :, :, :, 1 - core, :, side_of(k)], up_core.at[k % 2], CORE)

    def core_sum(k):
        cores[k].wait_recv()

        def add(i, a, b):
            c, d = i // 2, i % 2
            come = held[c, d].astype(f32)
            if k < 2:
                here = down_sum[core, a, b, c, d, :, side_of(k)].astype(f32)
                down_sum[core, a, b, c, d, :, side_of(k)] = (here + come).astype(bf16)
            else:
                here = up[a, b, c, d, core, :, side_of(k)].astype(f32)
                up[a, b, c, d, core, :, side_of(k)] = (here + come).astype(bf16)

        for a in range(2):
            for b in range(2):
                load((down_core if k < 2 else up_core).at[k % 2, a, b], held, 15 + k).wait()
                each(4, functools.partial(add, a=a, b=b))
        if k < 2:
            source = down_sum.at[core, 1 - x, :, :, :, :, side_of(k)]
            return send(source, down_near.at[:, :, :, :, side_of(k)], X)
        source = up.at[:, :, 1 - x, :, core, :, side_of(k)]
        return send(source, up_near.at[:, :, :, :, side_of(k)], X)

    def near_sum(k):
        nears[k].wait_recv()

        def add(i):
            a, b, c = i // 4, (i // 2) % 2, i % 2
            if k < 2:
                here = down_sum[core, x, a, b, c, :, side_of(k)].astype(f32)
                come = down_near[a, b, c, :, side_of(k)].astype(f32)
                down_sum[core, x, a, b, c, :, side_of(k)] = (here + come).astype(bf16)
            else:
                here = up[a, b, x, c, core, :, side_of(k)].astype(f32)
                come = up_near[a, b, c, :, side_of(k)].astype(f32)
                up[a, b, x, c, core, :, side_of(k)] = (here + come).astype(bf16)

        each(8, add)
        if k < 2:
            fars.append(
                send(
                    down_sum.at[core, x, 1 - far, :, :, :, side_of(k)],
                    down_come.at[:, :, :, side_of(k)],
                    FAR,
                )
            )
            source = down_sum.at[core, x, far, :, :, :, side_of(k)]
            keep.append(load(source, down_own.at[:, :, :, side_of(k)], 19 + k))
        else:
            source = up.at[1 - far, :, x, :, core, :, side_of(k)]
            fars.append(send(source, up_come.at[:, :, :, side_of(k)], FAR))
            source = up.at[far, :, x, :, core, :, side_of(k)]
            keep.append(load(source, up_own.at[:, :, :, side_of(k)], 19 + k))

    def add_low(total, k, low, side):
        def step(i):
            at = pl.ds(pl.multiple_of(k * rows + i * 32, 32), 32)
            come = low[side, pl.ds(pl.multiple_of(i * 32, 32), 32), :].astype(f32)
            total[at, :] = (total[at, :].astype(f32) + come).astype(bf16)

        each(rows // 32, step)

    cores, nears, fars, keep = [], [], [], []
    hidden_of(0)
    for copy in down_loads:
        copy.wait()
    mixed_of(0)
    mixed_one = send(mixed.at[slot(1)], mixed_low.at[0], Y)
    hidden_of(1)
    mixed_of(1)
    mixed_three = send(mixed.at[slot(3)], mixed_low.at[1], Y)
    cores.append(down_terms(0))
    cores.append(down_terms(1))
    dact_of(1)
    dact_two = send(dact.at[slot(2)], dact_low.at[0], Z)
    dact_three = send(dact.at[slot(3)], dact_low.at[1], Z)
    nears.append(core_sum(0))
    nears.append(core_sum(1))
    dact_of(0)
    out_load = load(out_ref, down, 13)
    x_load = load(x_ref, x_one, 14)
    top_load = load(top_zero, hid.at[slot(0)], 0)
    cores.append(up_terms(2))
    cores.append(up_terms(3))
    near_sum(0)
    nears.append(core_sum(2))
    nears.append(core_sum(3))
    near_sum(1)

    dact_two.wait_recv()
    dact_three.wait_recv()
    add_low(dact, 1, dact_low, 1)
    dact_last = send(dact.at[slot(1)], dact_come, Y)
    mixed_one.wait_recv()
    mixed_three.wait_recv()
    add_low(mixed, 2, mixed_low, 1)
    mixed_last = send(mixed.at[slot(2)], mixed_come, Z)
    add_low(mixed, 0, mixed_low, 0)
    add_low(dact, 0, dact_low, 0)
    near_sum(2)

    small[...] = jnp.zeros_like(small)
    x_load.wait()
    top_load.wait()
    mixed_last.wait_recv()
    dact_last.wait_recv()
    gain, bias = router_ref[4:5, :], router_ref[5:6, :]

    def back(i):
        def part(k):
            return pl.ds(pl.multiple_of(k * rows + i * 16, 16), 16)

        at = part(0)
        value = x_one[at, :]
        center = value - jnp.mean(value, axis=-1, keepdims=True)
        inv = lax.rsqrt(jnp.mean(center * center, axis=-1, keepdims=True) + norm_eps)
        normed = center * inv
        its_mixed = mixed[at, :].astype(f32) + mixed_come[at, :].astype(f32)
        grad = dact[at, :].astype(f32) + dact_come[at, :].astype(f32)
        top = hid[at, :].astype(f32)
        hid[part(3), :] = (value + its_mixed * scale[at, :][:, :1]).astype(bf16)
        logits = coef_ref[at, :] * jnp.sum(top * its_mixed, axis=-1, keepdims=True)
        ln_out = normed * gain + bias
        for c in range(WIDTHS):
            one = logits[:, c : c + 1]
            grad = grad + one * router_ref[c : c + 1, :]
            small[3 + c : 4 + c, :] += jnp.sum(ln_out * one, axis=0, keepdims=True)
        small[1:2, :] += jnp.sum(grad * normed, axis=0, keepdims=True)
        small[2:3, :] += jnp.sum(grad, axis=0, keepdims=True)
        grad = grad * gain
        mean = jnp.mean(grad, axis=-1, keepdims=True)
        along = jnp.mean(grad * normed, axis=-1, keepdims=True)
        total = top + inv * (grad - mean - normed * along)
        x_one[at, :] = total
        hid[part(2), :] = total.astype(bf16)

    each(rows // 16, back)
    keep.append(load(x_one, grad_x, 23))
    keep.append(load(hid.at[slot(2)], branch, 24))
    keep.append(load(hid.at[slot(3)], block_out, 25))
    out_load.wait()
    cols = dim // 8

    def dat_block(owner):
        at = pl.ds(pl.multiple_of(owner * cols, cols), cols)
        weight = down[owner // 4, (owner // 2) % 2, owner % 2]
        hid[slot(1), at] = dot(hid[slot(2), :], weight, ((1,), (1,))).astype(bf16)
        return hid.at[slot(1), at]

    dats = []
    for k in range(1, 8):
        owner = (w + k) % 8
        copy = pltpu.make_async_remote_copy(
            src_ref=dat_block(owner),
            dst_ref=dat_out.at[w],
            send_sem=dat_send_sem.at[k - 1],
            recv_sem=dat_recv_sem.at[k - 1],
            device_id={"wide": owner},
            device_id_type=MESH,
        )
        copy.start()
        dats.append(copy)
    keep.append(load(dat_block(w), dat_out.at[w], 26))

    low_load = load(low_ref, hid.at[slot(0)], 1)
    low_load.wait()
    shard = dim // 32
    half_rows = dim // 2

    def out_block(i):
        for k, place in enumerate((act, dpre)):
            at = pl.ds(pl.multiple_of(k * half_rows + i * cols, cols), cols)
            value = dot(hid[slot(0), at], hid[slot(2), :], ((0,), (0,))).astype(bf16)
            place[pl.ds(pl.multiple_of(i * cols, cols), cols), :] = value

    each(half_rows // cols, out_block)

    def out_rows(i, its_core):
        return pl.ds(pl.multiple_of((2 * (i % 8) + its_core) * shard, shard), shard)

    outs = []
    for i in range(16):
        copy = pltpu.make_async_remote_copy(
            src_ref=(act if i < 8 else dpre).at[out_rows(i, 1 - core)],
            dst_ref=dmix.at[pl.ds(i * shard, shard)],
            send_sem=out_send_sem.at[i],
            recv_sem=out_recv_sem.at[i],
            device_id=peers[CORE],
            device_id_type=MESH,
        )
        copy.start()
        outs.append(copy)
    for copy in outs:
        copy.wait_recv()

    def out_add(i):
        for k, place in enumerate((act, dpre)):
            at = pl.ds(pl.multiple_of((k * 8 + i) * shard, shard), shard)
            mine = place[out_rows(i, core), :].astype(f32)
            dmix[at, :] = (mine + dmix[at, :].astype(f32)).astype(bf16)

    each(8, out_add)
    y = n // 2
    for i in range(8):
        keep.append(load(dmix.at[pl.ds((2 * i + y) * shard, shard)], out_own.at[i], 43 + i))
    out_ys = []
    for i in range(8):
        source = dmix.at[pl.ds((2 * i + 1 - y) * shard, shard)]
        if i < 4:
            copy = pltpu.make_async_remote_copy(
                src_ref=source,
                dst_ref=out_come.at[i],
                send_sem=side_send_sem.at[i],
                recv_sem=side_recv_sem.at[i],
                device_id=peers[Y],
                device_id_type=MESH,
            )
            copy.start()
            out_ys.append(copy)
        else:
            keep.append(load(source, out_other.at[i - 4], 51 + i))
    near_sum(3)
    for copy in keep:
        copy.wait()
    for copy in fars + dats + out_ys:
        copy.wait_recv()
    for copy in started + dats + outs + out_ys:
        copy.wait_send()


def feed_forward(act, tops, facts, ups, downs, down, x_one, low, out_full, coef, router):
    rows, dim = x_one.shape
    any_space = pl.BlockSpec(memory_space=pl.ANY)
    in_vmem = pl.BlockSpec(memory_space=pltpu.VMEM)
    tokens = 4 * rows
    cut = dim // 2
    shard = dim // 32

    def shape(*dims):
        return jax.ShapeDtypeStruct(dims, bf16)

    return pl.pallas_call(
        feed_kernel,
        in_specs=[any_space] * 5 + [in_vmem] + [any_space] * 6 + [in_vmem] * 2,
        out_specs=[in_vmem] + [any_space] * 13,
        out_shape=[
            jax.ShapeDtypeStruct((8, dim), f32),
            shape(rows, dim),
            jax.ShapeDtypeStruct((rows, dim), f32),
            shape(rows, dim),
            shape(8, rows, dim // 8),
            shape(8, shard, dim),
            shape(4, shard, dim),
            shape(4, shard, dim),
            shape(2, 2, shard, dim),
            shape(2, 2, shard, dim),
            shape(2, 2, shard, dim),
            shape(2, 2, shard, dim),
            shape(2, 2, 2, 2, 2, shard, cut),
            shape(2, 2, 2, 2, 2, shard, cut),
        ],
        scratch_shapes=[
            pltpu.VMEM((2, 2, 2, 2, 2, shard, dim), bf16),
            pltpu.VMEM((2, 2, 2, dim // 8, dim), bf16),
            pltpu.VMEM((tokens, dim), bf16),
            pltpu.VMEM((tokens, dim), bf16),
            pltpu.VMEM((tokens, dim), bf16),
            pltpu.VMEM((tokens, dim), bf16),
            pltpu.VMEM((tokens, dim), bf16),
            pltpu.VMEM((tokens, dim), bf16),
            pltpu.VMEM((2, rows, dim), bf16),
            pltpu.VMEM((2, rows, dim), bf16),
            pltpu.VMEM((2, 2, 2, shard, dim), bf16),
            pltpu.VMEM((2, 2, 2, shard, dim), bf16),
            pltpu.VMEM((2, 2, shard, cut), bf16),
            pltpu.VMEM((2, 2, 2, 2, 2, shard, dim), bf16),
            pltpu.VMEM((rows, dim), bf16),
            pltpu.VMEM((rows, dim), bf16),
            pltpu.VMEM((rows, dim), f32),
            pltpu.SemaphoreType.DMA((59,)),
            pltpu.SemaphoreType.DMA((36,)),
            pltpu.SemaphoreType.DMA((36,)),
            pltpu.SemaphoreType.DMA((7,)),
            pltpu.SemaphoreType.DMA((7,)),
            pltpu.SemaphoreType.DMA((16,)),
            pltpu.SemaphoreType.DMA((16,)),
            pltpu.SemaphoreType.DMA((4,)),
            pltpu.SemaphoreType.DMA((4,)),
        ],
        compiler_params=pltpu.CompilerParams(
            collective_id=0, has_side_effects=True, vmem_limit_bytes=63 * 2**20 + 2**19
        ),
        cost_estimate=pl.CostEstimate(
            flops=12 * tokens * dim * dim, bytes_accessed=2**25, transcendentals=0
        ),
    )(act, *tops, facts, ups, downs, down, x_one, low, out_full, coef, router)


def ring_index(place):
    place = place % 8
    upper = place // 4
    return (1 - upper) * 2 * place + upper * (2 * (7 - place) + 1)


def first_kernel(
    split_ref,
    limit_ref,
    tokens_ref,
    gain_ref,
    cos_ref,
    sin_ref,
    qkv_part,
    out_part,
    up_part,
    down_part,
    top_zero,
    onehot_ref,
    router_ref,
    gain_two_ref,
    bias_two_ref,
    qkv,
    att,
    lse,
    x_one,
    coef,
    facts,
    low_out,
    act_many,
    act_out,
    weight_out,
    out_full,
    ups,
    downs,
    top_one,
    top_two,
    top_three,
    act,
    weight,
    low,
    out_held,
    act_two,
    local_sem,
    send_sem,
    recv_sem,
    qkv_send_sem,
    qkv_recv_sem,
    low_send_sem,
    low_recv_sem,
    up_send_sem,
    up_recv_sem,
    up_local_sem,
    out_sem,
):
    w = lax.axis_index("wide")
    n = lax.axis_index("narrow")
    core, y, far, z = n % 2, n // 2, w // 4, (w // 2) % 2
    odd = w % 2
    place = w // 2 + odd * (7 - 2 * (w // 2))
    rows, dim = tokens_ref.shape
    cols = weight.shape[3] // 3
    heads = cols // HEAD_DIM
    right, left = {"wide": ring_index(place + 1)}, {"wide": ring_index(place + 7)}
    to_y, to_core = {"narrow": (n + 2) % 4}, {"narrow": n + 1 - 2 * core}
    to_z, to_x = {"wide": w + 2 - 4 * z}, {"wide": w + 1 - 2 * odd}
    to_far = {"wide": (w + 4) % 8}
    to_both = {"wide": w + 2 - 4 * z, "narrow": (n + 2) % 4}
    barrier = pltpu.get_barrier_semaphore()
    peers = [{"wide": (w + k) % 8} for k in range(1, 8)] + [to_y, to_core, to_both]
    for peer in peers:
        pl.semaphore_signal(barrier, inc=1, device_id=peer, device_id_type=MESH)
    pl.semaphore_wait(barrier, len(peers))
    started, kept = [], []
    up_zero, up_far, up_next, up_both = (ups.at[0, k] for k in range(4))
    down_next = downs.at[0, 2]

    def send(source, target, peer):
        at = len(started)
        copy = pltpu.make_async_remote_copy(
            src_ref=source,
            dst_ref=target,
            send_sem=send_sem.at[at],
            recv_sem=recv_sem.at[at],
            device_id=peer,
            device_id_type=MESH,
        )
        copy.start()
        started.append(copy)
        return copy

    def keep(source, target):
        copy = pltpu.make_async_copy(source, target, local_sem.at[len(kept)])
        copy.start()
        kept.append(copy)
        return copy

    def norm(i):
        at = pl.ds(pl.multiple_of(i * 32, 32), 32)
        value = tokens_ref[at, :].astype(f32)
        inv = lax.rsqrt(jnp.mean(value * value, axis=-1, keepdims=True) + norm_eps)
        act[w, at, :] = (value * inv * gain_ref[...]).astype(bf16)

    each(rows // 32, norm)

    first, second = pl.ds(0, rows // 2), pl.ds(rows // 2, rows // 2)
    shard = out_part.shape[0]
    out_first, out_second = pl.ds(0, shard // 2), pl.ds(shard // 2, shard // 2)
    onward = send(act.at[w], act.at[w], right)
    back = send(act.at[w], act.at[w], left)
    exchanges = []
    for k in range(1, 8):
        target = (w + k) % 8
        for part in range(3):
            source = qkv_part.at[:, pl.ds(pl.multiple_of(part * dim + target * cols, cols), cols)]
            copy = pltpu.make_async_remote_copy(
                src_ref=source,
                dst_ref=weight.at[w, n, :, pl.ds(part * cols, cols)],
                send_sem=qkv_send_sem.at[k - 1, part],
                recv_sem=qkv_recv_sem.at[k - 1, part],
                device_id={"wide": target},
                device_id_type=MESH,
            )
            copy.start()
            exchanges.append(copy)
    for part in range(3):
        source = qkv_part.at[:, pl.ds(pl.multiple_of(part * dim + w * cols, cols), cols)]
        keep(source, weight.at[w, n, :, pl.ds(part * cols, cols)])
    out_onward = send(out_part, out_full.at[w, n], right)
    out_back = send(out_part, out_full.at[w, n], left)
    out_own = keep(out_part, out_full.at[w, n])
    out_y = [send(out_part, out_full.at[w, n], to_y)]
    team = z * 2 + y
    piece = down_part.shape[0]

    def up_block(its_z, its_y, share):
        its_w = (share % 2) * 4 + its_z * 2 + (share // 2) % 2
        its_n = its_y * 2 + share // 4
        return up_part.at[:, pl.ds(pl.multiple_of((its_w * 4 + its_n) * piece, piece), piece)]

    swaps, up_own = [], []
    for share in range(8):
        target = up_zero.at[team, :, pl.ds(share * piece, piece)]
        for k, (its_z, its_y, peer) in enumerate(((z, 1 - y, to_y), (1 - z, y, to_z), (1 - z, 1 - y, to_both))):
            copy = pltpu.make_async_remote_copy(
                src_ref=up_block(its_z, its_y, share),
                dst_ref=target,
                send_sem=up_send_sem.at[k, share],
                recv_sem=up_recv_sem.at[k, share],
                device_id=peer,
                device_id_type=MESH,
            )
            copy.start()
            swaps.append(copy)
        copy = pltpu.make_async_copy(up_block(z, y, share), target, up_local_sem.at[share])
        copy.start()
        up_own.append(copy)

    def ring_hop(step):
        nonlocal onward, back, out_onward, out_back
        behind, ahead = ring_index(place + 8 - step), ring_index(place + step)
        onward.wait_recv()
        back.wait_recv()
        if step < 3:
            onward = send(act.at[behind], act.at[behind], right)
            back = send(act.at[ahead], act.at[ahead], left)
        else:
            onward = send(act.at[behind, first], act.at[behind, first], right)
            back = send(act.at[ahead, second], act.at[ahead, second], left)
        out_onward.wait_recv()
        out_back.wait_recv()
        for owner in (behind, ahead):
            out_y.append(send(out_full.at[owner, n], out_full.at[owner, n], to_y))
        if step < 3:
            out_onward = send(out_full.at[behind, n], out_full.at[behind, n], right)
            out_back = send(out_full.at[ahead, n], out_full.at[ahead, n], left)
        else:
            out_onward = send(out_full.at[behind, n, out_first], out_full.at[behind, n, out_first], right)
            out_back = send(out_full.at[ahead, n, out_second], out_full.at[ahead, n, out_second], left)

    def project(owner):
        at = pl.ds(pl.multiple_of(owner * rows, rows), rows)
        for part in range(3):
            its = weight[:, :, :, pl.ds(part * cols, cols)].reshape(dim, cols)
            value = dot(act[owner], its, ((1,), (0,)))
            for h in range(heads):
                piece = value[:, h * HEAD_DIM : (h + 1) * HEAD_DIM]
                if part < 2:
                    piece = turn(piece, cos_ref[at, :], sin_ref[at, :])
                qkv[at, pl.ds(part * cols + h * HEAD_DIM, HEAD_DIM)] = piece.astype(bf16)

    def project_pair(step):
        each(2, lambda i: project(ring_index(place + 8 - step + 2 * step * i)))

    for copy in kept[:3]:
        copy.wait()
    for copy in exchanges:
        copy.wait_recv()
    weight_y = send(weight.at[:, n], weight.at[:, n], to_y)
    ring_hop(1)
    weight_y.wait_recv()
    weight_core = [
        send(weight.at[:, n], weight.at[:, n], to_core),
        send(weight.at[:, (n + 2) % 4], weight.at[:, (n + 2) % 4], to_core),
    ]
    beside = send(top_zero, top_one, to_y)
    for copy in weight_core:
        copy.wait_recv()
    each(1, lambda i: project(w + i))
    project_pair(1)
    ring_hop(2)
    project_pair(2)
    ring_hop(3)
    for copy in swaps:
        copy.wait_recv()
    for copy in up_own:
        copy.wait()
    up_to_far = send(up_zero, up_far, to_far)
    up_to_x = send(up_zero, up_next, to_x)
    down_to_x = send(down_part, down_next, to_x)
    cores = [send(up_zero, ups.at[1, 0], to_core), send(down_part, downs.at[1, 0], to_core)]
    across = send(top_zero, top_two, to_z)
    project_pair(3)
    onward.wait_recv()
    back.wait_recv()
    project(ring_index(place + 4))
    out_onward.wait_recv()
    out_back.wait_recv()
    out_own.wait()
    last = ring_index(place + 4)
    out_y.append(send(out_full.at[last, n], out_full.at[last, n], to_y))
    keep(act, act_out)
    keep(weight, weight_out)

    split = split_ref[0]
    factor = HEAD_DIM ** (-0.5) * LOG2E
    block = 2 * rows
    limit_one, limit_two, head_first = limit_ref[0, 0], limit_ref[0, 1], limit_ref[0, 2]

    def low_send(target):
        return pltpu.make_async_remote_copy(
            src_ref=low.at[pl.ds(target * rows, rows)],
            dst_ref=low_out.at[:, pl.ds(pl.multiple_of(w * cols, cols), cols)],
            send_sem=low_send_sem.at[target],
            recv_sem=low_recv_sem.at[w],
            device_id={"wide": target},
            device_id_type=MESH,
        )

    def low_come(source):
        return pltpu.make_async_remote_copy(
            src_ref=low.at[pl.ds(source * rows, rows)],
            dst_ref=low_out.at[:, pl.ds(source * cols, cols)],
            send_sem=low_send_sem.at[source],
            recv_sem=low_recv_sem.at[source],
            device_id={"wide": source},
            device_id_type=MESH,
        )

    def low_keep(target):
        return pltpu.make_async_copy(
            low.at[pl.ds(target * rows, rows)],
            low_out.at[:, pl.ds(target * cols, cols)],
            low_send_sem.at[target],
        )

    for i in range(4):
        at_rows = pl.ds(i * block, block)
        at = i * block + lax.broadcasted_iota(jnp.int32, (block, 1), 0)
        lowest = jnp.where(at >= split, split, 0)

        def keys_of(j, state, diagonal):
            keys = pl.ds(pl.multiple_of(j * block, block), block)
            kat = j * block + lax.broadcasted_iota(jnp.int32, (block, block), 1)
            ok = kat >= lowest
            if diagonal:
                ok = ok & (kat <= at)
            found = []
            for h in range(heads):
                top, total, acc = state[h]
                q = qkv[at_rows, pl.ds(h * HEAD_DIM, HEAD_DIM)]
                k = qkv[keys, pl.ds(cols + h * HEAD_DIM, HEAD_DIM)]
                v = qkv[keys, pl.ds(2 * cols + h * HEAD_DIM, HEAD_DIM)]
                s = jnp.where(ok, dot(q, k, ((1,), (1,))) * factor, masked_score)
                new_top = jnp.maximum(top, jnp.max(s, axis=1, keepdims=True))
                p = jnp.exp2(s - new_top)
                fade = jnp.exp2(top - new_top)
                total = total * fade + jnp.sum(p, axis=1, keepdims=True)
                acc = acc * fade + dot(p.astype(bf16), v, ((1,), (0,)))
                found.append((new_top, total, acc))
            return tuple(found)

        start = (
            jnp.full((block, 1), masked_score, f32),
            jnp.zeros((block, 1), f32),
            jnp.zeros((block, HEAD_DIM), f32),
        )
        state = (start,) * heads
        if i:
            state = lax.fori_loop(0, i, functools.partial(keys_of, diagonal=False), state)
        state = keys_of(i, state, True)
        limit = jnp.where(at < split, limit_one, limit_two)
        for h in range(heads):
            top, total, acc = state[h]
            value = acc / total
            head = pl.ds(h * HEAD_DIM, HEAD_DIM)
            active = (head_first + h < limit).astype(f32)
            att[at_rows, head] = value
            low[at_rows, head] = (value * active).astype(bf16)
            lse[at_rows, head] = jnp.broadcast_to(top + jnp.log2(total), (block, HEAD_DIM))
        for target in (2 * i, 2 * i + 1):

            @pl.when(w != target)
            def _():
                low_send(target).start()

            @pl.when(w == target)
            def _():
                low_keep(target).start()

        if i == 0:
            for copy in out_y:
                copy.wait_recv()
            out_core = [
                send(out_full.at[:, n], out_full.at[:, n], to_core),
                send(out_full.at[:, (n + 2) % 4], out_full.at[:, (n + 2) % 4], to_core),
            ]
        if i == 2:
            across.wait_recv()
            both = send(top_two, top_three, to_y)
    part_rows = down_part.shape[0] // 2
    parts = [pl.ds(0, part_rows), pl.ds(part_rows, part_rows)]
    down_fars = [send(down_part.at[parts[0]], downs.at[0, 1, parts[0]], to_far)]
    up_to_far.wait_recv()
    up_to_both = send(up_far, up_both, to_x)
    cores.append(send(up_far, ups.at[1, 1], to_core))
    for copy in out_core:
        copy.wait_recv()
    held = []
    for k in range(8):
        held.append(pltpu.make_async_copy(out_full.at[k], out_held.at[k], out_sem.at[k]))
        held[-1].start()
    for target in range(8):

        @pl.when(w != target)
        def _():
            low_send(target).wait_send()
            low_come(target).wait_recv()

        @pl.when(w == target)
        def _():
            low_keep(target).wait()

    down_fars.append(send(down_part.at[parts[1]], downs.at[0, 1, parts[1]], to_far))
    for copy in held:
        copy.wait()

    def branch(t):
        at = pl.ds(pl.multiple_of(t * 256, 256), 256)
        value = dot(low_out[...], out_held[:, :, :, at].reshape(dim, 256), ((1,), (0,)))
        x_one[:, at] = tokens_ref[:, at].astype(f32) + value

    each(dim // 256, branch)
    gain_two, bias_two = gain_two_ref[...], bias_two_ref[...]
    lane = lax.broadcasted_iota(jnp.int32, (32, 8), 1)
    wide_lane = lax.broadcasted_iota(jnp.int32, (32, 128), 1)

    def normalize(i):
        at = pl.ds(pl.multiple_of(i * 32, 32), 32)
        value = x_one[at, :]
        center = value - jnp.mean(value, axis=-1, keepdims=True)
        inv = lax.rsqrt(jnp.mean(center * center, axis=-1, keepdims=True) + norm_eps)
        ln_out = center * inv * gain_two + bias_two
        act_two[at, :] = ln_out.astype(bf16)
        logits = lax.dot_general(
            ln_out, router_ref[...], (((1,), (1,)), ((), ())), precision=highest, preferred_element_type=f32
        )
        logits = jnp.where(lane < WIDTHS, logits, masked_score)
        powers = jnp.exp(logits - jnp.max(logits, axis=-1, keepdims=True))
        prob = powers / jnp.sum(powers, axis=-1, keepdims=True)
        hot = onehot_ref[at, :]
        chosen = jnp.sum(prob * hot, axis=-1, keepdims=True)
        width = jnp.sum(hot * lane.astype(f32), axis=-1, keepdims=True)
        coef[at, :] = chosen * (hot - prob)
        facts[at, :] = jnp.where(wide_lane == 0, chosen, width)

    each(rows // 32, normalize)

    def slot(k):
        return pl.ds(k * rows, rows)

    act_y = send(act_two, act_many.at[slot(1)], to_y)
    act_z = send(act_two, act_many.at[slot(2)], to_z)
    mine = facts.at[slot(0)]
    facts_y = send(mine, facts.at[slot(1)], to_y)
    facts_z = send(mine, facts.at[slot(2)], to_z)
    keep(act_two, act_many.at[slot(0)])
    up_to_x.wait_recv()
    cores.append(send(up_next, ups.at[1, 2], to_core))
    down_to_x.wait_recv()
    cores.append(send(down_next, downs.at[1, 2], to_core))
    up_to_both.wait_recv()
    cores.append(send(up_both, ups.at[1, 3], to_core))
    down_boths = []

    def down_hop(k):
        down_fars[k].wait_recv()
        down_boths.append(send(downs.at[0, 1, parts[k]], downs.at[0, 3, parts[k]], to_x))
        cores.append(send(downs.at[0, 1, parts[k]], downs.at[1, 1, parts[k]], to_core))

    down_hop(0)
    act_y.wait_recv()
    act_z.wait_recv()
    half = rows // 2
    boths = [
        send(act_many.at[pl.ds(2 * rows, half)], act_many.at[pl.ds(3 * rows, half)], to_y),
        send(act_many.at[pl.ds(rows + half, half)], act_many.at[pl.ds(3 * rows + half, half)], to_z),
    ]
    facts_y.wait_recv()
    facts_z.wait_recv()
    boths.append(send(facts.at[slot(2)], facts.at[slot(3)], to_y))
    down_hop(1)
    for copy in [beside, both] + boths:
        copy.wait_recv()
    for k in range(2):
        down_boths[k].wait_recv()
        cores.append(send(downs.at[0, 3, parts[k]], downs.at[1, 3, parts[k]], to_core))
    for copy in cores:
        copy.wait_recv()
    for copy in kept[3:]:
        if copy is not out_own:
            copy.wait()
    for copy in started + exchanges + swaps:
        copy.wait_send()


def first_sums(
    split, limits, tokens, gain, cos2, sin2, w_qkv, w_out, w_up, w_down, top, onehot, router, gain_two, bias_two
):
    rows, dim = tokens.shape
    length = 8 * rows
    shard, wide_cols = w_qkv.shape
    cols = wide_cols // 24
    any_space = pl.BlockSpec(memory_space=pl.ANY)
    in_vmem = pl.BlockSpec(memory_space=pltpu.VMEM)
    smem = pl.BlockSpec(memory_space=pltpu.SMEM)
    dma = pltpu.SemaphoreType.DMA

    def shape(*dims):
        return jax.ShapeDtypeStruct(dims, bf16)

    def full(*dims):
        return jax.ShapeDtypeStruct(dims, f32)

    flops = 6 * length * dim * cols + 4 * length * length * cols
    return pl.pallas_call(
        first_kernel,
        in_specs=[smem] * 2 + [in_vmem] * 4 + [any_space] * 5 + [in_vmem] * 4,
        out_specs=[in_vmem] * 7 + [any_space] * 9,
        out_shape=[
            shape(length, 3 * cols),
            full(length, cols),
            full(length, cols),
            full(rows, dim),
            full(rows, 8),
            full(4 * rows, 128),
            shape(rows, dim),
            shape(4 * rows, dim),
            shape(8, rows, dim),
            shape(8, 4, shard, 3 * cols),
            shape(8, 4, shard, dim),
            shape(2, 4, 4, shard, dim),
            shape(2, 4, *w_down.shape),
            shape(rows, dim),
            shape(rows, dim),
            shape(rows, dim),
        ],
        scratch_shapes=[
            pltpu.VMEM((8, rows, dim), bf16),
            pltpu.VMEM((8, 4, shard, 3 * cols), bf16),
            pltpu.VMEM((length, cols), bf16),
            pltpu.VMEM((8, 4, shard, dim), bf16),
            pltpu.VMEM((rows, dim), bf16),
            dma((8,)),
            dma((60,)),
            dma((60,)),
            dma((7, 3)),
            dma((7, 3)),
            dma((8,)),
            dma((8,)),
            dma((3, 8)),
            dma((3, 8)),
            dma((8,)),
            dma((8,)),
        ],
        compiler_params=pltpu.CompilerParams(
            collective_id=2, has_side_effects=True, vmem_limit_bytes=60 * 2**20
        ),
        cost_estimate=pl.CostEstimate(flops=flops, bytes_accessed=2**25, transcendentals=2**22),
    )(
        split, limits, tokens, gain, cos2, sin2, w_qkv, w_out, w_up, w_down, top, onehot, router, gain_two, bias_two
    )


STRIP = 128


def last_kernel(
    dproj,
    weight,
    act_ref,
    out_own,
    out_low,
    out_high,
    small_ref,
    base_ref,
    tokens_ref,
    inv_ref,
    gain_ref,
    up_zero,
    up_one,
    up_two,
    up_three,
    input_grad,
    out_grad,
    qkv_grad,
    small_out,
    up_grad,
    act_grad,
    qkv_come,
    act,
    terms,
    core_come,
    side_come,
    act_send,
    act_recv,
    out_send,
    out_recv,
    small_sum,
    small_recv,
    out_come,
    load_sem,
    ring_send_sem,
    ring_recv_sem,
    send_sem,
    recv_sem,
):
    w = lax.axis_index("wide")
    n = lax.axis_index("narrow")
    core, y = n % 2, n // 2
    odd = w % 2
    place = w // 2 + odd * (7 - 2 * (w // 2))
    dim = weight.shape[0]
    half = dim // 2
    rows = act_grad.shape[0]
    shard = out_grad.shape[0]
    aims = ({"wide": ring_index(place + 1)}, {"wide": ring_index(place + 7)})
    other_core = {"narrow": n + 1 - 2 * core}
    other_y = {"narrow": (n + 2) % 4}
    others = [{"wide": (w + k) % 8} for k in range(1, 8)]
    z = (w // 2) % 2
    barrier = pltpu.get_barrier_semaphore()
    for peer in others + [other_core, other_y]:
        pl.semaphore_signal(barrier, inc=1, device_id=peer, device_id_type=MESH)
    pl.semaphore_wait(barrier, len(others) + 2)
    load = pltpu.make_async_copy(act_ref, act, load_sem)
    load.start()
    started = []

    def send(source, target, peer):
        at = len(started)
        copy = pltpu.make_async_remote_copy(
            src_ref=source,
            dst_ref=target,
            send_sem=send_sem.at[at],
            recv_sem=recv_sem.at[at],
            device_id=peer,
            device_id_type=MESH,
        )
        copy.start()
        started.append(copy)
        return copy

    def hop(step, stream):
        if stream < 4:
            source, target, side = act_send.at[step, stream], act_recv.at[step, stream], stream // 2
        else:
            source, target, side = out_send.at[step, stream - 4], out_recv.at[step, stream - 4], stream - 4
        return pltpu.make_async_remote_copy(
            src_ref=source,
            dst_ref=target,
            send_sem=ring_send_sem.at[step, stream],
            recv_sem=ring_recv_sem.at[step, stream],
            device_id=aims[side],
            device_id_type=MESH,
        )

    def owner_of(step, side):
        return ring_index(place + 7 - step) if side == 0 else ring_index(place + 1 + step)

    def ring_step(step):
        for stream in range(4):
            side, strip = stream // 2, stream % 2
            owner = owner_of(step, side)
            at = pl.ds(pl.multiple_of(owner * rows + strip * STRIP, STRIP), STRIP)
            for part in range(2):
                cols = pl.ds(part * 512, 512)
                wide_cols = pl.ds(side * half + part * 512, 512)
                value = dot(dproj[at, :], weight[wide_cols, :], ((1,), (1,)))
                if step == 0:
                    act_send[0, stream, :, cols] = value.astype(bf16)
                elif step < 7:
                    act_send[step, stream, :, cols] = value.astype(bf16)
                else:
                    act_grad[pl.ds(strip * STRIP, STRIP), wide_cols] = value
            if step > 0:
                hop(step - 1, stream).wait_recv()

                def add(i):
                    part = pl.ds(pl.multiple_of(i * 32, 32), 32)
                    come = act_recv[step - 1, stream, part, :].astype(f32)
                    if step < 7:
                        act_send[step, stream, part, :] = (
                            act_send[step, stream, part, :].astype(f32) + come
                        ).astype(bf16)
                    else:
                        row = pl.ds(pl.multiple_of(strip * STRIP + i * 32, 32), 32)
                        act_grad[row, pl.ds(side * half, half)] += come

                each(STRIP // 32, add)
            if step < 7:
                hop(step, stream).start()

    def out_step(step):
        for stream in (4, 5):
            side = stream - 4
            owner = owner_of(step, side)
            at = pl.ds(side * half, half)
            value = out_own[owner, :, at].astype(f32) + out_come[owner, :, at].astype(f32)
            if step > 0:
                hop(step - 1, stream).wait_recv()
                value = value + out_recv[step - 1, side].astype(f32)
            if step < 7:
                out_send[step, side] = value.astype(bf16)
                hop(step, stream).start()
            else:
                out_grad[:, pl.ds(side * half, half)] = value

    ring_step(0)
    out_come[0:4] = out_low[...]
    out_come[4:8] = out_high[...]
    out_step(0)
    load.wait()
    small_sum[0] = small_ref[...]

    def weight_terms(k):
        at = pl.ds(pl.multiple_of(k * rows, rows), rows)
        value = dot(act[:, at], dproj[...], ((0,), (0,)))
        product = value * weight[at, :].astype(f32)
        ones = jnp.ones((8, product.shape[1]), f32)
        sums = lax.dot_general(
            ones, product, (((1,), (1,)), ((), ())), precision=highest, preferred_element_type=f32
        )
        small_sum[0, 0:1, at] = small_sum[0, 0:1, at] + sums[0:1]
        terms[k] = value.astype(bf16).reshape(2, 2, shard, value.shape[1])

    each(8, weight_terms)
    to_core = send(terms.at[:, :, 1 - core], core_come, other_core)

    small_peers = [other_core, other_y] + [{"wide": w + b - 2 * b * ((w // b) % 2)} for b in (1, 2, 4)]

    def small_step(k):
        if k:
            pending.pop().wait_recv()
            small_sum[k] = small_sum[k - 1] + small_recv[k - 1]
        if k < 5:
            pending.append(send(small_sum.at[k], small_recv.at[k], small_peers[k]))
        else:
            small_out[...] = small_sum[k]

    pending = []
    small_step(0)
    ring_step(1)
    out_step(1)
    to_core.wait_recv()

    def add_core(i):
        a, b = i // 2, i % 2
        here = terms[a, b, core].astype(f32)
        terms[a, b, core] = (here + core_come[a, b].astype(f32)).astype(bf16)

    each(16, add_core)
    to_side = send(terms.at[:, 1 - y, core], side_come, other_y)
    small_step(1)
    ring_step(2)
    out_step(2)
    small_step(2)
    ring_step(3)
    out_step(3)
    to_side.wait_recv()

    def add_side(i):
        here = terms[i, y, core].astype(f32)
        terms[i, y, core] = (here + side_come[i].astype(f32)).astype(bf16)

    each(8, add_side)
    own = pltpu.make_async_copy(terms.at[w, y, core], qkv_come.at[w], load_sem)
    own.start()
    blocks = []
    for k, peer in enumerate(others):
        target = (w + 1 + k) % 8
        blocks.append(send(terms.at[target, y, core], qkv_come.at[w], peer))
    small_step(3)
    ring_step(4)
    out_step(4)
    small_step(4)
    ring_step(5)
    out_step(5)
    small_step(5)
    ring_step(6)
    out_step(6)
    ring_step(7)
    out_step(7)

    def finish(i):
        at = pl.ds(pl.multiple_of(i * 32, 32), 32)
        inv = inv_ref[at, :]
        normed = tokens_ref[at, :].astype(f32) * inv
        scaled = act_grad[at, :] * gain_ref[...]
        mean = jnp.mean(scaled * normed, axis=-1, keepdims=True)
        input_grad[at, :] = base_ref[at, :] + inv * (scaled - normed * mean)

    each(rows // 32, finish)
    own.wait()
    for copy in blocks:
        copy.wait_recv()
    piece = dim // 8
    for k, block in enumerate((up_zero, up_one, up_two, up_three)):
        its_z = z + (1 - 2 * z) * (k // 2)
        its_y = y + (1 - 2 * y) * (k % 2)
        for share in range(8):
            its_w = (share % 2) * 4 + its_z * 2 + (share // 2) % 2
            at = pl.multiple_of((its_w * 4 + its_y * 2 + share // 4) * piece, piece)
            up_grad[:, pl.ds(at, piece)] = block[:, pl.ds(share * piece, piece)].astype(f32)
    cols = weight.shape[1] // 3
    for k in range(8):
        for part in range(3):
            value = qkv_come[k, :, pl.ds(part * cols, cols)].astype(f32)
            qkv_grad[:, pl.ds(part * dim + k * cols, cols)] = value
    for copy in started:
        copy.wait_send()
    for step in range(7):
        for stream in range(6):
            hop(step, stream).wait_send()


def last_sums(dproj, weight, act, out_own, out_come, small, base, tokens_in, inv, gain, ups):
    tokens, cols = dproj.shape
    dim = weight.shape[0]
    rows, shard, half = tokens // 8, dim // 32, dim // 2
    any_space = pl.BlockSpec(memory_space=pl.ANY)
    in_vmem = pl.BlockSpec(memory_space=pltpu.VMEM)
    dma = pltpu.SemaphoreType.DMA
    return pl.pallas_call(
        last_kernel,
        in_specs=[in_vmem, in_vmem, any_space] + [in_vmem] * 12,
        out_specs=[in_vmem] * 5,
        out_shape=[
            jax.ShapeDtypeStruct((rows, dim), f32),
            jax.ShapeDtypeStruct((shard, dim), f32),
            jax.ShapeDtypeStruct((shard, 3 * dim), f32),
            jax.ShapeDtypeStruct((8, dim), f32),
            jax.ShapeDtypeStruct((shard, 4 * dim), f32),
        ],
        scratch_shapes=[
            pltpu.VMEM((rows, dim), f32),
            pltpu.VMEM((8, shard, cols), bf16),
            pltpu.VMEM((tokens, dim), bf16),
            pltpu.VMEM((8, 2, 2, shard, cols), bf16),
            pltpu.VMEM((8, 2, shard, cols), bf16),
            pltpu.VMEM((8, shard, cols), bf16),
            pltpu.VMEM((7, 4, STRIP, half), bf16),
            pltpu.VMEM((7, 4, STRIP, half), bf16),
            pltpu.VMEM((7, 2, shard, half), bf16),
            pltpu.VMEM((7, 2, shard, half), bf16),
            pltpu.VMEM((6, 8, dim), f32),
            pltpu.VMEM((5, 8, dim), f32),
            pltpu.VMEM((8, shard, dim), bf16),
            dma,
            dma((7, 6)),
            dma((7, 6)),
            dma((20,)),
            dma((20,)),
        ],
        compiler_params=pltpu.CompilerParams(
            collective_id=1, has_side_effects=True, vmem_limit_bytes=60 * 2**20
        ),
        cost_estimate=pl.CostEstimate(
            flops=4 * tokens * cols * dim, bytes_accessed=2**24, transcendentals=0
        ),
    )(dproj, weight, act, out_own, *out_come, small, base, tokens_in, inv, gain, *ups)


def swap(array, axis, size, bits):
    return lax.ppermute(array, axis, [(i, i ^ bits) for i in range(size)])


def on_device(
    wide,
    narrow,
    tokens,
    gain_one,
    w_qkv,
    w_out,
    gain_two,
    bias_two,
    router,
    w_up,
    w_down,
    doc_split,
    head_count,
    width_choice,
    out_grad,
):
    rows, part_len, dim = tokens.shape
    length = part_len * wide
    heads = dim // HEAD_DIM
    hidden = w_up.shape[1]
    head_groups = wide if heads % wide == 0 else heads
    row_groups = wide // head_groups
    my_heads = heads // head_groups
    my_rows = rows // row_groups
    cols = my_heads * HEAD_DIM
    count = rows * part_len
    w_at = lax.axis_index("wide")
    n_at = lax.axis_index("narrow")
    head_at = w_at % head_groups
    row_at = (w_at // head_groups) * my_rows
    ring = Ring("wide", wide)

    def pick_rows(array):
        return lax.dynamic_slice_in_dim(array, row_at, my_rows, 0) if row_groups > 1 else array

    def put_rows(array):
        if row_groups == 1:
            return array
        whole = jnp.zeros((rows,) + array.shape[1:], array.dtype)
        return lax.dynamic_update_slice_in_dim(whole, array, row_at, 0)

    def narrow_gather(part):
        found = part[None]
        for bits in [2**k for k in range(narrow.bit_length() - 1)]:
            other = swap(found, "narrow", narrow, bits)
            mine = (n_at & bits) == 0
            found = jnp.concatenate([jnp.where(mine, found, other), jnp.where(mine, other, found)])
        return found

    def narrow_scatter(array):
        for bits in [2**k for k in range(narrow.bit_length() - 1)]:
            array = array.reshape((wide, -1, 2) + array.shape[2:])
            at = (n_at // bits) & 1
            others = lax.dynamic_index_in_dim(array, 1 - at, 2, keepdims=False)
            array = lax.dynamic_index_in_dim(array, at, 2, keepdims=False)
            array = array + swap(others, "narrow", narrow, bits)
        return array[:, 0]

    shares = wide
    upper = wide // 4
    upper_bits = [2**k for k in range(2, wide.bit_length() - 1)][::-1]

    def share_of(w, n):
        return ((n & 1) * 2 + (w & 1)) * upper + (w >> 2)

    def wide_of(share, team):
        return (share % upper) * 4 + ((team >> 1) << 1) + ((share // upper) & 1)

    def narrow_of(share, team):
        return ((team & 1) << 1) + share // (2 * upper)

    def team_of(w, n):
        return ((w >> 1) & 1) * 2 + (n >> 1)

    def beside(part):
        return swap(part, "narrow", narrow, 2)

    def across(part):
        return swap(part, "wide", wide, 2)

    def team_swap(blocks):
        team = team_of(w_at, n_at)
        mine = [lax.dynamic_index_in_dim(blocks, team ^ k, 0, keepdims=False) for k in range(4)]
        both = [(i, i ^ (2 * narrow + 2)) for i in range(wide * narrow)]
        come = jnp.stack(
            [
                mine[0],
                beside(mine[1]),
                across(mine[2]),
                lax.ppermute(mine[3], ("wide", "narrow"), both),
            ]
        )
        return jnp.stack([lax.dynamic_index_in_dim(come, team ^ k, 0, keepdims=False) for k in range(4)])

    def pick(array, at):
        return lax.dynamic_index_in_dim(array, at, 0, keepdims=False)

    exponent = np.arange(HEAD_DIM // 2, dtype=np.float64) * (2.0 / HEAD_DIM)
    angles = np.arange(length, dtype=np.float64)[:, None] * np.power(rope_base, -exponent)[None, :]
    cosine, sine = np.cos(angles).astype(np.float32), np.sin(angles).astype(np.float32)
    cos2 = jnp.asarray(np.concatenate([cosine, cosine], axis=1))
    sin2 = jnp.asarray(np.concatenate([-sine, sine], axis=1))
    split = pick_rows(doc_split)
    limits = jnp.concatenate(
        [pick_rows(head_count), jnp.full((my_rows, 1), head_at * my_heads, jnp.int32)], axis=1
    )

    inputs = tokens.astype(f32)
    inv_one = lax.rsqrt(jnp.mean(inputs * inputs, axis=-1, keepdims=True) + norm_eps)
    normed_one = inputs * inv_one
    act_one = (normed_one * gain_one).astype(bf16)

    shard = w_qkv.shape[0]
    piece_rows = w_down.shape[0]
    top = out_grad.reshape(count, dim)
    width_flat = width_choice.reshape(count)
    share = jnp.arange(shares, dtype=jnp.int32)[:, None]
    team = team_of(w_at, n_at)
    units = (wide_of(share, team) * narrow + narrow_of(share, team)) * piece_rows
    units = (units + jnp.arange(piece_rows, dtype=jnp.int32)[None, :]).reshape(1, -1)
    need = units // (hidden // WIDTHS)

    kernels = wide == 8 and narrow == 4 and rows == 1
    if kernels:
        hot = (width_flat[:, None] == jnp.arange(2 * WIDTHS, dtype=jnp.int32)[None, :]).astype(f32)
        need_row = need.astype(f32)
        router_rows = jnp.concatenate([router.T, gain_two[None], bias_two[None], need_row, need_row])
        found = first_sums(
            split,
            limits,
            tokens.reshape(count, dim),
            gain_one[None],
            cos2,
            sin2,
            w_qkv,
            w_out,
            w_up,
            w_down,
            top,
            hot,
            router_rows,
            gain_two[None],
            bias_two[None],
        )
        qkv, att, lse, x_one, coef, facts, att_low, act_many, act_flat, my_qkv, out_full, ups, downs, *tops = found
        qkv, att, lse = qkv[None], att[None], lse[None]
        act_flat = act_flat.reshape(length, dim)
        my_qkv = my_qkv.reshape(dim, 3 * cols)
        onehot = hot[:, :WIDTHS]
    else:
        blocks = w_qkv.reshape(shard, 3, head_groups, cols).transpose(2, 0, 1, 3)
        blocks = jnp.tile(blocks.reshape(head_groups, shard, 3 * cols), (row_groups, 1, 1))
        blocks = lax.all_to_all(blocks, "wide", 0, 0, tiled=True)
        my_qkv = narrow_gather(blocks).transpose(1, 0, 2, 3).reshape(dim, 3 * cols)
        out_parts = narrow_gather(lax.all_gather(w_out, "wide", axis=0, tiled=False))
        out_full = out_parts.transpose(1, 0, 2, 3).reshape(dim, dim)

        up_blocks = w_up.reshape(shard, upper, 2, 2, 2, 2, piece_rows).transpose(2, 4, 0, 5, 3, 1, 6)
        up_part = team_swap(up_blocks.reshape(4, shard, shares * piece_rows))
        top_beside = beside(top)
        act_all = jnp.zeros((my_rows, wide, part_len, dim), bf16)
        for owner, piece in ring.gather(act_one.reshape(count, dim)):
            piece = pick_rows(piece.reshape(rows, part_len, dim))
            act_all = lax.dynamic_update_slice(act_all, piece[:, None], (0, owner, 0, 0))
        act_flat = act_all.reshape(my_rows * length, dim)
        act_flat, my_qkv, up_part, top_beside, down_part, top = join(
            act_flat, my_qkv, up_part, top_beside, w_down, top
        )

        up_found = [((0, 0), up_part)]

        def spread(found, bit):
            return found + [((w ^ bit, n), swap(piece, "wide", wide, bit)) for (w, n), piece in found]

        for bit in upper_bits:
            up_found = spread(up_found, bit)
        up_near = ((1, 0), swap(up_part, "wide", wide, 1))
        down_near = ((1, 0), swap(down_part, "wide", wide, 1))
        proj = dot(act_flat, my_qkv, ((1,), (0,))).reshape(my_rows, length, 3 * cols)
        qkv, att, att_part, lse = attend(proj, split, limits, cos2, sin2, my_heads)
        sends = att_part.reshape(my_rows, wide, part_len, cols).transpose(1, 0, 2, 3)
        sends, down_part = join(sends, down_part)

        come = lax.all_to_all(sends, "wide", 0, 0, tiled=True)
        down_found = [((0, 0), down_part)]
        for bit in upper_bits:
            down_found = spread(down_found, bit)
        come, out_full = join(come, out_full)
        up_far = [((w ^ 1, n), swap(piece, "wide", wide, 1)) for (w, n), piece in up_found[1:]]
        up_found = up_found + [up_near] + up_far
        top_across = across(top)
        come = come.reshape(row_groups, head_groups, my_rows, part_len, cols)
        att_low = come.transpose(0, 2, 3, 1, 4).reshape(count, dim)

        down_far = [((w ^ 1, n), swap(piece, "wide", wide, 1)) for (w, n), piece in down_found[1:]]
        down_found = down_found + [down_near] + down_far
        top_both = beside(top_across)
        tops = (top, top_beside, top_across, top_both)
        x_one = inputs.reshape(count, dim) + dot(att_low, out_full, ((1,), (0,)))

        center = x_one - jnp.mean(x_one, axis=-1, keepdims=True)
        inv_two = lax.rsqrt(jnp.mean(center * center, axis=-1, keepdims=True) + norm_eps)
        normed_two = center * inv_two
        ln_out = normed_two * gain_two + bias_two
        act_two = ln_out.astype(bf16)
        onehot = (width_flat[:, None] == jnp.arange(WIDTHS, dtype=jnp.int32)[None, :]).astype(f32)
        router_prob = jax.nn.softmax(jnp.dot(ln_out, router, precision=highest), axis=-1)
        chosen = jnp.sum(router_prob * onehot, axis=-1)
        grad_top = top.astype(f32)
    def share_core(array):
        return pick(array, n_at & 1) + swap(pick(array, 1 - (n_at & 1)), "narrow", narrow, 1)

    def share_near(array):
        return pick(array, w_at & 1) + swap(pick(array, 1 - (w_at & 1)), "wide", wide, 1)

    def share_far(array):
        for bit in upper_bits:
            array = array.reshape((2, -1) + array.shape[1:])
            at = (w_at // bit) & 1
            array = pick(array, at) + swap(pick(array, 1 - at), "wide", wide, bit)
        return array[0]

    if kernels:
        small, block_out, grad_x_one, _, dat, out_own, *outs, down_grad, down_come, up_sum, up_come, _, _ = feed_forward(
            act_many,
            (top, *tops),
            facts,
            ups.reshape(2, 4, 2, 2, shard, shares * piece_rows),
            downs,
            w_down,
            x_one,
            att_low,
            out_full.reshape(2, 2, 2, dim // 8, dim),
            coef,
            router_rows,
        )
        dat = dat.reshape(1, length, cols)
        down_grad = (down_grad.astype(f32) + down_come.astype(f32)).reshape(piece_rows, dim)
        out_come = [outs[0], beside(outs[1])]
        up_sum = (up_sum + up_come).reshape(4, shard, shares * piece_rows)
        up_blocks = [pick(up_sum, team ^ k) for k in range(4)]
        diagonal = [(i, i ^ (2 * narrow + 2)) for i in range(wide * narrow)]
        up_blocks[1:3] = beside(up_blocks[1]), across(up_blocks[2])
        up_blocks[3] = lax.ppermute(up_blocks[3], ("wide", "narrow"), diagonal)
        counts = jnp.pad(jnp.sum(onehot, axis=0), (0, dim - WIDTHS))[None]
        small = jnp.concatenate([small[:7], counts])
    else:
        up_found = up_found + [((w, n ^ 1), swap(piece, "narrow", narrow, 1)) for (w, n), piece in up_found]
        down_found = down_found + [((w, n ^ 1), swap(p, "narrow", narrow, 1)) for (w, n), p in down_found]

        def up_target(i, k):
            w, n = lax.axis_index("wide"), lax.axis_index("narrow")
            dw, dn = up_found[i][0]
            return ((w ^ dw) & ~2 | (k & 2)) * narrow + ((n ^ dn) & 1 | ((k & 1) * 2))

        def down_target(i, k):
            dw, dn = down_found[i][0]
            return share_of(lax.axis_index("wide") ^ dw, lax.axis_index("narrow") ^ dn)

        up_mine = place([piece for _, piece in up_found], wide * narrow, up_target)
        up_mine = up_mine.reshape(dim, shares * piece_rows)
        down_mine = place([piece[None] for _, piece in down_found], shares, down_target)
        down_mine = down_mine.reshape(shares * piece_rows, dim)

        def team_gather(part):
            far = across(part)
            return jnp.concatenate([part, beside(part), far, beside(far)])

        def team_scatter(terms):
            low = beside(jnp.stack([terms[1], terms[3]])).astype(f32)
            near, far = terms[0] + low[0], terms[2] + low[1]
            return near + across(far.astype(bf16)).astype(f32)

        act_many = team_gather(act_two)
        mask = need <= team_gather(width_flat)[:, None]
        pre = jnp.maximum(dot(act_many, up_mine, ((1,), (0,))), 0.0)
        pre = jnp.where(mask, pre, 0.0).astype(bf16).astype(f32)
        hid = (pre * pre).astype(bf16)
        dmix = (jnp.concatenate(tops).astype(f32) * team_gather(chosen)[:, None]).astype(bf16)
        mixed = dot(hid, down_mine, ((1,), (0,))).astype(bf16)
        dhid = dot(dmix, down_mine, ((1,), (1,)))
        dpre = (dhid * 2.0 * pre).astype(bf16)
        dact = dot(dpre, up_mine, ((1,), (1,))).astype(bf16)
        mixed = team_scatter(mixed.reshape(4, count, dim))
        grad_act_two = team_scatter(dact.reshape(4, count, dim))
        down_sum = dot(hid, dmix, ((0,), (0,))).astype(bf16).reshape(2, 2, upper, piece_rows, dim)
        down_grad = share_far(share_near(share_core(down_sum))).astype(f32)
        up_sum = up_sums(act_many, dpre, wide, narrow, shard)
        up_sum = share_far(share_near(share_core(up_sum)))


        block_out = (x_one + mixed * chosen[:, None]).astype(bf16)
        grad_prob = jnp.sum(grad_top * mixed, axis=-1)
        grad_logits = (grad_prob * chosen)[:, None] * (onehot - router_prob)
        grad_router = lax.dot_general(ln_out, grad_logits, (((0,), (0,)), ((), ())), precision=highest)
        grad_ln = grad_act_two + jnp.dot(grad_logits, router.T, precision=highest)
        grad_gain_two = jnp.sum(grad_ln * normed_two, axis=0)
        grad_bias_two = jnp.sum(grad_ln, axis=0)
        grad_normed = grad_ln * gain_two
        grad_x_one = grad_top + inv_two * (
            grad_normed
            - jnp.mean(grad_normed, axis=-1, keepdims=True)
            - normed_two * jnp.mean(grad_normed * normed_two, axis=-1, keepdims=True)
        )

        grad_branch = grad_x_one.astype(bf16)
        grad_att = dot(grad_branch, out_full, ((1,), (1,))).astype(bf16)
        sends = grad_att.reshape(row_groups, my_rows, part_len, head_groups, cols)
        sends = sends.transpose(0, 3, 1, 2, 4).reshape(wide, my_rows, part_len, cols)
        come = lax.all_to_all(sends, "wide", 0, 0, tiled=True)
        dat = come.transpose(1, 0, 2, 3).reshape(my_rows, length, cols)
        counts = jnp.pad(jnp.sum(onehot, axis=0), (0, dim - WIDTHS))[None]
        small = [jnp.zeros((1, dim), f32), grad_gain_two[None], grad_bias_two[None], grad_router.T, counts]
        small = jnp.concatenate(small)

    dproj = attend_back(qkv, att, lse, dat, split, limits, cos2, sin2, my_heads)
    if not kernels:
        grad_out = dot(att_low, grad_branch, ((0,), (0,))).astype(bf16)
        grad_out = narrow_scatter(grad_out.reshape(wide, narrow, shard, dim))
    if not kernels:
        up_sum = team_swap(up_sum)
        up_grad = up_sum.reshape(2, 2, shard, 2, 2, upper, piece_rows).transpose(2, 5, 0, 4, 1, 3, 6)
        up_grad = up_grad.reshape(shard, hidden).astype(f32)
    normed_flat = normed_one.reshape(count, dim)

    if kernels:
        input_grad, out_proj_grad, qkv_grad, small, up_grad = last_sums(
            dproj[0],
            my_qkv,
            act_flat,
            out_own,
            out_come,
            small,
            grad_x_one,
            tokens.reshape(count, dim),
            inv_one.reshape(count, 1),
            gain_one[None],
            up_blocks,
        )
    else:
        half = dim // 2

        def one_term(owner, side):
            rows_of = lax.dynamic_slice_in_dim(dproj, owner * part_len, part_len, 1)
            rows_of = rows_of.reshape(my_rows * part_len, 3 * cols)
            term = dot(rows_of, my_qkv[side * half : (side + 1) * half], ((1,), (1,)))
            return put_rows(term.reshape(my_rows, part_len, half)).reshape(count, half)

        out_proj_grad = lax.psum_scatter(
            grad_out.reshape(wide * shard, dim), "wide", scatter_dimension=0, tiled=True
        ).astype(f32)
        grad_act_one = jnp.concatenate(ring.scatter(one_term), axis=1)
        grad_qkv = dot(act_flat, dproj.reshape(my_rows * length, 3 * cols), ((0,), (0,)))
        gain_one_part = jnp.sum(grad_qkv * my_qkv.astype(f32), axis=1)
        small = small.at[0].set(gain_one_part)
        grad_qkv = narrow_scatter(grad_qkv.astype(bf16).reshape(wide, narrow, shard, 3 * cols))
        grad_qkv = lax.all_to_all(grad_qkv, "wide", 0, 0, tiled=True).astype(f32)
        for bits in (1, 2):
            small = small + swap(small, "narrow", narrow, bits)
        for bits in [2**k for k in range(wide.bit_length() - 1)]:
            small = small + swap(small, "wide", wide, bits)
        grad_qkv = jnp.sum(grad_qkv.reshape(row_groups, head_groups, shard, 3, cols), axis=0)
        qkv_grad = grad_qkv.transpose(1, 2, 0, 3).reshape(shard, 3 * dim)
        grad_scaled = grad_act_one * gain_one
        input_grad = grad_x_one + inv_one.reshape(count, 1) * (
            grad_scaled - normed_flat * jnp.mean(grad_scaled * normed_flat, axis=-1, keepdims=True)
        )
    gain_one_grad = small[0] / gain_one
    gain_two_grad, bias_two_grad = small[1], small[2]
    router_grad = small[3 : 3 + WIDTHS].T
    counts_all = small[3 + WIDTHS, :WIDTHS]
    return (
        block_out.reshape(rows, part_len, dim),
        input_grad.reshape(rows, part_len, dim),
        qkv_grad,
        out_proj_grad,
        up_grad,
        down_grad,
        gain_one_grad,
        gain_two_grad,
        bias_two_grad,
        router_grad,
        counts_all.astype(jnp.int32),
    )


def solution(mesh):
    in_specs = (
        P("narrow", "wide", None),
        P(),
        P(("wide", "narrow"), None),
        P(("wide", "narrow"), None),
        P(),
        P(),
        P(),
        P(("wide", "narrow"), None),
        P(("wide", "narrow"), None),
        P("narrow"),
        P("narrow", None),
        P("narrow", "wide"),
        P("narrow", "wide", None),
    )
    out_specs = (
        P("narrow", "wide", None),
        P("narrow", "wide", None),
        P(("wide", "narrow"), None),
        P(("wide", "narrow"), None),
        P(("wide", "narrow"), None),
        P(("wide", "narrow"), None),
        P(),
        P(),
        P(),
        P(),
        P(),
    )
    step = functools.partial(on_device, mesh.shape["wide"], mesh.shape["narrow"])
    return jax.shard_map(step, mesh=mesh, in_specs=in_specs, out_specs=out_specs, check_vma=False)
```

```python
import functools

import jax
import jax.numpy as jnp
import numpy as np
from jax import lax
from jax.experimental import pallas as pl
from jax.experimental.pallas import tpu as pltpu
from jax.sharding import PartitionSpec as P

HEAD_DIM = 128
WIDTHS = 4
BLOCK = 512

highest = lax.Precision.HIGHEST
norm_eps = 1e-05
rope_base = 10000.0
masked_score = -1e30
LOG2E = 1.4426950408889634
f32 = jnp.float32
bf16 = jnp.bfloat16


def dot(a, b, contract):
    return lax.dot_general(a, b, (contract, ((), ())), preferred_element_type=f32)


def turn(u, cos2, sin2):
    return u * cos2 + pltpu.roll(u, HEAD_DIM // 2, 1) * sin2


def first_key(split, row):
    return jnp.where(row >= split, split, 0)


def attend_kernel(heads, length, split_ref, limit_ref, proj_ref, cos_ref, sin_ref, qkv_ref, att_ref, low_ref, lse_ref):
    row = pl.program_id(0)
    split = split_ref[row]
    scale = HEAD_DIM ** (-0.5) * LOG2E
    block = min(BLOCK, length)
    blocks = length // block
    width = heads * HEAD_DIM

    def rotate_block(i, carry):
        rows = pl.ds(pl.multiple_of(i * block, block), block)
        cos2 = cos_ref[rows, :]
        sin2 = sin_ref[rows, :]
        for part in range(2 * heads):
            cols = pl.ds(part * HEAD_DIM, HEAD_DIM)
            qkv_ref[rows, cols] = turn(proj_ref[rows, cols], cos2, sin2).astype(bf16)
        cols = pl.ds(2 * width, width)
        qkv_ref[rows, cols] = proj_ref[rows, cols].astype(bf16)
        return carry

    lax.fori_loop(0, blocks, rotate_block, 0)
    for h in range(heads):
        qcol = pl.ds(h * HEAD_DIM, HEAD_DIM)
        kcol = pl.ds(width + h * HEAD_DIM, HEAD_DIM)
        vcol = pl.ds(2 * width + h * HEAD_DIM, HEAD_DIM)

        def query_block(i, carry):
            rows = pl.ds(pl.multiple_of(i * block, block), block)
            q = qkv_ref[rows, qcol]
            at = i * block + lax.broadcasted_iota(jnp.int32, (block, 1), 0)
            low = first_key(split, at)

            def key_block(j, state):
                top, total, acc = state
                keys = pl.ds(pl.multiple_of(j * block, block), block)
                s = dot(q, qkv_ref[keys, kcol], ((1,), (1,))) * scale
                kat = j * block + lax.broadcasted_iota(jnp.int32, (block, block), 1)
                ok = (kat <= at) & (kat >= low)
                s = jnp.where(ok, s, masked_score)
                new_top = jnp.maximum(top, jnp.max(s, axis=1, keepdims=True))
                p = jnp.exp2(s - new_top)
                fade = jnp.exp2(top - new_top)
                total = total * fade + jnp.sum(p, axis=1, keepdims=True)
                acc = acc * fade + dot(p.astype(bf16), qkv_ref[keys, vcol], ((1,), (0,)))
                return new_top, total, acc

            start = jnp.where(i * block >= split, split // block, 0)
            top, total, acc = lax.fori_loop(
                start,
                i + 1,
                key_block,
                (
                    jnp.full((block, 1), masked_score, f32),
                    jnp.zeros((block, 1), f32),
                    jnp.zeros((block, HEAD_DIM), f32),
                ),
            )
            att = acc / total
            limit = jnp.where(at < split, limit_ref[row, 0], limit_ref[row, 1])
            active = (limit_ref[row, 2] + h < limit).astype(f32)
            att_ref[rows, qcol] = att
            low_ref[rows, qcol] = (att * active).astype(bf16)
            lse_ref[rows, qcol] = jnp.broadcast_to(top + jnp.log2(total), (block, HEAD_DIM))
            return carry

        lax.fori_loop(0, blocks, query_block, 0)


def attend(proj, split, limits, cos2, sin2, heads):
    rows, length, _ = proj.shape
    width = heads * HEAD_DIM
    smem = pl.BlockSpec(memory_space=pltpu.SMEM)
    table = pl.BlockSpec((length, HEAD_DIM), lambda r: (0, 0))

    def whole(cols):
        return pl.BlockSpec((None, length, cols), lambda r: (r, 0, 0))

    flops = rows * heads * 4 * length * length * HEAD_DIM
    return pl.pallas_call(
        functools.partial(attend_kernel, heads, length),
        grid=(rows,),
        in_specs=[smem, smem, whole(3 * width), table, table],
        out_specs=[whole(3 * width), whole(width), whole(width), whole(width)],
        out_shape=[
            jax.ShapeDtypeStruct((rows, length, 3 * width), bf16),
            jax.ShapeDtypeStruct((rows, length, width), f32),
            jax.ShapeDtypeStruct((rows, length, width), bf16),
            jax.ShapeDtypeStruct((rows, length, width), f32),
        ],
        compiler_params=pltpu.CompilerParams(vmem_limit_bytes=56 * 2**20),
        cost_estimate=pl.CostEstimate(flops=flops, bytes_accessed=2**24, transcendentals=flops // 512),
    )(split, limits, proj, cos2, sin2)


def attend_back_kernel(
    heads,
    length,
    split_ref,
    limit_ref,
    qkv_ref,
    att_ref,
    lse_ref,
    dat_ref,
    cos_ref,
    sin_ref,
    dproj_ref,
    datt_ref,
    delta_ref,
    dq_ref,
):
    row = pl.program_id(0)
    split = split_ref[row]
    scale = HEAD_DIM ** (-0.5)
    block = min(BLOCK, length)
    blocks = length // block
    width = heads * HEAD_DIM
    qcols = [pl.ds(h * HEAD_DIM, HEAD_DIM) for h in range(heads)]
    kcols = [pl.ds(width + h * HEAD_DIM, HEAD_DIM) for h in range(heads)]
    vcols = [pl.ds(2 * width + h * HEAD_DIM, HEAD_DIM) for h in range(heads)]

    def rows_of(i):
        return pl.ds(pl.multiple_of(i * block, block), block)

    def prepare(i, carry):
        rows = rows_of(i)
        at = i * block + lax.broadcasted_iota(jnp.int32, (block, 1), 0)
        limit = jnp.where(at < split, limit_ref[row, 0], limit_ref[row, 1])
        for h in range(heads):
            active = (limit_ref[row, 2] + h < limit).astype(f32)
            datt = dat_ref[rows, qcols[h]].astype(f32) * active
            datt_ref[h, rows, :] = datt.astype(bf16)
            delta = jnp.sum(datt * att_ref[rows, qcols[h]], axis=1, keepdims=True)
            delta_ref[h, rows, :] = jnp.broadcast_to(delta, (block, HEAD_DIM))
            dq_ref[h, rows, :] = jnp.zeros((block, HEAD_DIM), f32)
        return carry

    lax.fori_loop(0, blocks, prepare, 0)

    def key_block(j, carry):
        keys = rows_of(j)
        kat = j * block + lax.broadcasted_iota(jnp.int32, (block, block), 1)

        def query_block(i, state):
            rows = rows_of(i)
            at = i * block + lax.broadcasted_iota(jnp.int32, (block, 1), 0)
            ok = (kat <= at) & (kat >= first_key(split, at))
            found = []
            for h in range(heads):
                dk, dv = state[h]
                q, k, v = qkv_ref[rows, qcols[h]], qkv_ref[keys, kcols[h]], qkv_ref[keys, vcols[h]]
                datt = datt_ref[h, rows, :]
                s = dot(q, k, ((1,), (1,))) * (scale * LOG2E)
                lse = lse_ref[rows, qcols[h]][:, :1]
                p = jnp.exp2(jnp.where(ok, s - lse, masked_score))
                dp = dot(datt, v, ((1,), (1,)))
                ds = (p * (dp - delta_ref[h, rows, :][:, :1])).astype(bf16)
                dv = dv + dot(p.astype(bf16), datt, ((0,), (0,)))
                dk = dk + dot(ds, q, ((0,), (0,)))
                dq_ref[h, rows, :] += dot(ds, k, ((1,), (0,)))
                found.append((dk, dv))
            return tuple(found)

        stop = jnp.where((j + 1) * block <= split, (split - 1) // block + 1, blocks)
        zero = jnp.zeros((block, HEAD_DIM), f32)
        state = lax.fori_loop(j, stop, query_block, ((zero, zero),) * heads)
        for h in range(heads):
            dk, dv = state[h]
            turned = turn(dk * scale, cos_ref[keys, :], -sin_ref[keys, :])
            dproj_ref[keys, kcols[h]] = turned.astype(bf16)
            dproj_ref[keys, vcols[h]] = dv.astype(bf16)
        return carry

    lax.fori_loop(0, blocks, key_block, 0)

    def finish(i, carry):
        rows = rows_of(i)
        for h in range(heads):
            dq = dq_ref[h, rows, :] * scale
            dproj_ref[rows, qcols[h]] = turn(dq, cos_ref[rows, :], -sin_ref[rows, :]).astype(bf16)
        return carry

    lax.fori_loop(0, blocks, finish, 0)


def attend_back(qkv, att, lse, dat, split, limits, cos2, sin2, heads):
    rows, length, _ = qkv.shape
    width = heads * HEAD_DIM
    smem = pl.BlockSpec(memory_space=pltpu.SMEM)
    table = pl.BlockSpec((length, HEAD_DIM), lambda r: (0, 0))

    def whole(cols):
        return pl.BlockSpec((None, length, cols), lambda r: (r, 0, 0))

    flops = rows * heads * 10 * length * length * HEAD_DIM
    return pl.pallas_call(
        functools.partial(attend_back_kernel, heads, length),
        grid=(rows,),
        in_specs=[smem, smem, whole(3 * width), whole(width), whole(width), whole(width), table, table],
        out_specs=whole(3 * width),
        out_shape=jax.ShapeDtypeStruct((rows, length, 3 * width), bf16),
        scratch_shapes=[
            pltpu.VMEM((heads, length, HEAD_DIM), bf16),
            pltpu.VMEM((heads, length, HEAD_DIM), f32),
            pltpu.VMEM((heads, length, HEAD_DIM), f32),
        ],
        compiler_params=pltpu.CompilerParams(vmem_limit_bytes=56 * 2**20),
        cost_estimate=pl.CostEstimate(flops=flops, bytes_accessed=2**24, transcendentals=flops // 1280),
    )(split, limits, qkv, att, lse, dat, cos2, sin2)


class Ring:
    def __init__(self, axis, size):
        self.axis = axis
        self.size = size
        self.order = list(range(0, size, 2)) + list(range(1, size, 2))[::-1]
        place = {w: p for p, w in enumerate(self.order)}
        self.table = [[self.order[(place[w] + k) % size] for k in range(size)] for w in range(size)]
        self.near = None
        self.right = [(w, self.order[(place[w] + 1) % size]) for w in range(size)]
        self.left = [(w, self.order[(place[w] - 1) % size]) for w in range(size)]

    def at(self, shift):
        if self.near is None:
            row = lax.dynamic_slice_in_dim(jnp.array(self.table, jnp.int32), lax.axis_index(self.axis), 1, 0)
            self.near = [row[0, k] for k in range(self.size)]
        return self.near[shift % self.size]

    def gather(self, part):
        found = [(self.at(0), part)]
        onward, back = part, part
        half = self.size // 2
        for step in range(1, half):
            onward = lax.ppermute(onward, self.axis, self.right)
            back = lax.ppermute(back, self.axis, self.left)
            found += [(self.at(-step), onward), (self.at(step), back)]
        cut = part.shape[0] // 2
        first = lax.ppermute(onward[:cut], self.axis, self.right)
        second = lax.ppermute(back[cut:], self.axis, self.left)
        found.append((self.at(half), jnp.concatenate([first, second], axis=0)))
        return found

    def gather_whole(self, part):
        whole = jnp.zeros((self.size,) + part.shape, part.dtype)
        for owner, piece in self.gather(part):
            whole = lax.dynamic_update_slice_in_dim(whole, piece[None], owner, 0)
        return whole

    def scatter(self, term):
        sums = [term(self.at(-1), 0), term(self.at(1), 1)]
        for step in range(2, self.size + 1):
            for side, perm, sign in ((0, self.right, -1), (1, self.left, 1)):
                come = lax.ppermute(sums[side].astype(bf16), self.axis, perm)
                sums[side] = come.astype(f32) + term(self.at(sign * step), side)
        return sums


def join(*arrays):
    return lax.optimization_barrier(arrays)


def after(array, *others):
    return lax.optimization_barrier((array,) + others)[0]


def place_kernel(count, targets, *refs):
    pieces, whole, held, in_sems, out_sems = refs[:-4], refs[-4], refs[-3], refs[-2], refs[-1]
    spots = [(i, k) for i in range(len(pieces)) for k in range(count)]
    loads = [
        pltpu.make_async_copy(pieces[i].at[k], held.at[at], in_sems.at[at]) for at, (i, k) in enumerate(spots)
    ]
    stores = [
        pltpu.make_async_copy(held.at[at], whole.at[targets(i, k)], out_sems.at[at])
        for at, (i, k) in enumerate(spots)
    ]
    for load in loads:
        load.start()
    for load, store in zip(loads, stores):
        load.wait()
        store.start()
    for store in stores:
        store.wait()


def place(pieces, total, targets):
    count = pieces[0].shape[0]
    anywhere = pl.BlockSpec(memory_space=pl.ANY)
    shape = (total,) + pieces[0].shape[1:]
    size = 2 * 2 * total * pieces[0][0].size
    return pl.pallas_call(
        functools.partial(place_kernel, count, targets),
        in_specs=[anywhere] * len(pieces),
        out_specs=anywhere,
        out_shape=jax.ShapeDtypeStruct(shape, pieces[0].dtype),
        scratch_shapes=[
            pltpu.VMEM((len(pieces) * count,) + pieces[0].shape[1:], pieces[0].dtype),
            pltpu.SemaphoreType.DMA((len(pieces) * count,)),
            pltpu.SemaphoreType.DMA((len(pieces) * count,)),
        ],
        compiler_params=pltpu.CompilerParams(vmem_limit_bytes=40 * 2**20),
        cost_estimate=pl.CostEstimate(flops=0, bytes_accessed=size, transcendentals=0),
    )(*pieces)


def up_sum_kernel(narrow, act_ref, dpre_ref, out_ref):
    shard = out_ref.shape[-2]
    total = dot(act_ref[...], dpre_ref[...], ((0,), (0,))).astype(bf16)
    for y in range(2):
        for core in range(2):
            at = (2 * y + core) * shard
            out_ref[core, 0, 0, y] = total[at : at + shard]


def up_sums(act, dpre, wide, narrow, shard):
    tokens, cols = dpre.shape
    upper = wide // 4
    if (narrow * shard) % 128:
        total = dot(act, dpre, ((0,), (0,))).astype(bf16)
        total = total.reshape(upper, 2, 2, 2, 2, shard, cols).transpose(4, 2, 0, 1, 3, 5, 6)
        return total.reshape(2, 2, upper, 4, shard, cols)
    return pl.pallas_call(
        functools.partial(up_sum_kernel, narrow),
        grid=(wide,),
        in_specs=[
            pl.BlockSpec((tokens, narrow * shard), lambda w: (0, w)),
            pl.BlockSpec((tokens, cols), lambda w: (0, 0)),
        ],
        out_specs=pl.BlockSpec((2, 1, 1, 2, shard, cols), lambda w: (0, w % 2, w // 4, (w // 2) % 2, 0, 0)),
        out_shape=jax.ShapeDtypeStruct((2, 2, upper, 4, shard, cols), bf16),
        compiler_params=pltpu.CompilerParams(vmem_limit_bytes=40 * 2**20),
        cost_estimate=pl.CostEstimate(
            flops=2 * tokens * cols * act.shape[1], bytes_accessed=2**24, transcendentals=0
        ),
    )(act, dpre)


MESH = pl.DeviceIdType.MESH
TILE = 512
Y, Z, CORE, X, FAR = range(5)


def each(count, body):
    def step(i, carry):
        body(i)
        return carry

    lax.fori_loop(0, count, step, 0)


def feed_kernel(
    act_many,
    top_zero,
    top_one,
    top_two,
    top_three,
    scale,
    ups,
    downs,
    down_zero,
    x_ref,
    low_ref,
    out_ref,
    coef_ref,
    router_ref,
    small,
    block_out,
    grad_x,
    branch,
    dat_out,
    out_own,
    out_come,
    out_other,
    down_own,
    down_come,
    up_own,
    up_come,
    down_core,
    up_core,
    up,
    down,
    act,
    dmix,
    hid,
    dpre,
    mixed,
    dact,
    mixed_low,
    dact_low,
    down_near,
    up_near,
    held,
    down_sum,
    mixed_come,
    dact_come,
    x_one,
    load_sem,
    send_sem,
    recv_sem,
    dat_send_sem,
    dat_recv_sem,
    out_send_sem,
    out_recv_sem,
    side_send_sem,
    side_recv_sem,
):
    w = lax.axis_index("wide")
    n = lax.axis_index("narrow")
    core, x, far = n % 2, w % 2, w // 4
    peers = {
        Y: {"narrow": (n + 2) % 4},
        Z: {"wide": w + 2 - 4 * ((w // 2) % 2)},
        CORE: {"narrow": n + 1 - 2 * core},
        X: {"wide": w + 1 - 2 * x},
        FAR: {"wide": (w + 4) % 8},
    }
    rows, dim = x_ref.shape
    started = []

    def send(source, target, peer):
        at = len(started)
        copy = pltpu.make_async_remote_copy(
            src_ref=source,
            dst_ref=target,
            send_sem=send_sem.at[at],
            recv_sem=recv_sem.at[at],
            device_id=peers[peer],
            device_id_type=MESH,
        )
        copy.start()
        started.append(copy)
        return copy

    def load(source, target, at):
        copy = pltpu.make_async_copy(source, target, load_sem.at[at])
        copy.start()
        return copy

    def slot(k):
        return pl.ds(k * rows, rows)

    barrier = pltpu.get_barrier_semaphore()
    others = [{"wide": (w + k) % 8} for k in range(1, 8)]
    for peer in others + [peers[Y], peers[CORE]]:
        pl.semaphore_signal(barrier, inc=1, device_id=peer, device_id_type=MESH)
    pl.semaphore_wait(barrier, len(others) + 2)

    loads = [load(act_many, act, 0)]
    for k, top in enumerate((top_zero, top_one, top_two, top_three)):
        loads.append(load(top, dmix.at[slot(k)], 1 + k))
    up_loads, down_loads = [], []
    for its in range(2):
        its_core = core + (1 - 2 * core) * its
        for k in range(4):
            its_far = far + (1 - 2 * far) * (k % 2)
            its_x = x + (1 - 2 * x) * (k // 2)
            source = downs.at[its, k] if its or k else down_zero
            up_loads.append(load(ups.at[its, k], up.at[its_far, :, its_x, :, its_core], 27 + 4 * its + k))
            down_loads.append(load(source, down.at[its_core, its_x, its_far], 35 + 4 * its + k))
    for copy in loads + up_loads:
        copy.wait()

    def columns(t):
        return pl.ds(pl.multiple_of(t * TILE, TILE), TILE)

    def group_of(pair):
        return pl.ds(pair * 2 * rows, 2 * rows)

    def hidden_of(pair):
        group = group_of(pair)
        width = scale[group, :][:, 1:2]

        def scaled(i):
            at = pl.ds(pl.multiple_of(pair * 2 * rows + i * 32, 32), 32)
            dmix[at, :] = (dmix[at, :].astype(f32) * scale[at, :][:, :1]).astype(bf16)

        def first(t):
            at = columns(t)
            weight = up[:, :, :, :, :, :, at].reshape(dim, TILE)
            pre = jnp.maximum(dot(act[group, :], weight, ((1,), (0,))), 0.0)
            pre = jnp.where(router_ref[6:7, at] <= width, pre, 0.0)
            dpre[group, at] = pre.astype(bf16)
            hid[group, at] = (pre * pre).astype(bf16)

        each(2 * rows // 32, scaled)
        each(dim // TILE, first)

    def mixed_of(pair):
        group = group_of(pair)

        def second(t):
            at = columns(t)
            weight = down[:, :, :, :, at].reshape(dim, TILE)
            mixed[group, at] = dot(hid[group, :], weight, ((1,), (0,))).astype(bf16)

        each(dim // TILE, second)

    def dact_of(pair):
        group = group_of(pair)

        def third(t):
            at = columns(t)
            weight = down[t // 2, t % 2].reshape(TILE, dim)
            value = dot(dmix[group, :], weight, ((1,), (1,)))
            dpre[group, at] = (value * 2.0 * dpre[group, at].astype(f32)).astype(bf16)

        def fourth(t):
            at = columns(t)
            weight = up[t // 2, t % 2].reshape(TILE, dim)
            dact[group, at] = dot(dpre[group, :], weight, ((1,), (1,))).astype(bf16)

        each(dim // TILE, third)
        each(dim // TILE, fourth)

    cut = dim // 2

    def side_of(k):
        return pl.ds((k % 2) * cut, cut)

    def down_terms(k):
        def block(i):
            rows_of = hid[:, columns(i)]
            value = dot(rows_of, dmix[:, side_of(k)], ((0,), (0,))).astype(bf16)
            down_sum[i // 2, i % 2, :, :, :, :, side_of(k)] = value.reshape(2, 2, 2, TILE // 8, cut)

        each(dim // TILE, block)
        return send(down_sum.at[1 - core, :, :, :, :, :, side_of(k)], down_core.at[k], CORE)

    def up_terms(k):
        def block(i):
            rows_of = act[:, columns(i)]
            value = dot(rows_of, dpre[:, side_of(k)], ((0,), (0,))).astype(bf16)
            up[i // 2, i % 2, :, :, :, :, side_of(k)] = value.reshape(2, 2, 2, TILE // 8, cut)

        each(dim // TILE, block)
        return send(up.at[:, :, :, :, 1 - core, :, side_of(k)], up_core.at[k % 2], CORE)

    def core_sum(k):
        cores[k].wait_recv()

        def add(i, a, b):
            c, d = i // 2, i % 2
            come = held[c, d].astype(f32)
            if k < 2:
                here = down_sum[core, a, b, c, d, :, side_of(k)].astype(f32)
                down_sum[core, a, b, c, d, :, side_of(k)] = (here + come).astype(bf16)
            else:
                here = up[a, b, c, d, core, :, side_of(k)].astype(f32)
                up[a, b, c, d, core, :, side_of(k)] = (here + come).astype(bf16)

        for a in range(2):
            for b in range(2):
                load((down_core if k < 2 else up_core).at[k % 2, a, b], held, 15 + k).wait()
                each(4, functools.partial(add, a=a, b=b))
        if k < 2:
            source = down_sum.at[core, 1 - x, :, :, :, :, side_of(k)]
            return send(source, down_near.at[:, :, :, :, side_of(k)], X)
        source = up.at[:, :, 1 - x, :, core, :, side_of(k)]
        return send(source, up_near.at[:, :, :, :, side_of(k)], X)

    def near_sum(k):
        nears[k].wait_recv()

        def add(i):
            a, b, c = i // 4, (i // 2) % 2, i % 2
            if k < 2:
                here = down_sum[core, x, a, b, c, :, side_of(k)].astype(f32)
                come = down_near[a, b, c, :, side_of(k)].astype(f32)
                down_sum[core, x, a, b, c, :, side_of(k)] = (here + come).astype(bf16)
            else:
                here = up[a, b, x, c, core, :, side_of(k)].astype(f32)
                come = up_near[a, b, c, :, side_of(k)].astype(f32)
                up[a, b, x, c, core, :, side_of(k)] = (here + come).astype(bf16)

        each(8, add)
        if k < 2:
            fars.append(
                send(
                    down_sum.at[core, x, 1 - far, :, :, :, side_of(k)],
                    down_come.at[:, :, :, side_of(k)],
                    FAR,
                )
            )
            source = down_sum.at[core, x, far, :, :, :, side_of(k)]
            keep.append(load(source, down_own.at[:, :, :, side_of(k)], 19 + k))
        else:
            source = up.at[1 - far, :, x, :, core, :, side_of(k)]
            fars.append(send(source, up_come.at[:, :, :, side_of(k)], FAR))
            source = up.at[far, :, x, :, core, :, side_of(k)]
            keep.append(load(source, up_own.at[:, :, :, side_of(k)], 19 + k))

    def add_low(total, k, low, side):
        def step(i):
            at = pl.ds(pl.multiple_of(k * rows + i * 32, 32), 32)
            come = low[side, pl.ds(pl.multiple_of(i * 32, 32), 32), :].astype(f32)
            total[at, :] = (total[at, :].astype(f32) + come).astype(bf16)

        each(rows // 32, step)

    cores, nears, fars, keep = [], [], [], []
    hidden_of(0)
    for copy in down_loads:
        copy.wait()
    mixed_of(0)
    mixed_one = send(mixed.at[slot(1)], mixed_low.at[0], Y)
    hidden_of(1)
    mixed_of(1)
    mixed_three = send(mixed.at[slot(3)], mixed_low.at[1], Y)
    cores.append(down_terms(0))
    cores.append(down_terms(1))
    dact_of(1)
    dact_two = send(dact.at[slot(2)], dact_low.at[0], Z)
    dact_three = send(dact.at[slot(3)], dact_low.at[1], Z)
    nears.append(core_sum(0))
    nears.append(core_sum(1))
    dact_of(0)
    out_load = load(out_ref, down, 13)
    x_load = load(x_ref, x_one, 14)
    top_load = load(top_zero, hid.at[slot(0)], 0)
    cores.append(up_terms(2))
    cores.append(up_terms(3))
    near_sum(0)
    nears.append(core_sum(2))
    nears.append(core_sum(3))
    near_sum(1)

    dact_two.wait_recv()
    dact_three.wait_recv()
    add_low(dact, 1, dact_low, 1)
    dact_last = send(dact.at[slot(1)], dact_come, Y)
    mixed_one.wait_recv()
    mixed_three.wait_recv()
    add_low(mixed, 2, mixed_low, 1)
    mixed_last = send(mixed.at[slot(2)], mixed_come, Z)
    add_low(mixed, 0, mixed_low, 0)
    add_low(dact, 0, dact_low, 0)
    near_sum(2)

    small[...] = jnp.zeros_like(small)
    x_load.wait()
    top_load.wait()
    mixed_last.wait_recv()
    dact_last.wait_recv()
    gain, bias = router_ref[4:5, :], router_ref[5:6, :]

    def back(i):
        def part(k):
            return pl.ds(pl.multiple_of(k * rows + i * 16, 16), 16)

        at = part(0)
        value = x_one[at, :]
        center = value - jnp.mean(value, axis=-1, keepdims=True)
        inv = lax.rsqrt(jnp.mean(center * center, axis=-1, keepdims=True) + norm_eps)
        normed = center * inv
        its_mixed = mixed[at, :].astype(f32) + mixed_come[at, :].astype(f32)
        grad = dact[at, :].astype(f32) + dact_come[at, :].astype(f32)
        top = hid[at, :].astype(f32)
        hid[part(3), :] = (value + its_mixed * scale[at, :][:, :1]).astype(bf16)
        logits = coef_ref[at, :] * jnp.sum(top * its_mixed, axis=-1, keepdims=True)
        ln_out = normed * gain + bias
        for c in range(WIDTHS):
            one = logits[:, c : c + 1]
            grad = grad + one * router_ref[c : c + 1, :]
            small[3 + c : 4 + c, :] += jnp.sum(ln_out * one, axis=0, keepdims=True)
        small[1:2, :] += jnp.sum(grad * normed, axis=0, keepdims=True)
        small[2:3, :] += jnp.sum(grad, axis=0, keepdims=True)
        grad = grad * gain
        mean = jnp.mean(grad, axis=-1, keepdims=True)
        along = jnp.mean(grad * normed, axis=-1, keepdims=True)
        total = top + inv * (grad - mean - normed * along)
        x_one[at, :] = total
        hid[part(2), :] = total.astype(bf16)

    each(rows // 16, back)
    keep.append(load(x_one, grad_x, 23))
    keep.append(load(hid.at[slot(2)], branch, 24))
    keep.append(load(hid.at[slot(3)], block_out, 25))
    out_load.wait()
    cols = dim // 8

    def dat_block(owner):
        at = pl.ds(pl.multiple_of(owner * cols, cols), cols)
        weight = down[owner // 4, (owner // 2) % 2, owner % 2]
        hid[slot(1), at] = dot(hid[slot(2), :], weight, ((1,), (1,))).astype(bf16)
        return hid.at[slot(1), at]

    dats = []
    for k in range(1, 8):
        owner = (w + k) % 8
        copy = pltpu.make_async_remote_copy(
            src_ref=dat_block(owner),
            dst_ref=dat_out.at[w],
            send_sem=dat_send_sem.at[k - 1],
            recv_sem=dat_recv_sem.at[k - 1],
            device_id={"wide": owner},
            device_id_type=MESH,
        )
        copy.start()
        dats.append(copy)
    keep.append(load(dat_block(w), dat_out.at[w], 26))

    low_load = load(low_ref, hid.at[slot(0)], 1)
    low_load.wait()
    shard = dim // 32
    half_rows = dim // 2

    def out_block(i):
        for k, place in enumerate((act, dpre)):
            at = pl.ds(pl.multiple_of(k * half_rows + i * cols, cols), cols)
            value = dot(hid[slot(0), at], hid[slot(2), :], ((0,), (0,))).astype(bf16)
            place[pl.ds(pl.multiple_of(i * cols, cols), cols), :] = value

    each(half_rows // cols, out_block)

    def out_rows(i, its_core):
        return pl.ds(pl.multiple_of((2 * (i % 8) + its_core) * shard, shard), shard)

    outs = []
    for i in range(16):
        copy = pltpu.make_async_remote_copy(
            src_ref=(act if i < 8 else dpre).at[out_rows(i, 1 - core)],
            dst_ref=dmix.at[pl.ds(i * shard, shard)],
            send_sem=out_send_sem.at[i],
            recv_sem=out_recv_sem.at[i],
            device_id=peers[CORE],
            device_id_type=MESH,
        )
        copy.start()
        outs.append(copy)
    for copy in outs:
        copy.wait_recv()

    def out_add(i):
        for k, place in enumerate((act, dpre)):
            at = pl.ds(pl.multiple_of((k * 8 + i) * shard, shard), shard)
            mine = place[out_rows(i, core), :].astype(f32)
            dmix[at, :] = (mine + dmix[at, :].astype(f32)).astype(bf16)

    each(8, out_add)
    y = n // 2
    for i in range(8):
        keep.append(load(dmix.at[pl.ds((2 * i + y) * shard, shard)], out_own.at[i], 43 + i))
    out_ys = []
    for i in range(8):
        source = dmix.at[pl.ds((2 * i + 1 - y) * shard, shard)]
        if i < 4:
            copy = pltpu.make_async_remote_copy(
                src_ref=source,
                dst_ref=out_come.at[i],
                send_sem=side_send_sem.at[i],
                recv_sem=side_recv_sem.at[i],
                device_id=peers[Y],
                device_id_type=MESH,
            )
            copy.start()
            out_ys.append(copy)
        else:
            keep.append(load(source, out_other.at[i - 4], 51 + i))
    near_sum(3)
    for copy in keep:
        copy.wait()
    for copy in fars + dats + out_ys:
        copy.wait_recv()
    for copy in started + dats + outs + out_ys:
        copy.wait_send()


def feed_forward(act, tops, facts, ups, downs, down, x_one, low, out_full, coef, router):
    rows, dim = x_one.shape
    any_space = pl.BlockSpec(memory_space=pl.ANY)
    in_vmem = pl.BlockSpec(memory_space=pltpu.VMEM)
    tokens = 4 * rows
    cut = dim // 2
    shard = dim // 32

    def shape(*dims):
        return jax.ShapeDtypeStruct(dims, bf16)

    return pl.pallas_call(
        feed_kernel,
        in_specs=[any_space] * 5 + [in_vmem] + [any_space] * 6 + [in_vmem] * 2,
        out_specs=[in_vmem] + [any_space] * 13,
        out_shape=[
            jax.ShapeDtypeStruct((8, dim), f32),
            shape(rows, dim),
            jax.ShapeDtypeStruct((rows, dim), f32),
            shape(rows, dim),
            shape(8, rows, dim // 8),
            shape(8, shard, dim),
            shape(4, shard, dim),
            shape(4, shard, dim),
            shape(2, 2, shard, dim),
            shape(2, 2, shard, dim),
            shape(2, 2, shard, dim),
            shape(2, 2, shard, dim),
            shape(2, 2, 2, 2, 2, shard, cut),
            shape(2, 2, 2, 2, 2, shard, cut),
        ],
        scratch_shapes=[
            pltpu.VMEM((2, 2, 2, 2, 2, shard, dim), bf16),
            pltpu.VMEM((2, 2, 2, dim // 8, dim), bf16),
            pltpu.VMEM((tokens, dim), bf16),
            pltpu.VMEM((tokens, dim), bf16),
            pltpu.VMEM((tokens, dim), bf16),
            pltpu.VMEM((tokens, dim), bf16),
            pltpu.VMEM((tokens, dim), bf16),
            pltpu.VMEM((tokens, dim), bf16),
            pltpu.VMEM((2, rows, dim), bf16),
            pltpu.VMEM((2, rows, dim), bf16),
            pltpu.VMEM((2, 2, 2, shard, dim), bf16),
            pltpu.VMEM((2, 2, 2, shard, dim), bf16),
            pltpu.VMEM((2, 2, shard, cut), bf16),
            pltpu.VMEM((2, 2, 2, 2, 2, shard, dim), bf16),
            pltpu.VMEM((rows, dim), bf16),
            pltpu.VMEM((rows, dim), bf16),
            pltpu.VMEM((rows, dim), f32),
            pltpu.SemaphoreType.DMA((59,)),
            pltpu.SemaphoreType.DMA((36,)),
            pltpu.SemaphoreType.DMA((36,)),
            pltpu.SemaphoreType.DMA((7,)),
            pltpu.SemaphoreType.DMA((7,)),
            pltpu.SemaphoreType.DMA((16,)),
            pltpu.SemaphoreType.DMA((16,)),
            pltpu.SemaphoreType.DMA((4,)),
            pltpu.SemaphoreType.DMA((4,)),
        ],
        compiler_params=pltpu.CompilerParams(
            collective_id=0, has_side_effects=True, vmem_limit_bytes=63 * 2**20 + 2**19
        ),
        cost_estimate=pl.CostEstimate(
            flops=12 * tokens * dim * dim, bytes_accessed=2**25, transcendentals=0
        ),
    )(act, *tops, facts, ups, downs, down, x_one, low, out_full, coef, router)


def ring_index(place):
    place = place % 8
    upper = place // 4
    return (1 - upper) * 2 * place + upper * (2 * (7 - place) + 1)


def first_kernel(
    split_ref,
    limit_ref,
    tokens_ref,
    gain_ref,
    cos_ref,
    sin_ref,
    qkv_part,
    out_part,
    up_part,
    down_part,
    top_zero,
    onehot_ref,
    router_ref,
    gain_two_ref,
    bias_two_ref,
    qkv,
    att,
    lse,
    x_one,
    coef,
    facts,
    low_out,
    act_many,
    act_out,
    weight_out,
    out_full,
    ups,
    downs,
    top_one,
    top_two,
    top_three,
    act,
    weight,
    low,
    out_held,
    act_two,
    local_sem,
    send_sem,
    recv_sem,
    qkv_send_sem,
    qkv_recv_sem,
    low_send_sem,
    low_recv_sem,
    up_send_sem,
    up_recv_sem,
    up_local_sem,
    out_sem,
):
    w = lax.axis_index("wide")
    n = lax.axis_index("narrow")
    core, y, far, z = n % 2, n // 2, w // 4, (w // 2) % 2
    odd = w % 2
    place = w // 2 + odd * (7 - 2 * (w // 2))
    rows, dim = tokens_ref.shape
    cols = weight.shape[3] // 3
    heads = cols // HEAD_DIM
    right, left = {"wide": ring_index(place + 1)}, {"wide": ring_index(place + 7)}
    to_y, to_core = {"narrow": (n + 2) % 4}, {"narrow": n + 1 - 2 * core}
    to_z, to_x = {"wide": w + 2 - 4 * z}, {"wide": w + 1 - 2 * odd}
    to_far = {"wide": (w + 4) % 8}
    to_both = {"wide": w + 2 - 4 * z, "narrow": (n + 2) % 4}
    barrier = pltpu.get_barrier_semaphore()
    peers = [{"wide": (w + k) % 8} for k in range(1, 8)] + [to_y, to_core, to_both]
    for peer in peers:
        pl.semaphore_signal(barrier, inc=1, device_id=peer, device_id_type=MESH)
    pl.semaphore_wait(barrier, len(peers))
    started, kept = [], []
    up_zero, up_far, up_next, up_both = (ups.at[0, k] for k in range(4))
    down_next = downs.at[0, 2]

    def send(source, target, peer):
        at = len(started)
        copy = pltpu.make_async_remote_copy(
            src_ref=source,
            dst_ref=target,
            send_sem=send_sem.at[at],
            recv_sem=recv_sem.at[at],
            device_id=peer,
            device_id_type=MESH,
        )
        copy.start()
        started.append(copy)
        return copy

    def keep(source, target):
        copy = pltpu.make_async_copy(source, target, local_sem.at[len(kept)])
        copy.start()
        kept.append(copy)
        return copy

    def norm(i):
        at = pl.ds(pl.multiple_of(i * 32, 32), 32)
        value = tokens_ref[at, :].astype(f32)
        inv = lax.rsqrt(jnp.mean(value * value, axis=-1, keepdims=True) + norm_eps)
        act[w, at, :] = (value * inv * gain_ref[...]).astype(bf16)

    each(rows // 32, norm)

    first, second = pl.ds(0, rows // 2), pl.ds(rows // 2, rows // 2)
    shard = out_part.shape[0]
    out_first, out_second = pl.ds(0, shard // 2), pl.ds(shard // 2, shard // 2)
    onward = send(act.at[w], act.at[w], right)
    back = send(act.at[w], act.at[w], left)
    exchanges = []
    for k in range(1, 8):
        target = (w + k) % 8
        for part in range(3):
            source = qkv_part.at[:, pl.ds(pl.multiple_of(part * dim + target * cols, cols), cols)]
            copy = pltpu.make_async_remote_copy(
                src_ref=source,
                dst_ref=weight.at[w, n, :, pl.ds(part * cols, cols)],
                send_sem=qkv_send_sem.at[k - 1, part],
                recv_sem=qkv_recv_sem.at[k - 1, part],
                device_id={"wide": target},
                device_id_type=MESH,
            )
            copy.start()
            exchanges.append(copy)
    for part in range(3):
        source = qkv_part.at[:, pl.ds(pl.multiple_of(part * dim + w * cols, cols), cols)]
        keep(source, weight.at[w, n, :, pl.ds(part * cols, cols)])
    out_onward = send(out_part, out_full.at[w, n], right)
    out_back = send(out_part, out_full.at[w, n], left)
    out_own = keep(out_part, out_full.at[w, n])
    out_y = [send(out_part, out_full.at[w, n], to_y)]
    team = z * 2 + y
    piece = down_part.shape[0]

    def up_block(its_z, its_y, share):
        its_w = (share % 2) * 4 + its_z * 2 + (share // 2) % 2
        its_n = its_y * 2 + share // 4
        return up_part.at[:, pl.ds(pl.multiple_of((its_w * 4 + its_n) * piece, piece), piece)]

    swaps, up_own = [], []
    for share in range(8):
        target = up_zero.at[team, :, pl.ds(share * piece, piece)]
        for k, (its_z, its_y, peer) in enumerate(((z, 1 - y, to_y), (1 - z, y, to_z), (1 - z, 1 - y, to_both))):
            copy = pltpu.make_async_remote_copy(
                src_ref=up_block(its_z, its_y, share),
                dst_ref=target,
                send_sem=up_send_sem.at[k, share],
                recv_sem=up_recv_sem.at[k, share],
                device_id=peer,
                device_id_type=MESH,
            )
            copy.start()
            swaps.append(copy)
        copy = pltpu.make_async_copy(up_block(z, y, share), target, up_local_sem.at[share])
        copy.start()
        up_own.append(copy)

    def ring_hop(step):
        nonlocal onward, back, out_onward, out_back
        behind, ahead = ring_index(place + 8 - step), ring_index(place + step)
        onward.wait_recv()
        back.wait_recv()
        if step < 3:
            onward = send(act.at[behind], act.at[behind], right)
            back = send(act.at[ahead], act.at[ahead], left)
        else:
            onward = send(act.at[behind, first], act.at[behind, first], right)
            back = send(act.at[ahead, second], act.at[ahead, second], left)
        out_onward.wait_recv()
        out_back.wait_recv()
        for owner in (behind, ahead):
            out_y.append(send(out_full.at[owner, n], out_full.at[owner, n], to_y))
        if step < 3:
            out_onward = send(out_full.at[behind, n], out_full.at[behind, n], right)
            out_back = send(out_full.at[ahead, n], out_full.at[ahead, n], left)
        else:
            out_onward = send(out_full.at[behind, n, out_first], out_full.at[behind, n, out_first], right)
            out_back = send(out_full.at[ahead, n, out_second], out_full.at[ahead, n, out_second], left)

    def project(owner):
        at = pl.ds(pl.multiple_of(owner * rows, rows), rows)
        for part in range(3):
            its = weight[:, :, :, pl.ds(part * cols, cols)].reshape(dim, cols)
            value = dot(act[owner], its, ((1,), (0,)))
            for h in range(heads):
                piece = value[:, h * HEAD_DIM : (h + 1) * HEAD_DIM]
                if part < 2:
                    piece = turn(piece, cos_ref[at, :], sin_ref[at, :])
                qkv[at, pl.ds(part * cols + h * HEAD_DIM, HEAD_DIM)] = piece.astype(bf16)

    def project_pair(step):
        each(2, lambda i: project(ring_index(place + 8 - step + 2 * step * i)))

    for copy in kept[:3]:
        copy.wait()
    for copy in exchanges:
        copy.wait_recv()
    weight_y = send(weight.at[:, n], weight.at[:, n], to_y)
    ring_hop(1)
    weight_y.wait_recv()
    weight_core = [
        send(weight.at[:, n], weight.at[:, n], to_core),
        send(weight.at[:, (n + 2) % 4], weight.at[:, (n + 2) % 4], to_core),
    ]
    beside = send(top_zero, top_one, to_y)
    for copy in weight_core:
        copy.wait_recv()
    each(1, lambda i: project(w + i))
    project_pair(1)
    ring_hop(2)
    project_pair(2)
    ring_hop(3)
    for copy in swaps:
        copy.wait_recv()
    for copy in up_own:
        copy.wait()
    up_to_far = send(up_zero, up_far, to_far)
    up_to_x = send(up_zero, up_next, to_x)
    down_to_x = send(down_part, down_next, to_x)
    cores = [send(up_zero, ups.at[1, 0], to_core), send(down_part, downs.at[1, 0], to_core)]
    across = send(top_zero, top_two, to_z)
    project_pair(3)
    onward.wait_recv()
    back.wait_recv()
    project(ring_index(place + 4))
    out_onward.wait_recv()
    out_back.wait_recv()
    out_own.wait()
    last = ring_index(place + 4)
    out_y.append(send(out_full.at[last, n], out_full.at[last, n], to_y))
    keep(act, act_out)
    keep(weight, weight_out)

    split = split_ref[0]
    factor = HEAD_DIM ** (-0.5) * LOG2E
    block = 2 * rows
    limit_one, limit_two, head_first = limit_ref[0, 0], limit_ref[0, 1], limit_ref[0, 2]

    def low_send(target):
        return pltpu.make_async_remote_copy(
            src_ref=low.at[pl.ds(target * rows, rows)],
            dst_ref=low_out.at[:, pl.ds(pl.multiple_of(w * cols, cols), cols)],
            send_sem=low_send_sem.at[target],
            recv_sem=low_recv_sem.at[w],
            device_id={"wide": target},
            device_id_type=MESH,
        )

    def low_come(source):
        return pltpu.make_async_remote_copy(
            src_ref=low.at[pl.ds(source * rows, rows)],
            dst_ref=low_out.at[:, pl.ds(source * cols, cols)],
            send_sem=low_send_sem.at[source],
            recv_sem=low_recv_sem.at[source],
            device_id={"wide": source},
            device_id_type=MESH,
        )

    def low_keep(target):
        return pltpu.make_async_copy(
            low.at[pl.ds(target * rows, rows)],
            low_out.at[:, pl.ds(target * cols, cols)],
            low_send_sem.at[target],
        )

    for i in range(4):
        at_rows = pl.ds(i * block, block)
        at = i * block + lax.broadcasted_iota(jnp.int32, (block, 1), 0)
        lowest = jnp.where(at >= split, split, 0)

        def keys_of(j, state, diagonal):
            keys = pl.ds(pl.multiple_of(j * block, block), block)
            kat = j * block + lax.broadcasted_iota(jnp.int32, (block, block), 1)
            ok = kat >= lowest
            if diagonal:
                ok = ok & (kat <= at)
            found = []
            for h in range(heads):
                top, total, acc = state[h]
                q = qkv[at_rows, pl.ds(h * HEAD_DIM, HEAD_DIM)]
                k = qkv[keys, pl.ds(cols + h * HEAD_DIM, HEAD_DIM)]
                v = qkv[keys, pl.ds(2 * cols + h * HEAD_DIM, HEAD_DIM)]
                s = jnp.where(ok, dot(q, k, ((1,), (1,))) * factor, masked_score)
                new_top = jnp.maximum(top, jnp.max(s, axis=1, keepdims=True))
                p = jnp.exp2(s - new_top)
                fade = jnp.exp2(top - new_top)
                total = total * fade + jnp.sum(p, axis=1, keepdims=True)
                acc = acc * fade + dot(p.astype(bf16), v, ((1,), (0,)))
                found.append((new_top, total, acc))
            return tuple(found)

        start = (
            jnp.full((block, 1), masked_score, f32),
            jnp.zeros((block, 1), f32),
            jnp.zeros((block, HEAD_DIM), f32),
        )
        state = (start,) * heads
        if i:
            state = lax.fori_loop(0, i, functools.partial(keys_of, diagonal=False), state)
        state = keys_of(i, state, True)
        limit = jnp.where(at < split, limit_one, limit_two)
        for h in range(heads):
            top, total, acc = state[h]
            value = acc / total
            head = pl.ds(h * HEAD_DIM, HEAD_DIM)
            active = (head_first + h < limit).astype(f32)
            att[at_rows, head] = value
            low[at_rows, head] = (value * active).astype(bf16)
            lse[at_rows, head] = jnp.broadcast_to(top + jnp.log2(total), (block, HEAD_DIM))
        for target in (2 * i, 2 * i + 1):

            @pl.when(w != target)
            def _():
                low_send(target).start()

            @pl.when(w == target)
            def _():
                low_keep(target).start()

        if i == 0:
            for copy in out_y:
                copy.wait_recv()
            out_core = [
                send(out_full.at[:, n], out_full.at[:, n], to_core),
                send(out_full.at[:, (n + 2) % 4], out_full.at[:, (n + 2) % 4], to_core),
            ]
        if i == 2:
            across.wait_recv()
            both = send(top_two, top_three, to_y)
    part_rows = down_part.shape[0] // 2
    parts = [pl.ds(0, part_rows), pl.ds(part_rows, part_rows)]
    down_fars = [send(down_part.at[parts[0]], downs.at[0, 1, parts[0]], to_far)]
    up_to_far.wait_recv()
    up_to_both = send(up_far, up_both, to_x)
    cores.append(send(up_far, ups.at[1, 1], to_core))
    for copy in out_core:
        copy.wait_recv()
    held = []
    for k in range(8):
        held.append(pltpu.make_async_copy(out_full.at[k], out_held.at[k], out_sem.at[k]))
        held[-1].start()
    for target in range(8):

        @pl.when(w != target)
        def _():
            low_send(target).wait_send()
            low_come(target).wait_recv()

        @pl.when(w == target)
        def _():
            low_keep(target).wait()

    down_fars.append(send(down_part.at[parts[1]], downs.at[0, 1, parts[1]], to_far))
    for copy in held:
        copy.wait()

    def branch(t):
        at = pl.ds(pl.multiple_of(t * 256, 256), 256)
        value = dot(low_out[...], out_held[:, :, :, at].reshape(dim, 256), ((1,), (0,)))
        x_one[:, at] = tokens_ref[:, at].astype(f32) + value

    each(dim // 256, branch)
    gain_two, bias_two = gain_two_ref[...], bias_two_ref[...]
    lane = lax.broadcasted_iota(jnp.int32, (32, 8), 1)
    wide_lane = lax.broadcasted_iota(jnp.int32, (32, 128), 1)

    def normalize(i):
        at = pl.ds(pl.multiple_of(i * 32, 32), 32)
        value = x_one[at, :]
        center = value - jnp.mean(value, axis=-1, keepdims=True)
        inv = lax.rsqrt(jnp.mean(center * center, axis=-1, keepdims=True) + norm_eps)
        ln_out = center * inv * gain_two + bias_two
        act_two[at, :] = ln_out.astype(bf16)
        logits = lax.dot_general(
            ln_out, router_ref[...], (((1,), (1,)), ((), ())), precision=highest, preferred_element_type=f32
        )
        logits = jnp.where(lane < WIDTHS, logits, masked_score)
        powers = jnp.exp(logits - jnp.max(logits, axis=-1, keepdims=True))
        prob = powers / jnp.sum(powers, axis=-1, keepdims=True)
        hot = onehot_ref[at, :]
        chosen = jnp.sum(prob * hot, axis=-1, keepdims=True)
        width = jnp.sum(hot * lane.astype(f32), axis=-1, keepdims=True)
        coef[at, :] = chosen * (hot - prob)
        facts[at, :] = jnp.where(wide_lane == 0, chosen, width)

    each(rows // 32, normalize)

    def slot(k):
        return pl.ds(k * rows, rows)

    act_y = send(act_two, act_many.at[slot(1)], to_y)
    act_z = send(act_two, act_many.at[slot(2)], to_z)
    mine = facts.at[slot(0)]
    facts_y = send(mine, facts.at[slot(1)], to_y)
    facts_z = send(mine, facts.at[slot(2)], to_z)
    keep(act_two, act_many.at[slot(0)])
    up_to_x.wait_recv()
    cores.append(send(up_next, ups.at[1, 2], to_core))
    down_to_x.wait_recv()
    cores.append(send(down_next, downs.at[1, 2], to_core))
    up_to_both.wait_recv()
    cores.append(send(up_both, ups.at[1, 3], to_core))
    down_boths = []

    def down_hop(k):
        down_fars[k].wait_recv()
        down_boths.append(send(downs.at[0, 1, parts[k]], downs.at[0, 3, parts[k]], to_x))
        cores.append(send(downs.at[0, 1, parts[k]], downs.at[1, 1, parts[k]], to_core))

    down_hop(0)
    act_y.wait_recv()
    act_z.wait_recv()
    half = rows // 2
    boths = [
        send(act_many.at[pl.ds(2 * rows, half)], act_many.at[pl.ds(3 * rows, half)], to_y),
        send(act_many.at[pl.ds(rows + half, half)], act_many.at[pl.ds(3 * rows + half, half)], to_z),
    ]
    facts_y.wait_recv()
    facts_z.wait_recv()
    boths.append(send(facts.at[slot(2)], facts.at[slot(3)], to_y))
    down_hop(1)
    for copy in [beside, both] + boths:
        copy.wait_recv()
    for k in range(2):
        down_boths[k].wait_recv()
        cores.append(send(downs.at[0, 3, parts[k]], downs.at[1, 3, parts[k]], to_core))
    for copy in cores:
        copy.wait_recv()
    for copy in kept[3:]:
        if copy is not out_own:
            copy.wait()
    for copy in started + exchanges + swaps:
        copy.wait_send()


def first_sums(
    split, limits, tokens, gain, cos2, sin2, w_qkv, w_out, w_up, w_down, top, onehot, router, gain_two, bias_two
):
    rows, dim = tokens.shape
    length = 8 * rows
    shard, wide_cols = w_qkv.shape
    cols = wide_cols // 24
    any_space = pl.BlockSpec(memory_space=pl.ANY)
    in_vmem = pl.BlockSpec(memory_space=pltpu.VMEM)
    smem = pl.BlockSpec(memory_space=pltpu.SMEM)
    dma = pltpu.SemaphoreType.DMA

    def shape(*dims):
        return jax.ShapeDtypeStruct(dims, bf16)

    def full(*dims):
        return jax.ShapeDtypeStruct(dims, f32)

    flops = 6 * length * dim * cols + 4 * length * length * cols
    return pl.pallas_call(
        first_kernel,
        in_specs=[smem] * 2 + [in_vmem] * 4 + [any_space] * 5 + [in_vmem] * 4,
        out_specs=[in_vmem] * 7 + [any_space] * 9,
        out_shape=[
            shape(length, 3 * cols),
            full(length, cols),
            full(length, cols),
            full(rows, dim),
            full(rows, 8),
            full(4 * rows, 128),
            shape(rows, dim),
            shape(4 * rows, dim),
            shape(8, rows, dim),
            shape(8, 4, shard, 3 * cols),
            shape(8, 4, shard, dim),
            shape(2, 4, 4, shard, dim),
            shape(2, 4, *w_down.shape),
            shape(rows, dim),
            shape(rows, dim),
            shape(rows, dim),
        ],
        scratch_shapes=[
            pltpu.VMEM((8, rows, dim), bf16),
            pltpu.VMEM((8, 4, shard, 3 * cols), bf16),
            pltpu.VMEM((length, cols), bf16),
            pltpu.VMEM((8, 4, shard, dim), bf16),
            pltpu.VMEM((rows, dim), bf16),
            dma((8,)),
            dma((60,)),
            dma((60,)),
            dma((7, 3)),
            dma((7, 3)),
            dma((8,)),
            dma((8,)),
            dma((3, 8)),
            dma((3, 8)),
            dma((8,)),
            dma((8,)),
        ],
        compiler_params=pltpu.CompilerParams(
            collective_id=2, has_side_effects=True, vmem_limit_bytes=60 * 2**20
        ),
        cost_estimate=pl.CostEstimate(flops=flops, bytes_accessed=2**25, transcendentals=2**22),
    )(
        split, limits, tokens, gain, cos2, sin2, w_qkv, w_out, w_up, w_down, top, onehot, router, gain_two, bias_two
    )


STRIP = 128


def last_kernel(
    dproj,
    weight,
    act_ref,
    out_own,
    out_low,
    out_high,
    small_ref,
    base_ref,
    tokens_ref,
    inv_ref,
    gain_ref,
    up_zero,
    up_one,
    up_two,
    up_three,
    input_grad,
    out_grad,
    qkv_grad,
    small_out,
    up_grad,
    act_grad,
    qkv_come,
    act,
    terms,
    core_come,
    side_come,
    act_send,
    act_recv,
    out_send,
    out_recv,
    small_sum,
    small_recv,
    out_come,
    load_sem,
    ring_send_sem,
    ring_recv_sem,
    send_sem,
    recv_sem,
):
    w = lax.axis_index("wide")
    n = lax.axis_index("narrow")
    core, y = n % 2, n // 2
    odd = w % 2
    place = w // 2 + odd * (7 - 2 * (w // 2))
    dim = weight.shape[0]
    half = dim // 2
    rows = act_grad.shape[0]
    shard = out_grad.shape[0]
    aims = ({"wide": ring_index(place + 1)}, {"wide": ring_index(place + 7)})
    other_core = {"narrow": n + 1 - 2 * core}
    other_y = {"narrow": (n + 2) % 4}
    others = [{"wide": (w + k) % 8} for k in range(1, 8)]
    z = (w // 2) % 2
    barrier = pltpu.get_barrier_semaphore()
    for peer in others + [other_core, other_y]:
        pl.semaphore_signal(barrier, inc=1, device_id=peer, device_id_type=MESH)
    pl.semaphore_wait(barrier, len(others) + 2)
    load = pltpu.make_async_copy(act_ref, act, load_sem)
    load.start()
    started = []

    def send(source, target, peer):
        at = len(started)
        copy = pltpu.make_async_remote_copy(
            src_ref=source,
            dst_ref=target,
            send_sem=send_sem.at[at],
            recv_sem=recv_sem.at[at],
            device_id=peer,
            device_id_type=MESH,
        )
        copy.start()
        started.append(copy)
        return copy

    def hop(step, stream):
        if stream < 4:
            source, target, side = act_send.at[step, stream], act_recv.at[step, stream], stream // 2
        else:
            source, target, side = out_send.at[step, stream - 4], out_recv.at[step, stream - 4], stream - 4
        return pltpu.make_async_remote_copy(
            src_ref=source,
            dst_ref=target,
            send_sem=ring_send_sem.at[step, stream],
            recv_sem=ring_recv_sem.at[step, stream],
            device_id=aims[side],
            device_id_type=MESH,
        )

    def owner_of(step, side):
        return ring_index(place + 7 - step) if side == 0 else ring_index(place + 1 + step)

    def ring_step(step):
        for stream in range(4):
            side, strip = stream // 2, stream % 2
            owner = owner_of(step, side)
            at = pl.ds(pl.multiple_of(owner * rows + strip * STRIP, STRIP), STRIP)
            for part in range(2):
                cols = pl.ds(part * 512, 512)
                wide_cols = pl.ds(side * half + part * 512, 512)
                value = dot(dproj[at, :], weight[wide_cols, :], ((1,), (1,)))
                if step == 0:
                    act_send[0, stream, :, cols] = value.astype(bf16)
                elif step < 7:
                    act_send[step, stream, :, cols] = value.astype(bf16)
                else:
                    act_grad[pl.ds(strip * STRIP, STRIP), wide_cols] = value
            if step > 0:
                hop(step - 1, stream).wait_recv()

                def add(i):
                    part = pl.ds(pl.multiple_of(i * 32, 32), 32)
                    come = act_recv[step - 1, stream, part, :].astype(f32)
                    if step < 7:
                        act_send[step, stream, part, :] = (
                            act_send[step, stream, part, :].astype(f32) + come
                        ).astype(bf16)
                    else:
                        row = pl.ds(pl.multiple_of(strip * STRIP + i * 32, 32), 32)
                        act_grad[row, pl.ds(side * half, half)] += come

                each(STRIP // 32, add)
            if step < 7:
                hop(step, stream).start()

    def out_step(step):
        for stream in (4, 5):
            side = stream - 4
            owner = owner_of(step, side)
            at = pl.ds(side * half, half)
            value = out_own[owner, :, at].astype(f32) + out_come[owner, :, at].astype(f32)
            if step > 0:
                hop(step - 1, stream).wait_recv()
                value = value + out_recv[step - 1, side].astype(f32)
            if step < 7:
                out_send[step, side] = value.astype(bf16)
                hop(step, stream).start()
            else:
                out_grad[:, pl.ds(side * half, half)] = value

    ring_step(0)
    out_come[0:4] = out_low[...]
    out_come[4:8] = out_high[...]
    out_step(0)
    load.wait()
    small_sum[0] = small_ref[...]

    def weight_terms(k):
        at = pl.ds(pl.multiple_of(k * rows, rows), rows)
        value = dot(act[:, at], dproj[...], ((0,), (0,)))
        product = value * weight[at, :].astype(f32)
        ones = jnp.ones((8, product.shape[1]), f32)
        sums = lax.dot_general(
            ones, product, (((1,), (1,)), ((), ())), precision=highest, preferred_element_type=f32
        )
        small_sum[0, 0:1, at] = small_sum[0, 0:1, at] + sums[0:1]
        terms[k] = value.astype(bf16).reshape(2, 2, shard, value.shape[1])

    each(8, weight_terms)
    to_core = send(terms.at[:, :, 1 - core], core_come, other_core)

    small_peers = [other_core, other_y] + [{"wide": w + b - 2 * b * ((w // b) % 2)} for b in (1, 2, 4)]

    def small_step(k):
        if k:
            pending.pop().wait_recv()
            small_sum[k] = small_sum[k - 1] + small_recv[k - 1]
        if k < 5:
            pending.append(send(small_sum.at[k], small_recv.at[k], small_peers[k]))
        else:
            small_out[...] = small_sum[k]

    pending = []
    small_step(0)
    ring_step(1)
    out_step(1)
    to_core.wait_recv()

    def add_core(i):
        a, b = i // 2, i % 2
        here = terms[a, b, core].astype(f32)
        terms[a, b, core] = (here + core_come[a, b].astype(f32)).astype(bf16)

    each(16, add_core)
    to_side = send(terms.at[:, 1 - y, core], side_come, other_y)
    small_step(1)
    ring_step(2)
    out_step(2)
    small_step(2)
    ring_step(3)
    out_step(3)
    to_side.wait_recv()

    def add_side(i):
        here = terms[i, y, core].astype(f32)
        terms[i, y, core] = (here + side_come[i].astype(f32)).astype(bf16)

    each(8, add_side)
    own = pltpu.make_async_copy(terms.at[w, y, core], qkv_come.at[w], load_sem)
    own.start()
    blocks = []
    for k, peer in enumerate(others):
        target = (w + 1 + k) % 8
        blocks.append(send(terms.at[target, y, core], qkv_come.at[w], peer))
    small_step(3)
    ring_step(4)
    out_step(4)
    small_step(4)
    ring_step(5)
    out_step(5)
    small_step(5)
    ring_step(6)
    out_step(6)
    ring_step(7)
    out_step(7)

    def finish(i):
        at = pl.ds(pl.multiple_of(i * 32, 32), 32)
        inv = inv_ref[at, :]
        normed = tokens_ref[at, :].astype(f32) * inv
        scaled = act_grad[at, :] * gain_ref[...]
        mean = jnp.mean(scaled * normed, axis=-1, keepdims=True)
        input_grad[at, :] = base_ref[at, :] + inv * (scaled - normed * mean)

    each(rows // 32, finish)
    own.wait()
    for copy in blocks:
        copy.wait_recv()
    piece = dim // 8
    for k, block in enumerate((up_zero, up_one, up_two, up_three)):
        its_z = z + (1 - 2 * z) * (k // 2)
        its_y = y + (1 - 2 * y) * (k % 2)
        for share in range(8):
            its_w = (share % 2) * 4 + its_z * 2 + (share // 2) % 2
            at = pl.multiple_of((its_w * 4 + its_y * 2 + share // 4) * piece, piece)
            up_grad[:, pl.ds(at, piece)] = block[:, pl.ds(share * piece, piece)].astype(f32)
    cols = weight.shape[1] // 3
    for k in range(8):
        for part in range(3):
            value = qkv_come[k, :, pl.ds(part * cols, cols)].astype(f32)
            qkv_grad[:, pl.ds(part * dim + k * cols, cols)] = value
    for copy in started:
        copy.wait_send()
    for step in range(7):
        for stream in range(6):
            hop(step, stream).wait_send()


def last_sums(dproj, weight, act, out_own, out_come, small, base, tokens_in, inv, gain, ups):
    tokens, cols = dproj.shape
    dim = weight.shape[0]
    rows, shard, half = tokens // 8, dim // 32, dim // 2
    any_space = pl.BlockSpec(memory_space=pl.ANY)
    in_vmem = pl.BlockSpec(memory_space=pltpu.VMEM)
    dma = pltpu.SemaphoreType.DMA
    return pl.pallas_call(
        last_kernel,
        in_specs=[in_vmem, in_vmem, any_space] + [in_vmem] * 12,
        out_specs=[in_vmem] * 5,
        out_shape=[
            jax.ShapeDtypeStruct((rows, dim), f32),
            jax.ShapeDtypeStruct((shard, dim), f32),
            jax.ShapeDtypeStruct((shard, 3 * dim), f32),
            jax.ShapeDtypeStruct((8, dim), f32),
            jax.ShapeDtypeStruct((shard, 4 * dim), f32),
        ],
        scratch_shapes=[
            pltpu.VMEM((rows, dim), f32),
            pltpu.VMEM((8, shard, cols), bf16),
            pltpu.VMEM((tokens, dim), bf16),
            pltpu.VMEM((8, 2, 2, shard, cols), bf16),
            pltpu.VMEM((8, 2, shard, cols), bf16),
            pltpu.VMEM((8, shard, cols), bf16),
            pltpu.VMEM((7, 4, STRIP, half), bf16),
            pltpu.VMEM((7, 4, STRIP, half), bf16),
            pltpu.VMEM((7, 2, shard, half), bf16),
            pltpu.VMEM((7, 2, shard, half), bf16),
            pltpu.VMEM((6, 8, dim), f32),
            pltpu.VMEM((5, 8, dim), f32),
            pltpu.VMEM((8, shard, dim), bf16),
            dma,
            dma((7, 6)),
            dma((7, 6)),
            dma((20,)),
            dma((20,)),
        ],
        compiler_params=pltpu.CompilerParams(
            collective_id=1, has_side_effects=True, vmem_limit_bytes=60 * 2**20
        ),
        cost_estimate=pl.CostEstimate(
            flops=4 * tokens * cols * dim, bytes_accessed=2**24, transcendentals=0
        ),
    )(dproj, weight, act, out_own, *out_come, small, base, tokens_in, inv, gain, *ups)


def swap(array, axis, size, bits):
    return lax.ppermute(array, axis, [(i, i ^ bits) for i in range(size)])


def on_device(
    wide,
    narrow,
    tokens,
    gain_one,
    w_qkv,
    w_out,
    gain_two,
    bias_two,
    router,
    w_up,
    w_down,
    doc_split,
    head_count,
    width_choice,
    out_grad,
):
    rows, part_len, dim = tokens.shape
    length = part_len * wide
    heads = dim // HEAD_DIM
    hidden = w_up.shape[1]
    head_groups = wide if heads % wide == 0 else heads
    row_groups = wide // head_groups
    my_heads = heads // head_groups
    my_rows = rows // row_groups
    cols = my_heads * HEAD_DIM
    count = rows * part_len
    w_at = lax.axis_index("wide")
    n_at = lax.axis_index("narrow")
    head_at = w_at % head_groups
    row_at = (w_at // head_groups) * my_rows
    ring = Ring("wide", wide)

    def pick_rows(array):
        return lax.dynamic_slice_in_dim(array, row_at, my_rows, 0) if row_groups > 1 else array

    def put_rows(array):
        if row_groups == 1:
            return array
        whole = jnp.zeros((rows,) + array.shape[1:], array.dtype)
        return lax.dynamic_update_slice_in_dim(whole, array, row_at, 0)

    def narrow_gather(part):
        found = part[None]
        for bits in [2**k for k in range(narrow.bit_length() - 1)]:
            other = swap(found, "narrow", narrow, bits)
            mine = (n_at & bits) == 0
            found = jnp.concatenate([jnp.where(mine, found, other), jnp.where(mine, other, found)])
        return found

    def narrow_scatter(array):
        for bits in [2**k for k in range(narrow.bit_length() - 1)]:
            array = array.reshape((wide, -1, 2) + array.shape[2:])
            at = (n_at // bits) & 1
            others = lax.dynamic_index_in_dim(array, 1 - at, 2, keepdims=False)
            array = lax.dynamic_index_in_dim(array, at, 2, keepdims=False)
            array = array + swap(others, "narrow", narrow, bits)
        return array[:, 0]

    shares = wide
    upper = wide // 4
    upper_bits = [2**k for k in range(2, wide.bit_length() - 1)][::-1]

    def share_of(w, n):
        return ((n & 1) * 2 + (w & 1)) * upper + (w >> 2)

    def wide_of(share, team):
        return (share % upper) * 4 + ((team >> 1) << 1) + ((share // upper) & 1)

    def narrow_of(share, team):
        return ((team & 1) << 1) + share // (2 * upper)

    def team_of(w, n):
        return ((w >> 1) & 1) * 2 + (n >> 1)

    def beside(part):
        return swap(part, "narrow", narrow, 2)

    def across(part):
        return swap(part, "wide", wide, 2)

    def team_swap(blocks):
        team = team_of(w_at, n_at)
        mine = [lax.dynamic_index_in_dim(blocks, team ^ k, 0, keepdims=False) for k in range(4)]
        both = [(i, i ^ (2 * narrow + 2)) for i in range(wide * narrow)]
        come = jnp.stack(
            [
                mine[0],
                beside(mine[1]),
                across(mine[2]),
                lax.ppermute(mine[3], ("wide", "narrow"), both),
            ]
        )
        return jnp.stack([lax.dynamic_index_in_dim(come, team ^ k, 0, keepdims=False) for k in range(4)])

    def pick(array, at):
        return lax.dynamic_index_in_dim(array, at, 0, keepdims=False)

    exponent = np.arange(HEAD_DIM // 2, dtype=np.float64) * (2.0 / HEAD_DIM)
    angles = np.arange(length, dtype=np.float64)[:, None] * np.power(rope_base, -exponent)[None, :]
    cosine, sine = np.cos(angles).astype(np.float32), np.sin(angles).astype(np.float32)
    cos2 = jnp.asarray(np.concatenate([cosine, cosine], axis=1))
    sin2 = jnp.asarray(np.concatenate([-sine, sine], axis=1))
    split = pick_rows(doc_split)
    limits = jnp.concatenate(
        [pick_rows(head_count), jnp.full((my_rows, 1), head_at * my_heads, jnp.int32)], axis=1
    )

    inputs = tokens.astype(f32)
    inv_one = lax.rsqrt(jnp.mean(inputs * inputs, axis=-1, keepdims=True) + norm_eps)
    normed_one = inputs * inv_one
    act_one = (normed_one * gain_one).astype(bf16)

    shard = w_qkv.shape[0]
    piece_rows = w_down.shape[0]
    top = out_grad.reshape(count, dim)
    width_flat = width_choice.reshape(count)
    share = jnp.arange(shares, dtype=jnp.int32)[:, None]
    team = team_of(w_at, n_at)
    units = (wide_of(share, team) * narrow + narrow_of(share, team)) * piece_rows
    units = (units + jnp.arange(piece_rows, dtype=jnp.int32)[None, :]).reshape(1, -1)
    need = units // (hidden // WIDTHS)

    kernels = wide == 8 and narrow == 4 and rows == 1
    if kernels:
        hot = (width_flat[:, None] == jnp.arange(2 * WIDTHS, dtype=jnp.int32)[None, :]).astype(f32)
        need_row = need.astype(f32)
        router_rows = jnp.concatenate([router.T, gain_two[None], bias_two[None], need_row, need_row])
        found = first_sums(
            split,
            limits,
            tokens.reshape(count, dim),
            gain_one[None],
            cos2,
            sin2,
            w_qkv,
            w_out,
            w_up,
            w_down,
            top,
            hot,
            router_rows,
            gain_two[None],
            bias_two[None],
        )
        qkv, att, lse, x_one, coef, facts, att_low, act_many, act_flat, my_qkv, out_full, ups, downs, *tops = found
        qkv, att, lse = qkv[None], att[None], lse[None]
        act_flat = act_flat.reshape(length, dim)
        my_qkv = my_qkv.reshape(dim, 3 * cols)
        onehot = hot[:, :WIDTHS]
    else:
        blocks = w_qkv.reshape(shard, 3, head_groups, cols).transpose(2, 0, 1, 3)
        blocks = jnp.tile(blocks.reshape(head_groups, shard, 3 * cols), (row_groups, 1, 1))
        blocks = lax.all_to_all(blocks, "wide", 0, 0, tiled=True)
        my_qkv = narrow_gather(blocks).transpose(1, 0, 2, 3).reshape(dim, 3 * cols)
        out_parts = narrow_gather(lax.all_gather(w_out, "wide", axis=0, tiled=False))
        out_full = out_parts.transpose(1, 0, 2, 3).reshape(dim, dim)

        up_blocks = w_up.reshape(shard, upper, 2, 2, 2, 2, piece_rows).transpose(2, 4, 0, 5, 3, 1, 6)
        up_part = team_swap(up_blocks.reshape(4, shard, shares * piece_rows))
        top_beside = beside(top)
        act_all = jnp.zeros((my_rows, wide, part_len, dim), bf16)
        for owner, piece in ring.gather(act_one.reshape(count, dim)):
            piece = pick_rows(piece.reshape(rows, part_len, dim))
            act_all = lax.dynamic_update_slice(act_all, piece[:, None], (0, owner, 0, 0))
        act_flat = act_all.reshape(my_rows * length, dim)
        act_flat, my_qkv, up_part, top_beside, down_part, top = join(
            act_flat, my_qkv, up_part, top_beside, w_down, top
        )

        up_found = [((0, 0), up_part)]

        def spread(found, bit):
            return found + [((w ^ bit, n), swap(piece, "wide", wide, bit)) for (w, n), piece in found]

        for bit in upper_bits:
            up_found = spread(up_found, bit)
        up_near = ((1, 0), swap(up_part, "wide", wide, 1))
        down_near = ((1, 0), swap(down_part, "wide", wide, 1))
        proj = dot(act_flat, my_qkv, ((1,), (0,))).reshape(my_rows, length, 3 * cols)
        qkv, att, att_part, lse = attend(proj, split, limits, cos2, sin2, my_heads)
        sends = att_part.reshape(my_rows, wide, part_len, cols).transpose(1, 0, 2, 3)
        sends, down_part = join(sends, down_part)

        come = lax.all_to_all(sends, "wide", 0, 0, tiled=True)
        down_found = [((0, 0), down_part)]
        for bit in upper_bits:
            down_found = spread(down_found, bit)
        come, out_full = join(come, out_full)
        up_far = [((w ^ 1, n), swap(piece, "wide", wide, 1)) for (w, n), piece in up_found[1:]]
        up_found = up_found + [up_near] + up_far
        top_across = across(top)
        come = come.reshape(row_groups, head_groups, my_rows, part_len, cols)
        att_low = come.transpose(0, 2, 3, 1, 4).reshape(count, dim)

        down_far = [((w ^ 1, n), swap(piece, "wide", wide, 1)) for (w, n), piece in down_found[1:]]
        down_found = down_found + [down_near] + down_far
        top_both = beside(top_across)
        tops = (top, top_beside, top_across, top_both)
        x_one = inputs.reshape(count, dim) + dot(att_low, out_full, ((1,), (0,)))

        center = x_one - jnp.mean(x_one, axis=-1, keepdims=True)
        inv_two = lax.rsqrt(jnp.mean(center * center, axis=-1, keepdims=True) + norm_eps)
        normed_two = center * inv_two
        ln_out = normed_two * gain_two + bias_two
        act_two = ln_out.astype(bf16)
        onehot = (width_flat[:, None] == jnp.arange(WIDTHS, dtype=jnp.int32)[None, :]).astype(f32)
        router_prob = jax.nn.softmax(jnp.dot(ln_out, router, precision=highest), axis=-1)
        chosen = jnp.sum(router_prob * onehot, axis=-1)
        grad_top = top.astype(f32)
    def share_core(array):
        return pick(array, n_at & 1) + swap(pick(array, 1 - (n_at & 1)), "narrow", narrow, 1)

    def share_near(array):
        return pick(array, w_at & 1) + swap(pick(array, 1 - (w_at & 1)), "wide", wide, 1)

    def share_far(array):
        for bit in upper_bits:
            array = array.reshape((2, -1) + array.shape[1:])
            at = (w_at // bit) & 1
            array = pick(array, at) + swap(pick(array, 1 - at), "wide", wide, bit)
        return array[0]

    if kernels:
        small, block_out, grad_x_one, _, dat, out_own, *outs, down_grad, down_come, up_sum, up_come, _, _ = feed_forward(
            act_many,
            (top, *tops),
            facts,
            ups.reshape(2, 4, 2, 2, shard, shares * piece_rows),
            downs,
            w_down,
            x_one,
            att_low,
            out_full.reshape(2, 2, 2, dim // 8, dim),
            coef,
            router_rows,
        )
        dat = dat.reshape(1, length, cols)
        down_grad = (down_grad.astype(f32) + down_come.astype(f32)).reshape(piece_rows, dim)
        out_come = [outs[0], beside(outs[1])]
        up_sum = (up_sum + up_come).reshape(4, shard, shares * piece_rows)
        up_blocks = [pick(up_sum, team ^ k) for k in range(4)]
        diagonal = [(i, i ^ (2 * narrow + 2)) for i in range(wide * narrow)]
        up_blocks[1:3] = beside(up_blocks[1]), across(up_blocks[2])
        up_blocks[3] = lax.ppermute(up_blocks[3], ("wide", "narrow"), diagonal)
        counts = jnp.pad(jnp.sum(onehot, axis=0), (0, dim - WIDTHS))[None]
        small = jnp.concatenate([small[:7], counts])
    else:
        up_found = up_found + [((w, n ^ 1), swap(piece, "narrow", narrow, 1)) for (w, n), piece in up_found]
        down_found = down_found + [((w, n ^ 1), swap(p, "narrow", narrow, 1)) for (w, n), p in down_found]

        def up_target(i, k):
            w, n = lax.axis_index("wide"), lax.axis_index("narrow")
            dw, dn = up_found[i][0]
            return ((w ^ dw) & ~2 | (k & 2)) * narrow + ((n ^ dn) & 1 | ((k & 1) * 2))

        def down_target(i, k):
            dw, dn = down_found[i][0]
            return share_of(lax.axis_index("wide") ^ dw, lax.axis_index("narrow") ^ dn)

        up_mine = place([piece for _, piece in up_found], wide * narrow, up_target)
        up_mine = up_mine.reshape(dim, shares * piece_rows)
        down_mine = place([piece[None] for _, piece in down_found], shares, down_target)
        down_mine = down_mine.reshape(shares * piece_rows, dim)

        def team_gather(part):
            far = across(part)
            return jnp.concatenate([part, beside(part), far, beside(far)])

        def team_scatter(terms):
            low = beside(jnp.stack([terms[1], terms[3]])).astype(f32)
            near, far = terms[0] + low[0], terms[2] + low[1]
            return near + across(far.astype(bf16)).astype(f32)

        act_many = team_gather(act_two)
        mask = need <= team_gather(width_flat)[:, None]
        pre = jnp.maximum(dot(act_many, up_mine, ((1,), (0,))), 0.0)
        pre = jnp.where(mask, pre, 0.0).astype(bf16).astype(f32)
        hid = (pre * pre).astype(bf16)
        dmix = (jnp.concatenate(tops).astype(f32) * team_gather(chosen)[:, None]).astype(bf16)
        mixed = dot(hid, down_mine, ((1,), (0,))).astype(bf16)
        dhid = dot(dmix, down_mine, ((1,), (1,)))
        dpre = (dhid * 2.0 * pre).astype(bf16)
        dact = dot(dpre, up_mine, ((1,), (1,))).astype(bf16)
        mixed = team_scatter(mixed.reshape(4, count, dim))
        grad_act_two = team_scatter(dact.reshape(4, count, dim))
        down_sum = dot(hid, dmix, ((0,), (0,))).astype(bf16).reshape(2, 2, upper, piece_rows, dim)
        down_grad = share_far(share_near(share_core(down_sum))).astype(f32)
        up_sum = up_sums(act_many, dpre, wide, narrow, shard)
        up_sum = share_far(share_near(share_core(up_sum)))


        block_out = (x_one + mixed * chosen[:, None]).astype(bf16)
        grad_prob = jnp.sum(grad_top * mixed, axis=-1)
        grad_logits = (grad_prob * chosen)[:, None] * (onehot - router_prob)
        grad_router = lax.dot_general(ln_out, grad_logits, (((0,), (0,)), ((), ())), precision=highest)
        grad_ln = grad_act_two + jnp.dot(grad_logits, router.T, precision=highest)
        grad_gain_two = jnp.sum(grad_ln * normed_two, axis=0)
        grad_bias_two = jnp.sum(grad_ln, axis=0)
        grad_normed = grad_ln * gain_two
        grad_x_one = grad_top + inv_two * (
            grad_normed
            - jnp.mean(grad_normed, axis=-1, keepdims=True)
            - normed_two * jnp.mean(grad_normed * normed_two, axis=-1, keepdims=True)
        )

        grad_branch = grad_x_one.astype(bf16)
        grad_att = dot(grad_branch, out_full, ((1,), (1,))).astype(bf16)
        sends = grad_att.reshape(row_groups, my_rows, part_len, head_groups, cols)
        sends = sends.transpose(0, 3, 1, 2, 4).reshape(wide, my_rows, part_len, cols)
        come = lax.all_to_all(sends, "wide", 0, 0, tiled=True)
        dat = come.transpose(1, 0, 2, 3).reshape(my_rows, length, cols)
        counts = jnp.pad(jnp.sum(onehot, axis=0), (0, dim - WIDTHS))[None]
        small = [jnp.zeros((1, dim), f32), grad_gain_two[None], grad_bias_two[None], grad_router.T, counts]
        small = jnp.concatenate(small)

    dproj = attend_back(qkv, att, lse, dat, split, limits, cos2, sin2, my_heads)
    if not kernels:
        grad_out = dot(att_low, grad_branch, ((0,), (0,))).astype(bf16)
        grad_out = narrow_scatter(grad_out.reshape(wide, narrow, shard, dim))
    if not kernels:
        up_sum = team_swap(up_sum)
        up_grad = up_sum.reshape(2, 2, shard, 2, 2, upper, piece_rows).transpose(2, 5, 0, 4, 1, 3, 6)
        up_grad = up_grad.reshape(shard, hidden).astype(f32)
    normed_flat = normed_one.reshape(count, dim)

    if kernels:
        input_grad, out_proj_grad, qkv_grad, small, up_grad = last_sums(
            dproj[0],
            my_qkv,
            act_flat,
            out_own,
            out_come,
            small,
            grad_x_one,
            tokens.reshape(count, dim),
            inv_one.reshape(count, 1),
            gain_one[None],
            up_blocks,
        )
    else:
        half = dim // 2

        def one_term(owner, side):
            rows_of = lax.dynamic_slice_in_dim(dproj, owner * part_len, part_len, 1)
            rows_of = rows_of.reshape(my_rows * part_len, 3 * cols)
            term = dot(rows_of, my_qkv[side * half : (side + 1) * half], ((1,), (1,)))
            return put_rows(term.reshape(my_rows, part_len, half)).reshape(count, half)

        out_proj_grad = lax.psum_scatter(
            grad_out.reshape(wide * shard, dim), "wide", scatter_dimension=0, tiled=True
        ).astype(f32)
        grad_act_one = jnp.concatenate(ring.scatter(one_term), axis=1)
        grad_qkv = dot(act_flat, dproj.reshape(my_rows * length, 3 * cols), ((0,), (0,)))
        gain_one_part = jnp.sum(grad_qkv * my_qkv.astype(f32), axis=1)
        small = small.at[0].set(gain_one_part)
        grad_qkv = narrow_scatter(grad_qkv.astype(bf16).reshape(wide, narrow, shard, 3 * cols))
        grad_qkv = lax.all_to_all(grad_qkv, "wide", 0, 0, tiled=True).astype(f32)
        for bits in (1, 2):
            small = small + swap(small, "narrow", narrow, bits)
        for bits in [2**k for k in range(wide.bit_length() - 1)]:
            small = small + swap(small, "wide", wide, bits)
        grad_qkv = jnp.sum(grad_qkv.reshape(row_groups, head_groups, shard, 3, cols), axis=0)
        qkv_grad = grad_qkv.transpose(1, 2, 0, 3).reshape(shard, 3 * dim)
        grad_scaled = grad_act_one * gain_one
        input_grad = grad_x_one + inv_one.reshape(count, 1) * (
            grad_scaled - normed_flat * jnp.mean(grad_scaled * normed_flat, axis=-1, keepdims=True)
        )
    gain_one_grad = small[0] / gain_one
    gain_two_grad, bias_two_grad = small[1], small[2]
    router_grad = small[3 : 3 + WIDTHS].T
    counts_all = small[3 + WIDTHS, :WIDTHS]
    return (
        block_out.reshape(rows, part_len, dim),
        input_grad.reshape(rows, part_len, dim),
        qkv_grad,
        out_proj_grad,
        up_grad,
        down_grad,
        gain_one_grad,
        gain_two_grad,
        bias_two_grad,
        router_grad,
        counts_all.astype(jnp.int32),
    )


def solution(mesh):
    in_specs = (
        P("narrow", "wide", None),
        P(),
        P(("wide", "narrow"), None),
        P(("wide", "narrow"), None),
        P(),
        P(),
        P(),
        P(("wide", "narrow"), None),
        P(("wide", "narrow"), None),
        P("narrow"),
        P("narrow", None),
        P("narrow", "wide"),
        P("narrow", "wide", None),
    )
    out_specs = (
        P("narrow", "wide", None),
        P("narrow", "wide", None),
        P(("wide", "narrow"), None),
        P(("wide", "narrow"), None),
        P(("wide", "narrow"), None),
        P(("wide", "narrow"), None),
        P(),
        P(),
        P(),
        P(),
        P(),
    )
    step = functools.partial(on_device, mesh.shape["wide"], mesh.shape["narrow"])
    return jax.shard_map(step, mesh=mesh, in_specs=in_specs, out_specs=out_specs, check_vma=False)
```

```python
import functools

import jax
import jax.numpy as jnp
import numpy as np
from jax import lax
from jax.experimental import pallas as pl
from jax.experimental.pallas import tpu as pltpu
from jax.sharding import PartitionSpec as P

HEAD_DIM = 128
WIDTHS = 4
BLOCK = 512

highest = lax.Precision.HIGHEST
norm_eps = 1e-05
rope_base = 10000.0
masked_score = -1e30
LOG2E = 1.4426950408889634
f32 = jnp.float32
bf16 = jnp.bfloat16


def dot(a, b, contract):
    return lax.dot_general(a, b, (contract, ((), ())), preferred_element_type=f32)


def turn(u, cos2, sin2):
    return u * cos2 + pltpu.roll(u, HEAD_DIM // 2, 1) * sin2


def first_key(split, row):
    return jnp.where(row >= split, split, 0)


def attend_kernel(heads, length, split_ref, limit_ref, proj_ref, cos_ref, sin_ref, qkv_ref, att_ref, low_ref, lse_ref):
    row = pl.program_id(0)
    split = split_ref[row]
    scale = HEAD_DIM ** (-0.5) * LOG2E
    block = min(BLOCK, length)
    blocks = length // block
    width = heads * HEAD_DIM

    def rotate_block(i, carry):
        rows = pl.ds(pl.multiple_of(i * block, block), block)
        cos2 = cos_ref[rows, :]
        sin2 = sin_ref[rows, :]
        for part in range(2 * heads):
            cols = pl.ds(part * HEAD_DIM, HEAD_DIM)
            qkv_ref[rows, cols] = turn(proj_ref[rows, cols], cos2, sin2).astype(bf16)
        cols = pl.ds(2 * width, width)
        qkv_ref[rows, cols] = proj_ref[rows, cols].astype(bf16)
        return carry

    lax.fori_loop(0, blocks, rotate_block, 0)
    for h in range(heads):
        qcol = pl.ds(h * HEAD_DIM, HEAD_DIM)
        kcol = pl.ds(width + h * HEAD_DIM, HEAD_DIM)
        vcol = pl.ds(2 * width + h * HEAD_DIM, HEAD_DIM)

        def query_block(i, carry):
            rows = pl.ds(pl.multiple_of(i * block, block), block)
            q = qkv_ref[rows, qcol]
            at = i * block + lax.broadcasted_iota(jnp.int32, (block, 1), 0)
            low = first_key(split, at)

            def key_block(j, state):
                top, total, acc = state
                keys = pl.ds(pl.multiple_of(j * block, block), block)
                s = dot(q, qkv_ref[keys, kcol], ((1,), (1,))) * scale
                kat = j * block + lax.broadcasted_iota(jnp.int32, (block, block), 1)
                ok = (kat <= at) & (kat >= low)
                s = jnp.where(ok, s, masked_score)
                new_top = jnp.maximum(top, jnp.max(s, axis=1, keepdims=True))
                p = jnp.exp2(s - new_top)
                fade = jnp.exp2(top - new_top)
                total = total * fade + jnp.sum(p, axis=1, keepdims=True)
                acc = acc * fade + dot(p.astype(bf16), qkv_ref[keys, vcol], ((1,), (0,)))
                return new_top, total, acc

            start = jnp.where(i * block >= split, split // block, 0)
            top, total, acc = lax.fori_loop(
                start,
                i + 1,
                key_block,
                (
                    jnp.full((block, 1), masked_score, f32),
                    jnp.zeros((block, 1), f32),
                    jnp.zeros((block, HEAD_DIM), f32),
                ),
            )
            att = acc / total
            limit = jnp.where(at < split, limit_ref[row, 0], limit_ref[row, 1])
            active = (limit_ref[row, 2] + h < limit).astype(f32)
            att_ref[rows, qcol] = att
            low_ref[rows, qcol] = (att * active).astype(bf16)
            lse_ref[rows, qcol] = jnp.broadcast_to(top + jnp.log2(total), (block, HEAD_DIM))
            return carry

        lax.fori_loop(0, blocks, query_block, 0)


def attend(proj, split, limits, cos2, sin2, heads):
    rows, length, _ = proj.shape
    width = heads * HEAD_DIM
    smem = pl.BlockSpec(memory_space=pltpu.SMEM)
    table = pl.BlockSpec((length, HEAD_DIM), lambda r: (0, 0))

    def whole(cols):
        return pl.BlockSpec((None, length, cols), lambda r: (r, 0, 0))

    flops = rows * heads * 4 * length * length * HEAD_DIM
    return pl.pallas_call(
        functools.partial(attend_kernel, heads, length),
        grid=(rows,),
        in_specs=[smem, smem, whole(3 * width), table, table],
        out_specs=[whole(3 * width), whole(width), whole(width), whole(width)],
        out_shape=[
            jax.ShapeDtypeStruct((rows, length, 3 * width), bf16),
            jax.ShapeDtypeStruct((rows, length, width), f32),
            jax.ShapeDtypeStruct((rows, length, width), bf16),
            jax.ShapeDtypeStruct((rows, length, width), f32),
        ],
        compiler_params=pltpu.CompilerParams(vmem_limit_bytes=56 * 2**20),
        cost_estimate=pl.CostEstimate(flops=flops, bytes_accessed=2**24, transcendentals=flops // 512),
    )(split, limits, proj, cos2, sin2)


def attend_back_kernel(
    heads,
    length,
    split_ref,
    limit_ref,
    qkv_ref,
    att_ref,
    lse_ref,
    dat_ref,
    cos_ref,
    sin_ref,
    dproj_ref,
    datt_ref,
    delta_ref,
    dq_ref,
):
    row = pl.program_id(0)
    split = split_ref[row]
    scale = HEAD_DIM ** (-0.5)
    block = min(BLOCK, length)
    blocks = length // block
    width = heads * HEAD_DIM
    qcols = [pl.ds(h * HEAD_DIM, HEAD_DIM) for h in range(heads)]
    kcols = [pl.ds(width + h * HEAD_DIM, HEAD_DIM) for h in range(heads)]
    vcols = [pl.ds(2 * width + h * HEAD_DIM, HEAD_DIM) for h in range(heads)]

    def rows_of(i):
        return pl.ds(pl.multiple_of(i * block, block), block)

    def prepare(i, carry):
        rows = rows_of(i)
        at = i * block + lax.broadcasted_iota(jnp.int32, (block, 1), 0)
        limit = jnp.where(at < split, limit_ref[row, 0], limit_ref[row, 1])
        for h in range(heads):
            active = (limit_ref[row, 2] + h < limit).astype(f32)
            datt = dat_ref[rows, qcols[h]].astype(f32) * active
            datt_ref[h, rows, :] = datt.astype(bf16)
            delta = jnp.sum(datt * att_ref[rows, qcols[h]], axis=1, keepdims=True)
            delta_ref[h, rows, :] = jnp.broadcast_to(delta, (block, HEAD_DIM))
            dq_ref[h, rows, :] = jnp.zeros((block, HEAD_DIM), f32)
        return carry

    lax.fori_loop(0, blocks, prepare, 0)

    def key_block(j, carry):
        keys = rows_of(j)
        kat = j * block + lax.broadcasted_iota(jnp.int32, (block, block), 1)

        def query_block(i, state):
            rows = rows_of(i)
            at = i * block + lax.broadcasted_iota(jnp.int32, (block, 1), 0)
            ok = (kat <= at) & (kat >= first_key(split, at))
            found = []
            for h in range(heads):
                dk, dv = state[h]
                q, k, v = qkv_ref[rows, qcols[h]], qkv_ref[keys, kcols[h]], qkv_ref[keys, vcols[h]]
                datt = datt_ref[h, rows, :]
                s = dot(q, k, ((1,), (1,))) * (scale * LOG2E)
                lse = lse_ref[rows, qcols[h]][:, :1]
                p = jnp.exp2(jnp.where(ok, s - lse, masked_score))
                dp = dot(datt, v, ((1,), (1,)))
                ds = (p * (dp - delta_ref[h, rows, :][:, :1])).astype(bf16)
                dv = dv + dot(p.astype(bf16), datt, ((0,), (0,)))
                dk = dk + dot(ds, q, ((0,), (0,)))
                dq_ref[h, rows, :] += dot(ds, k, ((1,), (0,)))
                found.append((dk, dv))
            return tuple(found)

        stop = jnp.where((j + 1) * block <= split, (split - 1) // block + 1, blocks)
        zero = jnp.zeros((block, HEAD_DIM), f32)
        state = lax.fori_loop(j, stop, query_block, ((zero, zero),) * heads)
        for h in range(heads):
            dk, dv = state[h]
            turned = turn(dk * scale, cos_ref[keys, :], -sin_ref[keys, :])
            dproj_ref[keys, kcols[h]] = turned.astype(bf16)
            dproj_ref[keys, vcols[h]] = dv.astype(bf16)
        return carry

    lax.fori_loop(0, blocks, key_block, 0)

    def finish(i, carry):
        rows = rows_of(i)
        for h in range(heads):
            dq = dq_ref[h, rows, :] * scale
            dproj_ref[rows, qcols[h]] = turn(dq, cos_ref[rows, :], -sin_ref[rows, :]).astype(bf16)
        return carry

    lax.fori_loop(0, blocks, finish, 0)


def attend_back(qkv, att, lse, dat, split, limits, cos2, sin2, heads):
    rows, length, _ = qkv.shape
    width = heads * HEAD_DIM
    smem = pl.BlockSpec(memory_space=pltpu.SMEM)
    table = pl.BlockSpec((length, HEAD_DIM), lambda r: (0, 0))

    def whole(cols):
        return pl.BlockSpec((None, length, cols), lambda r: (r, 0, 0))

    flops = rows * heads * 10 * length * length * HEAD_DIM
    return pl.pallas_call(
        functools.partial(attend_back_kernel, heads, length),
        grid=(rows,),
        in_specs=[smem, smem, whole(3 * width), whole(width), whole(width), whole(width), table, table],
        out_specs=whole(3 * width),
        out_shape=jax.ShapeDtypeStruct((rows, length, 3 * width), bf16),
        scratch_shapes=[
            pltpu.VMEM((heads, length, HEAD_DIM), bf16),
            pltpu.VMEM((heads, length, HEAD_DIM), f32),
            pltpu.VMEM((heads, length, HEAD_DIM), f32),
        ],
        compiler_params=pltpu.CompilerParams(vmem_limit_bytes=56 * 2**20),
        cost_estimate=pl.CostEstimate(flops=flops, bytes_accessed=2**24, transcendentals=flops // 1280),
    )(split, limits, qkv, att, lse, dat, cos2, sin2)


class Ring:
    def __init__(self, axis, size):
        self.axis = axis
        self.size = size
        self.order = list(range(0, size, 2)) + list(range(1, size, 2))[::-1]
        place = {w: p for p, w in enumerate(self.order)}
        self.table = [[self.order[(place[w] + k) % size] for k in range(size)] for w in range(size)]
        self.near = None
        self.right = [(w, self.order[(place[w] + 1) % size]) for w in range(size)]
        self.left = [(w, self.order[(place[w] - 1) % size]) for w in range(size)]

    def at(self, shift):
        if self.near is None:
            row = lax.dynamic_slice_in_dim(jnp.array(self.table, jnp.int32), lax.axis_index(self.axis), 1, 0)
            self.near = [row[0, k] for k in range(self.size)]
        return self.near[shift % self.size]

    def gather(self, part):
        found = [(self.at(0), part)]
        onward, back = part, part
        half = self.size // 2
        for step in range(1, half):
            onward = lax.ppermute(onward, self.axis, self.right)
            back = lax.ppermute(back, self.axis, self.left)
            found += [(self.at(-step), onward), (self.at(step), back)]
        cut = part.shape[0] // 2
        first = lax.ppermute(onward[:cut], self.axis, self.right)
        second = lax.ppermute(back[cut:], self.axis, self.left)
        found.append((self.at(half), jnp.concatenate([first, second], axis=0)))
        return found

    def gather_whole(self, part):
        whole = jnp.zeros((self.size,) + part.shape, part.dtype)
        for owner, piece in self.gather(part):
            whole = lax.dynamic_update_slice_in_dim(whole, piece[None], owner, 0)
        return whole

    def scatter(self, term):
        sums = [term(self.at(-1), 0), term(self.at(1), 1)]
        for step in range(2, self.size + 1):
            for side, perm, sign in ((0, self.right, -1), (1, self.left, 1)):
                come = lax.ppermute(sums[side].astype(bf16), self.axis, perm)
                sums[side] = come.astype(f32) + term(self.at(sign * step), side)
        return sums


def join(*arrays):
    return lax.optimization_barrier(arrays)


def after(array, *others):
    return lax.optimization_barrier((array,) + others)[0]


def place_kernel(count, targets, *refs):
    pieces, whole, held, in_sems, out_sems = refs[:-4], refs[-4], refs[-3], refs[-2], refs[-1]
    spots = [(i, k) for i in range(len(pieces)) for k in range(count)]
    loads = [
        pltpu.make_async_copy(pieces[i].at[k], held.at[at], in_sems.at[at]) for at, (i, k) in enumerate(spots)
    ]
    stores = [
        pltpu.make_async_copy(held.at[at], whole.at[targets(i, k)], out_sems.at[at])
        for at, (i, k) in enumerate(spots)
    ]
    for load in loads:
        load.start()
    for load, store in zip(loads, stores):
        load.wait()
        store.start()
    for store in stores:
        store.wait()


def place(pieces, total, targets):
    count = pieces[0].shape[0]
    anywhere = pl.BlockSpec(memory_space=pl.ANY)
    shape = (total,) + pieces[0].shape[1:]
    size = 2 * 2 * total * pieces[0][0].size
    return pl.pallas_call(
        functools.partial(place_kernel, count, targets),
        in_specs=[anywhere] * len(pieces),
        out_specs=anywhere,
        out_shape=jax.ShapeDtypeStruct(shape, pieces[0].dtype),
        scratch_shapes=[
            pltpu.VMEM((len(pieces) * count,) + pieces[0].shape[1:], pieces[0].dtype),
            pltpu.SemaphoreType.DMA((len(pieces) * count,)),
            pltpu.SemaphoreType.DMA((len(pieces) * count,)),
        ],
        compiler_params=pltpu.CompilerParams(vmem_limit_bytes=40 * 2**20),
        cost_estimate=pl.CostEstimate(flops=0, bytes_accessed=size, transcendentals=0),
    )(*pieces)


def up_sum_kernel(narrow, act_ref, dpre_ref, out_ref):
    shard = out_ref.shape[-2]
    total = dot(act_ref[...], dpre_ref[...], ((0,), (0,))).astype(bf16)
    for y in range(2):
        for core in range(2):
            at = (2 * y + core) * shard
            out_ref[core, 0, 0, y] = total[at : at + shard]


def up_sums(act, dpre, wide, narrow, shard):
    tokens, cols = dpre.shape
    upper = wide // 4
    if (narrow * shard) % 128:
        total = dot(act, dpre, ((0,), (0,))).astype(bf16)
        total = total.reshape(upper, 2, 2, 2, 2, shard, cols).transpose(4, 2, 0, 1, 3, 5, 6)
        return total.reshape(2, 2, upper, 4, shard, cols)
    return pl.pallas_call(
        functools.partial(up_sum_kernel, narrow),
        grid=(wide,),
        in_specs=[
            pl.BlockSpec((tokens, narrow * shard), lambda w: (0, w)),
            pl.BlockSpec((tokens, cols), lambda w: (0, 0)),
        ],
        out_specs=pl.BlockSpec((2, 1, 1, 2, shard, cols), lambda w: (0, w % 2, w // 4, (w // 2) % 2, 0, 0)),
        out_shape=jax.ShapeDtypeStruct((2, 2, upper, 4, shard, cols), bf16),
        compiler_params=pltpu.CompilerParams(vmem_limit_bytes=40 * 2**20),
        cost_estimate=pl.CostEstimate(
            flops=2 * tokens * cols * act.shape[1], bytes_accessed=2**24, transcendentals=0
        ),
    )(act, dpre)


MESH = pl.DeviceIdType.MESH
TILE = 512
Y, Z, CORE, X, FAR = range(5)


def each(count, body):
    def step(i, carry):
        body(i)
        return carry

    lax.fori_loop(0, count, step, 0)


def feed_kernel(
    act_many,
    top_zero,
    top_one,
    top_two,
    top_three,
    scale,
    ups,
    downs,
    down_zero,
    x_ref,
    low_ref,
    out_ref,
    coef_ref,
    router_ref,
    small,
    block_out,
    grad_x,
    branch,
    dat_out,
    out_own,
    out_come,
    out_other,
    down_own,
    down_come,
    up_own,
    up_come,
    down_core,
    up_core,
    up,
    down,
    act,
    dmix,
    hid,
    dpre,
    mixed,
    dact,
    mixed_low,
    dact_low,
    down_near,
    up_near,
    held,
    down_sum,
    mixed_come,
    dact_come,
    x_one,
    load_sem,
    send_sem,
    recv_sem,
    dat_send_sem,
    dat_recv_sem,
    out_send_sem,
    out_recv_sem,
    side_send_sem,
    side_recv_sem,
):
    w = lax.axis_index("wide")
    n = lax.axis_index("narrow")
    core, x, far = n % 2, w % 2, w // 4
    peers = {
        Y: {"narrow": (n + 2) % 4},
        Z: {"wide": w + 2 - 4 * ((w // 2) % 2)},
        CORE: {"narrow": n + 1 - 2 * core},
        X: {"wide": w + 1 - 2 * x},
        FAR: {"wide": (w + 4) % 8},
    }
    rows, dim = x_ref.shape
    started = []

    def send(source, target, peer):
        at = len(started)
        copy = pltpu.make_async_remote_copy(
            src_ref=source,
            dst_ref=target,
            send_sem=send_sem.at[at],
            recv_sem=recv_sem.at[at],
            device_id=peers[peer],
            device_id_type=MESH,
        )
        copy.start()
        started.append(copy)
        return copy

    def load(source, target, at):
        copy = pltpu.make_async_copy(source, target, load_sem.at[at])
        copy.start()
        return copy

    def slot(k):
        return pl.ds(k * rows, rows)

    barrier = pltpu.get_barrier_semaphore()
    others = [{"wide": (w + k) % 8} for k in range(1, 8)]
    for peer in others + [peers[Y], peers[CORE]]:
        pl.semaphore_signal(barrier, inc=1, device_id=peer, device_id_type=MESH)
    pl.semaphore_wait(barrier, len(others) + 2)

    loads = [load(act_many, act, 0)]
    for k, top in enumerate((top_zero, top_one, top_two, top_three)):
        loads.append(load(top, dmix.at[slot(k)], 1 + k))
    up_loads, down_loads = [], []
    for its in range(2):
        its_core = core + (1 - 2 * core) * its
        for k in range(4):
            its_far = far + (1 - 2 * far) * (k % 2)
            its_x = x + (1 - 2 * x) * (k // 2)
            source = downs.at[its, k] if its or k else down_zero
            up_loads.append(load(ups.at[its, k], up.at[its_far, :, its_x, :, its_core], 27 + 4 * its + k))
            down_loads.append(load(source, down.at[its_core, its_x, its_far], 35 + 4 * its + k))
    for copy in loads + up_loads:
        copy.wait()

    def columns(t):
        return pl.ds(pl.multiple_of(t * TILE, TILE), TILE)

    def group_of(pair):
        return pl.ds(pair * 2 * rows, 2 * rows)

    def hidden_of(pair):
        group = group_of(pair)
        width = scale[group, :][:, 1:2]

        def scaled(i):
            at = pl.ds(pl.multiple_of(pair * 2 * rows + i * 32, 32), 32)
            dmix[at, :] = (dmix[at, :].astype(f32) * scale[at, :][:, :1]).astype(bf16)

        def first(t):
            at = columns(t)
            weight = up[:, :, :, :, :, :, at].reshape(dim, TILE)
            pre = jnp.maximum(dot(act[group, :], weight, ((1,), (0,))), 0.0)
            pre = jnp.where(router_ref[6:7, at] <= width, pre, 0.0)
            dpre[group, at] = pre.astype(bf16)
            hid[group, at] = (pre * pre).astype(bf16)

        each(2 * rows // 32, scaled)
        each(dim // TILE, first)

    def mixed_of(pair):
        group = group_of(pair)

        def second(t):
            at = columns(t)
            weight = down[:, :, :, :, at].reshape(dim, TILE)
            mixed[group, at] = dot(hid[group, :], weight, ((1,), (0,))).astype(bf16)

        each(dim // TILE, second)

    def dact_of(pair):
        group = group_of(pair)

        def third(t):
            at = columns(t)
            weight = down[t // 2, t % 2].reshape(TILE, dim)
            value = dot(dmix[group, :], weight, ((1,), (1,)))
            dpre[group, at] = (value * 2.0 * dpre[group, at].astype(f32)).astype(bf16)

        def fourth(t):
            at = columns(t)
            weight = up[t // 2, t % 2].reshape(TILE, dim)
            dact[group, at] = dot(dpre[group, :], weight, ((1,), (1,))).astype(bf16)

        each(dim // TILE, third)
        each(dim // TILE, fourth)

    cut = dim // 2

    def side_of(k):
        return pl.ds((k % 2) * cut, cut)

    def down_terms(k):
        def block(i):
            rows_of = hid[:, columns(i)]
            value = dot(rows_of, dmix[:, side_of(k)], ((0,), (0,))).astype(bf16)
            down_sum[i // 2, i % 2, :, :, :, :, side_of(k)] = value.reshape(2, 2, 2, TILE // 8, cut)

        each(dim // TILE, block)
        return send(down_sum.at[1 - core, :, :, :, :, :, side_of(k)], down_core.at[k], CORE)

    def up_terms(k):
        def block(i):
            rows_of = act[:, columns(i)]
            value = dot(rows_of, dpre[:, side_of(k)], ((0,), (0,))).astype(bf16)
            up[i // 2, i % 2, :, :, :, :, side_of(k)] = value.reshape(2, 2, 2, TILE // 8, cut)

        each(dim // TILE, block)
        return send(up.at[:, :, :, :, 1 - core, :, side_of(k)], up_core.at[k % 2], CORE)

    def core_sum(k):
        cores[k].wait_recv()

        def add(i, a, b):
            c, d = i // 2, i % 2
            come = held[c, d].astype(f32)
            if k < 2:
                here = down_sum[core, a, b, c, d, :, side_of(k)].astype(f32)
                down_sum[core, a, b, c, d, :, side_of(k)] = (here + come).astype(bf16)
            else:
                here = up[a, b, c, d, core, :, side_of(k)].astype(f32)
                up[a, b, c, d, core, :, side_of(k)] = (here + come).astype(bf16)

        for a in range(2):
            for b in range(2):
                load((down_core if k < 2 else up_core).at[k % 2, a, b], held, 15 + k).wait()
                each(4, functools.partial(add, a=a, b=b))
        if k < 2:
            source = down_sum.at[core, 1 - x, :, :, :, :, side_of(k)]
            return send(source, down_near.at[:, :, :, :, side_of(k)], X)
        source = up.at[:, :, 1 - x, :, core, :, side_of(k)]
        return send(source, up_near.at[:, :, :, :, side_of(k)], X)

    def near_sum(k):
        nears[k].wait_recv()

        def add(i):
            a, b, c = i // 4, (i // 2) % 2, i % 2
            if k < 2:
                here = down_sum[core, x, a, b, c, :, side_of(k)].astype(f32)
                come = down_near[a, b, c, :, side_of(k)].astype(f32)
                down_sum[core, x, a, b, c, :, side_of(k)] = (here + come).astype(bf16)
            else:
                here = up[a, b, x, c, core, :, side_of(k)].astype(f32)
                come = up_near[a, b, c, :, side_of(k)].astype(f32)
                up[a, b, x, c, core, :, side_of(k)] = (here + come).astype(bf16)

        each(8, add)
        if k < 2:
            fars.append(
                send(
                    down_sum.at[core, x, 1 - far, :, :, :, side_of(k)],
                    down_come.at[:, :, :, side_of(k)],
                    FAR,
                )
            )
            source = down_sum.at[core, x, far, :, :, :, side_of(k)]
            keep.append(load(source, down_own.at[:, :, :, side_of(k)], 19 + k))
        else:
            source = up.at[1 - far, :, x, :, core, :, side_of(k)]
            fars.append(send(source, up_come.at[:, :, :, side_of(k)], FAR))
            source = up.at[far, :, x, :, core, :, side_of(k)]
            keep.append(load(source, up_own.at[:, :, :, side_of(k)], 19 + k))

    def add_low(total, k, low, side):
        def step(i):
            at = pl.ds(pl.multiple_of(k * rows + i * 32, 32), 32)
            come = low[side, pl.ds(pl.multiple_of(i * 32, 32), 32), :].astype(f32)
            total[at, :] = (total[at, :].astype(f32) + come).astype(bf16)

        each(rows // 32, step)

    cores, nears, fars, keep = [], [], [], []
    hidden_of(0)
    for copy in down_loads:
        copy.wait()
    mixed_of(0)
    mixed_one = send(mixed.at[slot(1)], mixed_low.at[0], Y)
    hidden_of(1)
    mixed_of(1)
    mixed_three = send(mixed.at[slot(3)], mixed_low.at[1], Y)
    cores.append(down_terms(0))
    cores.append(down_terms(1))
    dact_of(1)
    dact_two = send(dact.at[slot(2)], dact_low.at[0], Z)
    dact_three = send(dact.at[slot(3)], dact_low.at[1], Z)
    nears.append(core_sum(0))
    nears.append(core_sum(1))
    dact_of(0)
    out_load = load(out_ref, down, 13)
    x_load = load(x_ref, x_one, 14)
    top_load = load(top_zero, hid.at[slot(0)], 0)
    cores.append(up_terms(2))
    cores.append(up_terms(3))
    near_sum(0)
    nears.append(core_sum(2))
    nears.append(core_sum(3))
    near_sum(1)

    dact_two.wait_recv()
    dact_three.wait_recv()
    add_low(dact, 1, dact_low, 1)
    dact_last = send(dact.at[slot(1)], dact_come, Y)
    mixed_one.wait_recv()
    mixed_three.wait_recv()
    add_low(mixed, 2, mixed_low, 1)
    mixed_last = send(mixed.at[slot(2)], mixed_come, Z)
    add_low(mixed, 0, mixed_low, 0)
    add_low(dact, 0, dact_low, 0)
    near_sum(2)

    small[...] = jnp.zeros_like(small)
    x_load.wait()
    top_load.wait()
    mixed_last.wait_recv()
    dact_last.wait_recv()
    gain, bias = router_ref[4:5, :], router_ref[5:6, :]

    def back(i):
        def part(k):
            return pl.ds(pl.multiple_of(k * rows + i * 16, 16), 16)

        at = part(0)
        value = x_one[at, :]
        center = value - jnp.mean(value, axis=-1, keepdims=True)
        inv = lax.rsqrt(jnp.mean(center * center, axis=-1, keepdims=True) + norm_eps)
        normed = center * inv
        its_mixed = mixed[at, :].astype(f32) + mixed_come[at, :].astype(f32)
        grad = dact[at, :].astype(f32) + dact_come[at, :].astype(f32)
        top = hid[at, :].astype(f32)
        hid[part(3), :] = (value + its_mixed * scale[at, :][:, :1]).astype(bf16)
        logits = coef_ref[at, :] * jnp.sum(top * its_mixed, axis=-1, keepdims=True)
        ln_out = normed * gain + bias
        for c in range(WIDTHS):
            one = logits[:, c : c + 1]
            grad = grad + one * router_ref[c : c + 1, :]
            small[3 + c : 4 + c, :] += jnp.sum(ln_out * one, axis=0, keepdims=True)
        small[1:2, :] += jnp.sum(grad * normed, axis=0, keepdims=True)
        small[2:3, :] += jnp.sum(grad, axis=0, keepdims=True)
        grad = grad * gain
        mean = jnp.mean(grad, axis=-1, keepdims=True)
        along = jnp.mean(grad * normed, axis=-1, keepdims=True)
        total = top + inv * (grad - mean - normed * along)
        x_one[at, :] = total
        hid[part(2), :] = total.astype(bf16)

    each(rows // 16, back)
    keep.append(load(x_one, grad_x, 23))
    keep.append(load(hid.at[slot(2)], branch, 24))
    keep.append(load(hid.at[slot(3)], block_out, 25))
    out_load.wait()
    cols = dim // 8

    def dat_block(owner):
        at = pl.ds(pl.multiple_of(owner * cols, cols), cols)
        weight = down[owner // 4, (owner // 2) % 2, owner % 2]
        hid[slot(1), at] = dot(hid[slot(2), :], weight, ((1,), (1,))).astype(bf16)
        return hid.at[slot(1), at]

    dats = []
    for k in range(1, 8):
        owner = (w + k) % 8
        copy = pltpu.make_async_remote_copy(
            src_ref=dat_block(owner),
            dst_ref=dat_out.at[w],
            send_sem=dat_send_sem.at[k - 1],
            recv_sem=dat_recv_sem.at[k - 1],
            device_id={"wide": owner},
            device_id_type=MESH,
        )
        copy.start()
        dats.append(copy)
    keep.append(load(dat_block(w), dat_out.at[w], 26))
    near_sum(3)

    low_load = load(low_ref, hid.at[slot(0)], 1)
    low_load.wait()
    shard = dim // 32
    half_rows = dim // 2

    def out_block(i):
        for k, place in enumerate((act, dpre)):
            at = pl.ds(pl.multiple_of(k * half_rows + i * cols, cols), cols)
            value = dot(hid[slot(0), at], hid[slot(2), :], ((0,), (0,))).astype(bf16)
            place[pl.ds(pl.multiple_of(i * cols, cols), cols), :] = value

    each(half_rows // cols, out_block)

    def out_rows(i, its_core):
        return pl.ds(pl.multiple_of((2 * (i % 8) + its_core) * shard, shard), shard)

    outs = []
    for i in range(16):
        copy = pltpu.make_async_remote_copy(
            src_ref=(act if i < 8 else dpre).at[out_rows(i, 1 - core)],
            dst_ref=dmix.at[pl.ds(i * shard, shard)],
            send_sem=out_send_sem.at[i],
            recv_sem=out_recv_sem.at[i],
            device_id=peers[CORE],
            device_id_type=MESH,
        )
        copy.start()
        outs.append(copy)
    for copy in outs:
        copy.wait_recv()

    def out_add(i):
        for k, place in enumerate((act, dpre)):
            at = pl.ds(pl.multiple_of((k * 8 + i) * shard, shard), shard)
            mine = place[out_rows(i, core), :].astype(f32)
            dmix[at, :] = (mine + dmix[at, :].astype(f32)).astype(bf16)

    each(8, out_add)
    y = n // 2
    for i in range(8):
        keep.append(load(dmix.at[pl.ds((2 * i + y) * shard, shard)], out_own.at[i], 43 + i))
    out_ys = []
    for i in range(8):
        source = dmix.at[pl.ds((2 * i + 1 - y) * shard, shard)]
        if i < 4:
            copy = pltpu.make_async_remote_copy(
                src_ref=source,
                dst_ref=out_come.at[i],
                send_sem=side_send_sem.at[i],
                recv_sem=side_recv_sem.at[i],
                device_id=peers[Y],
                device_id_type=MESH,
            )
            copy.start()
            out_ys.append(copy)
        else:
            keep.append(load(source, out_other.at[i - 4], 51 + i))
    for copy in keep:
        copy.wait()
    for copy in fars + dats + out_ys:
        copy.wait_recv()
    for copy in started + dats + outs + out_ys:
        copy.wait_send()


def feed_forward(act, tops, facts, ups, downs, down, x_one, low, out_full, coef, router):
    rows, dim = x_one.shape
    any_space = pl.BlockSpec(memory_space=pl.ANY)
    in_vmem = pl.BlockSpec(memory_space=pltpu.VMEM)
    tokens = 4 * rows
    cut = dim // 2
    shard = dim // 32

    def shape(*dims):
        return jax.ShapeDtypeStruct(dims, bf16)

    return pl.pallas_call(
        feed_kernel,
        in_specs=[any_space] * 5 + [in_vmem] + [any_space] * 6 + [in_vmem] * 2,
        out_specs=[in_vmem] + [any_space] * 13,
        out_shape=[
            jax.ShapeDtypeStruct((8, dim), f32),
            shape(rows, dim),
            jax.ShapeDtypeStruct((rows, dim), f32),
            shape(rows, dim),
            shape(8, rows, dim // 8),
            shape(8, shard, dim),
            shape(4, shard, dim),
            shape(4, shard, dim),
            shape(2, 2, shard, dim),
            shape(2, 2, shard, dim),
            shape(2, 2, shard, dim),
            shape(2, 2, shard, dim),
            shape(2, 2, 2, 2, 2, shard, cut),
            shape(2, 2, 2, 2, 2, shard, cut),
        ],
        scratch_shapes=[
            pltpu.VMEM((2, 2, 2, 2, 2, shard, dim), bf16),
            pltpu.VMEM((2, 2, 2, dim // 8, dim), bf16),
            pltpu.VMEM((tokens, dim), bf16),
            pltpu.VMEM((tokens, dim), bf16),
            pltpu.VMEM((tokens, dim), bf16),
            pltpu.VMEM((tokens, dim), bf16),
            pltpu.VMEM((tokens, dim), bf16),
            pltpu.VMEM((tokens, dim), bf16),
            pltpu.VMEM((2, rows, dim), bf16),
            pltpu.VMEM((2, rows, dim), bf16),
            pltpu.VMEM((2, 2, 2, shard, dim), bf16),
            pltpu.VMEM((2, 2, 2, shard, dim), bf16),
            pltpu.VMEM((2, 2, shard, cut), bf16),
            pltpu.VMEM((2, 2, 2, 2, 2, shard, dim), bf16),
            pltpu.VMEM((rows, dim), bf16),
            pltpu.VMEM((rows, dim), bf16),
            pltpu.VMEM((rows, dim), f32),
            pltpu.SemaphoreType.DMA((59,)),
            pltpu.SemaphoreType.DMA((36,)),
            pltpu.SemaphoreType.DMA((36,)),
            pltpu.SemaphoreType.DMA((7,)),
            pltpu.SemaphoreType.DMA((7,)),
            pltpu.SemaphoreType.DMA((16,)),
            pltpu.SemaphoreType.DMA((16,)),
            pltpu.SemaphoreType.DMA((4,)),
            pltpu.SemaphoreType.DMA((4,)),
        ],
        compiler_params=pltpu.CompilerParams(
            collective_id=0, has_side_effects=True, vmem_limit_bytes=63 * 2**20 + 2**19
        ),
        cost_estimate=pl.CostEstimate(
            flops=12 * tokens * dim * dim, bytes_accessed=2**25, transcendentals=0
        ),
    )(act, *tops, facts, ups, downs, down, x_one, low, out_full, coef, router)


def ring_index(place):
    place = place % 8
    upper = place // 4
    return (1 - upper) * 2 * place + upper * (2 * (7 - place) + 1)


def first_kernel(
    split_ref,
    limit_ref,
    tokens_ref,
    gain_ref,
    cos_ref,
    sin_ref,
    qkv_part,
    out_part,
    up_part,
    down_part,
    top_zero,
    onehot_ref,
    router_ref,
    gain_two_ref,
    bias_two_ref,
    qkv,
    att,
    lse,
    x_one,
    coef,
    facts,
    low_out,
    act_many,
    act_out,
    weight_out,
    out_full,
    ups,
    downs,
    top_one,
    top_two,
    top_three,
    act,
    weight,
    low,
    out_held,
    act_two,
    local_sem,
    send_sem,
    recv_sem,
    qkv_send_sem,
    qkv_recv_sem,
    low_send_sem,
    low_recv_sem,
    up_send_sem,
    up_recv_sem,
    up_local_sem,
    out_sem,
):
    w = lax.axis_index("wide")
    n = lax.axis_index("narrow")
    core, y, far, z = n % 2, n // 2, w // 4, (w // 2) % 2
    odd = w % 2
    place = w // 2 + odd * (7 - 2 * (w // 2))
    rows, dim = tokens_ref.shape
    cols = weight.shape[3] // 3
    heads = cols // HEAD_DIM
    right, left = {"wide": ring_index(place + 1)}, {"wide": ring_index(place + 7)}
    to_y, to_core = {"narrow": (n + 2) % 4}, {"narrow": n + 1 - 2 * core}
    to_z, to_x = {"wide": w + 2 - 4 * z}, {"wide": w + 1 - 2 * odd}
    to_far = {"wide": (w + 4) % 8}
    to_both = {"wide": w + 2 - 4 * z, "narrow": (n + 2) % 4}
    barrier = pltpu.get_barrier_semaphore()
    peers = [{"wide": (w + k) % 8} for k in range(1, 8)] + [to_y, to_core, to_both]
    for peer in peers:
        pl.semaphore_signal(barrier, inc=1, device_id=peer, device_id_type=MESH)
    pl.semaphore_wait(barrier, len(peers))
    started, kept = [], []
    up_zero, up_far, up_next, up_both = (ups.at[0, k] for k in range(4))
    down_next = downs.at[0, 2]

    def send(source, target, peer):
        at = len(started)
        copy = pltpu.make_async_remote_copy(
            src_ref=source,
            dst_ref=target,
            send_sem=send_sem.at[at],
            recv_sem=recv_sem.at[at],
            device_id=peer,
            device_id_type=MESH,
        )
        copy.start()
        started.append(copy)
        return copy

    def keep(source, target):
        copy = pltpu.make_async_copy(source, target, local_sem.at[len(kept)])
        copy.start()
        kept.append(copy)
        return copy

    def norm(i):
        at = pl.ds(pl.multiple_of(i * 32, 32), 32)
        value = tokens_ref[at, :].astype(f32)
        inv = lax.rsqrt(jnp.mean(value * value, axis=-1, keepdims=True) + norm_eps)
        act[w, at, :] = (value * inv * gain_ref[...]).astype(bf16)

    each(rows // 32, norm)

    first, second = pl.ds(0, rows // 2), pl.ds(rows // 2, rows // 2)
    shard = out_part.shape[0]
    out_first, out_second = pl.ds(0, shard // 2), pl.ds(shard // 2, shard // 2)
    onward = send(act.at[w], act.at[w], right)
    back = send(act.at[w], act.at[w], left)
    exchanges = []
    for k in range(1, 8):
        target = (w + k) % 8
        for part in range(3):
            source = qkv_part.at[:, pl.ds(pl.multiple_of(part * dim + target * cols, cols), cols)]
            copy = pltpu.make_async_remote_copy(
                src_ref=source,
                dst_ref=weight.at[w, n, :, pl.ds(part * cols, cols)],
                send_sem=qkv_send_sem.at[k - 1, part],
                recv_sem=qkv_recv_sem.at[k - 1, part],
                device_id={"wide": target},
                device_id_type=MESH,
            )
            copy.start()
            exchanges.append(copy)
    for part in range(3):
        source = qkv_part.at[:, pl.ds(pl.multiple_of(part * dim + w * cols, cols), cols)]
        keep(source, weight.at[w, n, :, pl.ds(part * cols, cols)])
    out_onward = send(out_part, out_full.at[w, n], right)
    out_back = send(out_part, out_full.at[w, n], left)
    out_own = keep(out_part, out_full.at[w, n])
    out_y = [send(out_part, out_full.at[w, n], to_y)]
    team = z * 2 + y
    piece = down_part.shape[0]

    def up_block(its_z, its_y, share):
        its_w = (share % 2) * 4 + its_z * 2 + (share // 2) % 2
        its_n = its_y * 2 + share // 4
        return up_part.at[:, pl.ds(pl.multiple_of((its_w * 4 + its_n) * piece, piece), piece)]

    swaps, up_own = [], []
    for share in range(8):
        target = up_zero.at[team, :, pl.ds(share * piece, piece)]
        for k, (its_z, its_y, peer) in enumerate(((z, 1 - y, to_y), (1 - z, y, to_z), (1 - z, 1 - y, to_both))):
            copy = pltpu.make_async_remote_copy(
                src_ref=up_block(its_z, its_y, share),
                dst_ref=target,
                send_sem=up_send_sem.at[k, share],
                recv_sem=up_recv_sem.at[k, share],
                device_id=peer,
                device_id_type=MESH,
            )
            copy.start()
            swaps.append(copy)
        copy = pltpu.make_async_copy(up_block(z, y, share), target, up_local_sem.at[share])
        copy.start()
        up_own.append(copy)

    def ring_hop(step):
        nonlocal onward, back, out_onward, out_back
        behind, ahead = ring_index(place + 8 - step), ring_index(place + step)
        onward.wait_recv()
        back.wait_recv()
        if step < 3:
            onward = send(act.at[behind], act.at[behind], right)
            back = send(act.at[ahead], act.at[ahead], left)
        else:
            onward = send(act.at[behind, first], act.at[behind, first], right)
            back = send(act.at[ahead, second], act.at[ahead, second], left)
        out_onward.wait_recv()
        out_back.wait_recv()
        for owner in (behind, ahead):
            out_y.append(send(out_full.at[owner, n], out_full.at[owner, n], to_y))
        if step < 3:
            out_onward = send(out_full.at[behind, n], out_full.at[behind, n], right)
            out_back = send(out_full.at[ahead, n], out_full.at[ahead, n], left)
        else:
            out_onward = send(out_full.at[behind, n, out_first], out_full.at[behind, n, out_first], right)
            out_back = send(out_full.at[ahead, n, out_second], out_full.at[ahead, n, out_second], left)

    def project(owner):
        at = pl.ds(pl.multiple_of(owner * rows, rows), rows)
        for part in range(3):
            its = weight[:, :, :, pl.ds(part * cols, cols)].reshape(dim, cols)
            value = dot(act[owner], its, ((1,), (0,)))
            for h in range(heads):
                piece = value[:, h * HEAD_DIM : (h + 1) * HEAD_DIM]
                if part < 2:
                    piece = turn(piece, cos_ref[at, :], sin_ref[at, :])
                qkv[at, pl.ds(part * cols + h * HEAD_DIM, HEAD_DIM)] = piece.astype(bf16)

    def project_pair(step):
        each(2, lambda i: project(ring_index(place + 8 - step + 2 * step * i)))

    for copy in kept[:3]:
        copy.wait()
    for copy in exchanges:
        copy.wait_recv()
    weight_y = send(weight.at[:, n], weight.at[:, n], to_y)
    ring_hop(1)
    weight_y.wait_recv()
    weight_core = [
        send(weight.at[:, n], weight.at[:, n], to_core),
        send(weight.at[:, (n + 2) % 4], weight.at[:, (n + 2) % 4], to_core),
    ]
    beside = send(top_zero, top_one, to_y)
    for copy in weight_core:
        copy.wait_recv()
    each(1, lambda i: project(w + i))
    project_pair(1)
    ring_hop(2)
    project_pair(2)
    ring_hop(3)
    for copy in swaps:
        copy.wait_recv()
    for copy in up_own:
        copy.wait()
    up_to_far = send(up_zero, up_far, to_far)
    up_to_x = send(up_zero, up_next, to_x)
    down_to_x = send(down_part, down_next, to_x)
    cores = [send(up_zero, ups.at[1, 0], to_core), send(down_part, downs.at[1, 0], to_core)]
    across = send(top_zero, top_two, to_z)
    project_pair(3)
    onward.wait_recv()
    back.wait_recv()
    project(ring_index(place + 4))
    out_onward.wait_recv()
    out_back.wait_recv()
    out_own.wait()
    last = ring_index(place + 4)
    out_y.append(send(out_full.at[last, n], out_full.at[last, n], to_y))
    keep(act, act_out)
    keep(weight, weight_out)

    split = split_ref[0]
    factor = HEAD_DIM ** (-0.5) * LOG2E
    block = 2 * rows
    limit_one, limit_two, head_first = limit_ref[0, 0], limit_ref[0, 1], limit_ref[0, 2]

    def low_send(target):
        return pltpu.make_async_remote_copy(
            src_ref=low.at[pl.ds(target * rows, rows)],
            dst_ref=low_out.at[:, pl.ds(pl.multiple_of(w * cols, cols), cols)],
            send_sem=low_send_sem.at[target],
            recv_sem=low_recv_sem.at[w],
            device_id={"wide": target},
            device_id_type=MESH,
        )

    def low_come(source):
        return pltpu.make_async_remote_copy(
            src_ref=low.at[pl.ds(source * rows, rows)],
            dst_ref=low_out.at[:, pl.ds(source * cols, cols)],
            send_sem=low_send_sem.at[source],
            recv_sem=low_recv_sem.at[source],
            device_id={"wide": source},
            device_id_type=MESH,
        )

    def low_keep(target):
        return pltpu.make_async_copy(
            low.at[pl.ds(target * rows, rows)],
            low_out.at[:, pl.ds(target * cols, cols)],
            low_send_sem.at[target],
        )

    for i in range(4):
        at_rows = pl.ds(i * block, block)
        at = i * block + lax.broadcasted_iota(jnp.int32, (block, 1), 0)
        lowest = jnp.where(at >= split, split, 0)

        def keys_of(j, state, diagonal):
            keys = pl.ds(pl.multiple_of(j * block, block), block)
            kat = j * block + lax.broadcasted_iota(jnp.int32, (block, block), 1)
            ok = kat >= lowest
            if diagonal:
                ok = ok & (kat <= at)
            found = []
            for h in range(heads):
                top, total, acc = state[h]
                q = qkv[at_rows, pl.ds(h * HEAD_DIM, HEAD_DIM)]
                k = qkv[keys, pl.ds(cols + h * HEAD_DIM, HEAD_DIM)]
                v = qkv[keys, pl.ds(2 * cols + h * HEAD_DIM, HEAD_DIM)]
                s = jnp.where(ok, dot(q, k, ((1,), (1,))) * factor, masked_score)
                new_top = jnp.maximum(top, jnp.max(s, axis=1, keepdims=True))
                p = jnp.exp2(s - new_top)
                fade = jnp.exp2(top - new_top)
                total = total * fade + jnp.sum(p, axis=1, keepdims=True)
                acc = acc * fade + dot(p.astype(bf16), v, ((1,), (0,)))
                found.append((new_top, total, acc))
            return tuple(found)

        start = (
            jnp.full((block, 1), masked_score, f32),
            jnp.zeros((block, 1), f32),
            jnp.zeros((block, HEAD_DIM), f32),
        )
        state = (start,) * heads
        if i:
            state = lax.fori_loop(0, i, functools.partial(keys_of, diagonal=False), state)
        state = keys_of(i, state, True)
        limit = jnp.where(at < split, limit_one, limit_two)
        for h in range(heads):
            top, total, acc = state[h]
            value = acc / total
            head = pl.ds(h * HEAD_DIM, HEAD_DIM)
            active = (head_first + h < limit).astype(f32)
            att[at_rows, head] = value
            low[at_rows, head] = (value * active).astype(bf16)
            lse[at_rows, head] = jnp.broadcast_to(top + jnp.log2(total), (block, HEAD_DIM))
        for target in (2 * i, 2 * i + 1):

            @pl.when(w != target)
            def _():
                low_send(target).start()

            @pl.when(w == target)
            def _():
                low_keep(target).start()

        if i == 0:
            for copy in out_y:
                copy.wait_recv()
            out_core = [
                send(out_full.at[:, n], out_full.at[:, n], to_core),
                send(out_full.at[:, (n + 2) % 4], out_full.at[:, (n + 2) % 4], to_core),
            ]
        if i == 2:
            across.wait_recv()
            both = send(top_two, top_three, to_y)
    part_rows = down_part.shape[0] // 2
    parts = [pl.ds(0, part_rows), pl.ds(part_rows, part_rows)]
    down_fars = [send(down_part.at[parts[0]], downs.at[0, 1, parts[0]], to_far)]
    up_to_far.wait_recv()
    up_to_both = send(up_far, up_both, to_x)
    cores.append(send(up_far, ups.at[1, 1], to_core))
    for copy in out_core:
        copy.wait_recv()
    held = []
    for k in range(8):
        held.append(pltpu.make_async_copy(out_full.at[k], out_held.at[k], out_sem.at[k]))
        held[-1].start()
    for target in range(8):

        @pl.when(w != target)
        def _():
            low_send(target).wait_send()
            low_come(target).wait_recv()

        @pl.when(w == target)
        def _():
            low_keep(target).wait()

    down_fars.append(send(down_part.at[parts[1]], downs.at[0, 1, parts[1]], to_far))
    for copy in held:
        copy.wait()

    def branch(t):
        at = pl.ds(pl.multiple_of(t * 256, 256), 256)
        value = dot(low_out[...], out_held[:, :, :, at].reshape(dim, 256), ((1,), (0,)))
        x_one[:, at] = tokens_ref[:, at].astype(f32) + value

    each(dim // 256, branch)
    gain_two, bias_two = gain_two_ref[...], bias_two_ref[...]
    lane = lax.broadcasted_iota(jnp.int32, (32, 8), 1)
    wide_lane = lax.broadcasted_iota(jnp.int32, (32, 128), 1)

    def normalize(i):
        at = pl.ds(pl.multiple_of(i * 32, 32), 32)
        value = x_one[at, :]
        center = value - jnp.mean(value, axis=-1, keepdims=True)
        inv = lax.rsqrt(jnp.mean(center * center, axis=-1, keepdims=True) + norm_eps)
        ln_out = center * inv * gain_two + bias_two
        act_two[at, :] = ln_out.astype(bf16)
        logits = lax.dot_general(
            ln_out, router_ref[...], (((1,), (1,)), ((), ())), precision=highest, preferred_element_type=f32
        )
        logits = jnp.where(lane < WIDTHS, logits, masked_score)
        powers = jnp.exp(logits - jnp.max(logits, axis=-1, keepdims=True))
        prob = powers / jnp.sum(powers, axis=-1, keepdims=True)
        hot = onehot_ref[at, :]
        chosen = jnp.sum(prob * hot, axis=-1, keepdims=True)
        width = jnp.sum(hot * lane.astype(f32), axis=-1, keepdims=True)
        coef[at, :] = chosen * (hot - prob)
        facts[at, :] = jnp.where(wide_lane == 0, chosen, width)

    each(rows // 32, normalize)

    def slot(k):
        return pl.ds(k * rows, rows)

    act_y = send(act_two, act_many.at[slot(1)], to_y)
    act_z = send(act_two, act_many.at[slot(2)], to_z)
    mine = facts.at[slot(0)]
    facts_y = send(mine, facts.at[slot(1)], to_y)
    facts_z = send(mine, facts.at[slot(2)], to_z)
    keep(act_two, act_many.at[slot(0)])
    up_to_x.wait_recv()
    cores.append(send(up_next, ups.at[1, 2], to_core))
    down_to_x.wait_recv()
    cores.append(send(down_next, downs.at[1, 2], to_core))
    up_to_both.wait_recv()
    cores.append(send(up_both, ups.at[1, 3], to_core))
    down_boths = []

    def down_hop(k):
        down_fars[k].wait_recv()
        down_boths.append(send(downs.at[0, 1, parts[k]], downs.at[0, 3, parts[k]], to_x))
        cores.append(send(downs.at[0, 1, parts[k]], downs.at[1, 1, parts[k]], to_core))

    down_hop(0)
    act_y.wait_recv()
    act_z.wait_recv()
    half = rows // 2
    boths = [
        send(act_many.at[pl.ds(2 * rows, half)], act_many.at[pl.ds(3 * rows, half)], to_y),
        send(act_many.at[pl.ds(rows + half, half)], act_many.at[pl.ds(3 * rows + half, half)], to_z),
    ]
    facts_y.wait_recv()
    facts_z.wait_recv()
    boths.append(send(facts.at[slot(2)], facts.at[slot(3)], to_y))
    down_hop(1)
    for copy in [beside, both] + boths:
        copy.wait_recv()
    for k in range(2):
        down_boths[k].wait_recv()
        cores.append(send(downs.at[0, 3, parts[k]], downs.at[1, 3, parts[k]], to_core))
    for copy in cores:
        copy.wait_recv()
    for copy in kept[3:]:
        if copy is not out_own:
            copy.wait()
    for copy in started + exchanges + swaps:
        copy.wait_send()


def first_sums(
    split, limits, tokens, gain, cos2, sin2, w_qkv, w_out, w_up, w_down, top, onehot, router, gain_two, bias_two
):
    rows, dim = tokens.shape
    length = 8 * rows
    shard, wide_cols = w_qkv.shape
    cols = wide_cols // 24
    any_space = pl.BlockSpec(memory_space=pl.ANY)
    in_vmem = pl.BlockSpec(memory_space=pltpu.VMEM)
    smem = pl.BlockSpec(memory_space=pltpu.SMEM)
    dma = pltpu.SemaphoreType.DMA

    def shape(*dims):
        return jax.ShapeDtypeStruct(dims, bf16)

    def full(*dims):
        return jax.ShapeDtypeStruct(dims, f32)

    flops = 6 * length * dim * cols + 4 * length * length * cols
    return pl.pallas_call(
        first_kernel,
        in_specs=[smem] * 2 + [in_vmem] * 4 + [any_space] * 5 + [in_vmem] * 4,
        out_specs=[in_vmem] * 7 + [any_space] * 9,
        out_shape=[
            shape(length, 3 * cols),
            full(length, cols),
            full(length, cols),
            full(rows, dim),
            full(rows, 8),
            full(4 * rows, 128),
            shape(rows, dim),
            shape(4 * rows, dim),
            shape(8, rows, dim),
            shape(8, 4, shard, 3 * cols),
            shape(8, 4, shard, dim),
            shape(2, 4, 4, shard, dim),
            shape(2, 4, *w_down.shape),
            shape(rows, dim),
            shape(rows, dim),
            shape(rows, dim),
        ],
        scratch_shapes=[
            pltpu.VMEM((8, rows, dim), bf16),
            pltpu.VMEM((8, 4, shard, 3 * cols), bf16),
            pltpu.VMEM((length, cols), bf16),
            pltpu.VMEM((8, 4, shard, dim), bf16),
            pltpu.VMEM((rows, dim), bf16),
            dma((8,)),
            dma((60,)),
            dma((60,)),
            dma((7, 3)),
            dma((7, 3)),
            dma((8,)),
            dma((8,)),
            dma((3, 8)),
            dma((3, 8)),
            dma((8,)),
            dma((8,)),
        ],
        compiler_params=pltpu.CompilerParams(
            collective_id=2, has_side_effects=True, vmem_limit_bytes=60 * 2**20
        ),
        cost_estimate=pl.CostEstimate(flops=flops, bytes_accessed=2**25, transcendentals=2**22),
    )(
        split, limits, tokens, gain, cos2, sin2, w_qkv, w_out, w_up, w_down, top, onehot, router, gain_two, bias_two
    )


STRIP = 128


def last_kernel(
    dproj,
    weight,
    act_ref,
    out_own,
    out_low,
    out_high,
    small_ref,
    base_ref,
    tokens_ref,
    inv_ref,
    gain_ref,
    up_zero,
    up_one,
    up_two,
    up_three,
    input_grad,
    out_grad,
    qkv_grad,
    small_out,
    up_grad,
    act_grad,
    qkv_come,
    act,
    terms,
    core_come,
    side_come,
    act_send,
    act_recv,
    out_send,
    out_recv,
    small_sum,
    small_recv,
    out_come,
    load_sem,
    ring_send_sem,
    ring_recv_sem,
    send_sem,
    recv_sem,
):
    w = lax.axis_index("wide")
    n = lax.axis_index("narrow")
    core, y = n % 2, n // 2
    odd = w % 2
    place = w // 2 + odd * (7 - 2 * (w // 2))
    dim = weight.shape[0]
    half = dim // 2
    rows = act_grad.shape[0]
    shard = out_grad.shape[0]
    aims = ({"wide": ring_index(place + 1)}, {"wide": ring_index(place + 7)})
    other_core = {"narrow": n + 1 - 2 * core}
    other_y = {"narrow": (n + 2) % 4}
    others = [{"wide": (w + k) % 8} for k in range(1, 8)]
    z = (w // 2) % 2
    barrier = pltpu.get_barrier_semaphore()
    for peer in others + [other_core, other_y]:
        pl.semaphore_signal(barrier, inc=1, device_id=peer, device_id_type=MESH)
    pl.semaphore_wait(barrier, len(others) + 2)
    load = pltpu.make_async_copy(act_ref, act, load_sem)
    load.start()
    started = []

    def send(source, target, peer):
        at = len(started)
        copy = pltpu.make_async_remote_copy(
            src_ref=source,
            dst_ref=target,
            send_sem=send_sem.at[at],
            recv_sem=recv_sem.at[at],
            device_id=peer,
            device_id_type=MESH,
        )
        copy.start()
        started.append(copy)
        return copy

    def hop(step, stream):
        if stream < 4:
            source, target, side = act_send.at[step, stream], act_recv.at[step, stream], stream // 2
        else:
            source, target, side = out_send.at[step, stream - 4], out_recv.at[step, stream - 4], stream - 4
        return pltpu.make_async_remote_copy(
            src_ref=source,
            dst_ref=target,
            send_sem=ring_send_sem.at[step, stream],
            recv_sem=ring_recv_sem.at[step, stream],
            device_id=aims[side],
            device_id_type=MESH,
        )

    def owner_of(step, side):
        return ring_index(place + 7 - step) if side == 0 else ring_index(place + 1 + step)

    def ring_step(step):
        for stream in range(4):
            side, strip = stream // 2, stream % 2
            owner = owner_of(step, side)
            at = pl.ds(pl.multiple_of(owner * rows + strip * STRIP, STRIP), STRIP)
            for part in range(2):
                cols = pl.ds(part * 512, 512)
                wide_cols = pl.ds(side * half + part * 512, 512)
                value = dot(dproj[at, :], weight[wide_cols, :], ((1,), (1,)))
                if step == 0:
                    act_send[0, stream, :, cols] = value.astype(bf16)
                elif step < 7:
                    act_send[step, stream, :, cols] = value.astype(bf16)
                else:
                    act_grad[pl.ds(strip * STRIP, STRIP), wide_cols] = value
            if step > 0:
                hop(step - 1, stream).wait_recv()

                def add(i):
                    part = pl.ds(pl.multiple_of(i * 32, 32), 32)
                    come = act_recv[step - 1, stream, part, :].astype(f32)
                    if step < 7:
                        act_send[step, stream, part, :] = (
                            act_send[step, stream, part, :].astype(f32) + come
                        ).astype(bf16)
                    else:
                        row = pl.ds(pl.multiple_of(strip * STRIP + i * 32, 32), 32)
                        act_grad[row, pl.ds(side * half, half)] += come

                each(STRIP // 32, add)
            if step < 7:
                hop(step, stream).start()

    def out_step(step):
        for stream in (4, 5):
            side = stream - 4
            owner = owner_of(step, side)
            at = pl.ds(side * half, half)
            value = out_own[owner, :, at].astype(f32) + out_come[owner, :, at].astype(f32)
            if step > 0:
                hop(step - 1, stream).wait_recv()
                value = value + out_recv[step - 1, side].astype(f32)
            if step < 7:
                out_send[step, side] = value.astype(bf16)
                hop(step, stream).start()
            else:
                out_grad[:, pl.ds(side * half, half)] = value

    ring_step(0)
    out_come[0:4] = out_low[...]
    out_come[4:8] = out_high[...]
    out_step(0)
    load.wait()
    small_sum[0] = small_ref[...]

    def weight_terms(k):
        at = pl.ds(pl.multiple_of(k * rows, rows), rows)
        value = dot(act[:, at], dproj[...], ((0,), (0,)))
        product = value * weight[at, :].astype(f32)
        ones = jnp.ones((8, product.shape[1]), f32)
        sums = lax.dot_general(
            ones, product, (((1,), (1,)), ((), ())), precision=highest, preferred_element_type=f32
        )
        small_sum[0, 0:1, at] = small_sum[0, 0:1, at] + sums[0:1]
        terms[k] = value.astype(bf16).reshape(2, 2, shard, value.shape[1])

    each(8, weight_terms)
    to_core = send(terms.at[:, :, 1 - core], core_come, other_core)

    small_peers = [other_core, other_y] + [{"wide": w + b - 2 * b * ((w // b) % 2)} for b in (1, 2, 4)]

    def small_step(k):
        if k:
            pending.pop().wait_recv()
            small_sum[k] = small_sum[k - 1] + small_recv[k - 1]
        if k < 5:
            pending.append(send(small_sum.at[k], small_recv.at[k], small_peers[k]))
        else:
            small_out[...] = small_sum[k]

    pending = []
    small_step(0)
    ring_step(1)
    out_step(1)
    to_core.wait_recv()

    def add_core(i):
        a, b = i // 2, i % 2
        here = terms[a, b, core].astype(f32)
        terms[a, b, core] = (here + core_come[a, b].astype(f32)).astype(bf16)

    each(16, add_core)
    to_side = send(terms.at[:, 1 - y, core], side_come, other_y)
    small_step(1)
    ring_step(2)
    out_step(2)
    small_step(2)
    ring_step(3)
    out_step(3)
    to_side.wait_recv()

    def add_side(i):
        here = terms[i, y, core].astype(f32)
        terms[i, y, core] = (here + side_come[i].astype(f32)).astype(bf16)

    each(8, add_side)
    own = pltpu.make_async_copy(terms.at[w, y, core], qkv_come.at[w], load_sem)
    own.start()
    blocks = []
    for k, peer in enumerate(others):
        target = (w + 1 + k) % 8
        blocks.append(send(terms.at[target, y, core], qkv_come.at[w], peer))
    small_step(3)
    ring_step(4)
    out_step(4)
    small_step(4)
    ring_step(5)
    out_step(5)
    small_step(5)
    ring_step(6)
    out_step(6)
    ring_step(7)
    out_step(7)

    def finish(i):
        at = pl.ds(pl.multiple_of(i * 32, 32), 32)
        inv = inv_ref[at, :]
        normed = tokens_ref[at, :].astype(f32) * inv
        scaled = act_grad[at, :] * gain_ref[...]
        mean = jnp.mean(scaled * normed, axis=-1, keepdims=True)
        input_grad[at, :] = base_ref[at, :] + inv * (scaled - normed * mean)

    each(rows // 32, finish)
    own.wait()
    for copy in blocks:
        copy.wait_recv()
    piece = dim // 8
    for k, block in enumerate((up_zero, up_one, up_two, up_three)):
        its_z = z + (1 - 2 * z) * (k // 2)
        its_y = y + (1 - 2 * y) * (k % 2)
        for share in range(8):
            its_w = (share % 2) * 4 + its_z * 2 + (share // 2) % 2
            at = pl.multiple_of((its_w * 4 + its_y * 2 + share // 4) * piece, piece)
            up_grad[:, pl.ds(at, piece)] = block[:, pl.ds(share * piece, piece)].astype(f32)
    cols = weight.shape[1] // 3
    for k in range(8):
        for part in range(3):
            value = qkv_come[k, :, pl.ds(part * cols, cols)].astype(f32)
            qkv_grad[:, pl.ds(part * dim + k * cols, cols)] = value
    for copy in started:
        copy.wait_send()
    for step in range(7):
        for stream in range(6):
            hop(step, stream).wait_send()


def last_sums(dproj, weight, act, out_own, out_come, small, base, tokens_in, inv, gain, ups):
    tokens, cols = dproj.shape
    dim = weight.shape[0]
    rows, shard, half = tokens // 8, dim // 32, dim // 2
    any_space = pl.BlockSpec(memory_space=pl.ANY)
    in_vmem = pl.BlockSpec(memory_space=pltpu.VMEM)
    dma = pltpu.SemaphoreType.DMA
    return pl.pallas_call(
        last_kernel,
        in_specs=[in_vmem, in_vmem, any_space] + [in_vmem] * 12,
        out_specs=[in_vmem] * 5,
        out_shape=[
            jax.ShapeDtypeStruct((rows, dim), f32),
            jax.ShapeDtypeStruct((shard, dim), f32),
            jax.ShapeDtypeStruct((shard, 3 * dim), f32),
            jax.ShapeDtypeStruct((8, dim), f32),
            jax.ShapeDtypeStruct((shard, 4 * dim), f32),
        ],
        scratch_shapes=[
            pltpu.VMEM((rows, dim), f32),
            pltpu.VMEM((8, shard, cols), bf16),
            pltpu.VMEM((tokens, dim), bf16),
            pltpu.VMEM((8, 2, 2, shard, cols), bf16),
            pltpu.VMEM((8, 2, shard, cols), bf16),
            pltpu.VMEM((8, shard, cols), bf16),
            pltpu.VMEM((7, 4, STRIP, half), bf16),
            pltpu.VMEM((7, 4, STRIP, half), bf16),
            pltpu.VMEM((7, 2, shard, half), bf16),
            pltpu.VMEM((7, 2, shard, half), bf16),
            pltpu.VMEM((6, 8, dim), f32),
            pltpu.VMEM((5, 8, dim), f32),
            pltpu.VMEM((8, shard, dim), bf16),
            dma,
            dma((7, 6)),
            dma((7, 6)),
            dma((20,)),
            dma((20,)),
        ],
        compiler_params=pltpu.CompilerParams(
            collective_id=1, has_side_effects=True, vmem_limit_bytes=60 * 2**20
        ),
        cost_estimate=pl.CostEstimate(
            flops=4 * tokens * cols * dim, bytes_accessed=2**24, transcendentals=0
        ),
    )(dproj, weight, act, out_own, *out_come, small, base, tokens_in, inv, gain, *ups)


def swap(array, axis, size, bits):
    return lax.ppermute(array, axis, [(i, i ^ bits) for i in range(size)])


def on_device(
    wide,
    narrow,
    tokens,
    gain_one,
    w_qkv,
    w_out,
    gain_two,
    bias_two,
    router,
    w_up,
    w_down,
    doc_split,
    head_count,
    width_choice,
    out_grad,
):
    rows, part_len, dim = tokens.shape
    length = part_len * wide
    heads = dim // HEAD_DIM
    hidden = w_up.shape[1]
    head_groups = wide if heads % wide == 0 else heads
    row_groups = wide // head_groups
    my_heads = heads // head_groups
    my_rows = rows // row_groups
    cols = my_heads * HEAD_DIM
    count = rows * part_len
    w_at = lax.axis_index("wide")
    n_at = lax.axis_index("narrow")
    head_at = w_at % head_groups
    row_at = (w_at // head_groups) * my_rows
    ring = Ring("wide", wide)

    def pick_rows(array):
        return lax.dynamic_slice_in_dim(array, row_at, my_rows, 0) if row_groups > 1 else array

    def put_rows(array):
        if row_groups == 1:
            return array
        whole = jnp.zeros((rows,) + array.shape[1:], array.dtype)
        return lax.dynamic_update_slice_in_dim(whole, array, row_at, 0)

    def narrow_gather(part):
        found = part[None]
        for bits in [2**k for k in range(narrow.bit_length() - 1)]:
            other = swap(found, "narrow", narrow, bits)
            mine = (n_at & bits) == 0
            found = jnp.concatenate([jnp.where(mine, found, other), jnp.where(mine, other, found)])
        return found

    def narrow_scatter(array):
        for bits in [2**k for k in range(narrow.bit_length() - 1)]:
            array = array.reshape((wide, -1, 2) + array.shape[2:])
            at = (n_at // bits) & 1
            others = lax.dynamic_index_in_dim(array, 1 - at, 2, keepdims=False)
            array = lax.dynamic_index_in_dim(array, at, 2, keepdims=False)
            array = array + swap(others, "narrow", narrow, bits)
        return array[:, 0]

    shares = wide
    upper = wide // 4
    upper_bits = [2**k for k in range(2, wide.bit_length() - 1)][::-1]

    def share_of(w, n):
        return ((n & 1) * 2 + (w & 1)) * upper + (w >> 2)

    def wide_of(share, team):
        return (share % upper) * 4 + ((team >> 1) << 1) + ((share // upper) & 1)

    def narrow_of(share, team):
        return ((team & 1) << 1) + share // (2 * upper)

    def team_of(w, n):
        return ((w >> 1) & 1) * 2 + (n >> 1)

    def beside(part):
        return swap(part, "narrow", narrow, 2)

    def across(part):
        return swap(part, "wide", wide, 2)

    def team_swap(blocks):
        team = team_of(w_at, n_at)
        mine = [lax.dynamic_index_in_dim(blocks, team ^ k, 0, keepdims=False) for k in range(4)]
        both = [(i, i ^ (2 * narrow + 2)) for i in range(wide * narrow)]
        come = jnp.stack(
            [
                mine[0],
                beside(mine[1]),
                across(mine[2]),
                lax.ppermute(mine[3], ("wide", "narrow"), both),
            ]
        )
        return jnp.stack([lax.dynamic_index_in_dim(come, team ^ k, 0, keepdims=False) for k in range(4)])

    def pick(array, at):
        return lax.dynamic_index_in_dim(array, at, 0, keepdims=False)

    exponent = np.arange(HEAD_DIM // 2, dtype=np.float64) * (2.0 / HEAD_DIM)
    angles = np.arange(length, dtype=np.float64)[:, None] * np.power(rope_base, -exponent)[None, :]
    cosine, sine = np.cos(angles).astype(np.float32), np.sin(angles).astype(np.float32)
    cos2 = jnp.asarray(np.concatenate([cosine, cosine], axis=1))
    sin2 = jnp.asarray(np.concatenate([-sine, sine], axis=1))
    split = pick_rows(doc_split)
    limits = jnp.concatenate(
        [pick_rows(head_count), jnp.full((my_rows, 1), head_at * my_heads, jnp.int32)], axis=1
    )

    inputs = tokens.astype(f32)
    inv_one = lax.rsqrt(jnp.mean(inputs * inputs, axis=-1, keepdims=True) + norm_eps)
    normed_one = inputs * inv_one
    act_one = (normed_one * gain_one).astype(bf16)

    shard = w_qkv.shape[0]
    piece_rows = w_down.shape[0]
    top = out_grad.reshape(count, dim)
    width_flat = width_choice.reshape(count)
    share = jnp.arange(shares, dtype=jnp.int32)[:, None]
    team = team_of(w_at, n_at)
    units = (wide_of(share, team) * narrow + narrow_of(share, team)) * piece_rows
    units = (units + jnp.arange(piece_rows, dtype=jnp.int32)[None, :]).reshape(1, -1)
    need = units // (hidden // WIDTHS)

    kernels = wide == 8 and narrow == 4 and rows == 1
    if kernels:
        hot = (width_flat[:, None] == jnp.arange(2 * WIDTHS, dtype=jnp.int32)[None, :]).astype(f32)
        need_row = need.astype(f32)
        router_rows = jnp.concatenate([router.T, gain_two[None], bias_two[None], need_row, need_row])
        found = first_sums(
            split,
            limits,
            tokens.reshape(count, dim),
            gain_one[None],
            cos2,
            sin2,
            w_qkv,
            w_out,
            w_up,
            w_down,
            top,
            hot,
            router_rows,
            gain_two[None],
            bias_two[None],
        )
        qkv, att, lse, x_one, coef, facts, att_low, act_many, act_flat, my_qkv, out_full, ups, downs, *tops = found
        qkv, att, lse = qkv[None], att[None], lse[None]
        act_flat = act_flat.reshape(length, dim)
        my_qkv = my_qkv.reshape(dim, 3 * cols)
        onehot = hot[:, :WIDTHS]
    else:
        blocks = w_qkv.reshape(shard, 3, head_groups, cols).transpose(2, 0, 1, 3)
        blocks = jnp.tile(blocks.reshape(head_groups, shard, 3 * cols), (row_groups, 1, 1))
        blocks = lax.all_to_all(blocks, "wide", 0, 0, tiled=True)
        my_qkv = narrow_gather(blocks).transpose(1, 0, 2, 3).reshape(dim, 3 * cols)
        out_parts = narrow_gather(lax.all_gather(w_out, "wide", axis=0, tiled=False))
        out_full = out_parts.transpose(1, 0, 2, 3).reshape(dim, dim)

        up_blocks = w_up.reshape(shard, upper, 2, 2, 2, 2, piece_rows).transpose(2, 4, 0, 5, 3, 1, 6)
        up_part = team_swap(up_blocks.reshape(4, shard, shares * piece_rows))
        top_beside = beside(top)
        act_all = jnp.zeros((my_rows, wide, part_len, dim), bf16)
        for owner, piece in ring.gather(act_one.reshape(count, dim)):
            piece = pick_rows(piece.reshape(rows, part_len, dim))
            act_all = lax.dynamic_update_slice(act_all, piece[:, None], (0, owner, 0, 0))
        act_flat = act_all.reshape(my_rows * length, dim)
        act_flat, my_qkv, up_part, top_beside, down_part, top = join(
            act_flat, my_qkv, up_part, top_beside, w_down, top
        )

        up_found = [((0, 0), up_part)]

        def spread(found, bit):
            return found + [((w ^ bit, n), swap(piece, "wide", wide, bit)) for (w, n), piece in found]

        for bit in upper_bits:
            up_found = spread(up_found, bit)
        up_near = ((1, 0), swap(up_part, "wide", wide, 1))
        down_near = ((1, 0), swap(down_part, "wide", wide, 1))
        proj = dot(act_flat, my_qkv, ((1,), (0,))).reshape(my_rows, length, 3 * cols)
        qkv, att, att_part, lse = attend(proj, split, limits, cos2, sin2, my_heads)
        sends = att_part.reshape(my_rows, wide, part_len, cols).transpose(1, 0, 2, 3)
        sends, down_part = join(sends, down_part)

        come = lax.all_to_all(sends, "wide", 0, 0, tiled=True)
        down_found = [((0, 0), down_part)]
        for bit in upper_bits:
            down_found = spread(down_found, bit)
        come, out_full = join(come, out_full)
        up_far = [((w ^ 1, n), swap(piece, "wide", wide, 1)) for (w, n), piece in up_found[1:]]
        up_found = up_found + [up_near] + up_far
        top_across = across(top)
        come = come.reshape(row_groups, head_groups, my_rows, part_len, cols)
        att_low = come.transpose(0, 2, 3, 1, 4).reshape(count, dim)

        down_far = [((w ^ 1, n), swap(piece, "wide", wide, 1)) for (w, n), piece in down_found[1:]]
        down_found = down_found + [down_near] + down_far
        top_both = beside(top_across)
        tops = (top, top_beside, top_across, top_both)
        x_one = inputs.reshape(count, dim) + dot(att_low, out_full, ((1,), (0,)))

        center = x_one - jnp.mean(x_one, axis=-1, keepdims=True)
        inv_two = lax.rsqrt(jnp.mean(center * center, axis=-1, keepdims=True) + norm_eps)
        normed_two = center * inv_two
        ln_out = normed_two * gain_two + bias_two
        act_two = ln_out.astype(bf16)
        onehot = (width_flat[:, None] == jnp.arange(WIDTHS, dtype=jnp.int32)[None, :]).astype(f32)
        router_prob = jax.nn.softmax(jnp.dot(ln_out, router, precision=highest), axis=-1)
        chosen = jnp.sum(router_prob * onehot, axis=-1)
        grad_top = top.astype(f32)
    def share_core(array):
        return pick(array, n_at & 1) + swap(pick(array, 1 - (n_at & 1)), "narrow", narrow, 1)

    def share_near(array):
        return pick(array, w_at & 1) + swap(pick(array, 1 - (w_at & 1)), "wide", wide, 1)

    def share_far(array):
        for bit in upper_bits:
            array = array.reshape((2, -1) + array.shape[1:])
            at = (w_at // bit) & 1
            array = pick(array, at) + swap(pick(array, 1 - at), "wide", wide, bit)
        return array[0]

    if kernels:
        small, block_out, grad_x_one, _, dat, out_own, *outs, down_grad, down_come, up_sum, up_come, _, _ = feed_forward(
            act_many,
            (top, *tops),
            facts,
            ups.reshape(2, 4, 2, 2, shard, shares * piece_rows),
            downs,
            w_down,
            x_one,
            att_low,
            out_full.reshape(2, 2, 2, dim // 8, dim),
            coef,
            router_rows,
        )
        dat = dat.reshape(1, length, cols)
        down_grad = (down_grad.astype(f32) + down_come.astype(f32)).reshape(piece_rows, dim)
        out_come = [outs[0], beside(outs[1])]
        up_sum = (up_sum + up_come).reshape(4, shard, shares * piece_rows)
        up_blocks = [pick(up_sum, team ^ k) for k in range(4)]
        diagonal = [(i, i ^ (2 * narrow + 2)) for i in range(wide * narrow)]
        up_blocks[1:3] = beside(up_blocks[1]), across(up_blocks[2])
        up_blocks[3] = lax.ppermute(up_blocks[3], ("wide", "narrow"), diagonal)
        counts = jnp.pad(jnp.sum(onehot, axis=0), (0, dim - WIDTHS))[None]
        small = jnp.concatenate([small[:7], counts])
    else:
        up_found = up_found + [((w, n ^ 1), swap(piece, "narrow", narrow, 1)) for (w, n), piece in up_found]
        down_found = down_found + [((w, n ^ 1), swap(p, "narrow", narrow, 1)) for (w, n), p in down_found]

        def up_target(i, k):
            w, n = lax.axis_index("wide"), lax.axis_index("narrow")
            dw, dn = up_found[i][0]
            return ((w ^ dw) & ~2 | (k & 2)) * narrow + ((n ^ dn) & 1 | ((k & 1) * 2))

        def down_target(i, k):
            dw, dn = down_found[i][0]
            return share_of(lax.axis_index("wide") ^ dw, lax.axis_index("narrow") ^ dn)

        up_mine = place([piece for _, piece in up_found], wide * narrow, up_target)
        up_mine = up_mine.reshape(dim, shares * piece_rows)
        down_mine = place([piece[None] for _, piece in down_found], shares, down_target)
        down_mine = down_mine.reshape(shares * piece_rows, dim)

        def team_gather(part):
            far = across(part)
            return jnp.concatenate([part, beside(part), far, beside(far)])

        def team_scatter(terms):
            low = beside(jnp.stack([terms[1], terms[3]])).astype(f32)
            near, far = terms[0] + low[0], terms[2] + low[1]
            return near + across(far.astype(bf16)).astype(f32)

        act_many = team_gather(act_two)
        mask = need <= team_gather(width_flat)[:, None]
        pre = jnp.maximum(dot(act_many, up_mine, ((1,), (0,))), 0.0)
        pre = jnp.where(mask, pre, 0.0).astype(bf16).astype(f32)
        hid = (pre * pre).astype(bf16)
        dmix = (jnp.concatenate(tops).astype(f32) * team_gather(chosen)[:, None]).astype(bf16)
        mixed = dot(hid, down_mine, ((1,), (0,))).astype(bf16)
        dhid = dot(dmix, down_mine, ((1,), (1,)))
        dpre = (dhid * 2.0 * pre).astype(bf16)
        dact = dot(dpre, up_mine, ((1,), (1,))).astype(bf16)
        mixed = team_scatter(mixed.reshape(4, count, dim))
        grad_act_two = team_scatter(dact.reshape(4, count, dim))
        down_sum = dot(hid, dmix, ((0,), (0,))).astype(bf16).reshape(2, 2, upper, piece_rows, dim)
        down_grad = share_far(share_near(share_core(down_sum))).astype(f32)
        up_sum = up_sums(act_many, dpre, wide, narrow, shard)
        up_sum = share_far(share_near(share_core(up_sum)))


        block_out = (x_one + mixed * chosen[:, None]).astype(bf16)
        grad_prob = jnp.sum(grad_top * mixed, axis=-1)
        grad_logits = (grad_prob * chosen)[:, None] * (onehot - router_prob)
        grad_router = lax.dot_general(ln_out, grad_logits, (((0,), (0,)), ((), ())), precision=highest)
        grad_ln = grad_act_two + jnp.dot(grad_logits, router.T, precision=highest)
        grad_gain_two = jnp.sum(grad_ln * normed_two, axis=0)
        grad_bias_two = jnp.sum(grad_ln, axis=0)
        grad_normed = grad_ln * gain_two
        grad_x_one = grad_top + inv_two * (
            grad_normed
            - jnp.mean(grad_normed, axis=-1, keepdims=True)
            - normed_two * jnp.mean(grad_normed * normed_two, axis=-1, keepdims=True)
        )

        grad_branch = grad_x_one.astype(bf16)
        grad_att = dot(grad_branch, out_full, ((1,), (1,))).astype(bf16)
        sends = grad_att.reshape(row_groups, my_rows, part_len, head_groups, cols)
        sends = sends.transpose(0, 3, 1, 2, 4).reshape(wide, my_rows, part_len, cols)
        come = lax.all_to_all(sends, "wide", 0, 0, tiled=True)
        dat = come.transpose(1, 0, 2, 3).reshape(my_rows, length, cols)
        counts = jnp.pad(jnp.sum(onehot, axis=0), (0, dim - WIDTHS))[None]
        small = [jnp.zeros((1, dim), f32), grad_gain_two[None], grad_bias_two[None], grad_router.T, counts]
        small = jnp.concatenate(small)

    dproj = attend_back(qkv, att, lse, dat, split, limits, cos2, sin2, my_heads)
    if not kernels:
        grad_out = dot(att_low, grad_branch, ((0,), (0,))).astype(bf16)
        grad_out = narrow_scatter(grad_out.reshape(wide, narrow, shard, dim))
    if not kernels:
        up_sum = team_swap(up_sum)
        up_grad = up_sum.reshape(2, 2, shard, 2, 2, upper, piece_rows).transpose(2, 5, 0, 4, 1, 3, 6)
        up_grad = up_grad.reshape(shard, hidden).astype(f32)
    normed_flat = normed_one.reshape(count, dim)

    if kernels:
        input_grad, out_proj_grad, qkv_grad, small, up_grad = last_sums(
            dproj[0],
            my_qkv,
            act_flat,
            out_own,
            out_come,
            small,
            grad_x_one,
            tokens.reshape(count, dim),
            inv_one.reshape(count, 1),
            gain_one[None],
            up_blocks,
        )
    else:
        half = dim // 2

        def one_term(owner, side):
            rows_of = lax.dynamic_slice_in_dim(dproj, owner * part_len, part_len, 1)
            rows_of = rows_of.reshape(my_rows * part_len, 3 * cols)
            term = dot(rows_of, my_qkv[side * half : (side + 1) * half], ((1,), (1,)))
            return put_rows(term.reshape(my_rows, part_len, half)).reshape(count, half)

        out_proj_grad = lax.psum_scatter(
            grad_out.reshape(wide * shard, dim), "wide", scatter_dimension=0, tiled=True
        ).astype(f32)
        grad_act_one = jnp.concatenate(ring.scatter(one_term), axis=1)
        grad_qkv = dot(act_flat, dproj.reshape(my_rows * length, 3 * cols), ((0,), (0,)))
        gain_one_part = jnp.sum(grad_qkv * my_qkv.astype(f32), axis=1)
        small = small.at[0].set(gain_one_part)
        grad_qkv = narrow_scatter(grad_qkv.astype(bf16).reshape(wide, narrow, shard, 3 * cols))
        grad_qkv = lax.all_to_all(grad_qkv, "wide", 0, 0, tiled=True).astype(f32)
        for bits in (1, 2):
            small = small + swap(small, "narrow", narrow, bits)
        for bits in [2**k for k in range(wide.bit_length() - 1)]:
            small = small + swap(small, "wide", wide, bits)
        grad_qkv = jnp.sum(grad_qkv.reshape(row_groups, head_groups, shard, 3, cols), axis=0)
        qkv_grad = grad_qkv.transpose(1, 2, 0, 3).reshape(shard, 3 * dim)
        grad_scaled = grad_act_one * gain_one
        input_grad = grad_x_one + inv_one.reshape(count, 1) * (
            grad_scaled - normed_flat * jnp.mean(grad_scaled * normed_flat, axis=-1, keepdims=True)
        )
    gain_one_grad = small[0] / gain_one
    gain_two_grad, bias_two_grad = small[1], small[2]
    router_grad = small[3 : 3 + WIDTHS].T
    counts_all = small[3 + WIDTHS, :WIDTHS]
    return (
        block_out.reshape(rows, part_len, dim),
        input_grad.reshape(rows, part_len, dim),
        qkv_grad,
        out_proj_grad,
        up_grad,
        down_grad,
        gain_one_grad,
        gain_two_grad,
        bias_two_grad,
        router_grad,
        counts_all.astype(jnp.int32),
    )


def solution(mesh):
    in_specs = (
        P("narrow", "wide", None),
        P(),
        P(("wide", "narrow"), None),
        P(("wide", "narrow"), None),
        P(),
        P(),
        P(),
        P(("wide", "narrow"), None),
        P(("wide", "narrow"), None),
        P("narrow"),
        P("narrow", None),
        P("narrow", "wide"),
        P("narrow", "wide", None),
    )
    out_specs = (
        P("narrow", "wide", None),
        P("narrow", "wide", None),
        P(("wide", "narrow"), None),
        P(("wide", "narrow"), None),
        P(("wide", "narrow"), None),
        P(("wide", "narrow"), None),
        P(),
        P(),
        P(),
        P(),
        P(),
    )
    step = functools.partial(on_device, mesh.shape["wide"], mesh.shape["narrow"])
    return jax.shard_map(step, mesh=mesh, in_specs=in_specs, out_specs=out_specs, check_vma=False)
```
